32 devices in a mesh: dp: 4 (over z), seq: 8 (over y, x, core).
Axes of the slice: x: 2, y: 2, z: 4, core: 2. Of those that a mesh axis runs over, the one named last changes fastest.
Arguments:
- byte_ids: int32 [32, 2048], P('dp', 'seq'), may hold values from 1 to 258
- lengths: int32 [32], P('dp'), may hold values from 256 to 2048, as said below
- byte_table: bfloat16 [259, 768], replicated, may hold values from -6 to 6
- conv_kernel: float32 [5, 768], replicated, may hold values from -3 to 3
- score_vector: float32 [768], replicated, may hold values from -0.3 to 0.3
- norm_gain_one: float32 [768], replicated, may hold values from 0.5 to 1.5
- qkv_weight: bfloat16 [768, 2304], replicated, may hold values from -0.109375 to 0.109375
- bias_table: float32 [32, 12], replicated, may hold values from -4 to 4
- out_weight: bfloat16 [768, 768], replicated, may hold values from -2 to 2
- norm_gain_two: float32 [768], replicated, may hold values from 0.5 to 1.5
- in_weight: bfloat16 [768, 4096], replicated, may hold values from -0.21875 to 0.21875
- down_weight: bfloat16 [2048, 768], replicated, may hold values from -0.125 to 0.125
- cotangent: bfloat16 [32, 1024, 768], P('dp', 'seq'), may hold values from -6 to 6
Outputs:
- layer_out: float32 [32, 1024, 768], P('dp', 'seq')
- grad_byte_table: float32 [259, 768], replicated
- grad_conv_kernel: float32 [5, 768], replicated
- grad_score_vector: float32 [768], replicated
- grad_gain_one: float32 [768], replicated
- grad_qkv_weight: float32 [768, 2304], P('seq', 'dp')
- grad_bias_table: float32 [32, 12], replicated
- grad_out_weight: float32 [768, 768], P('seq', 'dp')
- grad_gain_two: float32 [768], replicated
- grad_in_weight: float32 [768, 4096], P('seq', 'dp')
- grad_down_weight: float32 [2048, 768], P('seq', 'dp')
The draws below stay inside these ranges and needn't reach their ends.
Inputs may be any that keep to these rules, and one draw needn't show every extreme that they name: `lengths`: each sequence holds 2048 bytes or from 256 to 1024 bytes; among sequences k * 8 to k * 8 + 7 one or more hold 2048.
All inputs are finite; a program needn't handle non-finite values.
Results may differ from the reference program's by a relative error of at most 0.02.
Values may be sent and summed in bfloat16 or wider, within the bound.
A program may use at most 320 MiB of HBM per device.

```python
import jax
import jax.numpy as jnp
from jax import lax

D = 768
HEADS = 12
DH = 64
FF = 2048
VOCAB = 259
BUCKETS = 32
KSIZE = 5
BLOCKS = 4
B_DEV = 8
SEQ_BYTES = 2048
TOKS = 1024
SEQS = 32


def draw_lengths(key, part):
    key = jax.random.fold_in(key, 11)
    key_short, key_long, key_pick = jax.random.split(key, 3)
    shorter = jax.random.randint(key_short, (SEQS,), SEQ_BYTES // 8, SEQ_BYTES // 2 + 1)
    longer = jax.random.randint(key_long, (SEQS,), 0, 3) == 0
    chosen = jax.random.randint(key_pick, (SEQS // B_DEV,), 0, B_DEV)
    within = jnp.arange(SEQS) % B_DEV
    forced = within == jnp.repeat(chosen, B_DEV)
    return jnp.where(forced | longer, SEQ_BYTES, shorter).astype(jnp.int32)


def touch_ends(entries, rng, least, high):
    longest = entries.shape.index(max(entries.shape))
    spots = []
    for shift in (0, 1):
        where = [jax.random.randint(jax.random.fold_in(rng, axis), (), 0, length) for axis, length in enumerate(entries.shape)]
        where[longest] = (where[longest] + shift) % entries.shape[longest]
        spots.append(tuple(where))
    return entries.at[spots[0]].set(least).at[spots[1]].set(high)


def level_of(key, extent, pieces, low, largest):
    factor_of, own = 1.0, jax.random.fold_in(key, 6)
    for axis_at, shards_of in pieces:
        draws = jnp.exp(jax.random.uniform(jax.random.fold_in(own, axis_at), (shards_of,), jnp.float32, low / len(pieces), largest / len(pieces)))
        factor_of = factor_of * jnp.repeat(draws, extent[axis_at] // shards_of).reshape([-1 if axis == axis_at else 1 for axis in range(len(extent))])
    return factor_of


def centred(own_key, shape, spread, bound, cuts=(), kind=jnp.bfloat16):
    values = jax.random.normal(own_key, shape, jnp.float32) * spread
    if len(cuts) > 0:
        values = level_of(own_key, shape, cuts, -0.22, 0.18) * values
    return jnp.clip(values, min=-bound, max=bound).astype(kind)


def setup_inputs(seed: int = 0) -> dict:
    key_list = jax.random.split(jax.random.key(seed), 14)
    return {
        "byte_ids": touch_ends(jax.random.randint(key_list[0], (SEQS, SEQ_BYTES), 1, VOCAB), jax.random.fold_in(key_list[0], 1), 1, VOCAB - 1).astype(jnp.int32),
        "lengths": draw_lengths(jax.random.fold_in(key_list[13], 71), 0),
        "byte_table": centred(key_list[2], (VOCAB, D), 1.0, 6.0),
        "conv_kernel": centred(key_list[3], (KSIZE, D), 0.5, 3.0, (), jnp.float32),
        "score_vector": centred(key_list[4], (D,), 0.05, 0.3, (), jnp.float32),
        "norm_gain_one": jnp.clip(1.0 + 0.1 * jax.random.normal(key_list[5], (D,), jnp.float32), 0.5, 1.5),
        "qkv_weight": centred(key_list[6], (D, 3 * D), (4 * D) ** -0.5, 0.109375),
        "bias_table": centred(key_list[7], (BUCKETS, HEADS), 1.0, 4.0, (), jnp.float32),
        "out_weight": centred(key_list[8], (D, D), 8 ** -0.5, 2.0),
        "norm_gain_two": jnp.clip(1.0 + 0.1 * jax.random.normal(key_list[9], (D,), jnp.float32), 0.5, 1.5),
        "in_weight": centred(key_list[10], (D, 2 * FF), D ** -0.5, 0.21875),
        "down_weight": centred(key_list[11], (FF, D), FF ** -0.5, 0.125),
        "cotangent": centred(key_list[12], (SEQS, TOKS, D), 1.0, 6.0, ((0, 4), (1, 8))),
    }


highest = lax.Precision.HIGHEST
thresholds = (12, 16, 23, 32, 46, 64, 91)

@jax.custom_vjp
def low(v):
    return lax.optimization_barrier(v.astype(jnp.bfloat16)).astype(jnp.float32)

@jax.custom_vjp
def low_back(v):
    return v

def low_keep(v):
    return (low(v), None)

def low_pass(kept, grad):
    return (grad,)

def back_keep(v):
    return (v, None)

def back_low(kept, grad):
    return (low(grad),)
low.defvjp(low_keep, low_pass)
low_back.defvjp(back_keep, back_low)

def rel_bucket(relative):
    distance = jnp.abs(relative).astype(jnp.int32)
    larger = 8 + sum(((distance >= boundary).astype(jnp.int32) for boundary in thresholds))
    bucket = jnp.where(distance < 8, distance, larger)
    return (bucket + 16 * (relative > 0).astype(jnp.int32)).astype(jnp.int32)

def rms_scale(values, gain_row):
    return values * lax.rsqrt(lax.optimization_barrier(jnp.mean(values * values, axis=-1, keepdims=True)) + 1e-06) * gain_row

def block_pool(embedded, kernel, score_vector):
    half_kernel = KSIZE // 2
    padded = jnp.pad(embedded, ((half_kernel, half_kernel), (0, 0)))
    convolved = sum((kernel[offset] * padded[offset:offset + SEQ_BYTES] for offset in range(KSIZE)))
    pooled_list = []
    for block_size in range(1, BLOCKS + 1):
        block_count = -(-SEQ_BYTES // block_size)
        grown = jnp.pad(convolved, ((0, block_count * block_size - SEQ_BYTES), (0, 0)))
        block_means = lax.optimization_barrier(jnp.sum(grown.reshape(block_count, block_size, -1), axis=1)) / block_size
        pooled_list.append(jnp.repeat(block_means, block_size, axis=0)[:SEQ_BYTES])
    pooled = jnp.stack(pooled_list)
    scores = jnp.einsum('kld,d->kl', pooled, score_vector, precision=highest)
    weights = jax.nn.softmax(scores, axis=0)
    mixture = lax.optimization_barrier(jnp.sum(weights[:, :, None] * pooled, axis=0))
    return lax.optimization_barrier(jnp.mean(mixture.reshape(SEQ_BYTES // 2, 2, -1), axis=1))

def attend_all(projected, bias_table, token_valid):
    per_head = projected.reshape(TOKS, HEADS, 3, DH)
    queries = per_head[:, :, 0]
    key_rows = per_head[:, :, 1]
    values = per_head[:, :, 2]
    block_rows = min(512, TOKS)
    key_position = jnp.arange(TOKS, dtype=jnp.int32)

    @jax.checkpoint
    def one_block(first_row):
        query_rows = lax.dynamic_slice_in_dim(queries, first_row, block_rows, 0)
        query_position = first_row + jnp.arange(block_rows, dtype=jnp.int32)
        logits = jnp.einsum('qhd,khd->hqk', query_rows, key_rows, precision=highest)
        buckets = rel_bucket(key_position[None, :] - query_position[:, None])
        logits = logits + jnp.transpose(bias_table[buckets], (2, 0, 1))
        logits = jnp.where(token_valid[None, None, :], logits, -1000000000.0)
        logits = low_back(logits)
        probabilities = low(jax.nn.softmax(logits, axis=-1))
        return jnp.einsum('hqk,khd->qhd', probabilities, values, precision=highest)
    firsts = (jnp.arange(TOKS // block_rows) * block_rows).astype(jnp.int32)
    blocks_out = lax.map(one_block, firsts)
    return blocks_out.reshape(TOKS, HEADS * DH)

def forward(params, byte_row, length):
    table, kernel, score_vector, gain_one, qkv_weight, bias_table, out_weight, gain_two, in_weight, down_weight = params
    positions = jnp.arange(SEQ_BYTES, dtype=jnp.int32)
    picked = jnp.where(positions < length, byte_row, 0).astype(jnp.int32)
    embedded = table[picked]
    hidden_in = block_pool(embedded, kernel, score_vector)
    normed = low(rms_scale(hidden_in, gain_one))
    projected = low_back(low(jnp.dot(normed, qkv_weight, precision=highest)))
    token_valid = 2 * jnp.arange(TOKS, dtype=jnp.int32) < length
    attended = low_back(low(attend_all(projected, bias_table, token_valid)))
    residual = hidden_in + low_back(jnp.dot(attended, out_weight, precision=highest))
    normed_two = low(rms_scale(residual, gain_two))
    gate_up = low_back(jnp.dot(normed_two, in_weight, precision=highest))
    activated = low(jax.nn.gelu(gate_up[:, :FF], approximate=True) * gate_up[:, FF:])
    return residual + low_back(jnp.dot(activated, down_weight, precision=highest))

def reference(byte_ids, lengths, byte_table, conv_kernel, score_vector, norm_gain_one, qkv_weight, bias_table, out_weight, norm_gain_two, in_weight, down_weight, cotangent):
    params = tuple((tensor.astype(jnp.float32) for tensor in (byte_table, conv_kernel, score_vector, norm_gain_one, qkv_weight, bias_table, out_weight, norm_gain_two, in_weight, down_weight)))

    def one_sequence(totals, inputs):
        byte_row, length, upstream = inputs

        def apply_layer(values):
            return forward(values, byte_row, length)
        result, backward = jax.vjp(apply_layer, params)
        gradients = backward(upstream.astype(jnp.float32))[0]
        totals = jax.tree.map(lambda left, right: left + right, totals, gradients)
        return (totals, result)
    initial = jax.tree.map(jnp.zeros_like, params)
    totals, results = lax.scan(one_sequence, initial, (byte_ids, lengths, cotangent))
    return (results, totals[0], totals[1], totals[2], totals[3], totals[4], totals[5], totals[6], totals[7], totals[8], totals[9])
```

```python
import functools
import jax
import jax.numpy as jnp
from jax import lax
from jax.experimental import pallas as pl
from jax.experimental.pallas import tpu as pltpu
from jax.sharding import PartitionSpec as P

thresholds = (12, 16, 23, 32, 46, 64, 91)
KB = 256
NEAR = 1024
F32 = jnp.float32
BF16 = jnp.bfloat16
NT = (((1,), (1,)), ((), ()))
NN = (((1,), (0,)), ((), ()))


def rel_bucket(relative):
    distance = jnp.abs(relative)
    larger = 8 + sum(((distance >= boundary).astype(jnp.int32) for boundary in thresholds))
    bucket = jnp.where(distance < 8, distance, larger)
    return bucket + 16 * (relative > 0).astype(jnp.int32)


def near_one_hot():
    place = jnp.arange(NEAR, dtype=jnp.int32)
    relative = jnp.where(place < NEAR - 128, KB - place, KB + NEAR - place)
    return (rel_bucket(relative)[:, None] == jnp.arange(32, dtype=jnp.int32)[None, :]).astype(F32)


def dot(a, b, dims):
    return lax.dot_general(a, b, dims, preferred_element_type=F32)


def fill_bias(strip, head, row, blocks):
    base = KB * (blocks - 2)
    width = KB * (2 * blocks - 1)
    spread = jnp.broadcast_to(row, (128, NEAR))
    rolled = pltpu.roll(spread, 0, 1, stride=1, stride_axis=0)
    far_right = jnp.broadcast_to(row[:, NEAR - 1 :], (KB, 128))
    far_left = jnp.broadcast_to(row[:, 768:769], (KB, 128))
    for start in range(0, base, 128):
        strip[head, :, start : start + 128] = far_right
    strip[head, 0:128, base : base + 768] = rolled[:, :768]
    strip[head, 128:256, base : base + 128] = far_right[:128]
    strip[head, 128:256, base + 128 : base + 768] = rolled[:, :640]
    for start in range(base + 768, width, 128):
        strip[head, :, start : start + 128] = far_left


def lanes_of(head, shape):
    lane = lax.broadcasted_iota(jnp.int32, shape, 1)
    own = (lane < 64) if head == 0 else (lane >= 64)
    return own, lane - (64 if head == 0 else 0)


def fill_keys(ka, head, keys, valid):
    own, spare = lanes_of(head, keys.shape)
    row = lax.broadcasted_iota(jnp.int32, keys.shape, 0)
    masked = jnp.where(row < valid, 0.0, -1e9)
    extra = jnp.where(spare == 0, masked, jnp.where((spare >= 1) & (spare <= 3), 1.0, 0.0))
    ka[head] = jnp.where(own, keys, extra.astype(BF16))


def fwd_kernel(blocks, valid_ref, pair_ref, qkv_ref, row_ref, out_ref, aug_ref, qa, ka, vt, strip, peak, acc, probs):
    item = pl.program_id(0)
    valid = valid_ref[item]
    tokens = blocks * KB
    joined = qkv_ref[:, 0].reshape(tokens, 384)
    queries = joined[:, 0:128]
    keys = joined[:, 128:256]
    turned = joined[:, 256:384].T
    filler = jnp.where(lax.broadcasted_iota(jnp.int32, (16, tokens), 0) == 0, 1.0, 0.0).astype(BF16)
    for head in range(2):
        own, spare = lanes_of(head, queries.shape)
        qa[head] = jnp.where(own, queries, jnp.where(spare == 0, 1.0, 0.0).astype(BF16))
        fill_keys(ka, head, keys, valid)
        vt[head, 0:64] = turned[64 * head : 64 * head + 64]
        vt[head, 64:80] = filler
        fill_bias(strip, head, row_ref[0, head : head + 1, :], blocks)
    peak[...] = jnp.full_like(peak, -1e30)
    acc[...] = jnp.zeros_like(acc)

    def step(block, unused):
        first = pl.multiple_of(block * KB, KB)
        shift = pl.multiple_of((blocks - 1 - block) * KB, KB)
        for head in range(2):
            alphas = []
            for part in range(blocks):
                here = slice(part * KB, part * KB + KB)
                logits = dot(ka[head, pl.ds(first, KB), :], qa[head, here, :], NT)
                logits = logits + strip[head, :, pl.ds(shift + part * KB, KB)]
                before = peak[head, :, here]
                after = jnp.maximum(before, jnp.max(logits, axis=0, keepdims=True))
                probs[head, :, here] = jnp.exp(logits - after).astype(BF16)
                peak[head, :, here] = after
                alphas.append(jnp.exp(before - after))
            acc[head] = acc[head] * jnp.concatenate(alphas, axis=1) + dot(
                    vt[head, :, pl.ds(first, KB)], probs[head], NN
                )
        return unused

    lax.fori_loop(0, (valid + KB - 1) // KB, step, 0)
    outs = []
    rows = []
    place = lax.broadcasted_iota(jnp.int32, (64, tokens), 0)
    for head in range(2):
        total = acc[head, 64:65, :]
        outs.append(acc[head, 0:64, :] / total)
        minus = -(peak[head] + jnp.log(total))
        high = minus.astype(BF16).astype(F32)
        rest = minus - high
        middle = rest.astype(BF16).astype(F32)
        low = rest - middle
        rows.append(jnp.where(place == 0, 1.0, jnp.where(place == 1, high, jnp.where(place == 2, middle, jnp.where(place == 3, low, 0.0)))))
    out_ref[:, 0] = jnp.concatenate(outs, axis=0).T.astype(BF16).reshape(out_ref.shape[0], out_ref.shape[2], 128)
    aug_ref[0] = jnp.concatenate([rows[1], rows[0]], axis=0).T.astype(BF16)


def bwd_kernel(
    blocks, valid_ref, pair_ref, qkv_ref, out_ref, aug_ref, grad_ref, row_ref,
    dqkv_ref, bias_ref, qa, ka, va, ga, kt, strip, tally, probs, slopes, dq,
):
    item = pl.program_id(0)
    valid = valid_ref[item]
    tokens = blocks * KB
    width = KB * (2 * blocks - 1)
    local = qkv_ref.shape[2]
    joined = qkv_ref[:, 0].reshape(tokens, 384)
    queries = joined[:, 0:128]
    keys = joined[:, 128:256]
    values = joined[:, 256:384]
    grads = grad_ref[:, 0].reshape(tokens, 128)
    outs = out_ref[:, 0].reshape(tokens, 128)
    kt[...] = keys.T
    product = grads.astype(F32) * outs.astype(F32)
    high = product.astype(BF16)
    low = (product - high.astype(F32)).astype(BF16)
    row_at = lax.broadcasted_iota(jnp.int32, (128, 128), 0)
    lane_at = lax.broadcasted_iota(jnp.int32, (128, 128), 1)
    pick = jnp.where((row_at < 64) == (lane_at >= 64), -1.0, 0.0).astype(BF16)
    shifts = dot(high, pick, NN) + dot(low, pick, NN)
    shift_high = shifts.astype(BF16)
    shift_low = (shifts - shift_high.astype(F32)).astype(BF16)
    for head in range(2):
        own, spare = lanes_of(head, queries.shape)
        qa[head] = jnp.where(own, queries, aug_ref[0])
        fill_keys(ka, head, keys, valid)
        va[head] = jnp.where(own, values, jnp.where((spare == 0) | (spare == 1), 1.0, 0.0).astype(BF16))
        ga[head] = jnp.where(own, grads, jnp.where(spare == 0, shift_high, jnp.where(spare == 1, shift_low, jnp.zeros_like(shift_low))))
        fill_bias(strip, head, row_ref[0, head : head + 1, :], blocks)
    tally[...] = jnp.zeros_like(tally)
    dq[...] = jnp.zeros_like(dq)
    dqkv_ref[...] = jnp.zeros_like(dqkv_ref)

    def step(block, unused):
        first = pl.multiple_of(block * KB, KB)
        shift = pl.multiple_of((blocks - 1 - block) * KB, KB)
        key_parts = []
        value_parts = []
        for head in range(2):
            for part in range(blocks):
                here = slice(part * KB, part * KB + KB)
                there = pl.ds(shift + part * KB, KB)
                logits = dot(ka[head, pl.ds(first, KB), :], qa[head, here, :], NT)
                weights = jnp.exp(logits + strip[head, :, there])
                change = dot(va[head, pl.ds(first, KB), :], ga[head, here, :], NT)
                slope = weights * change
                tally[head, :, there] += slope
                probs[head, :, here] = weights.astype(BF16)
                slopes[head, :, here] = slope.astype(BF16)
            value_parts.append(dot(probs[head], ga[head], NN))
            key_parts.append(dot(slopes[head], qa[head], NN))
            dq[pl.ds(64 * head, 64), :] += dot(kt[pl.ds(64 * head, 64), pl.ds(first, KB)], slopes[head], NN)
        own, unused_spare = lanes_of(0, (KB, 128))
        count = KB // local
        where = pl.ds(block * count, count)
        dqkv_ref[where, 0, :, 128:256] = jnp.where(own, key_parts[0], key_parts[1]).astype(BF16).reshape(count, local, 128)
        dqkv_ref[where, 0, :, 256:384] = jnp.where(own, value_parts[0], value_parts[1]).astype(BF16).reshape(count, local, 128)
        return unused

    lax.fori_loop(0, (valid + KB - 1) // KB, step, 0)
    dqkv_ref[:, 0, :, 0:128] = dq[...].T.astype(BF16).reshape(dqkv_ref.shape[0], local, 128)
    base = KB * (blocks - 2)
    lane = lax.broadcasted_iota(jnp.int32, (1, NEAR), 1)
    flip = jnp.where(row_at + lane_at == 127, 1.0, 0.0).astype(BF16)
    for head in range(2):
        far_right = sum(tally[head, :, start : start + 128] for start in range(0, base, 128)) if base else jnp.zeros((KB, 128), F32)
        far_right = far_right[:128] + far_right[128:] + tally[head, 128:256, base : base + 128]
        left_list = [tally[head, :, start : start + 128] for start in range(base + 768, width, 128)]
        far_left = sum(left_list) if left_list else jnp.zeros((KB, 128), F32)
        near = tally[head, 0:128, base : base + 768]
        near_low = tally[head, 128:256, base + 128 : base + 768]
        near = near + jnp.concatenate([near_low, jnp.zeros((128, 128), F32)], axis=1)
        near = jnp.concatenate([near, jnp.zeros((128, NEAR - 768), F32)], axis=1)
        near_high = near.astype(BF16)
        flipped = dot(flip, near_high, NN) + dot(flip, (near - near_high.astype(F32)).astype(BF16), NN)
        rolled = pltpu.roll(flipped, NEAR - 127, 1, stride=1, stride_axis=0)
        row = jnp.sum(rolled, axis=0, keepdims=True)
        row = row + jnp.where(lane == NEAR - 1, jnp.sum(far_right), 0.0) + jnp.where(lane == 768, jnp.sum(far_left), 0.0)
        bias_ref[0, head : head + 1, :] = row


def attention_forward(qkv, rows, valid, pair):
    sources, items, local, unused = qkv.shape
    blocks = sources * local // KB
    tokens = sources * local
    width = KB * (2 * blocks - 1)
    spec = pltpu.PrefetchScalarGridSpec(
        num_scalar_prefetch=2,
        grid=(items,),
        in_specs=[
            pl.BlockSpec((sources, 1, local, 384), lambda i, v, p: (0, i, 0, 0)),
            pl.BlockSpec((1, 2, NEAR), lambda i, v, p: (p[i], 0, 0)),
        ],
        out_specs=[
            pl.BlockSpec((sources, 1, local, 128), lambda i, v, p: (0, i, 0, 0)),
            pl.BlockSpec((1, tokens, 128), lambda i, v, p: (i, 0, 0)),
        ],
        scratch_shapes=[
            pltpu.VMEM((2, tokens, 128), BF16),
            pltpu.VMEM((2, tokens, 128), BF16),
            pltpu.VMEM((2, 80, tokens), BF16),
            pltpu.VMEM((2, KB, width), F32),
            pltpu.VMEM((2, 1, tokens), F32),
            pltpu.VMEM((2, 80, tokens), F32),
            pltpu.VMEM((2, KB, tokens), BF16),
        ],
    )
    return pl.pallas_call(
        functools.partial(fwd_kernel, blocks),
        grid_spec=spec,
        out_shape=[
            jax.ShapeDtypeStruct((sources, items, local, 128), BF16),
            jax.ShapeDtypeStruct((items, tokens, 128), BF16),
        ],
        compiler_params=pltpu.CompilerParams(vmem_limit_bytes=50 * 2**20),
        cost_estimate=pl.CostEstimate(flops=items * tokens * tokens * 512, bytes_accessed=items * tokens * 2048, transcendentals=items * tokens * tokens * 2),
        name="attention_forward",
    )(valid, pair, qkv, rows)


def attention_backward(qkv, outs, aug, grads, rows, valid, pair):
    sources, items, local, unused = qkv.shape
    blocks = sources * local // KB
    tokens = sources * local
    width = KB * (2 * blocks - 1)
    big = lambda lanes: pl.BlockSpec((sources, 1, local, lanes), lambda i, v, p: (0, i, 0, 0))
    spec = pltpu.PrefetchScalarGridSpec(
        num_scalar_prefetch=2,
        grid=(items,),
        in_specs=[
            big(384),
            big(128),
            pl.BlockSpec((1, tokens, 128), lambda i, v, p: (i, 0, 0)),
            big(128),
            pl.BlockSpec((1, 2, NEAR), lambda i, v, p: (p[i], 0, 0)),
        ],
        out_specs=[
            big(384),
            pl.BlockSpec((1, 2, NEAR), lambda i, v, p: (i, 0, 0)),
        ],
        scratch_shapes=[
            pltpu.VMEM((2, tokens, 128), BF16),
            pltpu.VMEM((2, tokens, 128), BF16),
            pltpu.VMEM((2, tokens, 128), BF16),
            pltpu.VMEM((2, tokens, 128), BF16),
            pltpu.VMEM((128, tokens), BF16),
            pltpu.VMEM((2, KB, width), F32),
            pltpu.VMEM((2, KB, width), F32),
            pltpu.VMEM((2, KB, tokens), BF16),
            pltpu.VMEM((2, KB, tokens), BF16),
            pltpu.VMEM((128, tokens), F32),
        ],
    )
    return pl.pallas_call(
        functools.partial(bwd_kernel, blocks),
        grid_spec=spec,
        out_shape=[
            jax.ShapeDtypeStruct((sources, items, local, 384), BF16),
            jax.ShapeDtypeStruct((items, 2, NEAR), F32),
        ],
        compiler_params=pltpu.CompilerParams(vmem_limit_bytes=50 * 2**20),
        cost_estimate=pl.CostEstimate(flops=items * tokens * tokens * 1280, bytes_accessed=items * tokens * 4096, transcendentals=items * tokens * tokens * 2),
        name="attention_backward",
    )(valid, pair, qkv, outs, aug, grads, rows)


VPAD = 384
HALVES = 2
PAIRS = 6
TN = (((0,), (0,)), ((), ()))
SQRT_2_OVER_PI = 0.7978845608028654


def block_masks(masks, first_byte, total_bytes):
    shape = masks.shape[2:]
    conv_at = first_byte - 2 + lax.broadcasted_iota(jnp.int32, shape, 1)
    token = lax.broadcasted_iota(jnp.int32, shape, 0)
    for side in range(2):
        place = first_byte + 2 * token + side
        for size in range(1, 5):
            start = (place // size) * size
            inside = (conv_at >= start) & (conv_at < start + size) & (conv_at < total_bytes)
            masks[side, size - 1] = jnp.where(inside, 1.0 / size, 0.0)


def split_two(values):
    high = values.astype(BF16)
    return high, (values - high.astype(F32)).astype(BF16)


def permute_weight(weight, out):
    rows = weight.shape[0]
    low = lax.broadcasted_iota(jnp.int32, (rows, 128), 1) < 64
    for pair in range(PAIRS):
        at = pair * 384
        one, two, three = (weight[:, at + 128 * k : at + 128 * k + 128] for k in range(3))
        out[:, at : at + 128] = jnp.where(low, one, two)
        out[:, at + 128 : at + 256] = pltpu.roll(jnp.where(low, three, one).astype(F32), 64, 1).astype(BF16)
        out[:, at + 256 : at + 384] = jnp.where(low, two, three)


def front_kernel(
    sizes, half, place_ref, ids_ref, taps_ref, weight_ref, gain_ref, score_ref,
    hidden_ref, normed_ref, conv_ref, mix_ref, share_ref, items_ref, masks, wide, permuted,
):
    local_tokens, window, devices, span = sizes
    step = pl.program_id(0)

    @pl.when(step == 0)
    def _():
        block_masks(masks, place_ref[0], place_ref[1])
        permute_weight(weight_ref, permuted)
        if devices * items_ref.shape[1] > PAIRS * span:
            items_ref[...] = jnp.zeros_like(items_ref)

    together = ids_ref.shape[0]
    score = score_ref[...]
    score_high, score_low = split_two(score)
    row8 = lax.broadcasted_iota(jnp.int32, (16, score.shape[1]), 0)
    score_rows = jnp.where(row8 == 0, score_high.astype(F32), jnp.where(row8 == 1, score_low.astype(F32), 0.0)).astype(BF16)
    lane = lax.broadcasted_iota(jnp.int32, (window, VPAD), 1)
    width = masks.shape[3]
    for one in range(together):
        ids = ids_ref[one]
        conv = jnp.zeros((window, score.shape[1]), F32)
        for tap in range(taps_ref.shape[0]):
            hot = jnp.where(ids[:, tap : tap + 1] == lane, 1.0, 0.0).astype(BF16)
            conv = conv + dot(hot, taps_ref[tap], NN)
        high, low = split_two(conv)
        conv_ref[one, 0:window] = high
        wide[one, 0, 0:window] = high
        wide[one, 1, 0:window] = low
        if width > window:
            wide[one, :, window:width] = jnp.zeros((2, width - window, score.shape[1]), BF16)
            conv_ref[one, window:width] = jnp.zeros((width - window, score.shape[1]), BF16)
        high = wide[one, 0]
        low = wide[one, 1]
        along = jnp.sum(dot(score_rows, high, NT), axis=0, keepdims=True) + dot(score_rows, low, NT)[0:1]
        total = jnp.zeros((local_tokens, width), F32)
        kept = jnp.zeros((local_tokens, 128), F32)
        lane128 = lax.broadcasted_iota(jnp.int32, (local_tokens, 128), 1)
        for side in range(2):
            scores = [jnp.sum(masks[side, k] * along, axis=1, keepdims=True) for k in range(4)]
            top = jnp.maximum(jnp.maximum(scores[0], scores[1]), jnp.maximum(scores[2], scores[3]))
            powers = [jnp.exp(value - top) for value in scores]
            under = 1.0 / (powers[0] + powers[1] + powers[2] + powers[3])
            for k in range(4):
                share = powers[k] * under
                total = total + share * masks[side, k]
                kept = jnp.where(lane128 == 4 * side + k, share, kept)
        share_ref[one] = kept
        mix_high, mix_low = split_two(total * 0.5)
        mix_ref[one] = mix_high
        hidden = dot(mix_high, high, NN) + dot(mix_high, low, NN) + dot(mix_low, high, NN)
        hidden_ref[one] = hidden
        scale = lax.rsqrt(jnp.mean(hidden * hidden, axis=1, keepdims=True) + 1e-06)
        normed_ref[one] = (hidden * scale * gain_ref[...]).astype(BF16)
    normed = normed_ref[...].reshape(together * local_tokens, score.shape[1])
    for pair in range(PAIRS):
        piece = dot(normed, permuted[:, pair * 384 : pair * 384 + 384], NN).astype(BF16)
        for one in range(together):
            item = (step * together + one) * PAIRS + pair
            items_ref[lax.rem(item, devices), item // devices] = piece[one * local_tokens : (one + 1) * local_tokens]


def mid_kernel(
    sizes, order_ref, att_ref, hidden_ref, cot_ref, out_weight_ref, in_weight_ref, down_ref, gain_ref, *refs,
):
    local_tokens, devices, span, aliased = sizes
    refs = refs[aliased:]
    (layer_ref, act_ref, gate_up_ref, normed_ref, attended_ref, branch_ref, residual_ref, items_ref, gain_out, keep_gain) = refs
    step = pl.program_id(0)
    pieces = []
    for pair in range(PAIRS):
        item = step * PAIRS + pair
        pieces.append(att_ref[lax.rem(item, devices), item // devices])
    attended = jnp.concatenate(pieces, axis=1)
    attended_ref[0] = attended
    residual = hidden_ref[0] + dot(attended, out_weight_ref[...], NN)
    gain = gain_ref[...]
    scale = lax.rsqrt(jnp.mean(residual * residual, axis=1, keepdims=True) + 1e-06)
    normed = (residual * scale * gain).astype(BF16)
    normed_ref[0] = normed
    cot = cot_ref[0]
    hidden_units = down_ref.shape[0]
    chunk = 512
    layer = residual
    back = jnp.zeros_like(residual)
    for first in range(0, hidden_units, chunk):
        here = slice(first, first + chunk)
        there = slice(hidden_units + first, hidden_units + first + chunk)
        gate = dot(normed, in_weight_ref[:, here], NN)
        up = dot(normed, in_weight_ref[:, there], NN)
        grad = dot(cot, down_ref[here, :], NT)
        square = gate * gate
        inner = gate * (SQRT_2_OVER_PI + (SQRT_2_OVER_PI * 0.044715) * square)
        curve = jnp.tanh(inner)
        half_plus = 0.5 + 0.5 * curve
        smooth = gate * half_plus
        slope = half_plus + (0.5 * gate) * (1.0 - curve * curve) * (SQRT_2_OVER_PI + (3 * SQRT_2_OVER_PI * 0.044715) * square)
        act = (smooth * up).astype(BF16)
        grad_gate = (grad * up * slope).astype(BF16)
        grad_up = (grad * smooth).astype(BF16)
        act_ref[0, :, here] = act
        gate_up_ref[0, :, here] = grad_gate
        gate_up_ref[0, :, there] = grad_up
        layer = layer + dot(act, down_ref[here, :], NN)
        back = back + dot(grad_gate, in_weight_ref[:, here], NT) + dot(grad_up, in_weight_ref[:, there], NT)
    layer_ref[0] = layer
    weighted = gain * back
    inner_mean = jnp.mean(residual * weighted, axis=1, keepdims=True)
    grad_residual = cot.astype(F32) + scale * weighted - residual * (scale * scale * scale * inner_mean)
    residual_ref[0] = grad_residual
    branch = grad_residual.astype(BF16)
    branch_ref[0] = branch
    grad_attended = dot(branch, out_weight_ref[...], NT).astype(BF16)
    for pair in range(PAIRS):
        item = step * PAIRS + pair
        items_ref[lax.rem(item, devices), item // devices] = grad_attended[:, pair * 128 : pair * 128 + 128]

    @pl.when(step == 0)
    def _():
        keep_gain[...] = jnp.zeros_like(keep_gain)

    keep_gain[...] += jnp.sum((back * residual * scale).reshape(local_tokens // 8, 8, residual.shape[1]), axis=0)
    gain_out[...] = jnp.sum(keep_gain[...], axis=0, keepdims=True)


def back_kernel(
    sizes, place_ref, grads_ref, hidden_ref, residual_ref, conv_ref, mix_ref, share_ref, ids_ref, weight_ref, taps_ref,
    table_ref, gain_ref, score_ref, table_out, small_out, flat_out, masks, permuted, slopes, keep_gain, keep_score,
):
    local_tokens, window, devices, span = sizes
    step = pl.program_id(0)
    model = gain_ref.shape[1]

    @pl.when(step == 0)
    def _():
        block_masks(masks, place_ref[0], place_ref[1])
        permute_weight(weight_ref, permuted)
        keep_gain[...] = jnp.zeros_like(keep_gain)
        keep_score[...] = jnp.zeros_like(keep_score)

    together = hidden_ref.shape[0]
    width = masks.shape[3]
    rows = together * local_tokens
    gathered = []
    for one in range(together):
        pieces = []
        for pair in range(PAIRS):
            item = (step * together + one) * PAIRS + pair
            pieces.append(grads_ref[lax.rem(item, devices), item // devices])
        gathered.append(jnp.concatenate(pieces, axis=1))
    projected = jnp.concatenate(gathered, axis=0)
    flat_out[...] = projected.reshape(flat_out.shape)
    grad_normed = dot(projected, permuted[...], NT)
    hidden = hidden_ref[...].reshape(rows, model)
    gain = gain_ref[...]
    scale = lax.rsqrt(jnp.mean(hidden * hidden, axis=1, keepdims=True) + 1e-06)
    weighted = gain * grad_normed
    inner_mean = jnp.mean(hidden * weighted, axis=1, keepdims=True)
    grad_hidden = residual_ref[...].reshape(rows, model) + scale * weighted - hidden * (scale * scale * scale * inner_mean)
    keep_gain[...] += jnp.sum((grad_normed * hidden * scale).reshape(rows // 8, 8, model), axis=0)
    high, low = split_two(grad_hidden)
    score_high, score_low = split_two(score_ref[...])
    row_at = lax.broadcasted_iota(jnp.int32, (local_tokens, model), 0)
    vector = jnp.broadcast_to(score_ref[...].astype(BF16), (local_tokens, model))
    for one in range(together):
        own = slice(one * local_tokens, (one + 1) * local_tokens)
        conv = conv_ref[one]
        cross = 0.5 * (dot(high[own], conv, NT) + dot(low[own], conv, NT))
        kept = share_ref[one]
        total = jnp.zeros((local_tokens, width), F32)
        for side in range(2):
            shares = [kept[:, 4 * side + k : 4 * side + k + 1] for k in range(4)]
            grads = [jnp.sum(masks[side, k] * cross, axis=1, keepdims=True) for k in range(4)]
            mean = sum(share * grad for share, grad in zip(shares, grads))
            for k in range(4):
                total = total + (shares[k] * (grads[k] - mean)) * masks[side, k]
        column = jnp.sum(total, axis=0, keepdims=True)
        column_high, column_low = split_two(column)
        row16 = lax.broadcasted_iota(jnp.int32, (16, width), 0)
        column_rows = jnp.where(row16 == 0, column_high.astype(F32), jnp.where(row16 == 1, column_low.astype(F32), 0.0)).astype(BF16)
        keep_score[...] += dot(column_rows, conv, NN)
        left = jnp.concatenate([mix_ref[one], total.astype(BF16)], axis=0)
        right = jnp.concatenate([high[own], vector], axis=0)
        slope = dot(left, right, TN)
        slopes[pl.ds((step * together + one) * window, window), :] = slope[0:window].astype(BF16)

    @pl.when(step == pl.num_programs(0) - 1)
    def _():
        count = slopes.shape[0]
        row = lax.broadcasted_iota(jnp.int32, (VPAD, count), 0)
        table_grad = jnp.zeros((VPAD, model), F32)
        table = table_ref[...].astype(F32)
        small_row = lax.broadcasted_iota(jnp.int32, (8, model), 0)
        small = jnp.where(small_row == 5, jnp.sum(keep_gain[...], axis=0, keepdims=True), 0.0)
        small = jnp.where(small_row == 6, jnp.sum(keep_score[...], axis=0, keepdims=True), small)
        for tap in range(taps_ref.shape[0]):
            hot = jnp.where(ids_ref[tap : tap + 1, :] == row, 1.0, 0.0).astype(BF16)
            sums = dot(hot, slopes[...], NN)
            table_grad = table_grad + taps_ref[tap : tap + 1, :] * sums
            small = jnp.where(small_row == tap, jnp.sum(sums * table, axis=0, keepdims=True), small)
        table_out[...] = table_grad
        small_out[...] = small


VMEM_LIMIT = 56 * 2**20


def call_front(half, place, ids, taps, weight, gain, score, local_tokens, devices, per_device):
    span = ids.shape[0]
    window = ids.shape[1]
    width = -(-window // 128) * 128
    model = weight.shape[0]
    together = 2
    whole = lambda *shape: pl.BlockSpec(shape, lambda s, *_: (0,) * len(shape))
    part = lambda *shape: pl.BlockSpec(shape, lambda s, *_: (s,) + (0,) * (len(shape) - 1))
    return pl.pallas_call(
        functools.partial(front_kernel, (local_tokens, window, devices, span), half),
        grid_spec=pltpu.PrefetchScalarGridSpec(
            num_scalar_prefetch=1,
            grid=(span // together,),
            in_specs=[part(together, window, 8), whole(*taps.shape), whole(*weight.shape), whole(1, model), whole(1, model)],
            out_specs=[
                part(together, local_tokens, model),
                part(together, local_tokens, model),
                part(together, width, model),
                part(together, local_tokens, width),
                part(together, local_tokens, 128),
                whole(devices, per_device, local_tokens, 384),
            ],
            scratch_shapes=[
                pltpu.VMEM((2, 4, local_tokens, width), F32),
                pltpu.VMEM((together, 2, width, model), BF16),
                pltpu.VMEM(weight.shape, BF16),
            ],
        ),
        out_shape=[
            jax.ShapeDtypeStruct((span, local_tokens, model), F32),
            jax.ShapeDtypeStruct((span, local_tokens, model), BF16),
            jax.ShapeDtypeStruct((span, width, model), BF16),
            jax.ShapeDtypeStruct((span, local_tokens, width), BF16),
            jax.ShapeDtypeStruct((span, local_tokens, 128), F32),
            jax.ShapeDtypeStruct((devices, per_device, local_tokens, 384), BF16),
        ],
        compiler_params=pltpu.CompilerParams(vmem_limit_bytes=VMEM_LIMIT),
        cost_estimate=pl.CostEstimate(flops=8 * 10**9, bytes_accessed=2 * 10**7, transcendentals=10**5),
        name="front",
    )(place, ids, taps, weight, gain, score)


def call_mid(half, order, att, hidden, cot, out_weight, in_weight, down_weight, gain, before):
    devices, per_device, local_tokens, unused = att.shape
    span, unused, model = hidden.shape
    sequences = cot.shape[0]
    hidden_units = down_weight.shape[0]
    aliased = len(before)
    whole = lambda *shape: pl.BlockSpec(shape, lambda s, *_: (0,) * len(shape))
    moved = lambda lanes: pl.BlockSpec((1, local_tokens, lanes), lambda s, order: (order[half * span + s], 0, 0))
    part = lambda lanes: pl.BlockSpec((1, local_tokens, lanes), lambda s, order: (s, 0, 0))
    full = lambda lanes, kind: jax.ShapeDtypeStruct((sequences, local_tokens, lanes), kind)
    return pl.pallas_call(
        functools.partial(mid_kernel, (local_tokens, devices, span, aliased)),
        grid_spec=pltpu.PrefetchScalarGridSpec(
            num_scalar_prefetch=1,
            grid=(span,),
            in_specs=[
                whole(*att.shape),
                part(model),
                moved(model),
                whole(*out_weight.shape),
                whole(*in_weight.shape),
                whole(*down_weight.shape),
                whole(1, model),
            ]
            + [pl.BlockSpec(memory_space=pl.ANY)] * aliased,
            out_specs=[
                moved(model),
                moved(hidden_units),
                moved(2 * hidden_units),
                moved(model),
                moved(model),
                moved(model),
                part(model),
                whole(*att.shape),
                whole(1, model),
            ],
            scratch_shapes=[pltpu.VMEM((8, model), F32)],
        ),
        out_shape=[
            full(model, F32),
            full(hidden_units, BF16),
            full(2 * hidden_units, BF16),
            full(model, BF16),
            full(model, BF16),
            full(model, BF16),
            jax.ShapeDtypeStruct((span, local_tokens, model), F32),
            jax.ShapeDtypeStruct(att.shape, BF16),
            jax.ShapeDtypeStruct((1, model), F32),
        ],
        input_output_aliases={8 + k: k for k in range(aliased)},
        compiler_params=pltpu.CompilerParams(vmem_limit_bytes=VMEM_LIMIT),
        cost_estimate=pl.CostEstimate(flops=11 * 10**9, bytes_accessed=4 * 10**7, transcendentals=10**6),
        name="middle",
    )(order, att, hidden, cot, out_weight, in_weight, down_weight, gain, *before)


def call_back(place, grads, hidden, residual, conv, mix, share, ids, weight, taps, table, gain, score):
    devices, per_device, local_tokens, unused = grads.shape
    span, unused, model = hidden.shape
    width = conv.shape[1]
    window = ids.shape[1] // span
    together = 2
    whole = lambda *shape: pl.BlockSpec(shape, lambda s, *_: (0,) * len(shape))
    part = lambda *shape: pl.BlockSpec(shape, lambda s, *_: (s,) + (0,) * (len(shape) - 1))
    return pl.pallas_call(
        functools.partial(back_kernel, (local_tokens, window, devices, span)),
        grid_spec=pltpu.PrefetchScalarGridSpec(
            num_scalar_prefetch=1,
            grid=(span // together,),
            in_specs=[
                whole(*grads.shape),
                part(together, local_tokens, model),
                part(together, local_tokens, model),
                part(together, width, model),
                part(together, local_tokens, width),
                part(together, local_tokens, 128),
                whole(*ids.shape),
                whole(*weight.shape),
                whole(*taps.shape),
                whole(*table.shape),
                whole(1, model),
                whole(1, model),
            ],
            out_specs=[whole(VPAD, model), whole(8, model), part(together, local_tokens, PAIRS * 384)],
            scratch_shapes=[
                pltpu.VMEM((2, 4, local_tokens, width), F32),
                pltpu.VMEM(weight.shape, BF16),
                pltpu.VMEM((span * window, model), BF16),
                pltpu.VMEM((8, model), F32),
                pltpu.VMEM((16, model), F32),
            ],
        ),
        out_shape=[
            jax.ShapeDtypeStruct((VPAD, model), F32),
            jax.ShapeDtypeStruct((8, model), F32),
            jax.ShapeDtypeStruct((span, local_tokens, PAIRS * 384), BF16),
        ],
        compiler_params=pltpu.CompilerParams(vmem_limit_bytes=VMEM_LIMIT),
        cost_estimate=pl.CostEstimate(flops=8 * 10**9, bytes_accessed=2 * 10**7, transcendentals=10**5),
        name="back",
    )(place, grads, hidden, residual, conv, mix, share, ids, weight, taps, table, gain, score)


def body(
    byte_ids,
    lengths,
    byte_table,
    conv_kernel,
    score_vector,
    norm_gain_one,
    qkv_weight,
    bias_table,
    out_weight,
    norm_gain_two,
    in_weight,
    down_weight,
    cotangent,
):
    devices = lax.axis_size("seq")
    me = lax.axis_index("seq")
    sequences, local_bytes = byte_ids.shape
    local_tokens = local_bytes // 2
    total_bytes = local_bytes * devices
    first_byte = me * local_bytes
    vocab, model = byte_table.shape
    span = sequences // HALVES
    window = local_bytes + 16
    per_device = -(-span * PAIRS // devices)
    place = jnp.stack([first_byte, jnp.int32(total_bytes)]).astype(jnp.int32)

    number = jnp.arange(sequences, dtype=jnp.int32)
    ahead = (lengths[None, :] > lengths[:, None]) | (
        (lengths[None, :] == lengths[:, None]) & (number[None, :] < number[:, None])
    )
    rank = jnp.sum(ahead.astype(jnp.int32), axis=1)
    placed = rank[None, :] == number[:, None]
    order = jnp.sum(jnp.where(placed, number[None, :], 0), axis=1)
    sorted_lengths = jnp.sum(jnp.where(placed, lengths[None, :], 0), axis=1)
    positions = first_byte + jnp.arange(local_bytes, dtype=jnp.int32)
    picked = jnp.where(positions[None, :] < lengths[:, None], byte_ids, 0)
    forward = [(i, i + 1) for i in range(devices - 1)]
    backward = [(target, source) for source, target in forward]
    before = jnp.where(me > 0, lax.ppermute(picked[:, -4:], "seq", forward), -1)
    after = jnp.where(me < devices - 1, lax.ppermute(picked[:, :4], "seq", backward), -1)
    outside = jnp.full((sequences, 12), -1, jnp.int32)
    extended = jnp.concatenate([before, picked, after, outside], axis=1)
    extended = jnp.sum(jnp.where(placed[:, :, None], extended[None, :, :], 0), axis=1)
    shifted = jnp.stack([extended[:, tap : tap + window] for tap in range(5)])
    ids_columns = jnp.concatenate([jnp.moveaxis(shifted, 0, 2), jnp.full((sequences, window, 3), -1, jnp.int32)], axis=2)

    table_padded = jnp.concatenate([byte_table, jnp.zeros((VPAD - vocab, model), BF16)], axis=0)
    taps = (conv_kernel[:, None, :] * table_padded.astype(F32)[None]).astype(BF16)
    rows = jnp.dot(near_one_hot(), bias_table, precision="highest").T.reshape(PAIRS, 2, NEAR)
    gain_one = norm_gain_one[None, :]
    gain_two = norm_gain_two[None, :]
    score = score_vector[None, :]

    def exchange(items):
        return lax.all_to_all(items, "seq", split_axis=0, concat_axis=0, tiled=True)

    valids, pairs = [], []
    for half in range(HALVES):
        item = me + devices * jnp.arange(per_device, dtype=jnp.int32)
        real = item < span * PAIRS
        at = half * span + item // PAIRS
        length = jnp.sum(jnp.where(at[:, None] == number[None, :], sorted_lengths[None, :], 0), axis=1)
        valids.append(jnp.where(real, (length + 1) // 2, 0).astype(jnp.int32))
        pairs.append(lax.rem(item, PAIRS).astype(jnp.int32))

    fronts, received, outs, augs, returned = [], [], [], [], []
    for half in range(HALVES):
        here = slice(half * span, half * span + span)
        front = call_front(half, place, ids_columns[here], taps, qkv_weight, gain_one, score, local_tokens, devices, per_device)
        fronts.append(front)
        received.append(exchange(front[5]))
    for half in range(HALVES):
        out, aug = attention_forward(received[half], rows, valids[half], pairs[half])
        outs.append(out)
        augs.append(aug)
        returned.append(exchange(out))
    mids, grad_items = [], []
    before_mid = ()
    for half in range(HALVES):
        mid = call_mid(half, order, returned[half], fronts[half][0], cotangent, out_weight, in_weight, down_weight, gain_two, before_mid)
        before_mid = tuple(mid[:6])
        mids.append(mid)
        grad_items.append(exchange(mid[7]))
    layer_out, act, gate_up, normed_two, attended, branch = mids[-1][:6]
    grad_gain_two = mids[0][8] + mids[1][8]
    grad_down = jnp.einsum("bti,btd->id", act, cotangent, preferred_element_type=F32).astype(BF16)
    grad_in = jnp.einsum("btd,bti->di", normed_two, gate_up, preferred_element_type=F32).astype(BF16)
    grad_out = jnp.einsum("btd,bte->de", attended, branch, preferred_element_type=F32).astype(BF16)

    def scatter(grad):
        rows_own = lax.psum_scatter(grad, "seq", scatter_dimension=0, tiled=True)
        return lax.psum_scatter(rows_own, "dp", scatter_dimension=1, tiled=True).astype(F32)

    summed_down = scatter(grad_down)
    summed_in = scatter(grad_in)
    summed_out = scatter(grad_out)
    back_items, bias_rows = [], []
    for half in range(HALVES):
        dqkv, bias_row = attention_backward(received[half], outs[half], augs[half], grad_items[half], rows, valids[half], pairs[half])
        back_items.append(exchange(dqkv))
        bias_rows.append(bias_row)
    backs = []
    for half in range(HALVES):
        hidden, normed, conv, mix, share, unused = fronts[half]
        ids_rows = shifted[:, half * span : half * span + span].reshape(5, span * window)
        backs.append(
            call_back(place, back_items[half], hidden, mids[half][6], conv, mix, share, ids_rows, qkv_weight, conv_kernel, table_padded, gain_one, score)
        )
    normed_all = jnp.concatenate([front[1] for front in fronts], axis=0)
    projected_all = jnp.concatenate([back[2] for back in backs], axis=0)
    grad_qkv = jnp.einsum("btd,bte->de", normed_all, projected_all, preferred_element_type=F32).astype(BF16)
    grad_qkv = jnp.swapaxes(grad_qkv.reshape(model, PAIRS, 3, 2, 64), 2, 3).reshape(model, PAIRS * 384)
    summed_qkv = scatter(grad_qkv)
    item_rows = jnp.concatenate(bias_rows, axis=0)
    item_bias = jnp.einsum("ihy,yb->bih", item_rows, near_one_hot(), precision="highest")
    pair_hot = (jnp.concatenate(pairs)[:, None] == jnp.arange(PAIRS, dtype=jnp.int32)[None, :]).astype(F32)
    grad_bias = jnp.einsum("bih,ip->bph", item_bias, pair_hot, precision="highest").reshape(32, 2 * PAIRS)
    grad_table = (backs[0][0] + backs[1][0])[:vocab]
    small = backs[0][1] + backs[1][1]
    totals = lax.psum((grad_table, small[0:5], small[6], small[5], grad_bias, grad_gain_two[0]), ("dp", "seq"))
    return (
        layer_out,
        totals[0],
        totals[1],
        totals[2],
        totals[3],
        summed_qkv,
        totals[4],
        summed_out,
        totals[5],
        summed_in,
        summed_down,
    )


def solution(mesh):
    return jax.shard_map(
        body,
        mesh=mesh,
        in_specs=(
            P("dp", "seq"),
            P("dp"),
            P(),
            P(),
            P(),
            P(),
            P(),
            P(),
            P(),
            P(),
            P(),
            P(),
            P("dp", "seq", None),
        ),
        out_specs=(
            P("dp", "seq", None),
            P(),
            P(),
            P(),
            P(),
            P("seq", "dp"),
            P(),
            P("seq", "dp"),
            P(),
            P("seq", "dp"),
            P("seq", "dp"),
        ),
        check_vma=False,
    )
```

```python
import functools
import jax
import jax.numpy as jnp
from jax import lax
from jax.experimental import pallas as pl
from jax.experimental.pallas import tpu as pltpu
from jax.sharding import PartitionSpec as P

thresholds = (12, 16, 23, 32, 46, 64, 91)
KB = 256
NEAR = 1024
F32 = jnp.float32
BF16 = jnp.bfloat16
NT = (((1,), (1,)), ((), ()))
NN = (((1,), (0,)), ((), ()))


def rel_bucket(relative):
    distance = jnp.abs(relative)
    larger = 8 + sum(((distance >= boundary).astype(jnp.int32) for boundary in thresholds))
    bucket = jnp.where(distance < 8, distance, larger)
    return bucket + 16 * (relative > 0).astype(jnp.int32)


def near_one_hot():
    place = jnp.arange(NEAR, dtype=jnp.int32)
    relative = jnp.where(place < NEAR - 128, KB - place, KB + NEAR - place)
    return (rel_bucket(relative)[:, None] == jnp.arange(32, dtype=jnp.int32)[None, :]).astype(F32)


def dot(a, b, dims):
    return lax.dot_general(a, b, dims, preferred_element_type=F32)


def fill_bias(strip, head, row, blocks):
    base = KB * (blocks - 2)
    width = KB * (2 * blocks - 1)
    spread = jnp.broadcast_to(row, (128, NEAR))
    rolled = pltpu.roll(spread, 0, 1, stride=1, stride_axis=0)
    far_right = jnp.broadcast_to(row[:, NEAR - 1 :], (KB, 128))
    far_left = jnp.broadcast_to(row[:, 768:769], (KB, 128))
    for start in range(0, base, 128):
        strip[head, :, start : start + 128] = far_right
    strip[head, 0:128, base : base + 768] = rolled[:, :768]
    strip[head, 128:256, base : base + 128] = far_right[:128]
    strip[head, 128:256, base + 128 : base + 768] = rolled[:, :640]
    for start in range(base + 768, width, 128):
        strip[head, :, start : start + 128] = far_left


def lanes_of(head, shape):
    lane = lax.broadcasted_iota(jnp.int32, shape, 1)
    own = (lane < 64) if head == 0 else (lane >= 64)
    return own, lane - (64 if head == 0 else 0)


def fill_keys(ka, head, keys, valid):
    own, spare = lanes_of(head, keys.shape)
    row = lax.broadcasted_iota(jnp.int32, keys.shape, 0)
    masked = jnp.where(row < valid, 0.0, -1e9)
    extra = jnp.where(spare == 0, masked, jnp.where((spare >= 1) & (spare <= 3), 1.0, 0.0))
    ka[head] = jnp.where(own, keys, extra.astype(BF16))


def fwd_kernel(blocks, valid_ref, pair_ref, qkv_ref, row_ref, out_ref, aug_ref, qa, ka, vt, strip, peak, acc, probs):
    item = pl.program_id(0)
    valid = valid_ref[item]
    tokens = blocks * KB
    joined = qkv_ref[:, 0].reshape(tokens, 384)
    queries = joined[:, 0:128]
    keys = joined[:, 128:256]
    turned = joined[:, 256:384].T
    filler = jnp.where(lax.broadcasted_iota(jnp.int32, (16, tokens), 0) == 0, 1.0, 0.0).astype(BF16)
    for head in range(2):
        own, spare = lanes_of(head, queries.shape)
        qa[head] = jnp.where(own, queries, jnp.where(spare == 0, 1.0, 0.0).astype(BF16))
        fill_keys(ka, head, keys, valid)
        vt[head, 0:64] = turned[64 * head : 64 * head + 64]
        vt[head, 64:80] = filler
        fill_bias(strip, head, row_ref[0, head : head + 1, :], blocks)
    peak[...] = jnp.full_like(peak, -1e30)
    acc[...] = jnp.zeros_like(acc)

    def step(block, unused):
        first = pl.multiple_of(block * KB, KB)
        shift = pl.multiple_of((blocks - 1 - block) * KB, KB)
        for head in range(2):
            alphas = []
            for part in range(blocks):
                here = slice(part * KB, part * KB + KB)
                logits = dot(ka[head, pl.ds(first, KB), :], qa[head, here, :], NT)
                logits = logits + strip[head, :, pl.ds(shift + part * KB, KB)]
                before = peak[head, :, here]
                after = jnp.maximum(before, jnp.max(logits, axis=0, keepdims=True))
                probs[head, :, here] = jnp.exp(logits - after).astype(BF16)
                peak[head, :, here] = after
                alphas.append(jnp.exp(before - after))
            acc[head] = acc[head] * jnp.concatenate(alphas, axis=1) + dot(
                    vt[head, :, pl.ds(first, KB)], probs[head], NN
                )
        return unused

    lax.fori_loop(0, (valid + KB - 1) // KB, step, 0)
    outs = []
    rows = []
    place = lax.broadcasted_iota(jnp.int32, (64, tokens), 0)
    for head in range(2):
        total = acc[head, 64:65, :]
        outs.append(acc[head, 0:64, :] / total)
        minus = -(peak[head] + jnp.log(total))
        high = minus.astype(BF16).astype(F32)
        rest = minus - high
        middle = rest.astype(BF16).astype(F32)
        low = rest - middle
        rows.append(jnp.where(place == 0, 1.0, jnp.where(place == 1, high, jnp.where(place == 2, middle, jnp.where(place == 3, low, 0.0)))))
    out_ref[:, 0] = jnp.concatenate(outs, axis=0).T.astype(BF16).reshape(out_ref.shape[0], out_ref.shape[2], 128)
    aug_ref[0] = jnp.concatenate([rows[1], rows[0]], axis=0).T.astype(BF16)


def bwd_kernel(
    blocks, valid_ref, pair_ref, qkv_ref, out_ref, aug_ref, grad_ref, row_ref, after,
    dqkv_ref, bias_ref, qa, ka, va, ga, kt, strip, tally, probs, slopes, dq,
):
    item = pl.program_id(0)
    valid = valid_ref[item]
    tokens = blocks * KB
    width = KB * (2 * blocks - 1)
    local = qkv_ref.shape[2]
    joined = qkv_ref[:, 0].reshape(tokens, 384)
    queries = joined[:, 0:128]
    keys = joined[:, 128:256]
    values = joined[:, 256:384]
    grads = grad_ref[:, 0].reshape(tokens, 128)
    outs = out_ref[:, 0].reshape(tokens, 128)
    kt[...] = keys.T
    product = grads.astype(F32) * outs.astype(F32)
    high = product.astype(BF16)
    low = (product - high.astype(F32)).astype(BF16)
    row_at = lax.broadcasted_iota(jnp.int32, (128, 128), 0)
    lane_at = lax.broadcasted_iota(jnp.int32, (128, 128), 1)
    pick = jnp.where((row_at < 64) == (lane_at >= 64), -1.0, 0.0).astype(BF16)
    shifts = dot(high, pick, NN) + dot(low, pick, NN)
    shift_high = shifts.astype(BF16)
    shift_low = (shifts - shift_high.astype(F32)).astype(BF16)
    for head in range(2):
        own, spare = lanes_of(head, queries.shape)
        qa[head] = jnp.where(own, queries, aug_ref[0])
        fill_keys(ka, head, keys, valid)
        va[head] = jnp.where(own, values, jnp.where((spare == 0) | (spare == 1), 1.0, 0.0).astype(BF16))
        ga[head] = jnp.where(own, grads, jnp.where(spare == 0, shift_high, jnp.where(spare == 1, shift_low, jnp.zeros_like(shift_low))))
        fill_bias(strip, head, row_ref[0, head : head + 1, :], blocks)
    tally[...] = jnp.zeros_like(tally)
    dq[...] = jnp.zeros_like(dq)
    dqkv_ref[...] = jnp.zeros_like(dqkv_ref)

    def step(block, unused):
        first = pl.multiple_of(block * KB, KB)
        shift = pl.multiple_of((blocks - 1 - block) * KB, KB)
        key_parts = []
        value_parts = []
        for head in range(2):
            for part in range(blocks):
                here = slice(part * KB, part * KB + KB)
                there = pl.ds(shift + part * KB, KB)
                logits = dot(ka[head, pl.ds(first, KB), :], qa[head, here, :], NT)
                weights = jnp.exp(logits + strip[head, :, there])
                change = dot(va[head, pl.ds(first, KB), :], ga[head, here, :], NT)
                slope = weights * change
                tally[head, :, there] += slope
                probs[head, :, here] = weights.astype(BF16)
                slopes[head, :, here] = slope.astype(BF16)
            value_parts.append(dot(probs[head], ga[head], NN))
            key_parts.append(dot(slopes[head], qa[head], NN))
            dq[pl.ds(64 * head, 64), :] += dot(kt[pl.ds(64 * head, 64), pl.ds(first, KB)], slopes[head], NN)
        own, unused_spare = lanes_of(0, (KB, 128))
        count = KB // local
        where = pl.ds(block * count, count)
        dqkv_ref[where, 0, :, 128:256] = jnp.where(own, key_parts[0], key_parts[1]).astype(BF16).reshape(count, local, 128)
        dqkv_ref[where, 0, :, 256:384] = jnp.where(own, value_parts[0], value_parts[1]).astype(BF16).reshape(count, local, 128)
        return unused

    lax.fori_loop(0, (valid + KB - 1) // KB, step, 0)
    dqkv_ref[:, 0, :, 0:128] = dq[...].T.astype(BF16).reshape(dqkv_ref.shape[0], local, 128)
    base = KB * (blocks - 2)
    lane = lax.broadcasted_iota(jnp.int32, (1, NEAR), 1)
    flip = jnp.where(row_at + lane_at == 127, 1.0, 0.0).astype(BF16)
    for head in range(2):
        far_right = sum(tally[head, :, start : start + 128] for start in range(0, base, 128)) if base else jnp.zeros((KB, 128), F32)
        far_right = far_right[:128] + far_right[128:] + tally[head, 128:256, base : base + 128]
        left_list = [tally[head, :, start : start + 128] for start in range(base + 768, width, 128)]
        far_left = sum(left_list) if left_list else jnp.zeros((KB, 128), F32)
        near = tally[head, 0:128, base : base + 768]
        near_low = tally[head, 128:256, base + 128 : base + 768]
        near = near + jnp.concatenate([near_low, jnp.zeros((128, 128), F32)], axis=1)
        near = jnp.concatenate([near, jnp.zeros((128, NEAR - 768), F32)], axis=1)
        near_high = near.astype(BF16)
        flipped = dot(flip, near_high, NN) + dot(flip, (near - near_high.astype(F32)).astype(BF16), NN)
        rolled = pltpu.roll(flipped, NEAR - 127, 1, stride=1, stride_axis=0)
        row = jnp.sum(rolled, axis=0, keepdims=True)
        row = row + jnp.where(lane == NEAR - 1, jnp.sum(far_right), 0.0) + jnp.where(lane == 768, jnp.sum(far_left), 0.0)
        bias_ref[0, head : head + 1, :] = row


def attention_forward(qkv, rows, valid, pair):
    sources, items, local, unused = qkv.shape
    blocks = sources * local // KB
    tokens = sources * local
    width = KB * (2 * blocks - 1)
    spec = pltpu.PrefetchScalarGridSpec(
        num_scalar_prefetch=2,
        grid=(items,),
        in_specs=[
            pl.BlockSpec((sources, 1, local, 384), lambda i, v, p: (0, i, 0, 0)),
            pl.BlockSpec((1, 2, NEAR), lambda i, v, p: (p[i], 0, 0)),
        ],
        out_specs=[
            pl.BlockSpec((sources, 1, local, 128), lambda i, v, p: (0, i, 0, 0)),
            pl.BlockSpec((1, tokens, 128), lambda i, v, p: (i, 0, 0)),
        ],
        scratch_shapes=[
            pltpu.VMEM((2, tokens, 128), BF16),
            pltpu.VMEM((2, tokens, 128), BF16),
            pltpu.VMEM((2, 80, tokens), BF16),
            pltpu.VMEM((2, KB, width), F32),
            pltpu.VMEM((2, 1, tokens), F32),
            pltpu.VMEM((2, 80, tokens), F32),
            pltpu.VMEM((2, KB, tokens), BF16),
        ],
    )
    return pl.pallas_call(
        functools.partial(fwd_kernel, blocks),
        grid_spec=spec,
        out_shape=[
            jax.ShapeDtypeStruct((sources, items, local, 128), BF16),
            jax.ShapeDtypeStruct((items, tokens, 128), BF16),
        ],
        compiler_params=pltpu.CompilerParams(vmem_limit_bytes=50 * 2**20),
        cost_estimate=pl.CostEstimate(flops=items * tokens * tokens * 512, bytes_accessed=items * tokens * 2048, transcendentals=items * tokens * tokens * 2),
        name="attention_forward",
    )(valid, pair, qkv, rows)


def attention_backward(qkv, outs, aug, grads, rows, valid, pair, after):
    sources, items, local, unused = qkv.shape
    blocks = sources * local // KB
    tokens = sources * local
    width = KB * (2 * blocks - 1)
    big = lambda lanes: pl.BlockSpec((sources, 1, local, lanes), lambda i, v, p: (0, i, 0, 0))
    spec = pltpu.PrefetchScalarGridSpec(
        num_scalar_prefetch=2,
        grid=(items,),
        in_specs=[
            big(384),
            big(128),
            pl.BlockSpec((1, tokens, 128), lambda i, v, p: (i, 0, 0)),
            big(128),
            pl.BlockSpec((1, 2, NEAR), lambda i, v, p: (p[i], 0, 0)),
            pl.BlockSpec(memory_space=pl.ANY),
        ],
        out_specs=[
            big(384),
            pl.BlockSpec((1, 2, NEAR), lambda i, v, p: (i, 0, 0)),
        ],
        scratch_shapes=[
            pltpu.VMEM((2, tokens, 128), BF16),
            pltpu.VMEM((2, tokens, 128), BF16),
            pltpu.VMEM((2, tokens, 128), BF16),
            pltpu.VMEM((2, tokens, 128), BF16),
            pltpu.VMEM((128, tokens), BF16),
            pltpu.VMEM((2, KB, width), F32),
            pltpu.VMEM((2, KB, width), F32),
            pltpu.VMEM((2, KB, tokens), BF16),
            pltpu.VMEM((2, KB, tokens), BF16),
            pltpu.VMEM((128, tokens), F32),
        ],
    )
    return pl.pallas_call(
        functools.partial(bwd_kernel, blocks),
        grid_spec=spec,
        out_shape=[
            jax.ShapeDtypeStruct((sources, items, local, 384), BF16),
            jax.ShapeDtypeStruct((items, 2, NEAR), F32),
        ],
        compiler_params=pltpu.CompilerParams(vmem_limit_bytes=50 * 2**20),
        cost_estimate=pl.CostEstimate(flops=items * tokens * tokens * 1280, bytes_accessed=items * tokens * 4096, transcendentals=items * tokens * tokens * 2),
        name="attention_backward",
    )(valid, pair, qkv, outs, aug, grads, rows, after)


VPAD = 384
PAIRS = 6
TN = (((0,), (0,)), ((), ()))
SQRT_2_OVER_PI = 0.7978845608028654


def block_masks(masks, first_byte, total_bytes):
    shape = masks.shape[2:]
    conv_at = first_byte - 2 + lax.broadcasted_iota(jnp.int32, shape, 1)
    token = lax.broadcasted_iota(jnp.int32, shape, 0)
    for side in range(2):
        place = first_byte + 2 * token + side
        for size in range(1, 5):
            start = (place // size) * size
            inside = (conv_at >= start) & (conv_at < start + size) & (conv_at < total_bytes)
            masks[side, size - 1] = jnp.where(inside, 1.0 / size, 0.0)


def split_two(values):
    high = values.astype(BF16)
    return high, (values - high.astype(F32)).astype(BF16)


def permute_weight(weight, out):
    rows = weight.shape[0]
    low = lax.broadcasted_iota(jnp.int32, (rows, 128), 1) < 64
    for pair in range(PAIRS):
        at = pair * 384
        one, two, three = (weight[:, at + 128 * k : at + 128 * k + 128] for k in range(3))
        out[:, at : at + 128] = jnp.where(low, one, two)
        out[:, at + 128 : at + 256] = pltpu.roll(jnp.where(low, three, one).astype(F32), 64, 1).astype(BF16)
        out[:, at + 256 : at + 384] = jnp.where(low, two, three)


def greet(axis, here, count):
    barrier = pltpu.get_barrier_semaphore()

    def signal(step, unused):
        pl.semaphore_signal(barrier, inc=1, device_id={axis: lax.rem(here + step, count)}, device_id_type=pl.DeviceIdType.MESH)
        return unused

    lax.fori_loop(1, count, signal, 0)


def item_copy(devices, me, source, target, other, slot, sems):
    send, recv, unused = sems

    def outward():
        offset = lax.rem(other - me + devices, devices)
        return pltpu.make_async_remote_copy(
            src_ref=source, dst_ref=target, send_sem=send.at[offset, slot], recv_sem=recv.at[offset, slot],
            device_id={"seq": other}, device_id_type=pl.DeviceIdType.MESH,
        )

    def inward():
        offset = lax.rem(me - other + devices, devices)
        return pltpu.make_async_remote_copy(
            src_ref=source, dst_ref=target, send_sem=send.at[offset, slot], recv_sem=recv.at[offset, slot],
            device_id={"seq": other}, device_id_type=pl.DeviceIdType.MESH,
        )

    return outward, inward


def start_item(devices, me, source, target, other, slot, sems):
    @pl.when(other == me)
    def _():
        pltpu.make_async_copy(source, target, sems[2].at[slot]).start()

    @pl.when(other != me)
    def _():
        item_copy(devices, me, source, target, other, slot, sems)[0]().start()


def finish_sends(devices, me, total, source_of, target_of, sems):
    def wait(item, unused):
        other, slot = lax.rem(item, devices), item // devices

        @pl.when(other != me)
        def _():
            item_copy(devices, me, source_of(other, slot), target_of(other, slot), other, slot, sems)[0]().wait_send()

        return unused

    lax.fori_loop(0, total, wait, 0)


def finish_receives(devices, me, total, source_of, target_of, sems):
    per_device = -(-total // devices)

    def wait(at, unused):
        other, slot = at // per_device, lax.rem(at, per_device)

        @pl.when((slot * devices + me < total) & (other != me))
        def _():
            item_copy(devices, me, source_of(other, slot), target_of(other, slot), other, slot, sems)[1]().wait_recv()

        @pl.when((slot * devices + me < total) & (other == me))
        def _():
            pltpu.make_async_copy(source_of(other, slot), target_of(other, slot), sems[2].at[slot]).wait()

        return unused

    lax.fori_loop(0, devices * per_device, wait, 0)


def front_kernel(
    sizes, ids_ref, taps_ref, weight_ref, gain_ref, score_ref,
    hidden_ref, normed_ref, conv_ref, mix_ref, share_ref, items_ref, masks, wide, permuted, stage, *sems,
):
    local_tokens, window, devices, total = sizes
    step = pl.program_id(0)
    me = lax.axis_index("seq")

    @pl.when(step == 0)
    def _():
        greet("seq", me, devices)
        block_masks(masks, me * 2 * local_tokens, devices * 2 * local_tokens)
        permute_weight(weight_ref, permuted)

    together = ids_ref.shape[0]
    score = score_ref[...]
    model = score.shape[1]
    score_high, score_low = split_two(score)
    row16 = lax.broadcasted_iota(jnp.int32, (16, model), 0)
    score_rows = jnp.where(row16 == 0, score_high.astype(F32), jnp.where(row16 == 1, score_low.astype(F32), 0.0)).astype(BF16)
    lane = lax.broadcasted_iota(jnp.int32, (together * window, VPAD), 1)
    width = masks.shape[3]
    ids = ids_ref[...].reshape(together * window, 8)
    conv_all = jnp.zeros((together * window, model), F32)
    for tap in range(taps_ref.shape[0]):
        hot = jnp.where(ids[:, tap : tap + 1] == lane, 1.0, 0.0).astype(BF16)
        conv_all = conv_all + dot(hot, taps_ref[tap], NN)
    for one in range(together):
        high, low = split_two(conv_all[one * window : (one + 1) * window])
        conv_ref[one, 0:window] = high
        wide[one, 0, 0:window] = high
        wide[one, 1, 0:window] = low
        if width > window:
            wide[one, :, window:width] = jnp.zeros((2, width - window, model), BF16)
            conv_ref[one, window:width] = jnp.zeros((width - window, model), BF16)
        high = wide[one, 0]
        low = wide[one, 1]
        along = jnp.sum(dot(score_rows, high, NT), axis=0, keepdims=True) + dot(score_rows, low, NT)[0:1]
        mixed = jnp.zeros((local_tokens, width), F32)
        kept = jnp.zeros((local_tokens, 128), F32)
        lane128 = lax.broadcasted_iota(jnp.int32, (local_tokens, 128), 1)
        for side in range(2):
            scores = [jnp.sum(masks[side, k] * along, axis=1, keepdims=True) for k in range(4)]
            top = jnp.maximum(jnp.maximum(scores[0], scores[1]), jnp.maximum(scores[2], scores[3]))
            powers = [jnp.exp(value - top) for value in scores]
            under = 1.0 / (powers[0] + powers[1] + powers[2] + powers[3])
            for k in range(4):
                share = powers[k] * under
                mixed = mixed + share * masks[side, k]
                kept = jnp.where(lane128 == 4 * side + k, share, kept)
        share_ref[one] = kept
        mix_high, mix_low = split_two(mixed * 0.5)
        mix_ref[one] = mix_high
        hidden = dot(mix_high, high, NN) + dot(mix_high, low, NN) + dot(mix_low, high, NN)
        hidden_ref[one] = hidden
        scale = lax.rsqrt(jnp.mean(hidden * hidden, axis=1, keepdims=True) + 1e-06)
        normed_ref[one] = (hidden * scale * gain_ref[...]).astype(BF16)
    normed = normed_ref[...].reshape(together * local_tokens, model)

    @pl.when(step == 0)
    def _():
        pl.semaphore_wait(pltpu.get_barrier_semaphore(), devices - 1)

    for pair in range(PAIRS):
        piece = dot(normed, permuted[:, pair * 384 : pair * 384 + 384], NN).astype(BF16)
        for one in range(together):
            item = (step * together + one) * PAIRS + pair
            other, slot = lax.rem(item, devices), item // devices
            stage[other, slot] = piece[one * local_tokens : (one + 1) * local_tokens]
            start_item(devices, me, stage.at[other, slot], items_ref.at[me, slot], other, slot, sems)

    @pl.when(step == pl.num_programs(0) - 1)
    def _():
        finish_sends(devices, me, total, lambda other, slot: stage.at[other, slot], lambda other, slot: items_ref.at[me, slot], sems)
        finish_receives(devices, me, total, lambda other, slot: stage.at[other, slot], lambda other, slot: items_ref.at[other, slot], sems)


def mid_kernel(
    sizes, att_ref, hidden_ref, cot_ref, out_weight_ref, in_weight_ref, down_ref, gain_ref,
    layer_ref, act_ref, gate_up_ref, normed_ref, attended_ref, branch_ref, residual_ref, items_ref, gain_out,
    arrived, stage, keep_gain, *sems,
):
    local_tokens, devices, total = sizes
    in_sems, out_sems = sems[:3], sems[3:]
    step = pl.program_id(0)
    me = lax.axis_index("seq")
    per_device = -(-total // devices)

    @pl.when(step == 0)
    def _():
        greet("seq", me, devices)
        keep_gain[...] = jnp.zeros_like(keep_gain)
        pl.semaphore_wait(pltpu.get_barrier_semaphore(), devices - 1)

        def send(at, unused):
            slot, offset = at // devices, lax.rem(at, devices)
            other = lax.rem(me + offset, devices)

            @pl.when(slot * devices + me < total)
            def _():
                start_item(devices, me, att_ref.at[other, slot], arrived.at[me, slot], other, slot, in_sems)

            return unused

        lax.fori_loop(0, devices * per_device, send, 0)

    together = hidden_ref.shape[0]
    rows = together * local_tokens
    model = gain_ref.shape[1]
    gathered = []
    for one in range(together):
        pieces = []
        for pair in range(PAIRS):
            item = (step * together + one) * PAIRS + pair
            other, slot = lax.rem(item, devices), item // devices

            @pl.when(other == me)
            def _():
                pltpu.make_async_copy(att_ref.at[me, slot], arrived.at[me, slot], in_sems[2].at[slot]).wait()

            @pl.when(other != me)
            def _():
                item_copy(devices, me, att_ref.at[other, slot], arrived.at[other, slot], other, slot, in_sems)[1]().wait_recv()

            pieces.append(arrived[other, slot])
        gathered.append(jnp.concatenate(pieces, axis=1))
    attended = jnp.concatenate(gathered, axis=0)
    attended_ref[...] = attended.reshape(attended_ref.shape)
    residual = hidden_ref[...].reshape(rows, model) + dot(attended, out_weight_ref[...], NN)
    gain = gain_ref[...]
    scale = lax.rsqrt(jnp.mean(residual * residual, axis=1, keepdims=True) + 1e-06)
    normed = (residual * scale * gain).astype(BF16)
    normed_ref[...] = normed.reshape(normed_ref.shape)
    cot = cot_ref[...].reshape(rows, model)
    hidden_units = down_ref.shape[0]
    chunk = 512
    layer = residual
    back = jnp.zeros_like(residual)
    for first in range(0, hidden_units, chunk):
        here = slice(first, first + chunk)
        there = slice(hidden_units + first, hidden_units + first + chunk)
        gate = dot(normed, in_weight_ref[:, here], NN)
        up = dot(normed, in_weight_ref[:, there], NN)
        grad = dot(cot, down_ref[here, :], NT)
        square = gate * gate
        inner = gate * (SQRT_2_OVER_PI + (SQRT_2_OVER_PI * 0.044715) * square)
        curve = jnp.tanh(inner)
        half_plus = 0.5 + 0.5 * curve
        smooth = gate * half_plus
        slope = half_plus + (0.5 * gate) * (1.0 - curve * curve) * (SQRT_2_OVER_PI + (3 * SQRT_2_OVER_PI * 0.044715) * square)
        act = (smooth * up).astype(BF16)
        grad_gate = (grad * up * slope).astype(BF16)
        grad_up = (grad * smooth).astype(BF16)
        act_ref[:, :, here] = act.reshape(together, local_tokens, chunk)
        gate_up_ref[:, :, here] = grad_gate.reshape(together, local_tokens, chunk)
        gate_up_ref[:, :, there] = grad_up.reshape(together, local_tokens, chunk)
        layer = layer + dot(act, down_ref[here, :], NN)
        back = back + dot(grad_gate, in_weight_ref[:, here], NT) + dot(grad_up, in_weight_ref[:, there], NT)
    layer_ref[...] = layer.reshape(layer_ref.shape)
    weighted = gain * back
    inner_mean = jnp.mean(residual * weighted, axis=1, keepdims=True)
    grad_residual = cot.astype(F32) + scale * weighted - residual * (scale * scale * scale * inner_mean)
    residual_ref[...] = grad_residual.reshape(residual_ref.shape)
    branch = grad_residual.astype(BF16)
    branch_ref[...] = branch.reshape(branch_ref.shape)
    grad_attended = dot(branch, out_weight_ref[...], NT).astype(BF16)
    for one in range(together):
        for pair in range(PAIRS):
            item = (step * together + one) * PAIRS + pair
            other, slot = lax.rem(item, devices), item // devices
            stage[other, slot] = grad_attended[one * local_tokens : (one + 1) * local_tokens, pair * 128 : pair * 128 + 128]
            start_item(devices, me, stage.at[other, slot], items_ref.at[me, slot], other, slot, out_sems)
    keep_gain[...] += jnp.sum((back * residual * scale).reshape(rows // 8, 8, model), axis=0)
    gain_out[...] = jnp.sum(keep_gain[...], axis=0, keepdims=True)

    @pl.when(step == pl.num_programs(0) - 1)
    def _():
        def wait(at, unused):
            slot, offset = at // devices, lax.rem(at, devices)
            other = lax.rem(me + offset, devices)

            @pl.when((slot * devices + me < total) & (offset != 0))
            def _():
                item_copy(devices, me, att_ref.at[other, slot], arrived.at[me, slot], other, slot, in_sems)[0]().wait_send()

            return unused

        lax.fori_loop(0, devices * per_device, wait, 0)
        finish_sends(devices, me, total, lambda other, slot: stage.at[other, slot], lambda other, slot: items_ref.at[me, slot], out_sems)
        finish_receives(devices, me, total, lambda other, slot: stage.at[other, slot], lambda other, slot: items_ref.at[other, slot], out_sems)


def back_kernel(
    sizes, grads_ref, hidden_ref, residual_ref, conv_ref, mix_ref, share_ref, ids_ref, weight_ref, taps_ref,
    table_ref, gain_ref, score_ref, after, table_out, flat_out, masks, permuted, slopes, keep_gain, keep_score, arrived, *sems,
):
    local_tokens, window, devices, item_total = sizes
    step = pl.program_id(0)
    me = lax.axis_index("seq")
    model = gain_ref.shape[1]
    per_device = -(-item_total // devices)

    @pl.when(step == 0)
    def _():
        greet("seq", me, devices)
        block_masks(masks, me * 2 * local_tokens, devices * 2 * local_tokens)
        permute_weight(weight_ref, permuted)
        keep_gain[...] = jnp.zeros_like(keep_gain)
        keep_score[...] = jnp.zeros_like(keep_score)
        pl.semaphore_wait(pltpu.get_barrier_semaphore(), devices - 1)

        def send(at, unused):
            slot, offset = at // devices, lax.rem(at, devices)
            other = lax.rem(me + offset, devices)

            @pl.when(slot * devices + me < item_total)
            def _():
                start_item(devices, me, grads_ref.at[other, slot], arrived.at[me, slot], other, slot, sems)

            return unused

        lax.fori_loop(0, devices * per_device, send, 0)

    together = hidden_ref.shape[0]
    width = masks.shape[3]
    rows = together * local_tokens
    gathered = []
    for one in range(together):
        pieces = []
        for pair in range(PAIRS):
            item = (step * together + one) * PAIRS + pair
            other, slot = lax.rem(item, devices), item // devices

            @pl.when(other == me)
            def _():
                pltpu.make_async_copy(grads_ref.at[me, slot], arrived.at[me, slot], sems[2].at[slot]).wait()

            @pl.when(other != me)
            def _():
                item_copy(devices, me, grads_ref.at[other, slot], arrived.at[other, slot], other, slot, sems)[1]().wait_recv()

            pieces.append(arrived[other, slot])
        gathered.append(jnp.concatenate(pieces, axis=1))
    projected = jnp.concatenate(gathered, axis=0)
    flat_out[...] = projected.reshape(flat_out.shape)
    grad_normed = dot(projected, permuted[...], NT)
    hidden = hidden_ref[...].reshape(rows, model)
    gain = gain_ref[...]
    scale = lax.rsqrt(jnp.mean(hidden * hidden, axis=1, keepdims=True) + 1e-06)
    weighted = gain * grad_normed
    inner_mean = jnp.mean(hidden * weighted, axis=1, keepdims=True)
    grad_hidden = residual_ref[...].reshape(rows, model) + scale * weighted - hidden * (scale * scale * scale * inner_mean)
    keep_gain[...] += jnp.sum((grad_normed * hidden * scale).reshape(rows // 8, 8, model), axis=0)
    high, low = split_two(grad_hidden)
    score_high, score_low = split_two(score_ref[...])
    row_at = lax.broadcasted_iota(jnp.int32, (local_tokens, model), 0)
    vector = jnp.broadcast_to(score_ref[...].astype(BF16), (local_tokens, model))
    for one in range(together):
        own = slice(one * local_tokens, (one + 1) * local_tokens)
        conv = conv_ref[one]
        cross = 0.5 * (dot(high[own], conv, NT) + dot(low[own], conv, NT))
        kept = share_ref[one]
        total = jnp.zeros((local_tokens, width), F32)
        for side in range(2):
            shares = [kept[:, 4 * side + k : 4 * side + k + 1] for k in range(4)]
            grads = [jnp.sum(masks[side, k] * cross, axis=1, keepdims=True) for k in range(4)]
            mean = sum(share * grad for share, grad in zip(shares, grads))
            for k in range(4):
                total = total + (shares[k] * (grads[k] - mean)) * masks[side, k]
        column = jnp.sum(total, axis=0, keepdims=True)
        column_high, column_low = split_two(column)
        row16 = lax.broadcasted_iota(jnp.int32, (16, width), 0)
        column_rows = jnp.where(row16 == 0, column_high.astype(F32), jnp.where(row16 == 1, column_low.astype(F32), 0.0)).astype(BF16)
        keep_score[...] += dot(column_rows, conv, NN)
        left = jnp.concatenate([mix_ref[one], total.astype(BF16)], axis=0)
        right = jnp.concatenate([high[own], vector], axis=0)
        slope = dot(left, right, TN)
        slopes[pl.ds((step * together + one) * window, window), :] = slope[0:window].astype(BF16)

    @pl.when(step == pl.num_programs(0) - 1)
    def _():
        def wait(at, unused):
            slot, offset = at // devices, lax.rem(at, devices)
            other = lax.rem(me + offset, devices)

            @pl.when((slot * devices + me < item_total) & (offset != 0))
            def _():
                item_copy(devices, me, grads_ref.at[other, slot], arrived.at[me, slot], other, slot, sems)[0]().wait_send()

            return unused

        lax.fori_loop(0, devices * per_device, wait, 0)
        count = slopes.shape[0]
        row = lax.broadcasted_iota(jnp.int32, (SMALL_ROWS, count), 0)
        table_grad = jnp.zeros((SMALL_ROWS, model), F32)
        table = table_ref[...].astype(F32)
        place = lax.broadcasted_iota(jnp.int32, (SMALL_ROWS, model), 0)
        extra = []
        for tap in range(taps_ref.shape[0]):
            hot = jnp.where(ids_ref[tap : tap + 1, :] == row, 1.0, 0.0).astype(BF16)
            sums = dot(hot, slopes[...], NN)
            table_grad = table_grad + taps_ref[tap : tap + 1, :] * sums
            extra.append(jnp.sum(sums * table, axis=0, keepdims=True))
        extra.append(jnp.sum(keep_gain[...], axis=0, keepdims=True))
        extra.append(jnp.sum(keep_score[...], axis=0, keepdims=True))
        for index, value in enumerate(extra):
            table_grad = jnp.where(place == 259 + index, value, table_grad)
        table_out[...] = table_grad


VMEM_LIMIT = 58 * 2**20
TOGETHER = 2


def item_sems(devices, per_device):
    dma = pltpu.SemaphoreType.DMA
    return [dma((devices, per_device)), dma((devices, per_device)), dma((per_device,))]


def whole(*shape):
    return pl.BlockSpec(shape, lambda s, *_: (0,) * len(shape))


def part(*shape):
    return pl.BlockSpec(shape, lambda s, *_: (s,) + (0,) * (len(shape) - 1))


ANYWHERE = pl.BlockSpec(memory_space=pl.ANY)


def remote_params(number):
    return pltpu.CompilerParams(vmem_limit_bytes=VMEM_LIMIT, collective_id=number, has_side_effects=True)


def call_front(ids, taps, weight, gain, score, local_tokens, devices, per_device):
    sequences, window, unused = ids.shape
    width = -(-window // 128) * 128
    model = weight.shape[0]
    return pl.pallas_call(
        functools.partial(front_kernel, (local_tokens, window, devices, sequences * PAIRS)),
        grid=(sequences // TOGETHER,),
        in_specs=[part(TOGETHER, window, 8), whole(*taps.shape), whole(*weight.shape), whole(1, model), whole(1, model)],
        out_specs=[
            part(TOGETHER, local_tokens, model),
            part(TOGETHER, local_tokens, model),
            part(TOGETHER, width, model),
            part(TOGETHER, local_tokens, width),
            part(TOGETHER, local_tokens, 128),
            ANYWHERE,
        ],
        scratch_shapes=[
            pltpu.VMEM((2, 4, local_tokens, width), F32),
            pltpu.VMEM((TOGETHER, 2, width, model), BF16),
            pltpu.VMEM(weight.shape, BF16),
            pltpu.VMEM((devices, per_device, local_tokens, 384), BF16),
        ]
        + item_sems(devices, per_device),
        out_shape=[
            jax.ShapeDtypeStruct((sequences, local_tokens, model), F32),
            jax.ShapeDtypeStruct((sequences, local_tokens, model), BF16),
            jax.ShapeDtypeStruct((sequences, width, model), BF16),
            jax.ShapeDtypeStruct((sequences, local_tokens, width), BF16),
            jax.ShapeDtypeStruct((sequences, local_tokens, 128), F32),
            jax.ShapeDtypeStruct((devices, per_device, local_tokens, 384), BF16),
        ],
        compiler_params=remote_params(3),
        cost_estimate=pl.CostEstimate(flops=5 * 10**10, bytes_accessed=2 * 10**7, transcendentals=10**5),
        name="front",
    )(ids, taps, weight, gain, score)


def call_mid(att, hidden, cot, out_weight, in_weight, down_weight, gain):
    devices, per_device, local_tokens, unused = att.shape
    sequences, unused, model = hidden.shape
    hidden_units = down_weight.shape[0]
    rows = lambda lanes: part(TOGETHER, local_tokens, lanes)
    full = lambda lanes, kind: jax.ShapeDtypeStruct((sequences, local_tokens, lanes), kind)
    return pl.pallas_call(
        functools.partial(mid_kernel, (local_tokens, devices, sequences * PAIRS)),
        grid=(sequences // TOGETHER,),
        in_specs=[
            ANYWHERE,
            rows(model),
            rows(model),
            whole(*out_weight.shape),
            whole(*in_weight.shape),
            whole(*down_weight.shape),
            whole(1, model),
        ],
        out_specs=[
            rows(model),
            rows(hidden_units),
            rows(2 * hidden_units),
            rows(model),
            rows(model),
            rows(model),
            rows(model),
            ANYWHERE,
            whole(1, model),
        ],
        scratch_shapes=[pltpu.VMEM(att.shape, BF16), pltpu.VMEM(att.shape, BF16), pltpu.VMEM((8, model), F32)]
        + item_sems(devices, per_device)
        + item_sems(devices, per_device),
        out_shape=[
            full(model, F32),
            full(hidden_units, BF16),
            full(2 * hidden_units, BF16),
            full(model, BF16),
            full(model, BF16),
            full(model, BF16),
            full(model, F32),
            jax.ShapeDtypeStruct(att.shape, BF16),
            jax.ShapeDtypeStruct((1, model), F32),
        ],
        compiler_params=remote_params(4),
        cost_estimate=pl.CostEstimate(flops=5 * 10**10, bytes_accessed=4 * 10**7, transcendentals=10**6),
        name="middle",
    )(att, hidden, cot, out_weight, in_weight, down_weight, gain)


def call_back(grads, hidden, residual, conv, mix, share, ids, weight, taps, table, gain, score, after):
    devices, per_device, local_tokens, unused = grads.shape
    sequences, unused, model = hidden.shape
    width = conv.shape[1]
    window = ids.shape[1] // sequences
    return pl.pallas_call(
        functools.partial(back_kernel, (local_tokens, window, devices, sequences * PAIRS)),
        grid=(sequences // TOGETHER,),
        in_specs=[
            ANYWHERE,
            part(TOGETHER, local_tokens, model),
            part(TOGETHER, local_tokens, model),
            part(TOGETHER, width, model),
            part(TOGETHER, local_tokens, width),
            part(TOGETHER, local_tokens, 128),
            whole(*ids.shape),
            whole(*weight.shape),
            whole(*taps.shape),
            whole(*table.shape),
            whole(1, model),
            whole(1, model),
            ANYWHERE,
        ],
        out_specs=[whole(SMALL_ROWS, model), part(TOGETHER, local_tokens, PAIRS * 384)],
        scratch_shapes=[
            pltpu.VMEM((2, 4, local_tokens, width), F32),
            pltpu.VMEM(weight.shape, BF16),
            pltpu.VMEM((sequences * window, model), BF16),
            pltpu.VMEM((8, model), F32),
            pltpu.VMEM((16, model), F32),
            pltpu.VMEM(grads.shape, BF16),
        ]
        + item_sems(devices, per_device),
        out_shape=[
            jax.ShapeDtypeStruct((SMALL_ROWS, model), F32),
            jax.ShapeDtypeStruct((sequences, local_tokens, PAIRS * 384), BF16),
        ],
        compiler_params=remote_params(5),
        cost_estimate=pl.CostEstimate(flops=5 * 10**10, bytes_accessed=2 * 10**7, transcendentals=10**5),
        name="back",
    )(grads, hidden, residual, conv, mix, share, ids, weight, taps, table, gain, score, after)


def move_kernel(order_ref, source_ref, out_ref):
    out_ref[...] = source_ref[...]


def reorder(source, order, inverse):
    block = (1,) + source.shape[1:]
    moved = pl.BlockSpec(block, lambda s, order: (order[s], 0, 0))
    plain = pl.BlockSpec(block, lambda s, order: (s, 0, 0))
    return pl.pallas_call(
        move_kernel,
        grid_spec=pltpu.PrefetchScalarGridSpec(
            num_scalar_prefetch=1,
            grid=(source.shape[0],),
            in_specs=[plain if inverse else moved],
            out_specs=moved if inverse else plain,
        ),
        out_shape=jax.ShapeDtypeStruct(source.shape, source.dtype),
        cost_estimate=pl.CostEstimate(flops=0, bytes_accessed=2 * source.size * source.dtype.itemsize, transcendentals=0),
        name="reorder",
    )(order, source)


EARLY_ROWS = 8 * 96 + 2 * 192 + 2 * 96
LATE_ROWS = 5 * 96


def meet_sibling(core):
    barrier = pltpu.get_barrier_semaphore()
    sibling = lax.axis_index("seq") + 1 - 2 * core
    pl.semaphore_signal(barrier, inc=1, device_id={"seq": sibling}, device_id_type=pl.DeviceIdType.MESH)
    pl.semaphore_wait(barrier, 1)


def to_sibling(core, source, target, send_sem, recv_sem):
    sibling = lax.axis_index("seq") + 1 - 2 * core
    return pltpu.make_async_remote_copy(
        src_ref=source, dst_ref=target, send_sem=send_sem, recv_sem=recv_sem,
        device_id={"seq": sibling}, device_id_type=pl.DeviceIdType.MESH,
    )


def spread_rows(core, source, lanes, keep_ref, send_ref, column, first):
    for chip in range(4):
        for other, ref in ((0, keep_ref), (1, send_ref)):
            device = 2 * chip + lax.rem(core + other, 2)
            rows = pl.ds(pl.multiple_of(device * 96, 32), 96)
            ref[chip, column, pl.ds(first, 96)] = source[rows, lanes]


def add_received(keep_ref, got):
    def add(at, unused):
        chip, column = at // 4, at % 4
        keep_ref[chip, column] = (keep_ref[chip, column].astype(F32) + got[chip, column].astype(F32)).astype(BF16)
        return unused

    lax.fori_loop(0, 16, add, 0)


def early_kernel(
    act_ref, cot_ref, normed_ref, gate_up_ref, attended_ref, branch_ref, keep_ref,
    send_ref, got, cot_t, normed_t, result, send_in, recv_in, send_down, recv_down, send_out, recv_out,
):
    step = pl.program_id(0)
    core = lax.rem(lax.axis_index("seq"), 2)
    model = cot_t.shape[0]
    tokens = cot_t.shape[1]
    out_rows = pl.ds(1152, 192)
    down_rows = pl.ds(768, 384)
    out_copy = to_sibling(core, send_ref.at[:, :, out_rows], got.at[:, :, out_rows], send_out, recv_out)

    def in_copy(at):
        rows = pl.ds(pl.multiple_of(384 * lax.rem(at, 2), 384), 384)
        return to_sibling(core, send_ref.at[:, at // 2, rows], got.at[:, at // 2, rows], send_in.at[at], recv_in.at[at])

    def down_copy(chip):
        return to_sibling(core, send_ref.at[chip, :, down_rows], got.at[chip, :, down_rows], send_down.at[chip], recv_down.at[chip])

    @pl.when(step == 0)
    def _():
        meet_sibling(core)
        cot_t[...] = cot_ref[...].reshape(tokens, model).T
        normed_t[...] = attended_ref[...].reshape(tokens, model).T
        for first in range(0, model, 256):
            result[:, 0:256] = dot(normed_t[...], branch_ref[:, :, first : first + 256].reshape(tokens, 256), NN).astype(BF16)
            for part in range(2):
                tile = first // 128 + part
                for column, slot in {0: ((0, 0),), 1: ((0, 1), (1, 0)), 2: ((1, 1),), 3: ((2, 0),), 4: ((2, 1), (3, 0)), 5: ((3, 1),)}[tile]:
                    spread_rows(core, result, slice(128 * part, 128 * part + 128), keep_ref, send_ref, column, 1152 + 96 * slot)
        out_copy.start()
        normed_t[...] = normed_ref[...].reshape(tokens, model).T

    result[...] = dot(normed_t[...], gate_up_ref[...].reshape(tokens, 512), NN).astype(BF16)
    for part in range(4):
        first = pl.multiple_of((4 * lax.rem(step, 2) + part) * 96, 32)
        spread_rows(core, result, slice(128 * part, 128 * part + 128), keep_ref, send_ref, step // 2, first)
    in_copy(step).start()
    down = dot(cot_t[...], act_ref[...].reshape(tokens, 256), NN).astype(BF16)

    def put_down(ref):
        for column in range(4):
            for part in range(2):
                ref[step // 2, column, 768 + 192 * part : 960 + 192 * part] = down[192 * column : 192 * column + 192, 128 * part : 128 * part + 128]

    @pl.when(lax.rem(step, 2) == core)
    def _():
        put_down(keep_ref)

    @pl.when(lax.rem(step, 2) != core)
    def _():
        put_down(send_ref)
        down_copy(step // 2).start()

    @pl.when(step == 7)
    def _():
        out_copy.wait()
        for at in range(8):
            in_copy(at).wait()
        for chip in range(4):
            down_copy(chip).wait()
        add_received(keep_ref, got)


def call_early(act, cot, normed, gate_up, attended, branch):
    sequences, local_tokens, model = cot.shape
    tokens = sequences * local_tokens
    whole = pl.BlockSpec((sequences, local_tokens, model), lambda s: (0, 0, 0))
    shape = (4, 4, EARLY_ROWS, 128)
    dma = pltpu.SemaphoreType.DMA
    return pl.pallas_call(
        early_kernel,
        grid=(8,),
        in_specs=[
            pl.BlockSpec((sequences, local_tokens, 256), lambda s: (0, 0, s)),
            whole,
            whole,
            pl.BlockSpec((sequences, local_tokens, 512), lambda s: (0, 0, s)),
            whole,
            whole,
        ],
        out_specs=pl.BlockSpec(shape, lambda s: (0, 0, 0, 0)),
        scratch_shapes=[
            pltpu.VMEM(shape, BF16),
            pltpu.VMEM(shape, BF16),
            pltpu.VMEM((model, tokens), BF16),
            pltpu.VMEM((model, tokens), BF16),
            pltpu.VMEM((model, 512), BF16),
            dma((8,)), dma((8,)), dma((4,)), dma((4,)), dma, dma,
        ],
        out_shape=jax.ShapeDtypeStruct(shape, BF16),
        compiler_params=pltpu.CompilerParams(vmem_limit_bytes=VMEM_LIMIT, collective_id=1, has_side_effects=True),
        cost_estimate=pl.CostEstimate(flops=11 * 10**9, bytes_accessed=3 * 10**7, transcendentals=0),
        name="early_gradients",
    )(act, cot, normed, gate_up, attended, branch)


def tail_kernel(
    normed_ref, grads_ref, plane_ref, one_ref, tail_ref, late_out, early_out, out_ref,
    keep, send_ref, got, normed_t, result, got_chips, planes_late, got_late, got_early,
    held, got_seq, planes, got_dp, whole_small, *sems,
):
    small_sems, (send_a, recv_a, send_b, recv_b, send_c, recv_c, send_e, recv_e) = sems[:8], sems[8:]
    me = lax.axis_index("seq")
    plane = lax.axis_index("dp")
    core = lax.rem(me, 2)
    chip = me // 2
    sequences, local_tokens, model = normed_ref.shape
    small = SmallSums(one_ref, tail_ref, out_ref, held, got_seq, planes, got_dp, whole_small, small_sems)
    greet("seq", me, 8)
    greet("dp", plane, 4)
    small.pack()
    normed_t[...] = normed_ref[...].reshape(sequences * local_tokens, model).T
    pl.semaphore_wait(pltpu.get_barrier_semaphore(), 10)
    small.one_start()

    def to_plane(offset, source, target, send, recv):
        return pltpu.make_async_remote_copy(
            src_ref=source, dst_ref=target, send_sem=send.at[offset - 1], recv_sem=recv.at[offset - 1],
            device_id={"dp": lax.rem(plane + offset, 4)}, device_id_type=pl.DeviceIdType.MESH,
        )

    early_copies = [to_plane(offset, plane_ref.at[lax.rem(plane + offset, 4)], got_early.at[offset - 1], send_e, recv_e) for offset in (1, 2, 3)]
    for copy in early_copies:
        copy.start()
    low = lax.broadcasted_iota(jnp.int32, (model, 128), 1) < 64
    copies = [to_sibling(core, send_ref.at[:, column], got.at[:, column], send_a.at[column], recv_a.at[column]) for column in range(4)]
    for pair in range(PAIRS):
        rows = grads_ref[:, :, pair * 384 : pair * 384 + 384].reshape(sequences * local_tokens, 384)
        sums = dot(normed_t[...], rows, NN)
        query, key, value = sums[:, 0:128], pltpu.roll(sums[:, 128:256], 64, 1), sums[:, 256:384]
        result[0] = jnp.where(low, query, key).astype(BF16)
        result[1] = jnp.where(low, value, query).astype(BF16)
        result[2] = jnp.where(low, key, value).astype(BF16)
        for third in range(3):
            tile = 3 * pair + third
            within = tile % 9
            spots = [(2 * (tile // 9), within)] if within <= 4 else []
            spots += [(2 * (tile // 9) + 1, within - 4)] if within >= 4 else []
            for column, slot in spots:
                spread_rows(core, result.at[third], slice(0, 128), keep, send_ref, column, 96 * slot)
        if pair in (1, 2, 4, 5):
            copies[(1, 2, 4, 5).index(pair)].start()
    small.one_finish()

    def chip_copy(offset, column):
        other = lax.rem(chip + offset, 4)
        return pltpu.make_async_remote_copy(
            src_ref=keep.at[other, column], dst_ref=got_chips.at[offset - 1, column],
            send_sem=send_b.at[offset - 1, column], recv_sem=recv_b.at[offset - 1, column],
            device_id={"seq": 2 * other + core}, device_id_type=pl.DeviceIdType.MESH,
        )

    for column in range(4):
        copies[column].wait()
        for at in range(4):
            keep[at, column] = (keep[at, column].astype(F32) + got[at, column].astype(F32)).astype(BF16)
        for offset in (1, 2, 3):
            chip_copy(offset, column).start()
    small.two_finish()
    for column in range(4):
        total = keep[chip, column].astype(F32)
        for offset in (1, 2, 3):
            chip_copy(offset, column).wait()
            total = total + got_chips[offset - 1, column].astype(F32)
        planes_late[column] = total.astype(BF16)
    late_copies = [to_plane(offset, planes_late.at[lax.rem(plane + offset, 4)], got_late.at[offset - 1], send_c, recv_c) for offset in (1, 2, 3)]
    for copy in late_copies:
        copy.start()
    small.three_finish()
    total = plane_ref[plane].astype(F32)
    for offset in (1, 2, 3):
        early_copies[offset - 1].wait()
        total = total + got_early[offset - 1].astype(F32)
    early_out[...] = total
    total = planes_late[plane].astype(F32)
    for offset in (1, 2, 3):
        late_copies[offset - 1].wait()
        total = total + got_late[offset - 1].astype(F32)
    late_out[...] = total
    small.four_finish()


def call_tail(normed, grads, plane, one, tail):
    model = normed.shape[2]
    tokens = normed.shape[0] * normed.shape[1]
    shape = (4, 4, LATE_ROWS, 128)
    dma = pltpu.SemaphoreType.DMA
    vmem = pl.BlockSpec(memory_space=pltpu.VMEM)
    return pl.pallas_call(
        tail_kernel,
        in_specs=[vmem] * 5,
        out_specs=[vmem] * 3,
        out_shape=[
            jax.ShapeDtypeStruct((LATE_ROWS, 128), F32),
            jax.ShapeDtypeStruct((EARLY_ROWS, 128), F32),
            jax.ShapeDtypeStruct(tail.shape, F32),
        ],
        scratch_shapes=[
            pltpu.VMEM(shape, BF16),
            pltpu.VMEM(shape, BF16),
            pltpu.VMEM(shape, BF16),
            pltpu.VMEM((model, tokens), BF16),
            pltpu.VMEM((3, model, 128), BF16),
            pltpu.VMEM((3, 4, LATE_ROWS, 128), BF16),
            pltpu.VMEM((4, LATE_ROWS, 128), BF16),
            pltpu.VMEM((3, LATE_ROWS, 128), BF16),
            pltpu.VMEM((3, EARLY_ROWS, 128), BF16),
        ]
        + small_scratch(8, 4)
        + [dma((4,)), dma((4,)), dma((3, 4)), dma((3, 4)), dma((3,)), dma((3,)), dma((3,)), dma((3,))],
        compiler_params=remote_params(2),
        cost_estimate=pl.CostEstimate(flops=5 * 10**10, bytes_accessed=10**7, transcendentals=0),
        name="tail",
    )(normed, grads, plane, one, tail)


def sum_kernel(parts_ref, after, out_ref):
    out_ref[0] = sum(parts_ref[k, 0].astype(F32) for k in range(parts_ref.shape[0])).astype(out_ref.dtype)


def sum_parts(parts, kind, after):
    count, columns, rows, lanes = parts.shape
    return pl.pallas_call(
        sum_kernel,
        grid=(columns,),
        in_specs=[pl.BlockSpec((count, 1, rows, lanes), lambda s: (0, s, 0, 0)), pl.BlockSpec(memory_space=pl.ANY)],
        out_specs=pl.BlockSpec((1, rows, lanes), lambda s: (s, 0, 0)),
        out_shape=jax.ShapeDtypeStruct((columns, rows, lanes), kind),
        compiler_params=pltpu.CompilerParams(vmem_limit_bytes=VMEM_LIMIT),
        cost_estimate=pl.CostEstimate(flops=10**6, bytes_accessed=parts.size * 3, transcendentals=0),
        name="sum_parts",
    )(parts, after)


def over_chips(chips):
    return lax.all_to_all(chips, "seq", split_axis=0, concat_axis=0, axis_index_groups=[[0, 2, 4, 6], [1, 3, 5, 7]], tiled=True)


def over_planes(plane):
    return lax.all_to_all(plane, "dp", split_axis=0, concat_axis=0, tiled=True)


SMALL_ROWS = 288


class SmallSums:
    def __init__(self, one, tail, out, held, got_seq, planes, got_dp, whole_small, sems):
        self.one, self.tail, self.out = one, tail, out
        self.held, self.got_seq, self.planes, self.got_dp, self.whole = held, got_seq, planes, got_dp, whole_small
        self.sems = sems
        self.me, self.plane = lax.axis_index("seq"), lax.axis_index("dp")
        self.across, self.along = held.shape[0], held.shape[1]

    def places(self):
        half = self.held.shape[2] // 2
        units = SMALL_ROWS // half
        tiles = self.one.shape[1] // 128
        for at in range(2 * self.along * self.across):
            spot = (at // (2 * self.along), at // 2 % self.along, slice((at % 2) * half, (at % 2) * half + half))
            tile, unit = at // units, at % units
            if tile < tiles:
                yield spot, (slice(unit * half, unit * half + half), slice(128 * tile, 128 * tile + 128))
            else:
                yield spot, None

    def pack(self):
        for spot, source in self.places():
            if source is None:
                self.held[spot] = jnp.zeros((self.held.shape[2] // 2, 128), BF16)
            else:
                self.held[spot] = (self.one[source] + self.tail[source]).astype(BF16)

    def copies(self, axis, source, target, number):
        here, count = (self.me, self.across) if axis == "seq" else (self.plane, self.along)
        send, recv = self.sems[2 * number], self.sems[2 * number + 1]
        made = []
        for step in range(1, count):
            peer = lax.rem(here + step, count)
            made.append(
                pltpu.make_async_remote_copy(
                    src_ref=source(peer), dst_ref=target(step - 1), send_sem=send.at[step - 1], recv_sem=recv.at[step - 1],
                    device_id={axis: peer}, device_id_type=pl.DeviceIdType.MESH,
                )
            )
        for copy in made:
            copy.start()
        return made

    def one_start(self):
        self.waiting = self.copies("seq", lambda peer: self.held.at[peer], lambda slot: self.got_seq.at[slot], 0)

    def one_finish(self):
        for copy in self.waiting:
            copy.wait()
        total = self.held[self.me].astype(F32)
        for slot in range(self.across - 1):
            total = total + self.got_seq[slot].astype(F32)
        self.planes[...] = total.astype(BF16)
        self.waiting = self.copies("dp", lambda peer: self.planes.at[peer], lambda slot: self.got_dp.at[slot], 1)

    def two_finish(self):
        for copy in self.waiting:
            copy.wait()
        mine = self.planes[self.plane].astype(F32)
        for slot in range(self.along - 1):
            mine = mine + self.got_dp[slot].astype(F32)
        self.whole[self.me, self.plane] = mine.astype(BF16)
        self.waiting = self.copies("dp", lambda peer: self.whole.at[self.me, self.plane], lambda slot: self.whole.at[self.me, self.plane], 2)

    def three_finish(self):
        for copy in self.waiting:
            copy.wait()
        self.waiting = self.copies("seq", lambda peer: self.whole.at[self.me], lambda slot: self.whole.at[self.me], 3)

    def four_finish(self):
        for copy in self.waiting:
            copy.wait()
        for spot, target in self.places():
            if target is not None:
                self.out[target] = self.whole[spot].astype(F32)


def small_scratch(across, along):
    chunk = max(16, 2048 // (across * along))
    dma = lambda count: pltpu.SemaphoreType.DMA((count,))
    return [
        pltpu.VMEM((across, along, chunk, 128), BF16),
        pltpu.VMEM((across - 1, along, chunk, 128), BF16),
        pltpu.VMEM((along, chunk, 128), BF16),
        pltpu.VMEM((along - 1, chunk, 128), BF16),
        pltpu.VMEM((across, along, chunk, 128), BF16),
        dma(across - 1), dma(across - 1), dma(along - 1), dma(along - 1),
        dma(along - 1), dma(along - 1), dma(across - 1), dma(across - 1),
    ]


def small_kernel(one_ref, tail_ref, out_ref, held, got_seq, planes, got_dp, whole_small, *sems):
    small = SmallSums(one_ref, tail_ref, out_ref, held, got_seq, planes, got_dp, whole_small, sems)
    greet("seq", small.me, small.across)
    greet("dp", small.plane, small.along)
    small.pack()
    pl.semaphore_wait(pltpu.get_barrier_semaphore(), small.across + small.along - 2)
    small.one_start()
    small.one_finish()
    small.two_finish()
    small.three_finish()
    small.four_finish()


def call_small(one, tail, across, along):
    return pl.pallas_call(
        small_kernel,
        in_specs=[pl.BlockSpec(memory_space=pltpu.VMEM)] * 2,
        out_specs=pl.BlockSpec(memory_space=pltpu.VMEM),
        out_shape=jax.ShapeDtypeStruct(tail.shape, F32),
        scratch_shapes=small_scratch(across, along),
        compiler_params=remote_params(0),
        cost_estimate=pl.CostEstimate(flops=10**6, bytes_accessed=3 * 10**6, transcendentals=0),
        name="small_sums",
    )(one, tail)


def body(
    byte_ids,
    lengths,
    byte_table,
    conv_kernel,
    score_vector,
    norm_gain_one,
    qkv_weight,
    bias_table,
    out_weight,
    norm_gain_two,
    in_weight,
    down_weight,
    cotangent,
):
    devices = lax.axis_size("seq")
    me = lax.axis_index("seq")
    sequences, local_bytes = byte_ids.shape
    local_tokens = local_bytes // 2
    total_bytes = local_bytes * devices
    first_byte = me * local_bytes
    vocab, model = byte_table.shape
    window = local_bytes + 16
    total = sequences * PAIRS
    per_device = -(-total // devices)

    number = jnp.arange(sequences, dtype=jnp.int32)
    ahead = (lengths[None, :] > lengths[:, None]) | (
        (lengths[None, :] == lengths[:, None]) & (number[None, :] < number[:, None])
    )
    rank = jnp.sum(ahead.astype(jnp.int32), axis=1)
    placed = rank[None, :] == number[:, None]
    order = jnp.sum(jnp.where(placed, number[None, :], 0), axis=1)
    sorted_lengths = jnp.sum(jnp.where(placed, lengths[None, :], 0), axis=1)
    positions = first_byte + jnp.arange(local_bytes, dtype=jnp.int32)
    picked = jnp.where(positions[None, :] < lengths[:, None], byte_ids, 0)
    forward = [(i, i + 1) for i in range(devices - 1)]
    backward = [(target, source) for source, target in forward]
    before = jnp.where(me > 0, lax.ppermute(picked[:, -4:], "seq", forward), -1)
    after = jnp.where(me < devices - 1, lax.ppermute(picked[:, :4], "seq", backward), -1)
    outside = jnp.full((sequences, 12), -1, jnp.int32)
    extended = jnp.concatenate([before, picked, after, outside], axis=1)
    extended = jnp.sum(jnp.where(placed[:, :, None], extended[None, :, :], 0), axis=1)
    shifted = jnp.stack([extended[:, tap : tap + window] for tap in range(5)])
    ids_columns = jnp.concatenate([jnp.moveaxis(shifted, 0, 2), jnp.full((sequences, window, 3), -1, jnp.int32)], axis=2)

    table_padded = jnp.concatenate([byte_table, jnp.zeros((VPAD - vocab, model), BF16)], axis=0)
    taps = (conv_kernel[:, None, :] * table_padded.astype(F32)[None]).astype(BF16)
    rows = jnp.dot(near_one_hot(), bias_table, precision="highest").T.reshape(PAIRS, 2, NEAR)
    gain_one = norm_gain_one[None, :]
    gain_two = norm_gain_two[None, :]
    score = score_vector[None, :]

    item = me + devices * jnp.arange(per_device, dtype=jnp.int32)
    length = jnp.sum(jnp.where((item // PAIRS)[:, None] == number[None, :], sorted_lengths[None, :], 0), axis=1)
    valid = jnp.where(item < total, (length + 1) // 2, 0).astype(jnp.int32)
    pair = lax.rem(item, PAIRS).astype(jnp.int32)
    cot = reorder(cotangent, order, False)

    hidden, normed, conv, mix, share, received = call_front(ids_columns, taps, qkv_weight, gain_one, score, local_tokens, devices, per_device)
    out, aug = attention_forward(received, rows, valid, pair)
    layer, act, gate_up, normed_two, attended, branch, grad_residual, grad_items, grad_gain_two = call_mid(
        out, hidden, cot, out_weight, in_weight, down_weight, gain_two
    )
    layer_out = reorder(layer, order, True)
    along_count = lax.axis_size("dp")
    custom = devices == 8 and along_count == 4

    def scatter(grad):
        rows_own = lax.psum_scatter(grad, "seq", scatter_dimension=0, tiled=True)
        return lax.psum_scatter(rows_own, "dp", scatter_dimension=1, tiled=True).astype(F32)

    if custom:
        early_chips = call_early(act, cot, normed_two, gate_up, attended, branch)
        early_across = over_chips(early_chips)
        after = early_chips
    else:
        summed_down = scatter(jnp.einsum("bti,btd->id", act, cot, preferred_element_type=F32).astype(BF16))
        summed_in = scatter(jnp.einsum("btd,bti->di", normed_two, gate_up, preferred_element_type=F32).astype(BF16))
        summed_out = scatter(jnp.einsum("btd,bte->de", attended, branch, preferred_element_type=F32).astype(BF16))
        after = grad_gain_two
    dqkv, bias_rows = attention_backward(received, out, aug, grad_items, rows, valid, pair, after)
    after = bias_rows
    if custom:
        early_plane = sum_parts(early_across, BF16, bias_rows)
        after = early_plane
    ids_rows = shifted.reshape(5, sequences * window)
    table_block, projected = call_back(
        dqkv, hidden, grad_residual, conv, mix, share, ids_rows, qkv_weight, conv_kernel, table_padded[:SMALL_ROWS], gain_one, score, after
    )
    item_bias = jnp.einsum("ihy,yb->bih", bias_rows, near_one_hot(), precision="highest")
    pair_hot = (pair[:, None] == jnp.arange(PAIRS, dtype=jnp.int32)[None, :]).astype(F32)
    grad_bias = jnp.einsum("bih,ip->bph", item_bias, pair_hot, precision="highest").reshape(32 * 2 * PAIRS)
    tail = jnp.concatenate(
        [
            jnp.zeros((267, model), F32),
            grad_gain_two,
            jnp.pad(grad_bias, (0, model - grad_bias.shape[0]))[None, :],
            jnp.zeros((SMALL_ROWS - 269, model), F32),
        ],
        axis=0,
    )
    if custom:
        late, early, sums = call_tail(normed, projected, early_plane, table_block, tail)
        odd = lax.rem(lax.axis_index("dp"), 2) == 1

        def joined(block, tiles, columns):
            block = jnp.concatenate([block[96 * k : 96 * k + 96] for k in range(tiles)], axis=1)
            return jnp.where(odd, block[:, 64 : 64 + columns], block[:, :columns])

        summed_in = jnp.concatenate([early[96 * k : 96 * k + 96] for k in range(8)], axis=1)
        summed_down = jnp.concatenate([early[768:960], early[960:1152]], axis=1).T
        summed_out = joined(early[1152:1344], 2, 192)
        summed_qkv = joined(late, 5, 576)
    else:
        grad_qkv = jnp.einsum("btd,bte->de", normed, projected, preferred_element_type=F32).astype(BF16)
        grad_qkv = jnp.swapaxes(grad_qkv.reshape(model, PAIRS, 3, 2, 64), 2, 3).reshape(model, PAIRS * 384)
        summed_qkv = scatter(grad_qkv)
        sums = call_small(table_block, tail, devices, along_count)
    return (
        layer_out,
        sums[:vocab],
        sums[259:264],
        sums[265],
        sums[264],
        summed_qkv,
        sums[268, : 32 * 2 * PAIRS].reshape(32, 2 * PAIRS),
        summed_out,
        sums[267],
        summed_in,
        summed_down,
    )


def solution(mesh):
    return jax.shard_map(
        body,
        mesh=mesh,
        in_specs=(
            P("dp", "seq"),
            P("dp"),
            P(),
            P(),
            P(),
            P(),
            P(),
            P(),
            P(),
            P(),
            P(),
            P(),
            P("dp", "seq", None),
        ),
        out_specs=(
            P("dp", "seq", None),
            P(),
            P(),
            P(),
            P(),
            P("seq", "dp"),
            P(),
            P("seq", "dp"),
            P(),
            P("seq", "dp"),
            P("seq", "dp"),
        ),
        check_vma=False,
    )
```

```python
import functools
import jax
import jax.numpy as jnp
from jax import lax
from jax.experimental import pallas as pl
from jax.experimental.pallas import tpu as pltpu
from jax.sharding import PartitionSpec as P

thresholds = (12, 16, 23, 32, 46, 64, 91)
KB = 256
NEAR = 1024
F32 = jnp.float32
BF16 = jnp.bfloat16
NT = (((1,), (1,)), ((), ()))
NN = (((1,), (0,)), ((), ()))


def rel_bucket(relative):
    distance = jnp.abs(relative)
    larger = 8 + sum(((distance >= boundary).astype(jnp.int32) for boundary in thresholds))
    bucket = jnp.where(distance < 8, distance, larger)
    return bucket + 16 * (relative > 0).astype(jnp.int32)


def near_one_hot():
    place = jnp.arange(NEAR, dtype=jnp.int32)
    relative = jnp.where(place < NEAR - 128, KB - place, KB + NEAR - place)
    return (rel_bucket(relative)[:, None] == jnp.arange(32, dtype=jnp.int32)[None, :]).astype(F32)


def dot(a, b, dims):
    return lax.dot_general(a, b, dims, preferred_element_type=F32)


def fill_bias(strip, head, row, blocks):
    base = KB * (blocks - 2)
    width = KB * (2 * blocks - 1)
    spread = jnp.broadcast_to(row, (128, NEAR))
    rolled = pltpu.roll(spread, 0, 1, stride=1, stride_axis=0)
    far_right = jnp.broadcast_to(row[:, NEAR - 1 :], (KB, 128))
    far_left = jnp.broadcast_to(row[:, 768:769], (KB, 128))
    for start in range(0, base, 128):
        strip[head, :, start : start + 128] = far_right
    strip[head, 0:128, base : base + 768] = rolled[:, :768]
    strip[head, 128:256, base : base + 128] = far_right[:128]
    strip[head, 128:256, base + 128 : base + 768] = rolled[:, :640]
    for start in range(base + 768, width, 128):
        strip[head, :, start : start + 128] = far_left


def lanes_of(head, shape):
    lane = lax.broadcasted_iota(jnp.int32, shape, 1)
    own = (lane < 64) if head == 0 else (lane >= 64)
    return own, lane - (64 if head == 0 else 0)


def fill_keys(ka, head, keys, valid):
    own, spare = lanes_of(head, keys.shape)
    row = lax.broadcasted_iota(jnp.int32, keys.shape, 0)
    masked = jnp.where(row < valid, 0.0, -1e9)
    extra = jnp.where(spare == 0, masked, jnp.where((spare >= 1) & (spare <= 3), 1.0, 0.0))
    ka[head] = jnp.where(own, keys, extra.astype(BF16))


def move_rows(item, order_ref, source, buffer, target, sems, sorting):
    def inward(number):
        place = order_ref[number] if sorting else number
        return pltpu.make_async_copy(source.at[place], buffer.at[number], sems.at[0, number])

    def outward(number):
        place = number if sorting else order_ref[number]
        return pltpu.make_async_copy(buffer.at[number], target.at[place], sems.at[1, number])

    count = source.shape[0]

    @pl.when(item == 0)
    def _():
        for number in range(count):
            inward(number).start()

    @pl.when(item == jnp.minimum(1, pl.num_programs(0) - 1))
    def _():
        for number in range(count):
            inward(number).wait()
            outward(number).start()

    def finish():
        @pl.when(item == pl.num_programs(0) - 1)
        def _():
            for number in range(count):
                outward(number).wait()

    return finish


def fwd_kernel(
    blocks, valid_ref, pair_ref, order_ref, qkv_ref, row_ref, cot_ref, out_ref, aug_ref, sorted_ref,
    qa, ka, vt, strip, peak, acc, probs, moving, sems,
):
    item = pl.program_id(0)
    finish = move_rows(item, order_ref, cot_ref, moving, sorted_ref, sems, True)
    valid = valid_ref[item]
    tokens = blocks * KB
    joined = qkv_ref[:, 0].reshape(tokens, 384)
    queries = joined[:, 0:128]
    keys = joined[:, 128:256]
    turned = joined[:, 256:384].T
    filler = jnp.where(lax.broadcasted_iota(jnp.int32, (16, tokens), 0) == 0, 1.0, 0.0).astype(BF16)
    for head in range(2):
        own, spare = lanes_of(head, queries.shape)
        qa[head] = jnp.where(own, queries, jnp.where(spare == 0, 1.0, 0.0).astype(BF16))
        fill_keys(ka, head, keys, valid)
        vt[head, 0:64] = turned[64 * head : 64 * head + 64]
        vt[head, 64:80] = filler
        fill_bias(strip, head, row_ref[0, head : head + 1, :], blocks)
    peak[...] = jnp.full_like(peak, -1e30)
    acc[...] = jnp.zeros_like(acc)

    def step(block, unused):
        first = pl.multiple_of(block * KB, KB)
        shift = pl.multiple_of((blocks - 1 - block) * KB, KB)
        for head in range(2):
            alphas = []
            for part in range(blocks):
                here = slice(part * KB, part * KB + KB)
                logits = dot(ka[head, pl.ds(first, KB), :], qa[head, here, :], NT)
                logits = logits + strip[head, :, pl.ds(shift + part * KB, KB)]
                before = peak[head, :, here]
                after = jnp.maximum(before, jnp.max(logits, axis=0, keepdims=True))
                probs[head, :, here] = jnp.exp(logits - after).astype(BF16)
                peak[head, :, here] = after
                alphas.append(jnp.exp(before - after))
            acc[head] = acc[head] * jnp.concatenate(alphas, axis=1) + dot(
                    vt[head, :, pl.ds(first, KB)], probs[head], NN
                )
        return unused

    lax.fori_loop(0, (valid + KB - 1) // KB, step, 0)
    outs = []
    rows = []
    place = lax.broadcasted_iota(jnp.int32, (64, tokens), 0)
    for head in range(2):
        total = acc[head, 64:65, :]
        outs.append(acc[head, 0:64, :] / total)
        minus = -(peak[head] + jnp.log(total))
        high = minus.astype(BF16).astype(F32)
        rest = minus - high
        middle = rest.astype(BF16).astype(F32)
        low = rest - middle
        rows.append(jnp.where(place == 0, 1.0, jnp.where(place == 1, high, jnp.where(place == 2, middle, jnp.where(place == 3, low, 0.0)))))
    out_ref[:, 0] = jnp.concatenate(outs, axis=0).T.astype(BF16).reshape(out_ref.shape[0], out_ref.shape[2], 128)
    aug_ref[0] = jnp.concatenate([rows[1], rows[0]], axis=0).T.astype(BF16)
    finish()


def bwd_kernel(
    blocks, base_slot, moves, valid_ref, pair_ref, order_ref, qkv_ref, out_ref, aug_ref, grad_ref, row_ref, layer_ref, after,
    dqkv_ref, bias_ref, moved_ref, qa, ka, va, ga, kt, strip, tally, probs, slopes, dq, *moving,
):
    item = pl.program_id(0)
    finish = move_rows(item, order_ref, layer_ref, moving[0], moved_ref, moving[1], False) if moves else lambda: None
    valid = valid_ref[item + base_slot]
    tokens = blocks * KB
    width = KB * (2 * blocks - 1)
    local = qkv_ref.shape[2]
    joined = qkv_ref[:, 0].reshape(tokens, 384)
    queries = joined[:, 0:128]
    keys = joined[:, 128:256]
    values = joined[:, 256:384]
    grads = grad_ref[:, 0].reshape(tokens, 128)
    outs = out_ref[:, 0].reshape(tokens, 128)
    kt[...] = keys.T
    product = grads.astype(F32) * outs.astype(F32)
    high = product.astype(BF16)
    low = (product - high.astype(F32)).astype(BF16)
    row_at = lax.broadcasted_iota(jnp.int32, (128, 128), 0)
    lane_at = lax.broadcasted_iota(jnp.int32, (128, 128), 1)
    pick = jnp.where((row_at < 64) == (lane_at >= 64), -1.0, 0.0).astype(BF16)
    shifts = dot(high, pick, NN) + dot(low, pick, NN)
    shift_high = shifts.astype(BF16)
    shift_low = (shifts - shift_high.astype(F32)).astype(BF16)
    for head in range(2):
        own, spare = lanes_of(head, queries.shape)
        qa[head] = jnp.where(own, queries, aug_ref[0])
        fill_keys(ka, head, keys, valid)
        va[head] = jnp.where(own, values, jnp.where((spare == 0) | (spare == 1), 1.0, 0.0).astype(BF16))
        ga[head] = jnp.where(own, grads, jnp.where(spare == 0, shift_high, jnp.where(spare == 1, shift_low, jnp.zeros_like(shift_low))))
        fill_bias(strip, head, row_ref[0, head : head + 1, :], blocks)
    tally[...] = jnp.zeros_like(tally)
    dq[...] = jnp.zeros_like(dq)
    dqkv_ref[...] = jnp.zeros_like(dqkv_ref)

    def step(block, unused):
        first = pl.multiple_of(block * KB, KB)
        shift = pl.multiple_of((blocks - 1 - block) * KB, KB)
        key_parts = []
        value_parts = []
        for head in range(2):
            for part in range(blocks):
                here = slice(part * KB, part * KB + KB)
                there = pl.ds(shift + part * KB, KB)
                logits = dot(ka[head, pl.ds(first, KB), :], qa[head, here, :], NT)
                weights = jnp.exp(logits + strip[head, :, there])
                change = dot(va[head, pl.ds(first, KB), :], ga[head, here, :], NT)
                slope = weights * change
                tally[head, :, there] += slope
                probs[head, :, here] = weights.astype(BF16)
                slopes[head, :, here] = slope.astype(BF16)
            value_parts.append(dot(probs[head], ga[head], NN))
            key_parts.append(dot(slopes[head], qa[head], NN))
            dq[pl.ds(64 * head, 64), :] += dot(kt[pl.ds(64 * head, 64), pl.ds(first, KB)], slopes[head], NN)
        own, unused_spare = lanes_of(0, (KB, 128))
        count = KB // local
        where = pl.ds(block * count, count)
        dqkv_ref[where, 0, :, 128:256] = jnp.where(own, key_parts[0], key_parts[1]).astype(BF16).reshape(count, local, 128)
        dqkv_ref[where, 0, :, 256:384] = jnp.where(own, value_parts[0], value_parts[1]).astype(BF16).reshape(count, local, 128)
        return unused

    lax.fori_loop(0, (valid + KB - 1) // KB, step, 0)
    dqkv_ref[:, 0, :, 0:128] = dq[...].T.astype(BF16).reshape(dqkv_ref.shape[0], local, 128)
    base = KB * (blocks - 2)
    lane = lax.broadcasted_iota(jnp.int32, (1, NEAR), 1)
    flip = jnp.where(row_at + lane_at == 127, 1.0, 0.0).astype(BF16)
    for head in range(2):
        far_right = sum(tally[head, :, start : start + 128] for start in range(0, base, 128)) if base else jnp.zeros((KB, 128), F32)
        far_right = far_right[:128] + far_right[128:] + tally[head, 128:256, base : base + 128]
        left_list = [tally[head, :, start : start + 128] for start in range(base + 768, width, 128)]
        far_left = sum(left_list) if left_list else jnp.zeros((KB, 128), F32)
        near = tally[head, 0:128, base : base + 768]
        near_low = tally[head, 128:256, base + 128 : base + 768]
        near = near + jnp.concatenate([near_low, jnp.zeros((128, 128), F32)], axis=1)
        near = jnp.concatenate([near, jnp.zeros((128, NEAR - 768), F32)], axis=1)
        near_high = near.astype(BF16)
        flipped = dot(flip, near_high, NN) + dot(flip, (near - near_high.astype(F32)).astype(BF16), NN)
        rolled = pltpu.roll(flipped, NEAR - 127, 1, stride=1, stride_axis=0)
        row = jnp.sum(rolled, axis=0, keepdims=True)
        row = row + jnp.where(lane == NEAR - 1, jnp.sum(far_right), 0.0) + jnp.where(lane == 768, jnp.sum(far_left), 0.0)
        bias_ref[0, head : head + 1, :] = row
    finish()


def attention_forward(qkv, rows, valid, pair, order, cot):
    sources, items, local, unused = qkv.shape
    blocks = sources * local // KB
    tokens = sources * local
    width = KB * (2 * blocks - 1)
    spec = pltpu.PrefetchScalarGridSpec(
        num_scalar_prefetch=3,
        grid=(items,),
        in_specs=[
            pl.BlockSpec((sources, 1, local, 384), lambda i, v, p, o: (0, i, 0, 0)),
            pl.BlockSpec((1, 2, NEAR), lambda i, v, p, o: (p[i], 0, 0)),
            pl.BlockSpec(memory_space=pl.ANY),
        ],
        out_specs=[
            pl.BlockSpec((sources, 1, local, 128), lambda i, v, p, o: (0, i, 0, 0)),
            pl.BlockSpec((1, tokens, 128), lambda i, v, p, o: (i, 0, 0)),
            pl.BlockSpec(memory_space=pl.ANY),
        ],
        scratch_shapes=[
            pltpu.VMEM((2, tokens, 128), BF16),
            pltpu.VMEM((2, tokens, 128), BF16),
            pltpu.VMEM((2, 80, tokens), BF16),
            pltpu.VMEM((2, KB, width), F32),
            pltpu.VMEM((2, 1, tokens), F32),
            pltpu.VMEM((2, 80, tokens), F32),
            pltpu.VMEM((2, KB, tokens), BF16),
            pltpu.VMEM(cot.shape, cot.dtype),
            pltpu.SemaphoreType.DMA((2,) + cot.shape[:1]),
        ],
    )
    return pl.pallas_call(
        functools.partial(fwd_kernel, blocks),
        grid_spec=spec,
        out_shape=[
            jax.ShapeDtypeStruct((sources, items, local, 128), BF16),
            jax.ShapeDtypeStruct((items, tokens, 128), BF16),
            jax.ShapeDtypeStruct(cot.shape, cot.dtype),
        ],
        compiler_params=pltpu.CompilerParams(vmem_limit_bytes=50 * 2**20),
        cost_estimate=pl.CostEstimate(flops=items * tokens * tokens * 512, bytes_accessed=items * tokens * 2048, transcendentals=items * tokens * tokens * 2),
        name="attention_forward",
    )(valid, pair, order, qkv, rows, cot)


def attention_backward(qkv, outs, aug, grads, rows, valid, pair, order, layer, after, first, items):
    sources, unused, local, unused = qkv.shape
    moves = layer is not None
    layer = after if layer is None else layer
    moved = layer if moves else jnp.zeros((8, 128), F32)
    blocks = sources * local // KB
    tokens = sources * local
    width = KB * (2 * blocks - 1)
    big = lambda lanes: pl.BlockSpec((sources, 1, local, lanes), lambda i, v, p, o: (0, i + first, 0, 0))
    spec = pltpu.PrefetchScalarGridSpec(
        num_scalar_prefetch=3,
        grid=(items,),
        in_specs=[
            big(384),
            big(128),
            pl.BlockSpec((1, tokens, 128), lambda i, v, p, o: (i + first, 0, 0)),
            big(128),
            pl.BlockSpec((1, 2, NEAR), lambda i, v, p, o: (p[i + first], 0, 0)),
            pl.BlockSpec(memory_space=pl.ANY),
            pl.BlockSpec(memory_space=pl.ANY),
        ],
        out_specs=[
            pl.BlockSpec((sources, 1, local, 384), lambda i, v, p, o: (0, i, 0, 0)),
            pl.BlockSpec((1, 2, NEAR), lambda i, v, p, o: (i, 0, 0)),
            pl.BlockSpec(memory_space=pl.ANY),
        ],
        scratch_shapes=[
            pltpu.VMEM((2, tokens, 128), BF16),
            pltpu.VMEM((2, tokens, 128), BF16),
            pltpu.VMEM((2, tokens, 128), BF16),
            pltpu.VMEM((2, tokens, 128), BF16),
            pltpu.VMEM((128, tokens), BF16),
            pltpu.VMEM((2, KB, width), F32),
            pltpu.VMEM((2, KB, width), F32),
            pltpu.VMEM((2, KB, tokens), BF16),
            pltpu.VMEM((2, KB, tokens), BF16),
            pltpu.VMEM((128, tokens), F32),
        ]
        + ([pltpu.VMEM(layer.shape, layer.dtype), pltpu.SemaphoreType.DMA((2,) + layer.shape[:1])] if moves else []),
    )
    return pl.pallas_call(
        functools.partial(bwd_kernel, blocks, first, moves),
        grid_spec=spec,
        out_shape=[
            jax.ShapeDtypeStruct((sources, items, local, 384), BF16),
            jax.ShapeDtypeStruct((items, 2, NEAR), F32),
            jax.ShapeDtypeStruct(moved.shape, moved.dtype),
        ],
        compiler_params=pltpu.CompilerParams(vmem_limit_bytes=50 * 2**20),
        cost_estimate=pl.CostEstimate(flops=items * tokens * tokens * 1280, bytes_accessed=items * tokens * 4096, transcendentals=items * tokens * tokens * 2),
        name="attention_backward",
    )(valid, pair, order, qkv, outs, aug, grads, rows, layer, after)


VPAD = 384
PAIRS = 6
TN = (((0,), (0,)), ((), ()))
SQRT_2_OVER_PI = 0.7978845608028654


def block_masks(masks, first_byte, total_bytes):
    shape = masks.shape[2:]
    conv_at = first_byte - 2 + lax.broadcasted_iota(jnp.int32, shape, 1)
    token = lax.broadcasted_iota(jnp.int32, shape, 0)
    for side in range(2):
        place = first_byte + 2 * token + side
        for size in range(1, 5):
            start = (place // size) * size
            inside = (conv_at >= start) & (conv_at < start + size) & (conv_at < total_bytes)
            masks[side, size - 1] = jnp.where(inside, 1.0 / size, 0.0)


def split_two(values):
    high = values.astype(BF16)
    return high, (values - high.astype(F32)).astype(BF16)


def permute_weight(weight, out):
    rows = weight.shape[0]
    low = lax.broadcasted_iota(jnp.int32, (rows, 128), 1) < 64
    for pair in range(PAIRS):
        at = pair * 384
        one, two, three = (weight[:, at + 128 * k : at + 128 * k + 128] for k in range(3))
        out[:, at : at + 128] = jnp.where(low, one, two)
        out[:, at + 128 : at + 256] = pltpu.roll(jnp.where(low, three, one).astype(F32), 64, 1).astype(BF16)
        out[:, at + 256 : at + 384] = jnp.where(low, two, three)


def greet(axis, here, count):
    barrier = pltpu.get_barrier_semaphore()

    def signal(step, unused):
        pl.semaphore_signal(barrier, inc=1, device_id={axis: lax.rem(here + step, count)}, device_id_type=pl.DeviceIdType.MESH)
        return unused

    lax.fori_loop(1, count, signal, 0)


def item_copy(devices, me, source, target, other, slot, sems):
    send, recv, unused = sems

    def outward():
        offset = lax.rem(other - me + devices, devices)
        return pltpu.make_async_remote_copy(
            src_ref=source, dst_ref=target, send_sem=send.at[offset, slot], recv_sem=recv.at[offset, slot],
            device_id={"seq": other}, device_id_type=pl.DeviceIdType.MESH,
        )

    def inward():
        offset = lax.rem(me - other + devices, devices)
        return pltpu.make_async_remote_copy(
            src_ref=source, dst_ref=target, send_sem=send.at[offset, slot], recv_sem=recv.at[offset, slot],
            device_id={"seq": other}, device_id_type=pl.DeviceIdType.MESH,
        )

    return outward, inward


def start_item(devices, me, source, target, other, slot, sems):
    @pl.when(other == me)
    def _():
        pltpu.make_async_copy(source, target, sems[2].at[slot]).start()

    @pl.when(other != me)
    def _():
        item_copy(devices, me, source, target, other, slot, sems)[0]().start()


def finish_sends(devices, me, total, source_of, target_of, sems):
    def wait(item, unused):
        other, slot = lax.rem(item, devices), item // devices

        @pl.when(other != me)
        def _():
            item_copy(devices, me, source_of(other, slot), target_of(other, slot), other, slot, sems)[0]().wait_send()

        return unused

    lax.fori_loop(0, total, wait, 0)


def finish_receives(devices, me, total, source_of, target_of, sems):
    per_device = -(-total // devices)

    def wait(at, unused):
        other, slot = at // per_device, lax.rem(at, per_device)

        @pl.when((slot * devices + me < total) & (other != me))
        def _():
            item_copy(devices, me, source_of(other, slot), target_of(other, slot), other, slot, sems)[1]().wait_recv()

        @pl.when((slot * devices + me < total) & (other == me))
        def _():
            pltpu.make_async_copy(source_of(other, slot), target_of(other, slot), sems[2].at[slot]).wait()

        return unused

    lax.fori_loop(0, devices * per_device, wait, 0)


def front_kernel(
    sizes, ids_ref, table_ref, weight_ref, vectors_ref,
    hidden_ref, normed_ref, conv_ref, mix_ref, share_ref, items_ref, masks, wide, permuted, stage, taps, *sems,
):
    local_tokens, window, devices, total = sizes
    step = pl.program_id(0)
    me = lax.axis_index("seq")

    @pl.when(step == 0)
    def _():
        greet("seq", me, devices)
        block_masks(masks, me * 2 * local_tokens, devices * 2 * local_tokens)
        permute_weight(weight_ref, permuted)
        table = table_ref[...].astype(F32)
        for tap in range(5):
            taps[tap] = (vectors_ref[tap : tap + 1, :] * table).astype(BF16)

    together = ids_ref.shape[0]
    score = vectors_ref[7:8, :]
    gain = vectors_ref[5:6, :]
    model = score.shape[1]
    score_high, score_low = split_two(score)
    row16 = lax.broadcasted_iota(jnp.int32, (16, model), 0)
    score_rows = jnp.where(row16 == 0, score_high.astype(F32), jnp.where(row16 == 1, score_low.astype(F32), 0.0)).astype(BF16)
    lane = lax.broadcasted_iota(jnp.int32, (together * window, VPAD), 1)
    width = masks.shape[3]
    ids = ids_ref[...].reshape(together * window, 8)
    conv_all = jnp.zeros((together * window, model), F32)
    for tap in range(5):
        hot = jnp.where(ids[:, tap : tap + 1] == lane, 1.0, 0.0).astype(BF16)
        conv_all = conv_all + dot(hot, taps[tap], NN)
    for one in range(together):
        high, low = split_two(conv_all[one * window : (one + 1) * window])
        conv_ref[one, 0:window] = high
        wide[one, 0, 0:window] = high
        wide[one, 1, 0:window] = low
        if width > window:
            wide[one, :, window:width] = jnp.zeros((2, width - window, model), BF16)
            conv_ref[one, window:width] = jnp.zeros((width - window, model), BF16)
        high = wide[one, 0]
        low = wide[one, 1]
        along = jnp.sum(dot(score_rows, high, NT), axis=0, keepdims=True) + dot(score_rows, low, NT)[0:1]
        mixed = jnp.zeros((local_tokens, width), F32)
        kept = jnp.zeros((local_tokens, 128), F32)
        lane128 = lax.broadcasted_iota(jnp.int32, (local_tokens, 128), 1)
        for side in range(2):
            scores = [jnp.sum(masks[side, k] * along, axis=1, keepdims=True) for k in range(4)]
            top = jnp.maximum(jnp.maximum(scores[0], scores[1]), jnp.maximum(scores[2], scores[3]))
            powers = [jnp.exp(value - top) for value in scores]
            under = 1.0 / (powers[0] + powers[1] + powers[2] + powers[3])
            for k in range(4):
                share = powers[k] * under
                mixed = mixed + share * masks[side, k]
                kept = jnp.where(lane128 == 4 * side + k, share, kept)
        share_ref[one] = kept
        mix_high, mix_low = split_two(mixed * 0.5)
        mix_ref[one] = mix_high
        hidden = dot(mix_high, high, NN) + dot(mix_high, low, NN) + dot(mix_low, high, NN)
        hidden_ref[one] = hidden
        scale = lax.rsqrt(jnp.mean(hidden * hidden, axis=1, keepdims=True) + 1e-06)
        normed_ref[one] = (hidden * scale * gain).astype(BF16)
    normed = normed_ref[...].reshape(together * local_tokens, model)
    for pair in range(PAIRS):
        piece = dot(normed, permuted[:, pair * 384 : pair * 384 + 384], NN).astype(BF16)
        for one in range(together):
            item = (step * together + one) * PAIRS + pair
            other, slot = lax.rem(item, devices), item // devices
            stage[other, slot] = piece[one * local_tokens : (one + 1) * local_tokens]

    @pl.when(step == 0)
    def _():
        pl.semaphore_wait(pltpu.get_barrier_semaphore(), devices - 1)

    send_items(devices, me, step * together * PAIRS, together * PAIRS, stage, items_ref, sems)

    @pl.when(step == pl.num_programs(0) - 1)
    def _():
        finish_sends(devices, me, total, lambda other, slot: stage.at[other, slot], lambda other, slot: items_ref.at[me, slot], sems)
        finish_receives(devices, me, total, lambda other, slot: stage.at[other, slot], lambda other, slot: items_ref.at[other, slot], sems)


def send_group(devices, me, total, group, number, source, arrived, sems):
    for slot in range(-(-total // devices)):
        item = slot * devices + me

        @pl.when((item < total) & (item // group == number))
        def _():
            def send(offset, unused):
                other = lax.rem(me + offset, devices)
                start_item(devices, me, source.at[other, slot], arrived.at[me, slot], other, slot, sems)
                return unused

            lax.fori_loop(0, devices, send, 0)


def send_items(devices, me, first, count, stage, target, sems):
    def send(at, unused):
        item = first + at
        other, slot = lax.rem(item, devices), item // devices
        start_item(devices, me, stage.at[other, slot], target.at[me, slot], other, slot, sems)
        return unused

    lax.fori_loop(0, count, send, 0)


def take_items(devices, me, first, count, source, arrived, sems):
    def take(at, unused):
        item = first + at
        take_item(devices, me, lax.rem(item, devices), item // devices, source, arrived, sems)
        return unused

    lax.fori_loop(0, count, take, 0)


def finish_groups(devices, me, total, source, arrived, sems):
    per_device = -(-total // devices)

    def wait(at, unused):
        slot, offset = at // devices, lax.rem(at, devices)
        other = lax.rem(me + offset, devices)

        @pl.when((slot * devices + me < total) & (offset != 0))
        def _():
            item_copy(devices, me, source.at[other, slot], arrived.at[me, slot], other, slot, sems)[0]().wait_send()

        return unused

    lax.fori_loop(0, devices * per_device, wait, 0)


def take_item(devices, me, other, slot, source, arrived, sems):
    @pl.when(other == me)
    def _():
        pltpu.make_async_copy(source.at[me, slot], arrived.at[me, slot], sems[2].at[slot]).wait()

    @pl.when(other != me)
    def _():
        item_copy(devices, me, source.at[other, slot], arrived.at[other, slot], other, slot, sems)[1]().wait_recv()


def mid_kernel(
    sizes, att_ref, hidden_ref, cot_ref, out_weight_ref, in_weight_ref, down_ref, vectors_ref,
    layer_ref, act_ref, gate_up_ref, normed_ref, attended_ref, branch_ref, residual_ref, items_ref, gain_out,
    arrived, stage, keep_gain, grad_act, *sems,
):
    local_tokens, devices, total = sizes
    in_sems, out_sems = sems[:3], sems[3:]
    step = pl.program_id(0)
    me = lax.axis_index("seq")

    @pl.when(step == 0)
    def _():
        greet("seq", me, devices)
        keep_gain[...] = jnp.zeros_like(keep_gain)
        pl.semaphore_wait(pltpu.get_barrier_semaphore(), devices - 1)

    together = hidden_ref.shape[0]
    group = together * PAIRS
    rows = together * local_tokens
    model = vectors_ref.shape[1]

    here_rows = pl.ds(pl.multiple_of(step * rows, 128), rows)

    @pl.when(step == 0)
    def _():
        send_group(devices, me, total, group, 0, att_ref, arrived, in_sems)
        every = cot_ref[...].reshape(grad_act.shape[0], model)
        for first in range(0, down_ref.shape[0], 512):
            grad_act[:, first : first + 512] = dot(every, down_ref[first : first + 512, :], NT)

    take_items(devices, me, step * group, group, att_ref, arrived, in_sems)

    @pl.when(step + 1 < pl.num_programs(0))
    def _():
        send_group(devices, me, total, group, step + 1, att_ref, arrived, in_sems)

    gathered = []
    for one in range(together):
        pieces = []
        for pair in range(PAIRS):
            item = (step * together + one) * PAIRS + pair
            other, slot = lax.rem(item, devices), item // devices
            pieces.append(arrived[other, slot])
        gathered.append(jnp.concatenate(pieces, axis=1))
    attended = jnp.concatenate(gathered, axis=0)
    attended_ref[...] = attended.reshape(attended_ref.shape)
    residual = hidden_ref[...].reshape(rows, model) + dot(attended, out_weight_ref[...], NN)
    gain = vectors_ref[6:7, :]
    scale = lax.rsqrt(jnp.mean(residual * residual, axis=1, keepdims=True) + 1e-06)
    normed = (residual * scale * gain).astype(BF16)
    normed_ref[...] = normed.reshape(normed_ref.shape)
    cot = cot_ref[pl.ds(step * together, together)].reshape(rows, model)
    hidden_units = down_ref.shape[0]
    chunk = 512
    layer = residual
    back = jnp.zeros_like(residual)
    for first in range(0, hidden_units, chunk):
        here = slice(first, first + chunk)
        there = slice(hidden_units + first, hidden_units + first + chunk)
        gate = dot(normed, in_weight_ref[:, here], NN)
        up = dot(normed, in_weight_ref[:, there], NN)
        grad = grad_act[here_rows, here]
        square = gate * gate
        inner = gate * (SQRT_2_OVER_PI + (SQRT_2_OVER_PI * 0.044715) * square)
        curve = jnp.tanh(inner)
        half_plus = 0.5 + 0.5 * curve
        smooth = gate * half_plus
        slope = half_plus + (0.5 * gate) * (1.0 - curve * curve) * (SQRT_2_OVER_PI + (3 * SQRT_2_OVER_PI * 0.044715) * square)
        act = (smooth * up).astype(BF16)
        grad_gate = (grad * up * slope).astype(BF16)
        grad_up = (grad * smooth).astype(BF16)
        act_ref[:, :, here] = act.reshape(together, local_tokens, chunk)
        gate_up_ref[:, :, here] = grad_gate.reshape(together, local_tokens, chunk)
        gate_up_ref[:, :, there] = grad_up.reshape(together, local_tokens, chunk)
        layer = layer + dot(act, down_ref[here, :], NN)
        back = back + dot(grad_gate, in_weight_ref[:, here], NT) + dot(grad_up, in_weight_ref[:, there], NT)
    layer_ref[...] = layer.reshape(layer_ref.shape)
    weighted = gain * back
    inner_mean = jnp.mean(residual * weighted, axis=1, keepdims=True)
    grad_residual = cot.astype(F32) + scale * weighted - residual * (scale * scale * scale * inner_mean)
    residual_ref[...] = grad_residual.reshape(residual_ref.shape)
    branch = grad_residual.astype(BF16)
    branch_ref[...] = branch.reshape(branch_ref.shape)
    grad_attended = dot(branch, out_weight_ref[...], NT).astype(BF16)
    for one in range(together):
        for pair in range(PAIRS):
            item = (step * together + one) * PAIRS + pair
            other, slot = lax.rem(item, devices), item // devices
            stage[other, slot] = grad_attended[one * local_tokens : (one + 1) * local_tokens, pair * 128 : pair * 128 + 128]
    keep_gain[...] += jnp.sum((back * residual * scale).reshape(rows // 8, 8, model), axis=0)
    gain_out[...] = jnp.sum(keep_gain[...], axis=0, keepdims=True)
    send_items(devices, me, step * group, group, stage, items_ref, out_sems)

    @pl.when(step == pl.num_programs(0) - 1)
    def _():
        finish_groups(devices, me, total, att_ref, arrived, in_sems)
        finish_sends(devices, me, total, lambda other, slot: stage.at[other, slot], lambda other, slot: items_ref.at[me, slot], out_sems)
        finish_receives(devices, me, total, lambda other, slot: stage.at[other, slot], lambda other, slot: items_ref.at[other, slot], out_sems)


def back_kernel(
    sizes, custom, one_ref, two_ref, hidden_ref, residual_ref, conv_ref, mix_ref, share_ref, ids_ref, weight_ref,
    table_ref, vectors_ref, bias_ref, bias_hot_ref, gain_two_ref, *refs,
):
    local_tokens, window, devices = sizes
    step = pl.program_id(0)
    last = step == pl.num_programs(0) - 1
    me = lax.axis_index("seq")
    plane = lax.axis_index("dp")
    model = vectors_ref.shape[1]
    if custom:
        normed_ref, across_ref, planes_ref = refs[:3]
        block, qkv_out, in_out, down_out, weight_out = refs[3:8]
        refs = refs[8:]
    else:
        block, flat_out, refs = refs[0], refs[1], refs[2:]
    masks, permuted, tap_sums, keep_gain, keep_score = refs[:5]
    refs = refs[5:]
    small = SmallSums(block, refs[:5], refs[5:13])
    refs = refs[13:]

    @pl.when(step == 0)
    def _():
        greet("seq", me, devices)
        greet("dp", plane, small.along)
        keep_gain[...] = jnp.zeros_like(keep_gain)
        keep_score[...] = jnp.zeros_like(keep_score)
        tap_sums[...] = jnp.zeros_like(tap_sums)
        pl.semaphore_wait(pltpu.get_barrier_semaphore(), devices + small.along - 2)

    half = one_ref.shape[1]

    def block_of(item):
        other, slot = lax.rem(item, devices), item // devices
        if isinstance(item, int):
            return (one_ref if slot < half else two_ref)[other, slot % half]
        return jnp.where(slot < half, one_ref[other, jnp.minimum(slot, half - 1)], two_ref[other, jnp.maximum(slot - half, 0)])

    if custom:
        reduce = WeightSums(normed_ref, across_ref, planes_ref, block_of, refs)

        @pl.when(step == 0)
        def _():
            reduce.begin()
            reduce.late()

        @pl.when(step == 1)
        def _():
            reduce.second()

        @pl.when(step == 5)
        def _():
            reduce.third()
            reduce.between()

    @pl.when(step == 0)
    def _():
        block_masks(masks, me * 2 * local_tokens, devices * 2 * local_tokens)
        permute_weight(weight_ref, permuted)

    projected = jnp.concatenate([block_of(step * PAIRS + pair) for pair in range(PAIRS)], axis=1)
    if not custom:
        flat_out[0] = projected
    width = masks.shape[3]
    grad_normed = dot(projected, permuted[...], NT)
    hidden = hidden_ref[0]
    gain = vectors_ref[5:6, :]
    score = vectors_ref[7:8, :]
    scale = lax.rsqrt(jnp.mean(hidden * hidden, axis=1, keepdims=True) + 1e-06)
    weighted = gain * grad_normed
    inner_mean = jnp.mean(hidden * weighted, axis=1, keepdims=True)
    grad_hidden = residual_ref[0] + scale * weighted - hidden * (scale * scale * scale * inner_mean)
    keep_gain[...] += jnp.sum((grad_normed * hidden * scale).reshape(local_tokens // 8, 8, model), axis=0)
    high, low = split_two(grad_hidden)
    vector = jnp.broadcast_to(score.astype(BF16), (local_tokens, model))
    conv = conv_ref[0]
    cross = 0.5 * (dot(high, conv, NT) + dot(low, conv, NT))
    kept = share_ref[0]
    total = jnp.zeros((local_tokens, width), F32)
    for side in range(2):
        shares = [kept[:, 4 * side + k : 4 * side + k + 1] for k in range(4)]
        grads = [jnp.sum(masks[side, k] * cross, axis=1, keepdims=True) for k in range(4)]
        mean = sum(share * grad for share, grad in zip(shares, grads))
        for k in range(4):
            total = total + (shares[k] * (grads[k] - mean)) * masks[side, k]
    column = jnp.sum(total, axis=0, keepdims=True)
    column_high, column_low = split_two(column)
    row16 = lax.broadcasted_iota(jnp.int32, (16, width), 0)
    column_rows = jnp.where(row16 == 0, column_high.astype(F32), jnp.where(row16 == 1, column_low.astype(F32), 0.0)).astype(BF16)
    keep_score[...] += dot(column_rows, conv, NN)
    left = jnp.concatenate([mix_ref[0], total.astype(BF16)], axis=0)
    right = jnp.concatenate([high, vector], axis=0)
    slope = dot(left, right, TN)
    slope = slope[0:window].astype(BF16)
    row = lax.broadcasted_iota(jnp.int32, (SMALL_ROWS, window), 0)
    hots = [jnp.where(ids_ref[0, tap : tap + 1, :] == row, 1.0, 0.0).astype(BF16) for tap in range(5)]
    for tap in range(5):
        tap_sums[tap] += dot(hots[tap], slope, NN)

    @pl.when(last)
    def _():
        table_grad = jnp.zeros((SMALL_ROWS, model), F32)
        table = table_ref[0:SMALL_ROWS, :].astype(F32)
        place = lax.broadcasted_iota(jnp.int32, (SMALL_ROWS, model), 0)
        extra = []
        for tap in range(5):
            sums = tap_sums[tap]
            table_grad = table_grad + vectors_ref[tap : tap + 1, :] * sums
            extra.append(jnp.sum(sums * table, axis=0, keepdims=True))
        extra.append(jnp.sum(keep_gain[...], axis=0, keepdims=True))
        extra.append(jnp.sum(keep_score[...], axis=0, keepdims=True))
        extra.append(gain_two_ref[...])
        for index, value in enumerate(extra):
            table_grad = jnp.where(place == 259 + index, value, table_grad)
        block[...] = table_grad
        heads = jnp.zeros((16, 128), F32)
        head_row = lax.broadcasted_iota(jnp.int32, (16, 128), 0)
        for slot in range(bias_ref.shape[0]):
            first, second = split_two(bias_ref[slot])
            sums = dot(first, bias_hot_ref[...], NN) + dot(second, bias_hot_ref[...], NN)
            pair = lax.rem(slot * devices + me, PAIRS)
            heads = heads + jnp.where(head_row == 2 * pair, sums[0:1], 0.0) + jnp.where(head_row == 2 * pair + 1, sums[1:2], 0.0)
        block[272:288, 0:128] = heads
        small.pack()
        small.one_start()
        if custom:
            reduce.fourth()
        small.one_finish()
        small.two_finish()
        if custom:
            reduce.finish(in_out, down_out, weight_out)
        small.three_finish()
        if custom:
            reduce.finish_late(qkv_out)
        small.four_finish()


def finish_kernel(block, *refs):
    refs = list(refs)
    count = (len(refs) - 6) // 2
    for source, target in zip(refs[:count], refs[count : 2 * count]):
        target[...] = source[...]
    table_out, taps_out, one_out, score_out, two_out, bias_out = refs[2 * count :]
    table_out[...] = block[0:259, :]
    taps_out[...] = block[259:264, :]
    one_out[...] = block[264, :]
    score_out[...] = block[265, :]
    two_out[...] = block[266, :]
    bias_out[...] = block[272:288, 0:128].T[0:32, 0:12]


def call_finish(block, sums):
    model = block.shape[1]
    shape = lambda *dims: jax.ShapeDtypeStruct(dims, F32)
    return pl.pallas_call(
        finish_kernel,
        out_shape=[shape(*x.shape) for x in sums] + [shape(259, model), shape(5, model), shape(model), shape(model), shape(model), shape(32, 12)],
        compiler_params=pltpu.CompilerParams(vmem_limit_bytes=VMEM_LIMIT),
        name="finish",
    )(block, *sums)


VMEM_LIMIT = 58 * 2**20
TOGETHER = 2


def item_sems(devices, per_device):
    dma = pltpu.SemaphoreType.DMA
    return [dma((devices, per_device)), dma((devices, per_device)), dma((per_device,))]


def whole(*shape):
    return pl.BlockSpec(shape, lambda s, *_: (0,) * len(shape), pipeline_mode=pl.Buffered(1))


def part(*shape):
    return pl.BlockSpec(shape, lambda s, *_: (s,) + (0,) * (len(shape) - 1))


ANYWHERE = pl.BlockSpec(memory_space=pl.ANY)


def remote_params(number):
    return pltpu.CompilerParams(vmem_limit_bytes=VMEM_LIMIT, collective_id=number, has_side_effects=True)


def call_front(ids, table, weight, vectors, local_tokens, devices, per_device):
    sequences, window, unused = ids.shape
    width = -(-window // 128) * 128
    model = weight.shape[0]
    return pl.pallas_call(
        functools.partial(front_kernel, (local_tokens, window, devices, sequences * PAIRS)),
        grid=(sequences,),
        in_specs=[part(1, window, 8), whole(*table.shape), whole(*weight.shape), whole(*vectors.shape)],
        out_specs=[
            part(1, local_tokens, model),
            part(1, local_tokens, model),
            part(1, width, model),
            part(1, local_tokens, width),
            part(1, local_tokens, 128),
            ANYWHERE,
        ],
        scratch_shapes=[
            pltpu.VMEM((2, 4, local_tokens, width), F32),
            pltpu.VMEM((1, 2, width, model), BF16),
            pltpu.VMEM(weight.shape, BF16),
            pltpu.VMEM((devices, per_device, local_tokens, 384), BF16),
            pltpu.VMEM((5,) + table.shape, BF16),
        ]
        + item_sems(devices, per_device),
        out_shape=[
            jax.ShapeDtypeStruct((sequences, local_tokens, model), F32),
            jax.ShapeDtypeStruct((sequences, local_tokens, model), BF16),
            jax.ShapeDtypeStruct((sequences, width, model), BF16),
            jax.ShapeDtypeStruct((sequences, local_tokens, width), BF16),
            jax.ShapeDtypeStruct((sequences, local_tokens, 128), F32),
            jax.ShapeDtypeStruct((devices, per_device, local_tokens, 384), BF16),
        ],
        compiler_params=remote_params(3),
        cost_estimate=pl.CostEstimate(flops=5 * 10**10, bytes_accessed=2 * 10**7, transcendentals=10**5),
        name="front",
    )(ids, table, weight, vectors)


def call_mid(att, hidden, cot, out_weight, in_weight, down_weight, vectors):
    devices, per_device, local_tokens, unused = att.shape
    sequences, unused, model = hidden.shape
    hidden_units = down_weight.shape[0]
    rows = lambda lanes: part(TOGETHER, local_tokens, lanes)
    full = lambda lanes, kind: jax.ShapeDtypeStruct((sequences, local_tokens, lanes), kind)
    return pl.pallas_call(
        functools.partial(mid_kernel, (local_tokens, devices, sequences * PAIRS)),
        grid=(sequences // TOGETHER,),
        in_specs=[
            ANYWHERE,
            rows(model),
            whole(*cot.shape),
            whole(*out_weight.shape),
            whole(*in_weight.shape),
            whole(*down_weight.shape),
            whole(*vectors.shape),
        ],
        out_specs=[
            rows(model),
            rows(hidden_units),
            rows(2 * hidden_units),
            rows(model),
            rows(model),
            rows(model),
            rows(model),
            ANYWHERE,
            whole(1, model),
        ],
        scratch_shapes=[pltpu.VMEM(att.shape, BF16), pltpu.VMEM(att.shape, BF16), pltpu.VMEM((8, model), F32), pltpu.VMEM((sequences * local_tokens, hidden_units), F32)]
        + item_sems(devices, per_device)
        + item_sems(devices, per_device),
        out_shape=[
            full(model, F32),
            full(hidden_units, BF16),
            full(2 * hidden_units, BF16),
            full(model, BF16),
            full(model, BF16),
            full(model, BF16),
            full(model, F32),
            jax.ShapeDtypeStruct(att.shape, BF16),
            jax.ShapeDtypeStruct((1, model), F32),
        ],
        compiler_params=remote_params(4),
        cost_estimate=pl.CostEstimate(flops=5 * 10**10, bytes_accessed=4 * 10**7, transcendentals=10**6),
        name="middle",
    )(att, hidden, cot, out_weight, in_weight, down_weight, vectors)


def call_back(custom, one, two, hidden, residual, conv, mix, share, ids, weight, table, vectors, bias_rows, gain_two, along, extra):
    devices, unused, local_tokens, unused = one.shape
    sequences, unused, model = hidden.shape
    width = conv.shape[1]
    window = ids.shape[2]
    bias_hot = jnp.pad(near_one_hot(), ((0, 0), (0, 96))).astype(BF16)
    out_specs = [whole(SMALL_ROWS, model)]
    out_shape = [jax.ShapeDtypeStruct((SMALL_ROWS, model), F32)]
    scratch = []
    specs = []
    if custom:
        specs = [whole(*x.shape) for x in extra]
        sums = [(96, 576), (96, 1024), (256, 192), (96, 192)]
        out_specs = out_specs + [whole(*shape) for shape in sums]
        out_shape = out_shape + [jax.ShapeDtypeStruct(shape, F32) for shape in sums]
        scratch = weight_scratch(model, sequences * local_tokens)
    else:
        out_specs = out_specs + [part(1, local_tokens, PAIRS * 384)]
        out_shape = out_shape + [jax.ShapeDtypeStruct((sequences, local_tokens, PAIRS * 384), BF16)]
    return pl.pallas_call(
        functools.partial(back_kernel, (local_tokens, window, devices), custom),
        grid=(sequences,),
        in_specs=[
            whole(*one.shape),
            whole(*two.shape),
            part(1, local_tokens, model),
            part(1, local_tokens, model),
            part(1, width, model),
            part(1, local_tokens, width),
            part(1, local_tokens, 128),
            part(1, 8, window),
            whole(*weight.shape),
            whole(*table.shape),
            whole(*vectors.shape),
            whole(*bias_rows.shape),
            whole(*bias_hot.shape),
            whole(1, model),
        ]
        + specs,
        out_specs=out_specs,
        scratch_shapes=[
            pltpu.VMEM((2, 4, local_tokens, width), F32),
            pltpu.VMEM(weight.shape, BF16),
            pltpu.VMEM((5, SMALL_ROWS, model), F32),
            pltpu.VMEM((8, model), F32),
            pltpu.VMEM((16, model), F32),
        ]
        + small_scratch(devices, along)
        + scratch,
        out_shape=out_shape,
        compiler_params=remote_params(5),
        cost_estimate=pl.CostEstimate(flops=10**11, bytes_accessed=2 * 10**7, transcendentals=10**5),
        name="back",
    )(one, two, hidden, residual, conv, mix, share, ids, weight, table, vectors, bias_rows, bias_hot, gain_two, *extra)


IN_ROWS = 8 * 96 + 2 * 96
REST_ROWS = 2 * 192
LATE_ROWS = 5 * 96


def meet_sibling(core):
    barrier = pltpu.get_barrier_semaphore()
    sibling = lax.axis_index("seq") + 1 - 2 * core
    pl.semaphore_signal(barrier, inc=1, device_id={"seq": sibling}, device_id_type=pl.DeviceIdType.MESH)
    pl.semaphore_wait(barrier, 1)


def to_sibling(core, source, target, send_sem, recv_sem):
    sibling = lax.axis_index("seq") + 1 - 2 * core
    return pltpu.make_async_remote_copy(
        src_ref=source, dst_ref=target, send_sem=send_sem, recv_sem=recv_sem,
        device_id={"seq": sibling}, device_id_type=pl.DeviceIdType.MESH,
    )


def spread_rows(core, source, lanes, keep_ref, send_ref, index_of):
    for chip in range(4):
        for other, ref in ((0, keep_ref), (1, send_ref)):
            device = 2 * chip + lax.rem(core + other, 2)
            rows = pl.ds(pl.multiple_of(device * 96, 32), 96)
            ref[index_of(chip)] = source[rows, lanes]


def early_kernel(
    act_ref, cot_ref, normed_ref, gate_up_ref, attended_ref, branch_ref, after, keep_in, keep_rest,
    other_in, got_in, other_rest, got_rest, cot_t, normed_t, result, send_in, recv_in, send_down, recv_down, send_out, recv_out,
):
    step = pl.program_id(0)
    core = lax.rem(lax.axis_index("seq"), 2)
    model = cot_t.shape[0]
    tokens = cot_t.shape[1]
    out_rows = pl.ds(768, 192)
    out_copy = to_sibling(core, other_in.at[:, :, out_rows], got_in.at[:, :, out_rows], send_out, recv_out)

    def in_copy(at):
        rows = pl.ds(pl.multiple_of(384 * lax.rem(at, 2), 384), 384)
        return to_sibling(core, other_in.at[:, at // 2, rows], got_in.at[:, at // 2, rows], send_in.at[at], recv_in.at[at])

    def down_copy(chip):
        return to_sibling(core, other_rest.at[:, chip], got_rest.at[:, chip], send_down.at[chip], recv_down.at[chip])

    @pl.when(step == 0)
    def _():
        meet_sibling(core)
        cot_t[...] = cot_ref[...].reshape(tokens, model).T
        normed_t[...] = attended_ref[...].reshape(tokens, model).T
        for first in range(0, model, 256):
            result[:, 0:256] = dot(normed_t[...], branch_ref[:, :, first : first + 256].reshape(tokens, 256), NN).astype(BF16)
            for half in range(2):
                tile = first // 128 + half
                for column, slot in {0: ((0, 0),), 1: ((0, 1), (1, 0)), 2: ((1, 1),), 3: ((2, 0),), 4: ((2, 1), (3, 0)), 5: ((3, 1),)}[tile]:
                    rows = slice(768 + 96 * slot, 864 + 96 * slot)
                    spread_rows(core, result, slice(128 * half, 128 * half + 128), keep_in, other_in, lambda chip: (chip, column, rows))
        normed_t[...] = normed_ref[...].reshape(tokens, model).T

    result[...] = dot(normed_t[...], gate_up_ref[...].reshape(tokens, 512), NN).astype(BF16)
    column_at = step // 2
    for quarter in range(4):
        rows = pl.ds(pl.multiple_of((4 * lax.rem(step, 2) + quarter) * 96, 32), 96)
        spread_rows(core, result, slice(128 * quarter, 128 * quarter + 128), keep_in, other_in, lambda chip: (chip, column_at, rows))
    down = dot(cot_t[...], act_ref[...].reshape(tokens, 256), NN).astype(BF16)

    def put_down(ref):
        for column in range(4):
            for half in range(2):
                ref[column, step // 2, 192 * half : 192 * half + 192] = down[192 * column : 192 * column + 192, 128 * half : 128 * half + 128]

    @pl.when(lax.rem(step, 2) == core)
    def _():
        put_down(keep_rest)

    @pl.when(lax.rem(step, 2) != core)
    def _():
        put_down(other_rest)
        down_copy(step // 2).start()

    in_copy(step).start()

    @pl.when(step == 0)
    def _():
        out_copy.start()

    @pl.when(step == 7)
    def _():
        for at in range(8):
            in_copy(at).wait()
        out_copy.wait()
        for chip in range(4):
            down_copy(chip).wait()

        def add(at, unused):
            one, two = at // 4, lax.rem(at, 4)
            keep_in[one, two] = (keep_in[one, two].astype(F32) + got_in[one, two].astype(F32)).astype(BF16)
            keep_rest[one, two] = (keep_rest[one, two].astype(F32) + got_rest[one, two].astype(F32)).astype(BF16)
            return unused

        lax.fori_loop(0, 16, add, 0)


def call_early(act, cot, normed, gate_up, attended, branch, after):
    sequences, local_tokens, model = cot.shape
    tokens = sequences * local_tokens
    every = whole(sequences, local_tokens, model)
    shapes = [(4, 4, IN_ROWS, 128), (4, 4, REST_ROWS, 128)]
    dma = pltpu.SemaphoreType.DMA
    return pl.pallas_call(
        early_kernel,
        grid=(8,),
        in_specs=[
            pl.BlockSpec((sequences, local_tokens, 256), lambda s: (0, 0, s)),
            every,
            every,
            pl.BlockSpec((sequences, local_tokens, 512), lambda s: (0, 0, s)),
            every,
            every,
            ANYWHERE,
        ],
        out_specs=[whole(*shape) for shape in shapes],
        scratch_shapes=[
            pltpu.VMEM(shapes[0], BF16),
            pltpu.VMEM(shapes[0], BF16),
            pltpu.VMEM(shapes[1], BF16),
            pltpu.VMEM(shapes[1], BF16),
            pltpu.VMEM((model, tokens), BF16),
            pltpu.VMEM((model, tokens), BF16),
            pltpu.VMEM((model, 512), BF16),
            dma((8,)), dma((8,)), dma((4,)), dma((4,)), dma, dma,
        ],
        out_shape=[jax.ShapeDtypeStruct(shape, BF16) for shape in shapes],
        compiler_params=pltpu.CompilerParams(vmem_limit_bytes=VMEM_LIMIT, collective_id=1, has_side_effects=True),
        cost_estimate=pl.CostEstimate(flops=11 * 10**9, bytes_accessed=3 * 10**7, transcendentals=0),
        name="early_gradients",
    )(act, cot, normed, gate_up, attended, branch, after)


class WeightSums:
    def __init__(self, normed_ref, across_ref, planes_ref, block_of, refs):
        self.normed, self.across, self.planes, self.block_of = normed_ref, across_ref, planes_ref, block_of
        (
            self.in_sum, self.in_got, self.rest_got, self.rest_sum, self.rest_chips, self.normed_t, self.result,
            self.keep, self.other, self.got, self.chips, self.late_sum, self.late_got, self.in_chips,
        ) = refs[:14]
        (
            self.send_in, self.recv_in, self.send_rest, self.recv_rest, self.send_chip, self.recv_chip,
            self.send_a, self.recv_a, self.send_b, self.recv_b, self.send_c, self.recv_c, self.send_i, self.recv_i,
        ) = refs[14:]
        self.me, self.plane = lax.axis_index("seq"), lax.axis_index("dp")
        self.core, self.chip = lax.rem(self.me, 2), self.me // 2

    def to_plane(self, offset, source, target, send, recv):
        return pltpu.make_async_remote_copy(
            src_ref=source, dst_ref=target, send_sem=send.at[offset - 1], recv_sem=recv.at[offset - 1],
            device_id={"dp": lax.rem(self.plane + offset, 4)}, device_id_type=pl.DeviceIdType.MESH,
        )

    def to_chip(self, offset, source, target, send, recv):
        other = lax.rem(self.chip + offset, 4)
        return pltpu.make_async_remote_copy(
            src_ref=source, dst_ref=target, send_sem=send, recv_sem=recv,
            device_id={"seq": 2 * other + self.core}, device_id_type=pl.DeviceIdType.MESH,
        )

    def rest_plane(self, offset):
        peer = lax.rem(self.plane + offset, 4)
        return self.to_plane(offset, self.planes.at[peer], self.rest_got.at[offset - 1], self.send_rest, self.recv_rest)

    def in_plane(self, offset):
        peer = lax.rem(self.plane + offset, 4)
        return self.to_plane(offset, self.in_sum.at[peer], self.in_got.at[offset - 1], self.send_in, self.recv_in)

    def late_plane(self, offset):
        peer = lax.rem(self.plane + offset, 4)
        return self.to_plane(offset, self.late_sum.at[peer], self.late_got.at[offset - 1], self.send_c, self.recv_c)

    def rest_chip(self, offset):
        other = lax.rem(self.chip + offset, 4)
        return self.to_chip(offset, self.rest_sum.at[other], self.rest_chips.at[offset - 1], self.send_chip.at[offset - 1], self.recv_chip.at[offset - 1])

    def late_chip(self, offset, column):
        other = lax.rem(self.chip + offset, 4)
        return self.to_chip(
            offset, self.keep.at[other, column], self.chips.at[offset - 1, column], self.send_b.at[offset - 1, column], self.recv_b.at[offset - 1, column]
        )

    def late_core(self, column):
        return to_sibling(self.core, self.other.at[:, column], self.got.at[:, column], self.send_a.at[column], self.recv_a.at[column])

    def in_chip(self, offset):
        other = lax.rem(self.chip + offset, 4)
        return self.to_chip(offset, self.across.at[other], self.in_chips.at[offset - 1], self.send_i.at[offset - 1], self.recv_i.at[offset - 1])

    def begin(self):
        for offset in (1, 2, 3):
            self.in_chip(offset).start()
            self.rest_plane(offset).start()

    def late(self):
        sequences, count, model = self.normed.shape
        self.normed_t[...] = self.normed[...].reshape(sequences * count, model).T
        low = lax.broadcasted_iota(jnp.int32, (model, 128), 1) < 64
        for pair in range(PAIRS):
            rows = jnp.concatenate([self.block_of(one * PAIRS + pair) for one in range(sequences)], axis=0)
            sums = dot(self.normed_t[...], rows, NN)
            query, key, value = sums[:, 0:128], pltpu.roll(sums[:, 128:256], 64, 1), sums[:, 256:384]
            self.result[3 * pair] = jnp.where(low, query, key).astype(BF16)
            self.result[3 * pair + 1] = jnp.where(low, value, query).astype(BF16)
            self.result[3 * pair + 2] = jnp.where(low, key, value).astype(BF16)
        for tile in range(3 * PAIRS):
            within = tile % 9
            spots = [(2 * (tile // 9), within)] if within <= 4 else []
            spots += [(2 * (tile // 9) + 1, within - 4)] if within >= 4 else []
            for column, slot in spots:
                rows_at = slice(96 * slot, 96 * slot + 96)
                spread_rows(self.core, self.result.at[tile], slice(0, 128), self.keep, self.other, lambda chip: (chip, column, rows_at))
        for column in range(4):
            self.late_core(column).start()

    def second(self):
        for column in range(4):
            self.late_core(column).wait()
            for at in range(4):
                self.keep[at, column] = (self.keep[at, column].astype(F32) + self.got[at, column].astype(F32)).astype(BF16)
            for offset in (1, 2, 3):
                self.late_chip(offset, column).start()

    def third(self):
        for offset in (1, 2, 3):
            self.in_chip(offset).wait()
        for column in range(4):
            total = self.across[self.chip, column].astype(F32)
            for slot in range(3):
                total = total + self.in_chips[slot, column].astype(F32)
            self.in_sum[column] = total.astype(BF16)
        for offset in (1, 2, 3):
            self.in_plane(offset).start()

    def between(self):
        for offset in (1, 2, 3):
            self.rest_plane(offset).wait()
        for chip in range(4):
            total = self.planes[self.plane, chip].astype(F32)
            for slot in range(3):
                total = total + self.rest_got[slot, chip].astype(F32)
            self.rest_sum[chip] = total.astype(BF16)
        for offset in (1, 2, 3):
            self.rest_chip(offset).start()

    def fourth(self):
        for column in range(4):
            total = self.keep[self.chip, column].astype(F32)
            for offset in (1, 2, 3):
                self.late_chip(offset, column).wait()
                total = total + self.chips[offset - 1, column].astype(F32)
            self.late_sum[column] = total.astype(BF16)
        for offset in (1, 2, 3):
            self.late_plane(offset).start()

    def joined(self, block, columns):
        odd = lax.rem(self.plane, 2) == 1
        count = block.shape[1]
        return jnp.where(odd, pltpu.roll(block, count - 64, 1), block)[:, :columns]

    def finish(self, in_out, down_out, weight_out):
        total = self.in_sum[self.plane].astype(F32)
        for offset in (1, 2, 3):
            self.in_plane(offset).wait()
            total = total + self.in_got[offset - 1].astype(F32)
        for tile in range(8):
            in_out[:, 128 * tile : 128 * tile + 128] = total[96 * tile : 96 * tile + 96]
        weight_out[...] = self.joined(jnp.concatenate([total[768:864], total[864:960]], axis=1), 192)
        total = self.rest_sum[self.chip].astype(F32)
        for offset in (1, 2, 3):
            self.rest_chip(offset).wait()
            total = total + self.rest_chips[offset - 1].astype(F32)
        down_out[0:128, :] = total[0:192].T
        down_out[128:256, :] = total[192:384].T

    def finish_late(self, qkv_out):
        total = self.late_sum[self.plane].astype(F32)
        for offset in (1, 2, 3):
            self.late_plane(offset).wait()
            total = total + self.late_got[offset - 1].astype(F32)
        qkv_out[...] = self.joined(jnp.concatenate([total[96 * k : 96 * k + 96] for k in range(5)], axis=1), 576)


def weight_scratch(model, tokens):
    dma = pltpu.SemaphoreType.DMA
    late = (4, 4, LATE_ROWS, 128)
    return [
        pltpu.VMEM((4, IN_ROWS, 128), BF16),
        pltpu.VMEM((3, IN_ROWS, 128), BF16),
        pltpu.VMEM((3, 4, REST_ROWS, 128), BF16),
        pltpu.VMEM((4, REST_ROWS, 128), BF16),
        pltpu.VMEM((3, REST_ROWS, 128), BF16),
        pltpu.VMEM((model, tokens), BF16),
        pltpu.VMEM((3 * PAIRS, model, 128), BF16),
        pltpu.VMEM(late, BF16),
        pltpu.VMEM(late, BF16),
        pltpu.VMEM(late, BF16),
        pltpu.VMEM((3, 4, LATE_ROWS, 128), BF16),
        pltpu.VMEM((4, LATE_ROWS, 128), BF16),
        pltpu.VMEM((3, LATE_ROWS, 128), BF16),
        pltpu.VMEM((3, 4, IN_ROWS, 128), BF16),
        dma((3,)), dma((3,)), dma((3,)), dma((3,)), dma((3,)), dma((3,)),
        dma((4,)), dma((4,)), dma((3, 4)), dma((3, 4)), dma((3,)), dma((3,)), dma((3,)), dma((3,)),
    ]


SMALL_ROWS = 288


class SmallSums:
    def __init__(self, block, buffers, sems):
        self.block = block
        self.held, self.got_seq, self.planes, self.got_dp, self.whole = buffers
        self.sems = sems
        self.me, self.plane = lax.axis_index("seq"), lax.axis_index("dp")
        self.across, self.along = self.held.shape[0], self.held.shape[1]

    def places(self):
        half = self.held.shape[2] // 2
        units = SMALL_ROWS // half
        tiles = self.block.shape[1] // 128
        for at in range(2 * self.along * self.across):
            spot = (at // (2 * self.along), at // 2 % self.along, slice((at % 2) * half, (at % 2) * half + half))
            tile, unit = at // units, at % units
            if tile < tiles:
                yield spot, (slice(unit * half, unit * half + half), slice(128 * tile, 128 * tile + 128))
            else:
                yield spot, None

    def pack(self):
        for spot, source in self.places():
            if source is None:
                self.held[spot] = jnp.zeros((self.held.shape[2] // 2, 128), BF16)
            else:
                self.held[spot] = self.block[source].astype(BF16)

    def copies(self, axis, source, target, number):
        here, count = (self.me, self.across) if axis == "seq" else (self.plane, self.along)
        send, recv = self.sems[2 * number], self.sems[2 * number + 1]
        made = []
        for step in range(1, count):
            peer = lax.rem(here + step, count)
            made.append(
                pltpu.make_async_remote_copy(
                    src_ref=source(peer), dst_ref=target(step - 1), send_sem=send.at[step - 1], recv_sem=recv.at[step - 1],
                    device_id={axis: peer}, device_id_type=pl.DeviceIdType.MESH,
                )
            )
        for copy in made:
            copy.start()
        return made

    def one_start(self):
        self.waiting = self.copies("seq", lambda peer: self.held.at[peer], lambda slot: self.got_seq.at[slot], 0)

    def one_finish(self):
        for copy in self.waiting:
            copy.wait()
        total = self.held[self.me].astype(F32)
        for slot in range(self.across - 1):
            total = total + self.got_seq[slot].astype(F32)
        self.planes[...] = total.astype(BF16)
        self.waiting = self.copies("dp", lambda peer: self.planes.at[peer], lambda slot: self.got_dp.at[slot], 1)

    def two_finish(self):
        for copy in self.waiting:
            copy.wait()
        mine = self.planes[self.plane].astype(F32)
        for slot in range(self.along - 1):
            mine = mine + self.got_dp[slot].astype(F32)
        self.whole[self.me, self.plane] = mine.astype(BF16)
        self.waiting = self.copies("dp", lambda peer: self.whole.at[self.me, self.plane], lambda slot: self.whole.at[self.me, self.plane], 2)

    def three_finish(self):
        for copy in self.waiting:
            copy.wait()
        self.waiting = self.copies("seq", lambda peer: self.whole.at[self.me], lambda slot: self.whole.at[self.me], 3)

    def four_finish(self):
        for copy in self.waiting:
            copy.wait()
        for spot, target in self.places():
            if target is not None:
                self.block[target] = self.whole[spot].astype(F32)


def small_scratch(across, along):
    chunk = max(16, 2048 // (across * along))
    dma = lambda count: pltpu.SemaphoreType.DMA((count,))
    return [
        pltpu.VMEM((across, along, chunk, 128), BF16),
        pltpu.VMEM((across - 1, along, chunk, 128), BF16),
        pltpu.VMEM((along, chunk, 128), BF16),
        pltpu.VMEM((along - 1, chunk, 128), BF16),
        pltpu.VMEM((across, along, chunk, 128), BF16),
        dma(across - 1), dma(across - 1), dma(along - 1), dma(along - 1),
        dma(along - 1), dma(along - 1), dma(across - 1), dma(across - 1),
    ]


def body(
    byte_ids,
    lengths,
    byte_table,
    conv_kernel,
    score_vector,
    norm_gain_one,
    qkv_weight,
    bias_table,
    out_weight,
    norm_gain_two,
    in_weight,
    down_weight,
    cotangent,
):
    devices = lax.axis_size("seq")
    me = lax.axis_index("seq")
    sequences, local_bytes = byte_ids.shape
    local_tokens = local_bytes // 2
    total_bytes = local_bytes * devices
    first_byte = me * local_bytes
    vocab, model = byte_table.shape
    window = local_bytes + 16
    total = sequences * PAIRS
    per_device = -(-total // devices)

    number = jnp.arange(sequences, dtype=jnp.int32)
    ahead = (lengths[None, :] > lengths[:, None]) | (
        (lengths[None, :] == lengths[:, None]) & (number[None, :] < number[:, None])
    )
    rank = jnp.sum(ahead.astype(jnp.int32), axis=1)
    placed = rank[None, :] == number[:, None]
    order = jnp.sum(jnp.where(placed, number[None, :], 0), axis=1)
    sorted_lengths = jnp.sum(jnp.where(placed, lengths[None, :], 0), axis=1)
    positions = first_byte + jnp.arange(local_bytes, dtype=jnp.int32)
    picked = jnp.where(positions[None, :] < lengths[:, None], byte_ids, 0)
    forward = [(i, i + 1) for i in range(devices - 1)]
    backward = [(target, source) for source, target in forward]
    before = jnp.where(me > 0, lax.ppermute(picked[:, -4:], "seq", forward), -1)
    after = jnp.where(me < devices - 1, lax.ppermute(picked[:, :4], "seq", backward), -1)
    outside = jnp.full((sequences, 12), -1, jnp.int32)
    extended = jnp.concatenate([before, picked, after, outside], axis=1)
    extended = jnp.sum(jnp.where(placed[:, :, None], extended[None, :, :], 0), axis=1)
    shifted = jnp.stack([extended[:, tap : tap + window] for tap in range(5)])
    ids_columns = jnp.concatenate([jnp.moveaxis(shifted, 0, 2), jnp.full((sequences, window, 3), -1, jnp.int32)], axis=2)

    table_padded = jnp.concatenate([byte_table, jnp.zeros((VPAD - vocab, model), BF16)], axis=0)
    vectors = jnp.concatenate([conv_kernel, norm_gain_one[None, :], norm_gain_two[None, :], score_vector[None, :]], axis=0)
    rows = jnp.dot(near_one_hot(), bias_table, precision="highest").T.reshape(PAIRS, 2, NEAR)

    item = me + devices * jnp.arange(per_device, dtype=jnp.int32)
    length = jnp.sum(jnp.where((item // PAIRS)[:, None] == number[None, :], sorted_lengths[None, :], 0), axis=1)
    valid = jnp.where(item < total, (length + 1) // 2, 0).astype(jnp.int32)
    pair = lax.rem(item, PAIRS).astype(jnp.int32)
    def exchange(items):
        return lax.all_to_all(items, "seq", split_axis=0, concat_axis=0, tiled=True)

    hidden, normed, conv, mix, share, received = call_front(ids_columns, table_padded, qkv_weight, vectors, local_tokens, devices, per_device)
    out, aug, cot = attention_forward(received, rows, valid, pair, order, cotangent)
    layer, act, gate_up, normed_two, attended, branch, grad_residual, grad_items, grad_gain_two = call_mid(
        out, hidden, cot, out_weight, in_weight, down_weight, vectors
    )
    along_count = lax.axis_size("dp")
    custom = devices == 8 and along_count == 4

    def scatter(grad):
        rows_own = lax.psum_scatter(grad, "seq", scatter_dimension=0, tiled=True)
        return lax.psum_scatter(rows_own, "dp", scatter_dimension=1, tiled=True).astype(F32)

    if not custom:
        summed_down = scatter(jnp.einsum("bti,btd->id", act, cot, preferred_element_type=F32).astype(BF16))
        summed_in = scatter(jnp.einsum("btd,bti->di", normed_two, gate_up, preferred_element_type=F32).astype(BF16))
        summed_out = scatter(jnp.einsum("btd,bte->de", attended, branch, preferred_element_type=F32).astype(BF16))
    half = per_device // 2
    dqkv_two, bias_two, layer_out = attention_backward(received, out, aug, grad_items, rows, valid, pair, order, layer, grad_gain_two, half, per_device - half)
    items_two = exchange(dqkv_two)
    dqkv_one, bias_one, unused = attention_backward(received, out, aug, grad_items, rows, valid, pair, order, None, bias_two, 0, half)
    items_one = exchange(dqkv_one)
    bias_rows = jnp.concatenate([bias_one, bias_two], axis=0)
    if custom:
        in_chips, rest_planes = call_early(act, cot, normed_two, gate_up, attended, branch, items_two)
    ids_rows = jnp.concatenate([jnp.moveaxis(shifted, 0, 1), jnp.full((sequences, 3, window), -1, jnp.int32)], axis=1)
    extra = (normed, in_chips, rest_planes) if custom else ()
    results = call_back(
        custom, items_one, items_two, hidden, grad_residual, conv, mix, share, ids_rows, qkv_weight, table_padded, vectors, bias_rows, grad_gain_two, along_count, extra
    )
    if custom:
        summed_qkv, summed_in, summed_down, summed_out, *smalls = call_finish(results[0], results[1:])
    else:
        smalls = call_finish(results[0], ())
        grad_qkv = jnp.einsum("btd,bte->de", normed, results[1], preferred_element_type=F32).astype(BF16)
        grad_qkv = jnp.swapaxes(grad_qkv.reshape(model, PAIRS, 3, 2, 64), 2, 3).reshape(model, PAIRS * 384)
        summed_qkv = scatter(grad_qkv)
    grad_table, grad_taps, grad_gain_one, grad_score, grad_gain_two, grad_bias = smalls
    return (
        layer_out,
        grad_table,
        grad_taps,
        grad_score,
        grad_gain_one,
        summed_qkv,
        grad_bias,
        summed_out,
        grad_gain_two,
        summed_in,
        summed_down,
    )


def solution(mesh):
    return jax.shard_map(
        body,
        mesh=mesh,
        in_specs=(
            P("dp", "seq"),
            P("dp"),
            P(),
            P(),
            P(),
            P(),
            P(),
            P(),
            P(),
            P(),
            P(),
            P(),
            P("dp", "seq", None),
        ),
        out_specs=(
            P("dp", "seq", None),
            P(),
            P(),
            P(),
            P(),
            P("seq", "dp"),
            P(),
            P("seq", "dp"),
            P(),
            P("seq", "dp"),
            P("seq", "dp"),
        ),
        check_vma=False,
    )
```

```python
import functools
import jax
import jax.numpy as jnp
from jax import lax
from jax.experimental import pallas as pl
from jax.experimental.pallas import tpu as pltpu
from jax.sharding import PartitionSpec as P

thresholds = (12, 16, 23, 32, 46, 64, 91)
KB = 256
NEAR = 1024
F32 = jnp.float32
BF16 = jnp.bfloat16
NT = (((1,), (1,)), ((), ()))
NN = (((1,), (0,)), ((), ()))


def rel_bucket(relative):
    distance = jnp.abs(relative)
    larger = 8 + sum(((distance >= boundary).astype(jnp.int32) for boundary in thresholds))
    bucket = jnp.where(distance < 8, distance, larger)
    return bucket + 16 * (relative > 0).astype(jnp.int32)


def near_one_hot():
    place = jnp.arange(NEAR, dtype=jnp.int32)
    relative = jnp.where(place < NEAR - 128, KB - place, KB + NEAR - place)
    return (rel_bucket(relative)[:, None] == jnp.arange(32, dtype=jnp.int32)[None, :]).astype(F32)


def dot(a, b, dims):
    return lax.dot_general(a, b, dims, preferred_element_type=F32)


def fill_bias(strip, head, row, blocks):
    base = KB * (blocks - 2)
    width = KB * (2 * blocks - 1)
    spread = jnp.broadcast_to(row, (128, NEAR))
    rolled = pltpu.roll(spread, 0, 1, stride=1, stride_axis=0)
    far_right = jnp.broadcast_to(row[:, NEAR - 1 :], (KB, 128))
    far_left = jnp.broadcast_to(row[:, 768:769], (KB, 128))
    for start in range(0, base, 128):
        strip[head, :, start : start + 128] = far_right
    strip[head, 0:128, base : base + 768] = rolled[:, :768]
    strip[head, 128:256, base : base + 128] = far_right[:128]
    strip[head, 128:256, base + 128 : base + 768] = rolled[:, :640]
    for start in range(base + 768, width, 128):
        strip[head, :, start : start + 128] = far_left


def lanes_of(head, shape):
    lane = lax.broadcasted_iota(jnp.int32, shape, 1)
    own = (lane < 64) if head == 0 else (lane >= 64)
    return own, lane - (64 if head == 0 else 0)


def fill_keys(ka, head, keys, valid):
    own, spare = lanes_of(head, keys.shape)
    row = lax.broadcasted_iota(jnp.int32, keys.shape, 0)
    masked = jnp.where(row < valid, 0.0, -1e9)
    extra = jnp.where(spare == 0, masked, jnp.where((spare >= 1) & (spare <= 3), 1.0, 0.0))
    ka[head] = jnp.where(own, keys, extra.astype(BF16))


def item_length(lengths_ref, item):
    length = jnp.int32(0)
    for number, rank in enumerate(ranks_of(lengths_ref)):
        length = jnp.where(rank == item // 6, lengths_ref[number], length)
    return (length + 1) // 2


def move_rows(item, lengths_ref, source, buffer, target, sems, sorting):
    def inward(number):
        return pltpu.make_async_copy(source.at[number if sorting else ranks[number]], buffer.at[number], sems.at[0, number])

    def outward(number):
        return pltpu.make_async_copy(buffer.at[number], target.at[ranks[number] if sorting else number], sems.at[1, number])

    count = source.shape[0]
    ranks = ranks_of(lengths_ref)

    @pl.when(item == 0)
    def _():
        for number in range(count):
            inward(number).start()

    @pl.when(item == jnp.minimum(1, pl.num_programs(0) - 1))
    def _():
        for number in range(count):
            inward(number).wait()
            outward(number).start()

    def finish():
        @pl.when(item == pl.num_programs(0) - 1)
        def _():
            for number in range(count):
                outward(number).wait()

    return finish


def fwd_kernel(
    blocks, lengths_ref, place_ref, qkv_ref, row_ref, cot_ref, out_ref, aug_ref, sorted_ref,
    qa, ka, vt, strip, peak, acc, probs, moving, sems,
):
    item = pl.program_id(0)
    finish = move_rows(item, lengths_ref, cot_ref, moving, sorted_ref, sems, True)
    valid = item_length(lengths_ref, place_ref[0] + qkv_ref.shape[0] * item)
    tokens = blocks * KB
    joined = qkv_ref[:, 0].reshape(tokens, 384)
    queries = joined[:, 0:128]
    keys = joined[:, 128:256]
    turned = joined[:, 256:384].T
    filler = jnp.where(lax.broadcasted_iota(jnp.int32, (16, tokens), 0) == 0, 1.0, 0.0).astype(BF16)
    for head in range(2):
        own, spare = lanes_of(head, queries.shape)
        qa[head] = jnp.where(own, queries, jnp.where(spare == 0, 1.0, 0.0).astype(BF16))
        fill_keys(ka, head, keys, valid)
        vt[head, 0:64] = turned[64 * head : 64 * head + 64]
        vt[head, 64:80] = filler
        fill_bias(strip, head, row_ref[0, head : head + 1, :], blocks)
    peak[...] = jnp.full_like(peak, -1e30)
    acc[...] = jnp.zeros_like(acc)

    def step(block, unused):
        first = pl.multiple_of(block * KB, KB)
        shift = pl.multiple_of((blocks - 1 - block) * KB, KB)
        alphas = [[], []]
        for part in range(blocks):
            for head in range(2):
                here = slice(part * KB, part * KB + KB)
                logits = dot(ka[head, pl.ds(first, KB), :], qa[head, here, :], NT)
                logits = logits + strip[head, :, pl.ds(shift + part * KB, KB)]
                before = peak[head, :, here]
                after = jnp.maximum(before, jnp.max(logits, axis=0, keepdims=True))
                probs[head, :, here] = jnp.exp(logits - after).astype(BF16)
                peak[head, :, here] = after
                alphas[head].append(jnp.exp(before - after))
        for head in range(2):
            acc[head] = acc[head] * jnp.concatenate(alphas[head], axis=1) + dot(vt[head, :, pl.ds(first, KB)], probs[head], NN)
        return unused

    lax.fori_loop(0, (valid + KB - 1) // KB, step, 0)
    outs = []
    rows = []
    place = lax.broadcasted_iota(jnp.int32, (64, tokens), 0)
    for head in range(2):
        total = acc[head, 64:65, :]
        outs.append(acc[head, 0:64, :] / total)
        minus = -(peak[head] + jnp.log(total))
        high = minus.astype(BF16).astype(F32)
        rest = minus - high
        middle = rest.astype(BF16).astype(F32)
        low = rest - middle
        rows.append(jnp.where(place == 0, 1.0, jnp.where(place == 1, high, jnp.where(place == 2, middle, jnp.where(place == 3, low, 0.0)))))
    out_ref[:, 0] = jnp.concatenate(outs, axis=0).T.astype(BF16).reshape(out_ref.shape[0], out_ref.shape[2], 128)
    aug_ref[0] = jnp.concatenate([rows[1], rows[0]], axis=0).T.astype(BF16)
    finish()


def bwd_kernel(
    blocks, base_slot, moves, lengths_ref, place_ref, qkv_ref, out_ref, aug_ref, grad_ref, row_ref, layer_ref, after,
    dqkv_ref, bias_ref, moved_ref, qa, ka, va, ga, kt, strip, tally, probs, slopes, dq, *moving,
):
    item = pl.program_id(0)
    finish = move_rows(item, lengths_ref, layer_ref, moving[0], moved_ref, moving[1], False) if moves else lambda: None
    valid = item_length(lengths_ref, place_ref[0] + qkv_ref.shape[0] * (item + base_slot))
    tokens = blocks * KB
    width = KB * (2 * blocks - 1)
    local = qkv_ref.shape[2]
    joined = qkv_ref[:, 0].reshape(tokens, 384)
    queries = joined[:, 0:128]
    keys = joined[:, 128:256]
    values = joined[:, 256:384]
    grads = grad_ref[:, 0].reshape(tokens, 128)
    outs = out_ref[:, 0].reshape(tokens, 128)
    kt[...] = keys.T
    product = grads.astype(F32) * outs.astype(F32)
    high = product.astype(BF16)
    low = (product - high.astype(F32)).astype(BF16)
    row_at = lax.broadcasted_iota(jnp.int32, (128, 128), 0)
    lane_at = lax.broadcasted_iota(jnp.int32, (128, 128), 1)
    pick = jnp.where((row_at < 64) == (lane_at >= 64), -1.0, 0.0).astype(BF16)
    shifts = dot(high, pick, NN) + dot(low, pick, NN)
    shift_high = shifts.astype(BF16)
    shift_low = (shifts - shift_high.astype(F32)).astype(BF16)
    for head in range(2):
        own, spare = lanes_of(head, queries.shape)
        qa[head] = jnp.where(own, queries, aug_ref[0])
        fill_keys(ka, head, keys, valid)
        va[head] = jnp.where(own, values, jnp.where((spare == 0) | (spare == 1), 1.0, 0.0).astype(BF16))
        ga[head] = jnp.where(own, grads, jnp.where(spare == 0, shift_high, jnp.where(spare == 1, shift_low, jnp.zeros_like(shift_low))))
        fill_bias(strip, head, row_ref[0, head : head + 1, :], blocks)
    tally[...] = jnp.zeros_like(tally)
    dq[...] = jnp.zeros_like(dq)
    dqkv_ref[...] = jnp.zeros_like(dqkv_ref)

    def step(block, unused):
        first = pl.multiple_of(block * KB, KB)
        shift = pl.multiple_of((blocks - 1 - block) * KB, KB)
        key_parts = []
        value_parts = []
        for part in range(blocks):
            for head in range(2):
                here = slice(part * KB, part * KB + KB)
                there = pl.ds(shift + part * KB, KB)
                logits = dot(ka[head, pl.ds(first, KB), :], qa[head, here, :], NT)
                weights = jnp.exp(logits + strip[head, :, there])
                change = dot(va[head, pl.ds(first, KB), :], ga[head, here, :], NT)
                slope = weights * change
                tally[head, :, there] += slope
                probs[head, :, here] = weights.astype(BF16)
                slopes[head, :, here] = slope.astype(BF16)
        for head in range(2):
            value_parts.append(dot(probs[head], ga[head], NN))
            key_parts.append(dot(slopes[head], qa[head], NN))
            dq[pl.ds(64 * head, 64), :] += dot(kt[pl.ds(64 * head, 64), pl.ds(first, KB)], slopes[head], NN)
        own, unused_spare = lanes_of(0, (KB, 128))
        count = KB // local
        where = pl.ds(block * count, count)
        dqkv_ref[where, 0, :, 128:256] = jnp.where(own, key_parts[0], key_parts[1]).astype(BF16).reshape(count, local, 128)
        dqkv_ref[where, 0, :, 256:384] = jnp.where(own, value_parts[0], value_parts[1]).astype(BF16).reshape(count, local, 128)
        return unused

    lax.fori_loop(0, (valid + KB - 1) // KB, step, 0)
    dqkv_ref[:, 0, :, 0:128] = dq[...].T.astype(BF16).reshape(dqkv_ref.shape[0], local, 128)
    base = KB * (blocks - 2)
    lane = lax.broadcasted_iota(jnp.int32, (1, NEAR), 1)
    flip = jnp.where(row_at + lane_at == 127, 1.0, 0.0).astype(BF16)
    for head in range(2):
        far_right = sum(tally[head, :, start : start + 128] for start in range(0, base, 128)) if base else jnp.zeros((KB, 128), F32)
        far_right = far_right[:128] + far_right[128:] + tally[head, 128:256, base : base + 128]
        left_list = [tally[head, :, start : start + 128] for start in range(base + 768, width, 128)]
        far_left = sum(left_list) if left_list else jnp.zeros((KB, 128), F32)
        near = tally[head, 0:128, base : base + 768]
        near_low = tally[head, 128:256, base + 128 : base + 768]
        near = near + jnp.concatenate([near_low, jnp.zeros((128, 128), F32)], axis=1)
        near = jnp.concatenate([near, jnp.zeros((128, NEAR - 768), F32)], axis=1)
        near_high = near.astype(BF16)
        flipped = dot(flip, near_high, NN) + dot(flip, (near - near_high.astype(F32)).astype(BF16), NN)
        rolled = pltpu.roll(flipped, NEAR - 127, 1, stride=1, stride_axis=0)
        row = jnp.sum(rolled, axis=0, keepdims=True)
        row = row + jnp.where(lane == NEAR - 1, jnp.sum(far_right), 0.0) + jnp.where(lane == 768, jnp.sum(far_left), 0.0)
        bias_ref[0, head : head + 1, :] = row
    finish()


def attention_forward(qkv, rows, lengths, place, cot):
    sources, items, local, unused = qkv.shape
    blocks = sources * local // KB
    tokens = sources * local
    width = KB * (2 * blocks - 1)
    spec = pltpu.PrefetchScalarGridSpec(
        num_scalar_prefetch=2,
        grid=(items,),
        in_specs=[
            pl.BlockSpec((sources, 1, local, 384), lambda i, l, p: (0, i, 0, 0)),
            pl.BlockSpec((1, 2, NEAR), lambda i, l, p: (lax.rem(p[0] + sources * i, 6), 0, 0)),
            pl.BlockSpec(memory_space=pl.ANY),
        ],
        out_specs=[
            pl.BlockSpec((sources, 1, local, 128), lambda i, l, p: (0, i, 0, 0)),
            pl.BlockSpec((1, tokens, 128), lambda i, l, p: (i, 0, 0)),
            pl.BlockSpec(memory_space=pl.ANY),
        ],
        scratch_shapes=[
            pltpu.VMEM((2, tokens, 128), BF16),
            pltpu.VMEM((2, tokens, 128), BF16),
            pltpu.VMEM((2, 80, tokens), BF16),
            pltpu.VMEM((2, KB, width), F32),
            pltpu.VMEM((2, 1, tokens), F32),
            pltpu.VMEM((2, 80, tokens), F32),
            pltpu.VMEM((2, KB, tokens), BF16),
            pltpu.VMEM(cot.shape, cot.dtype),
            pltpu.SemaphoreType.DMA((2,) + cot.shape[:1]),
        ],
    )
    return pl.pallas_call(
        functools.partial(fwd_kernel, blocks),
        grid_spec=spec,
        out_shape=[
            jax.ShapeDtypeStruct((sources, items, local, 128), BF16),
            jax.ShapeDtypeStruct((items, tokens, 128), BF16),
            jax.ShapeDtypeStruct(cot.shape, cot.dtype),
        ],
        compiler_params=pltpu.CompilerParams(vmem_limit_bytes=50 * 2**20),
        cost_estimate=pl.CostEstimate(flops=items * tokens * tokens * 512, bytes_accessed=items * tokens * 2048, transcendentals=items * tokens * tokens * 2),
        name="attention_forward",
    )(lengths, place, qkv, rows, cot)


def attention_backward(qkv, outs, aug, grads, rows, lengths, place, layer, after, first, items, grads_at):
    sources, unused, local, unused = qkv.shape
    moves = layer is not None
    layer = after if layer is None else layer
    moved = layer if moves else jnp.zeros((8, 128), F32)
    blocks = sources * local // KB
    tokens = sources * local
    width = KB * (2 * blocks - 1)
    big = lambda lanes: pl.BlockSpec((sources, 1, local, lanes), lambda i, l, p: (0, i + first, 0, 0))
    spec = pltpu.PrefetchScalarGridSpec(
        num_scalar_prefetch=2,
        grid=(items,),
        in_specs=[
            big(384),
            big(128),
            pl.BlockSpec((1, tokens, 128), lambda i, l, p: (i + first, 0, 0)),
            pl.BlockSpec((sources, 1, local, 128), lambda i, l, p: (0, i + grads_at, 0, 0)),
            pl.BlockSpec((1, 2, NEAR), lambda i, l, p: (lax.rem(p[0] + sources * (i + first), 6), 0, 0)),
            pl.BlockSpec(memory_space=pl.ANY),
            pl.BlockSpec(memory_space=pl.ANY),
        ],
        out_specs=[
            pl.BlockSpec((sources, 1, local, 384), lambda i, l, p: (0, i, 0, 0)),
            pl.BlockSpec((1, 2, NEAR), lambda i, l, p: (i, 0, 0)),
            pl.BlockSpec(memory_space=pl.ANY),
        ],
        scratch_shapes=[
            pltpu.VMEM((2, tokens, 128), BF16),
            pltpu.VMEM((2, tokens, 128), BF16),
            pltpu.VMEM((2, tokens, 128), BF16),
            pltpu.VMEM((2, tokens, 128), BF16),
            pltpu.VMEM((128, tokens), BF16),
            pltpu.VMEM((2, KB, width), F32),
            pltpu.VMEM((2, KB, width), F32),
            pltpu.VMEM((2, KB, tokens), BF16),
            pltpu.VMEM((2, KB, tokens), BF16),
            pltpu.VMEM((128, tokens), F32),
        ]
        + ([pltpu.VMEM(layer.shape, layer.dtype), pltpu.SemaphoreType.DMA((2,) + layer.shape[:1])] if moves else []),
    )
    return pl.pallas_call(
        functools.partial(bwd_kernel, blocks, first, moves),
        grid_spec=spec,
        out_shape=[
            jax.ShapeDtypeStruct((sources, items, local, 384), BF16),
            jax.ShapeDtypeStruct((items, 2, NEAR), F32),
            jax.ShapeDtypeStruct(moved.shape, moved.dtype),
        ],
        compiler_params=pltpu.CompilerParams(vmem_limit_bytes=50 * 2**20),
        cost_estimate=pl.CostEstimate(flops=items * tokens * tokens * 1280, bytes_accessed=items * tokens * 4096, transcendentals=items * tokens * tokens * 2),
        name="attention_backward",
    )(lengths, place, qkv, outs, aug, grads, rows, layer, after)


VPAD = 384
PAIRS = 6
TN = (((0,), (0,)), ((), ()))
SQRT_2_OVER_PI = 0.7978845608028654


def block_masks(masks, first_byte, total_bytes):
    shape = masks.shape[2:]
    conv_at = first_byte - 2 + lax.broadcasted_iota(jnp.int32, shape, 1)
    token = lax.broadcasted_iota(jnp.int32, shape, 0)
    for side in range(2):
        place = first_byte + 2 * token + side
        for size in range(1, 5):
            start = (place // size) * size
            inside = (conv_at >= start) & (conv_at < start + size) & (conv_at < total_bytes)
            masks[side, size - 1] = jnp.where(inside, 1.0 / size, 0.0)


def split_two(values):
    high = values.astype(BF16)
    return high, (values - high.astype(F32)).astype(BF16)


def permute_weight(weight, out):
    rows = weight.shape[0]
    low = lax.broadcasted_iota(jnp.int32, (rows, 128), 1) < 64
    for pair in range(PAIRS):
        at = pair * 384
        one, two, three = (weight[:, at + 128 * k : at + 128 * k + 128] for k in range(3))
        out[:, at : at + 128] = jnp.where(low, one, two)
        out[:, at + 128 : at + 256] = pltpu.roll(jnp.where(low, three, one).astype(F32), 64, 1).astype(BF16)
        out[:, at + 256 : at + 384] = jnp.where(low, two, three)


def greet(axis, here, count):
    barrier = pltpu.get_barrier_semaphore()

    def signal(step, unused):
        pl.semaphore_signal(barrier, inc=1, device_id={axis: lax.rem(here + step, count)}, device_id_type=pl.DeviceIdType.MESH)
        return unused

    lax.fori_loop(1, count, signal, 0)


def item_copy(devices, me, source, target, other, slot, sems):
    send, recv, unused = sems

    def outward():
        offset = lax.rem(other - me + devices, devices)
        return pltpu.make_async_remote_copy(
            src_ref=source, dst_ref=target, send_sem=send.at[offset, slot], recv_sem=recv.at[offset, slot],
            device_id={"seq": other}, device_id_type=pl.DeviceIdType.MESH,
        )

    def inward():
        offset = lax.rem(me - other + devices, devices)
        return pltpu.make_async_remote_copy(
            src_ref=source, dst_ref=target, send_sem=send.at[offset, slot], recv_sem=recv.at[offset, slot],
            device_id={"seq": other}, device_id_type=pl.DeviceIdType.MESH,
        )

    return outward, inward


def start_item(devices, me, source, target, other, slot, sems):
    @pl.when(other == me)
    def _():
        pltpu.make_async_copy(source, target, sems[2].at[slot]).start()

    @pl.when(other != me)
    def _():
        item_copy(devices, me, source, target, other, slot, sems)[0]().start()


def finish_sends(devices, me, total, source_of, target_of, sems):
    def wait(item, unused):
        other, slot = lax.rem(item, devices), item // devices

        @pl.when(other != me)
        def _():
            item_copy(devices, me, source_of(other, slot), target_of(other, slot), other, slot, sems)[0]().wait_send()

        return unused

    lax.fori_loop(0, total, wait, 0)


def finish_receives(devices, me, total, source_of, target_of, sems):
    per_device = -(-total // devices)

    def wait(at, unused):
        other, slot = at // per_device, lax.rem(at, per_device)

        @pl.when((slot * devices + me < total) & (other != me))
        def _():
            item_copy(devices, me, source_of(other, slot), target_of(other, slot), other, slot, sems)[1]().wait_recv()

        @pl.when((slot * devices + me < total) & (other == me))
        def _():
            pltpu.make_async_copy(source_of(other, slot), target_of(other, slot), sems[2].at[slot]).wait()

        return unused

    lax.fori_loop(0, devices * per_device, wait, 0)


def ranks_of(lengths_ref):
    count = lengths_ref.shape[0]
    ranks = []
    for one in range(count):
        rank = jnp.int32(0)
        for two in range(count):
            if two != one:
                ahead = lengths_ref[two] > lengths_ref[one] if two > one else lengths_ref[two] >= lengths_ref[one]
                rank = rank + ahead.astype(jnp.int32)
        ranks.append(rank)
    return ranks


def spread_ids(lengths_ref, ids_ref, from_left, from_right, extended, sems, me, devices):
    sequences, local_bytes = ids_ref.shape
    left_copy = pltpu.make_async_remote_copy(
        src_ref=ids_ref.at[:, 0:128], dst_ref=from_right, send_sem=sems.at[0], recv_sem=sems.at[1],
        device_id={"seq": jnp.maximum(me - 1, 0)}, device_id_type=pl.DeviceIdType.MESH,
    )
    right_copy = pltpu.make_async_remote_copy(
        src_ref=ids_ref.at[:, local_bytes - 128 : local_bytes], dst_ref=from_left, send_sem=sems.at[2], recv_sem=sems.at[3],
        device_id={"seq": jnp.minimum(me + 1, devices - 1)}, device_id_type=pl.DeviceIdType.MESH,
    )

    @pl.when(me > 0)
    def _():
        left_copy.start()

    @pl.when(me < devices - 1)
    def _():
        right_copy.start()

    @pl.when(me > 0)
    def _():
        left_copy.wait_send()
        right_copy.wait_recv()

    @pl.when(me < devices - 1)
    def _():
        right_copy.wait_send()
        left_copy.wait_recv()

    joined = jnp.concatenate([from_left[...], ids_ref[...], from_right[...]], axis=1).astype(F32)
    width = joined.shape[1]
    moved = pltpu.roll(joined, width - 124, 1)
    row = lax.broadcasted_iota(jnp.int32, (sequences, width), 0)
    lane = lax.broadcasted_iota(jnp.int32, (sequences, width), 1)
    position = me * local_bytes - 4 + lane
    length = jnp.zeros((sequences, width), jnp.int32)
    for one in range(sequences):
        length = jnp.where(row == one, lengths_ref[one], length)
    outside = (position < 0) | (position >= local_bytes * devices) | (lane >= local_bytes + 8)
    picked = jnp.where(outside, -1.0, jnp.where(position < length, moved, 0.0))
    ordered = jnp.zeros((sequences, width), F32)
    for one, rank in enumerate(ranks_of(lengths_ref)):
        ordered = jnp.where(row == rank, picked[one : one + 1, :], ordered)
    extended[...] = ordered


def front_kernel(
    sizes, lengths_ref, ids_ref, table_ref, weight_ref, vectors_ref,
    hidden_ref, normed_ref, conv_ref, mix_ref, share_ref, rows_ref, items_ref,
    masks, wide, permuted, stage, taps, from_left, from_right, extended, side_sems, *sems,
):
    local_tokens, window, devices, total = sizes
    step = pl.program_id(0)
    me = lax.axis_index("seq")

    @pl.when(step == 0)
    def _():
        from_left[...] = jnp.zeros_like(from_left)
        from_right[...] = jnp.zeros_like(from_right)
        greet("seq", me, devices)
        block_masks(masks, me * 2 * local_tokens, devices * 2 * local_tokens)
        permute_weight(weight_ref, permuted)
        table = table_ref[...].astype(F32)
        taps[...] = jnp.zeros_like(taps)
        for tap in range(5):
            taps[tap, 0 : table.shape[0], :] = (vectors_ref[tap : tap + 1, :] * table).astype(BF16)
        pl.semaphore_wait(pltpu.get_barrier_semaphore(), devices - 1)
        spread_ids(lengths_ref, ids_ref, from_left, from_right, extended, side_sems, me, devices)

    together = 1
    width_ids = extended.shape[1]
    row = jnp.broadcast_to(extended[pl.ds(step, 1), :], (8, width_ids))
    rows = pltpu.roll(pltpu.roll(row, width_ids - 4, 1), 0, 1, stride=1, stride_axis=0)
    rows_ref[0] = rows
    ids = rows.T[0:window]
    score = vectors_ref[7:8, :]
    gain = vectors_ref[5:6, :]
    model = score.shape[1]
    score_high, score_low = split_two(score)
    row16 = lax.broadcasted_iota(jnp.int32, (16, model), 0)
    score_rows = jnp.where(row16 == 0, score_high.astype(F32), jnp.where(row16 == 1, score_low.astype(F32), 0.0)).astype(BF16)
    lane = lax.broadcasted_iota(jnp.int32, (together * window, VPAD), 1).astype(F32)
    width = masks.shape[3]
    conv_all = jnp.zeros((together * window, model), F32)
    for tap in range(5):
        hot = jnp.where(ids[:, 4 - tap : 5 - tap] == lane, 1.0, 0.0).astype(BF16)
        conv_all = conv_all + dot(hot, taps[tap], NN)
    for one in range(together):
        high, low = split_two(conv_all[one * window : (one + 1) * window])
        conv_ref[one, 0:window] = high
        wide[one, 0, 0:window] = high
        wide[one, 1, 0:window] = low
        if width > window:
            wide[one, :, window:width] = jnp.zeros((2, width - window, model), BF16)
            conv_ref[one, window:width] = jnp.zeros((width - window, model), BF16)
        high = wide[one, 0]
        low = wide[one, 1]
        along = jnp.sum(dot(score_rows, high, NT), axis=0, keepdims=True) + dot(score_rows, low, NT)[0:1]
        mixed = jnp.zeros((local_tokens, width), F32)
        kept = jnp.zeros((local_tokens, 128), F32)
        lane128 = lax.broadcasted_iota(jnp.int32, (local_tokens, 128), 1)
        for side in range(2):
            scores = [jnp.sum(masks[side, k] * along, axis=1, keepdims=True) for k in range(4)]
            top = jnp.maximum(jnp.maximum(scores[0], scores[1]), jnp.maximum(scores[2], scores[3]))
            powers = [jnp.exp(value - top) for value in scores]
            under = 1.0 / (powers[0] + powers[1] + powers[2] + powers[3])
            for k in range(4):
                share = powers[k] * under
                mixed = mixed + share * masks[side, k]
                kept = jnp.where(lane128 == 4 * side + k, share, kept)
        share_ref[one] = kept
        mix_high, mix_low = split_two(mixed * 0.5)
        mix_ref[one] = mix_high
        hidden = dot(mix_high, high, NN) + dot(mix_high, low, NN) + dot(mix_low, high, NN)
        hidden_ref[one] = hidden
        scale = lax.rsqrt(jnp.mean(hidden * hidden, axis=1, keepdims=True) + 1e-06)
        normed_ref[one] = (hidden * scale * gain).astype(BF16)
    normed = normed_ref[...].reshape(together * local_tokens, model)
    for pair in range(PAIRS):
        piece = dot(normed, permuted[:, pair * 384 : pair * 384 + 384], NN).astype(BF16)
        for one in range(together):
            item = (step * together + one) * PAIRS + pair
            other, slot = lax.rem(item, devices), item // devices
            stage[other, slot] = piece[one * local_tokens : (one + 1) * local_tokens]

    if devices == 8:

        def send(at, unused):
            item = step * PAIRS + at
            other, slot = lax.rem(item, 8), item // 8

            @pl.when(other != me)
            def _():
                to_device(other, stage.at[other, slot], items_ref.at[me, slot], sems[0].at[0], sems[1].at[0]).start()

            return unused

        lax.fori_loop(0, PAIRS, send, 0)

        @pl.when(step == pl.num_programs(0) - 1)
        def _():
            finish_back(me, stage, items_ref, sems)

        return
    send_items(devices, me, step * together * PAIRS, together * PAIRS, stage, items_ref, sems)

    @pl.when(step == pl.num_programs(0) - 1)
    def _():
        finish_sends(devices, me, total, lambda other, slot: stage.at[other, slot], lambda other, slot: items_ref.at[me, slot], sems)
        finish_receives(devices, me, total, lambda other, slot: stage.at[other, slot], lambda other, slot: items_ref.at[other, slot], sems)


def to_device(other, source, target, send, recv):
    return pltpu.make_async_remote_copy(
        src_ref=source, dst_ref=target, send_sem=send, recv_sem=recv, device_id={"seq": other}, device_id_type=pl.DeviceIdType.MESH
    )


SLOT_GROUPS = ((0, 2), (2, 1), (3, 2), (5, 1))


def send_slots(me, number, source, arrived, sems):
    first, count = SLOT_GROUPS[number]
    slots = pl.ds(first, count)

    def send(offset, unused):
        other = lax.rem(me + offset, 8)
        to_device(other, source.at[other, slots], arrived.at[me, slots], sems[0].at[number], sems[1].at[number]).start()
        return unused

    lax.fori_loop(1, 8, send, 0)
    pltpu.make_async_copy(source.at[me, slots], arrived.at[me, slots], sems[2].at[number]).start()


def wait_slots(me, number, source, arrived, sems, sends):
    first, count = SLOT_GROUPS[number]
    slots = pl.ds(first, count)
    seven = pl.ds(0, 7)
    copies = to_device(lax.rem(me + 1, 8), source.at[seven, slots], arrived.at[seven, slots], sems[0].at[number], sems[1].at[number])
    if sends:
        copies.wait_send()
    else:
        copies.wait_recv()
        pltpu.make_async_copy(source.at[me, slots], arrived.at[me, slots], sems[2].at[number]).wait()


def send_back(me, step, stage, target, sems):
    base, base_to = 3, 0
    for parity in range(2):

        def send(offset, unused):
            other = lax.rem(me + offset, 8)

            @pl.when(other < 4)
            def _():
                first, count = (0, 2) if parity == 0 else (2, 1)
                to_device(other, stage.at[other, pl.ds(base + first, count)], target.at[me, pl.ds(base_to + first, count)], sems[0].at[0], sems[1].at[0]).start()

            @pl.when(other >= 4)
            def _():
                first, count = (0, 1) if parity == 0 else (1, 2)
                to_device(other, stage.at[other, pl.ds(base + first, count)], target.at[me, pl.ds(base_to + first, count)], sems[0].at[0], sems[1].at[0]).start()

            return unused

        @pl.when(lax.rem(step, 2) == parity)
        def _():
            lax.fori_loop(1, 8, send, 0)


def finish_half(me, stage, target, sems):
    slots = pl.ds(3, 3)
    local = pltpu.make_async_copy(stage.at[me, slots], target.at[me], sems[2].at[0])
    local.start()
    seven = pl.ds(0, 7)
    copies = to_device(lax.rem(me + 1, 8), stage.at[seven, slots], target.at[seven], sems[0].at[0], sems[1].at[0])
    copies.wait_send()
    copies.wait_recv()
    local.wait()


def finish_back(me, stage, target, sems):
    local = pltpu.make_async_copy(stage.at[me], target.at[me], sems[2].at[0])
    local.start()
    seven = pl.ds(0, 7)
    copies = to_device(lax.rem(me + 1, 8), stage.at[seven], target.at[seven], sems[0].at[0], sems[1].at[0])
    copies.wait_send()
    copies.wait_recv()
    local.wait()


def send_group(devices, me, total, group, number, source, arrived, sems):
    for slot in range(-(-total // devices)):
        item = slot * devices + me

        @pl.when((item < total) & (item // group == number))
        def _():
            def send(offset, unused):
                other = lax.rem(me + offset, devices)
                start_item(devices, me, source.at[other, slot], arrived.at[me, slot], other, slot, sems)
                return unused

            lax.fori_loop(0, devices, send, 0)


def send_items(devices, me, first, count, stage, target, sems):
    def send(at, unused):
        item = first + at
        other, slot = lax.rem(item, devices), item // devices
        start_item(devices, me, stage.at[other, slot], target.at[me, slot], other, slot, sems)
        return unused

    lax.fori_loop(0, count, send, 0)


def take_items(devices, me, first, count, source, arrived, sems):
    def take(at, unused):
        item = first + at
        take_item(devices, me, lax.rem(item, devices), item // devices, source, arrived, sems)
        return unused

    lax.fori_loop(0, count, take, 0)


def finish_groups(devices, me, total, source, arrived, sems):
    per_device = -(-total // devices)

    def wait(at, unused):
        slot, offset = at // devices, lax.rem(at, devices)
        other = lax.rem(me + offset, devices)

        @pl.when((slot * devices + me < total) & (offset != 0))
        def _():
            item_copy(devices, me, source.at[other, slot], arrived.at[me, slot], other, slot, sems)[0]().wait_send()

        return unused

    lax.fori_loop(0, devices * per_device, wait, 0)


def take_item(devices, me, other, slot, source, arrived, sems):
    @pl.when(other == me)
    def _():
        pltpu.make_async_copy(source.at[me, slot], arrived.at[me, slot], sems[2].at[slot]).wait()

    @pl.when(other != me)
    def _():
        item_copy(devices, me, source.at[other, slot], arrived.at[other, slot], other, slot, sems)[1]().wait_recv()


def mid_kernel(
    sizes, att_ref, hidden_ref, cot_ref, out_weight_ref, in_weight_ref, down_ref, vectors_ref,
    layer_ref, act_ref, gate_up_ref, normed_ref, attended_ref, branch_ref, residual_ref, items_ref, gain_out, rest_ref,
    arrived, stage, keep_gain, grad_act, *sems,
):
    local_tokens, devices, total = sizes
    in_sems, out_sems = sems[:3], sems[3:]
    step = pl.program_id(0)
    me = lax.axis_index("seq")

    @pl.when(step == 0)
    def _():
        greet("seq", me, devices)
        keep_gain[...] = jnp.zeros_like(keep_gain)
        pl.semaphore_wait(pltpu.get_barrier_semaphore(), devices - 1)

    together = hidden_ref.shape[0]
    group = together * PAIRS
    turn = lax.rem(step + 2, 4) if devices == 8 else step
    rows = together * local_tokens
    model = vectors_ref.shape[1]

    here_rows = pl.ds(pl.multiple_of(turn * rows, 128), rows)

    @pl.when(step == 0)
    def _():
        if devices == 8:
            for number in (2, 3, 0, 1):
                send_slots(me, number, att_ref, arrived, in_sems)
        else:
            send_group(devices, me, total, group, 0, att_ref, arrived, in_sems)
        every = cot_ref[...].reshape(grad_act.shape[0], model)
        for first in range(0, down_ref.shape[0], 512):
            grad_act[:, first : first + 512] = dot(every, down_ref[first : first + 512, :], NT)

    if devices == 8:
        for number in range(4):

            @pl.when(turn == number)
            def _():
                wait_slots(me, number, att_ref, arrived, in_sems, False)

    else:
        take_items(devices, me, step * group, group, att_ref, arrived, in_sems)

        @pl.when(step + 1 < pl.num_programs(0))
        def _():
            send_group(devices, me, total, group, step + 1, att_ref, arrived, in_sems)

    gathered = []
    for one in range(together):
        pieces = []
        for pair in range(PAIRS):
            item = (turn * together + one) * PAIRS + pair
            other, slot = lax.rem(item, devices), item // devices
            pieces.append(arrived[other, slot])
        gathered.append(jnp.concatenate(pieces, axis=1))
    attended = jnp.concatenate(gathered, axis=0)
    attended_ref[...] = attended.reshape(attended_ref.shape)
    residual = hidden_ref[...].reshape(rows, model) + dot(attended, out_weight_ref[...], NN)
    gain = vectors_ref[6:7, :]
    scale = lax.rsqrt(jnp.mean(residual * residual, axis=1, keepdims=True) + 1e-06)
    normed = (residual * scale * gain).astype(BF16)
    normed_ref[...] = normed.reshape(normed_ref.shape)
    cot = cot_ref[pl.ds(turn * together, together)].reshape(rows, model)
    hidden_units = down_ref.shape[0]
    chunk = 512
    layer = residual
    back = jnp.zeros_like(residual)
    for first in range(0, hidden_units, chunk):
        here = slice(first, first + chunk)
        there = slice(hidden_units + first, hidden_units + first + chunk)
        gate = dot(normed, in_weight_ref[:, here], NN)
        up = dot(normed, in_weight_ref[:, there], NN)
        grad = grad_act[here_rows, here]
        square = gate * gate
        inner = gate * (SQRT_2_OVER_PI + (SQRT_2_OVER_PI * 0.044715) * square)
        curve = jnp.tanh(inner)
        half_plus = 0.5 + 0.5 * curve
        smooth = gate * half_plus
        slope = half_plus + (0.5 * gate) * (1.0 - curve * curve) * (SQRT_2_OVER_PI + (3 * SQRT_2_OVER_PI * 0.044715) * square)
        act = (smooth * up).astype(BF16)
        grad_gate = (grad * up * slope).astype(BF16)
        grad_up = (grad * smooth).astype(BF16)
        act_ref[:, :, here] = act.reshape(together, local_tokens, chunk)
        gate_up_ref[:, :, here] = grad_gate.reshape(together, local_tokens, chunk)
        gate_up_ref[:, :, there] = grad_up.reshape(together, local_tokens, chunk)
        layer = layer + dot(act, down_ref[here, :], NN)
        back = back + dot(grad_gate, in_weight_ref[:, here], NT) + dot(grad_up, in_weight_ref[:, there], NT)
    layer_ref[...] = layer.reshape(layer_ref.shape)
    weighted = gain * back
    inner_mean = jnp.mean(residual * weighted, axis=1, keepdims=True)
    grad_residual = cot.astype(F32) + scale * weighted - residual * (scale * scale * scale * inner_mean)
    residual_ref[...] = grad_residual.reshape(residual_ref.shape)
    branch = grad_residual.astype(BF16)
    branch_ref[...] = branch.reshape(branch_ref.shape)
    grad_attended = dot(branch, out_weight_ref[...], NT).astype(BF16)
    for one in range(together):
        for pair in range(PAIRS):
            item = (turn * together + one) * PAIRS + pair
            other, slot = lax.rem(item, devices), item // devices
            stage[other, slot] = grad_attended[one * local_tokens : (one + 1) * local_tokens, pair * 128 : pair * 128 + 128]
    keep_gain[...] += jnp.sum((back * residual * scale).reshape(rows // 8, 8, model), axis=0)
    gain_out[...] = jnp.sum(keep_gain[...], axis=0, keepdims=True)
    if devices == 8:
        @pl.when(step < 2)
        def _():
            send_back(me, turn, stage, items_ref, out_sems)

        @pl.when(step == 3)
        def _():
            for number in range(4):
                wait_slots(me, number, att_ref, arrived, in_sems, True)
            finish_half(me, stage, items_ref, out_sems)
            rest_ref[...] = stage[:, 0:3]

        return
    send_items(devices, me, step * group, group, stage, items_ref, out_sems)

    @pl.when(step == pl.num_programs(0) - 1)
    def _():
        finish_groups(devices, me, total, att_ref, arrived, in_sems)
        finish_sends(devices, me, total, lambda other, slot: stage.at[other, slot], lambda other, slot: items_ref.at[me, slot], out_sems)
        finish_receives(devices, me, total, lambda other, slot: stage.at[other, slot], lambda other, slot: items_ref.at[other, slot], out_sems)


def back_kernel(
    sizes, custom, one_ref, two_ref, hidden_ref, residual_ref, conv_ref, mix_ref, share_ref, ids_ref, weight_ref,
    table_ref, vectors_ref, bias_ref, bias_hot_ref, gain_two_ref, *refs,
):
    local_tokens, window, devices = sizes
    step = pl.program_id(0)
    last = step == pl.num_programs(0) - 1
    me = lax.axis_index("seq")
    plane = lax.axis_index("dp")
    model = vectors_ref.shape[1]
    if custom:
        normed_ref, across_ref, planes_ref = refs[:3]
        block, qkv_out, in_out, down_out, weight_out = refs[3:8]
        refs = refs[8:]
    else:
        block, flat_out, refs = refs[0], refs[1], refs[2:]
    masks, permuted, tap_sums, keep_gain, keep_score = refs[:5]
    refs = refs[5:]
    small = SmallSums(block, refs[:5], refs[5:13])
    refs = refs[13:]

    @pl.when(step == 0)
    def _():
        greet("seq", me, devices)
        greet("dp", plane, small.along)
        keep_gain[...] = jnp.zeros_like(keep_gain)
        keep_score[...] = jnp.zeros_like(keep_score)
        tap_sums[...] = jnp.zeros_like(tap_sums)
        pl.semaphore_wait(pltpu.get_barrier_semaphore(), devices + small.along - 2)

    half = one_ref.shape[1]

    def block_of(item):
        other, slot = lax.rem(item, devices), item // devices
        if isinstance(item, int):
            return (one_ref if slot < half else two_ref)[other, slot % half]
        return jnp.where(slot < half, one_ref[other, jnp.minimum(slot, half - 1)], two_ref[other, jnp.maximum(slot - half, 0)])

    if custom:
        reduce = WeightSums(normed_ref, across_ref, planes_ref, block_of, refs)

        @pl.when(step == 0)
        def _():
            reduce.begin()
            reduce.late()

        @pl.when(step == 1)
        def _():
            reduce.in_two()

        @pl.when(step == 2)
        def _():
            reduce.late_one()

        @pl.when(step == 3)
        def _():
            reduce.in_three()
            reduce.rest_two()

    @pl.when(step == 0)
    def _():
        block_masks(masks, me * 2 * local_tokens, devices * 2 * local_tokens)
        permute_weight(weight_ref, permuted)

    together = hidden_ref.shape[0]
    rows = together * local_tokens
    projected = jnp.concatenate(
        [
            jnp.concatenate([block_of((step * together + one) * PAIRS + pair) for pair in range(PAIRS)], axis=1)
            for one in range(together)
        ],
        axis=0,
    )
    if not custom:
        flat_out[...] = projected.reshape(flat_out.shape)
    width = masks.shape[3]
    grad_normed = dot(projected, permuted[...], NT)
    hidden = hidden_ref[...].reshape(rows, model)
    gain = vectors_ref[5:6, :]
    score = vectors_ref[7:8, :]
    scale = lax.rsqrt(jnp.mean(hidden * hidden, axis=1, keepdims=True) + 1e-06)
    weighted = gain * grad_normed
    inner_mean = jnp.mean(hidden * weighted, axis=1, keepdims=True)
    grad_hidden = residual_ref[...].reshape(rows, model) + scale * weighted - hidden * (scale * scale * scale * inner_mean)
    keep_gain[...] += jnp.sum((grad_normed * hidden * scale).reshape(rows // 8, 8, model), axis=0)
    high_all, low_all = split_two(grad_hidden)
    vector = jnp.broadcast_to(score.astype(BF16), (local_tokens, model))
    row16 = lax.broadcasted_iota(jnp.int32, (16, width), 0)
    slopes = []
    for one in range(together):
        own = slice(one * local_tokens, (one + 1) * local_tokens)
        high, low = high_all[own], low_all[own]
        conv = conv_ref[one]
        cross = 0.5 * (dot(high, conv, NT) + dot(low, conv, NT))
        kept = share_ref[one]
        total = jnp.zeros((local_tokens, width), F32)
        for side in range(2):
            shares = [kept[:, 4 * side + k : 4 * side + k + 1] for k in range(4)]
            grads = [jnp.sum(masks[side, k] * cross, axis=1, keepdims=True) for k in range(4)]
            mean = sum(share * grad for share, grad in zip(shares, grads))
            for k in range(4):
                total = total + (shares[k] * (grads[k] - mean)) * masks[side, k]
        column = jnp.sum(total, axis=0, keepdims=True)
        column_high, column_low = split_two(column)
        column_rows = jnp.where(row16 == 0, column_high.astype(F32), jnp.where(row16 == 1, column_low.astype(F32), 0.0)).astype(BF16)
        keep_score[...] += dot(column_rows, conv, NN)
        left = jnp.concatenate([mix_ref[one], total.astype(BF16)], axis=0)
        right = jnp.concatenate([high, vector], axis=0)
        slopes.append(dot(left, right, TN)[0:window].astype(BF16))
    slope = jnp.concatenate(slopes, axis=0)
    row = lax.broadcasted_iota(jnp.int32, (SMALL_ROWS, window), 0).astype(F32)
    for tap in range(5):
        hot = jnp.concatenate(
            [jnp.where(ids_ref[one, 4 - tap : 5 - tap, 0:window] == row, 1.0, 0.0).astype(BF16) for one in range(together)], axis=1
        )
        tap_sums[tap] += dot(hot, slope, NN)

    @pl.when(last)
    def _():
        if custom:
            reduce.late_two()
        table_grad = jnp.zeros((SMALL_ROWS, model), F32)
        table = table_ref[...].astype(F32)
        place = lax.broadcasted_iota(jnp.int32, (SMALL_ROWS, model), 0)
        extra = []
        for tap in range(5):
            sums = tap_sums[tap]
            table_grad = table_grad + vectors_ref[tap : tap + 1, :] * sums
            extra.append(jnp.sum(sums[0 : table.shape[0]] * table, axis=0, keepdims=True))
        extra.append(jnp.sum(keep_gain[...], axis=0, keepdims=True))
        extra.append(jnp.sum(keep_score[...], axis=0, keepdims=True))
        extra.append(gain_two_ref[...])
        for index, value in enumerate(extra):
            table_grad = jnp.where(place == 259 + index, value, table_grad)
        block[...] = table_grad
        heads = jnp.zeros((16, 128), F32)
        head_row = lax.broadcasted_iota(jnp.int32, (16, 128), 0)
        for slot in range(bias_ref.shape[0]):
            first, second = split_two(bias_ref[slot])
            sums = dot(first, bias_hot_ref[...], NN) + dot(second, bias_hot_ref[...], NN)
            pair = lax.rem(slot * devices + me, PAIRS)
            heads = heads + jnp.where(head_row == 2 * pair, sums[0:1], 0.0) + jnp.where(head_row == 2 * pair + 1, sums[1:2], 0.0)
        block[272:288, 0:128] = heads
        small.pack()
        small.one_start()
        small.one_middle()
        if custom:
            reduce.late_three()
        small.one_finish()
        if custom:
            reduce.finish_rest(down_out)
        if custom:
            reduce.finish_in(in_out, weight_out)
        small.two_finish()
        if custom:
            reduce.finish_late(qkv_out)
        small.three_finish()
        small.three_more()
        small.four_finish()


def finish_kernel(block, *refs):
    refs = list(refs)
    count = (len(refs) - 6) // 2
    for source, target in zip(refs[:count], refs[count : 2 * count]):
        target[...] = source[...]
    table_out, taps_out, one_out, score_out, two_out, bias_out = refs[2 * count :]
    table_out[...] = block[0:259, :]
    taps_out[...] = block[259:264, :]
    one_out[...] = block[264, :]
    score_out[...] = block[265, :]
    two_out[...] = block[266, :]
    bias_out[...] = block[272:288, 0:128].T[0:32, 0:12]


def call_finish(block, sums):
    model = block.shape[1]
    shape = lambda *dims: jax.ShapeDtypeStruct(dims, F32)
    return pl.pallas_call(
        finish_kernel,
        out_shape=[shape(*x.shape) for x in sums] + [shape(259, model), shape(5, model), shape(model), shape(model), shape(model), shape(32, 12)],
        compiler_params=pltpu.CompilerParams(vmem_limit_bytes=VMEM_LIMIT),
        name="finish",
    )(block, *sums)


VMEM_LIMIT = 58 * 2**20
TOGETHER = 2


def item_sems(devices, per_device):
    dma = pltpu.SemaphoreType.DMA
    if devices == 8:
        return [dma((4,)), dma((4,)), dma((4,))]
    return [dma((devices, per_device)), dma((devices, per_device)), dma((per_device,))]


def whole(*shape):
    return pl.BlockSpec(shape, lambda s, *_: (0,) * len(shape), pipeline_mode=pl.Buffered(1))


def part(*shape):
    return pl.BlockSpec(shape, lambda s, *_: (s,) + (0,) * (len(shape) - 1))


ANYWHERE = pl.BlockSpec(memory_space=pl.ANY)


def remote_params(number):
    return pltpu.CompilerParams(vmem_limit_bytes=VMEM_LIMIT, collective_id=number, has_side_effects=True)


def call_front(lengths, ids, table, weight, vectors, devices, per_device):
    sequences, local_bytes = ids.shape
    local_tokens = local_bytes // 2
    window = local_bytes + 16
    width = -(-window // 128) * 128
    model = weight.shape[0]
    return pl.pallas_call(
        functools.partial(front_kernel, (local_tokens, window, devices, sequences * PAIRS)),
        grid=(sequences,),
        in_specs=[pl.BlockSpec(memory_space=pltpu.SMEM), whole(*ids.shape), whole(*table.shape), whole(*weight.shape), whole(*vectors.shape)],
        out_specs=[
            part(1, local_tokens, model),
            part(1, local_tokens, model),
            part(1, width, model),
            part(1, local_tokens, width),
            part(1, local_tokens, 128),
            part(1, 8, local_bytes + 256),
            ANYWHERE,
        ],
        scratch_shapes=[
            pltpu.VMEM((2, 4, local_tokens, width), F32),
            pltpu.VMEM((1, 2, width, model), BF16),
            pltpu.VMEM(weight.shape, BF16),
            pltpu.VMEM((devices, per_device, local_tokens, 384), BF16),
            pltpu.VMEM((5, VPAD, model), BF16),
            pltpu.VMEM((sequences, 128), jnp.int32),
            pltpu.VMEM((sequences, 128), jnp.int32),
            pltpu.VMEM((sequences, local_bytes + 256), F32),
            pltpu.SemaphoreType.DMA((4,)),
        ]
        + item_sems(devices, per_device),
        out_shape=[
            jax.ShapeDtypeStruct((sequences, local_tokens, model), F32),
            jax.ShapeDtypeStruct((sequences, local_tokens, model), BF16),
            jax.ShapeDtypeStruct((sequences, width, model), BF16),
            jax.ShapeDtypeStruct((sequences, local_tokens, width), BF16),
            jax.ShapeDtypeStruct((sequences, local_tokens, 128), F32),
            jax.ShapeDtypeStruct((sequences, 8, local_bytes + 256), F32),
            jax.ShapeDtypeStruct((devices, per_device, local_tokens, 384), BF16),
        ],
        compiler_params=remote_params(3),
        cost_estimate=pl.CostEstimate(flops=5 * 10**10, bytes_accessed=2 * 10**7, transcendentals=10**5),
        name="front",
    )(lengths, ids, table, weight, vectors)


def call_mid(att, hidden, cot, out_weight, in_weight, down_weight, vectors):
    devices, per_device, local_tokens, unused = att.shape
    sequences, unused, model = hidden.shape
    hidden_units = down_weight.shape[0]
    fast = devices == 8
    rows = lambda lanes: pl.BlockSpec((TOGETHER, local_tokens, lanes), lambda s: (lax.rem(s + 2, 4) if fast else s, 0, 0))
    shape = (devices, per_device // 2 if fast else per_device, local_tokens, 128)
    rest = shape if fast else (1, 1, 8, 128)
    full = lambda lanes, kind: jax.ShapeDtypeStruct((sequences, local_tokens, lanes), kind)
    return pl.pallas_call(
        functools.partial(mid_kernel, (local_tokens, devices, sequences * PAIRS)),
        grid=(sequences // TOGETHER,),
        in_specs=[
            ANYWHERE,
            rows(model),
            whole(*cot.shape),
            whole(*out_weight.shape),
            whole(*in_weight.shape),
            whole(*down_weight.shape),
            whole(*vectors.shape),
        ],
        out_specs=[
            rows(model),
            rows(hidden_units),
            rows(2 * hidden_units),
            rows(model),
            rows(model),
            rows(model),
            rows(model),
            ANYWHERE,
            whole(1, model),
            whole(*rest),
        ],
        scratch_shapes=[pltpu.VMEM(att.shape, BF16), pltpu.VMEM(att.shape, BF16), pltpu.VMEM((8, model), F32), pltpu.VMEM((sequences * local_tokens, hidden_units), F32)]
        + item_sems(devices, per_device)
        + item_sems(devices, per_device),
        out_shape=[
            full(model, F32),
            full(hidden_units, BF16),
            full(2 * hidden_units, BF16),
            full(model, BF16),
            full(model, BF16),
            full(model, BF16),
            full(model, F32),
            jax.ShapeDtypeStruct(shape, BF16),
            jax.ShapeDtypeStruct((1, model), F32),
            jax.ShapeDtypeStruct(rest, BF16),
        ],
        compiler_params=remote_params(4),
        cost_estimate=pl.CostEstimate(flops=5 * 10**10, bytes_accessed=4 * 10**7, transcendentals=10**6),
        name="middle",
    )(att, hidden, cot, out_weight, in_weight, down_weight, vectors)


def call_back(custom, one, two, hidden, residual, conv, mix, share, ids, weight, table, vectors, bias_rows, gain_two, along, extra):
    devices, unused, local_tokens, unused = one.shape
    sequences, unused, model = hidden.shape
    width = conv.shape[1]
    window = 2 * local_tokens + 16
    bias_hot = jnp.pad(near_one_hot(), ((0, 0), (0, 96))).astype(BF16)
    out_specs = [whole(SMALL_ROWS, model)]
    out_shape = [jax.ShapeDtypeStruct((SMALL_ROWS, model), F32)]
    scratch = []
    specs = []
    if custom:
        specs = [whole(*x.shape) for x in extra]
        sums = [(96, 576), (96, 1024), (256, 192), (96, 192)]
        out_specs = out_specs + [whole(*shape) for shape in sums]
        out_shape = out_shape + [jax.ShapeDtypeStruct(shape, F32) for shape in sums]
        scratch = weight_scratch(model, sequences * local_tokens)
    else:
        out_specs = out_specs + [part(TOGETHER, local_tokens, PAIRS * 384)]
        out_shape = out_shape + [jax.ShapeDtypeStruct((sequences, local_tokens, PAIRS * 384), BF16)]
    return pl.pallas_call(
        functools.partial(back_kernel, (local_tokens, window, devices), custom),
        grid=(sequences // TOGETHER,),
        in_specs=[
            whole(*one.shape),
            whole(*two.shape),
            part(TOGETHER, local_tokens, model),
            part(TOGETHER, local_tokens, model),
            part(TOGETHER, width, model),
            part(TOGETHER, local_tokens, width),
            part(TOGETHER, local_tokens, 128),
            part(TOGETHER, 8, ids.shape[2]),
            whole(*weight.shape),
            whole(*table.shape),
            whole(*vectors.shape),
            whole(*bias_rows.shape),
            whole(*bias_hot.shape),
            whole(1, model),
        ]
        + specs,
        out_specs=out_specs,
        scratch_shapes=[
            pltpu.VMEM((2, 4, local_tokens, width), F32),
            pltpu.VMEM(weight.shape, BF16),
            pltpu.VMEM((5, SMALL_ROWS, model), F32),
            pltpu.VMEM((8, model), F32),
            pltpu.VMEM((16, model), F32),
        ]
        + small_scratch(devices, along)
        + scratch,
        out_shape=out_shape,
        compiler_params=remote_params(5),
        cost_estimate=pl.CostEstimate(flops=10**11, bytes_accessed=2 * 10**7, transcendentals=10**5),
        name="back",
    )(one, two, hidden, residual, conv, mix, share, ids, weight, table, vectors, bias_rows, bias_hot, gain_two, *extra)


IN_ROWS = 8 * 96 + 2 * 96
REST_ROWS = 2 * 192
LATE_ROWS = 5 * 96


def meet_sibling(core):
    barrier = pltpu.get_barrier_semaphore()
    sibling = lax.axis_index("seq") + 1 - 2 * core
    pl.semaphore_signal(barrier, inc=1, device_id={"seq": sibling}, device_id_type=pl.DeviceIdType.MESH)
    pl.semaphore_wait(barrier, 1)


def to_sibling(core, source, target, send_sem, recv_sem):
    sibling = lax.axis_index("seq") + 1 - 2 * core
    return pltpu.make_async_remote_copy(
        src_ref=source, dst_ref=target, send_sem=send_sem, recv_sem=recv_sem,
        device_id={"seq": sibling}, device_id_type=pl.DeviceIdType.MESH,
    )


def spread_rows(core, source, lanes, keep_ref, send_ref, index_of):
    for chip in range(4):
        for other, ref in ((0, keep_ref), (1, send_ref)):
            device = 2 * chip + lax.rem(core + other, 2)
            rows = pl.ds(pl.multiple_of(device * 96, 32), 96)
            ref[index_of(chip)] = source[rows, lanes]


def early_kernel(
    act_ref, cot_ref, normed_ref, gate_up_ref, attended_ref, branch_ref, after, keep_in, keep_rest,
    other_in, got_in, other_rest, got_rest, cot_t, normed_t, result, send_in, recv_in, send_down, recv_down, send_out, recv_out,
):
    step = pl.program_id(0)
    core = lax.rem(lax.axis_index("seq"), 2)
    model = cot_t.shape[0]
    tokens = cot_t.shape[1]
    out_rows = pl.ds(768, 192)
    out_copy = to_sibling(core, other_in.at[:, :, out_rows], got_in.at[:, :, out_rows], send_out, recv_out)

    def in_copy(at):
        rows = pl.ds(pl.multiple_of(384 * lax.rem(at, 2), 384), 384)
        return to_sibling(core, other_in.at[:, at // 2, rows], got_in.at[:, at // 2, rows], send_in.at[at], recv_in.at[at])

    def down_copy(chip):
        return to_sibling(core, other_rest.at[:, chip], got_rest.at[:, chip], send_down.at[chip], recv_down.at[chip])

    @pl.when(step == 0)
    def _():
        meet_sibling(core)
        cot_t[...] = cot_ref[...].reshape(tokens, model).T
        normed_t[...] = attended_ref[...].reshape(tokens, model).T
        for first in range(0, model, 256):
            result[:, 0:256] = dot(normed_t[...], branch_ref[:, :, first : first + 256].reshape(tokens, 256), NN).astype(BF16)
            for half in range(2):
                tile = first // 128 + half
                for column, slot in {0: ((0, 0),), 1: ((0, 1), (1, 0)), 2: ((1, 1),), 3: ((2, 0),), 4: ((2, 1), (3, 0)), 5: ((3, 1),)}[tile]:
                    rows = slice(768 + 96 * slot, 864 + 96 * slot)
                    spread_rows(core, result, slice(128 * half, 128 * half + 128), keep_in, other_in, lambda chip: (chip, column, rows))
        normed_t[...] = normed_ref[...].reshape(tokens, model).T

    result[...] = dot(normed_t[...], gate_up_ref[...].reshape(tokens, 512), NN).astype(BF16)
    column_at = step // 2
    for quarter in range(4):
        rows = pl.ds(pl.multiple_of((4 * lax.rem(step, 2) + quarter) * 96, 32), 96)
        spread_rows(core, result, slice(128 * quarter, 128 * quarter + 128), keep_in, other_in, lambda chip: (chip, column_at, rows))
    down = dot(cot_t[...], act_ref[...].reshape(tokens, 256), NN).astype(BF16)

    def put_down(ref):
        for column in range(4):
            for half in range(2):
                ref[column, step // 2, 192 * half : 192 * half + 192] = down[192 * column : 192 * column + 192, 128 * half : 128 * half + 128]

    @pl.when(lax.rem(step, 2) == core)
    def _():
        put_down(keep_rest)

    @pl.when(lax.rem(step, 2) != core)
    def _():
        put_down(other_rest)
        down_copy(step // 2).start()

    in_copy(step).start()

    @pl.when(step == 0)
    def _():
        out_copy.start()

    @pl.when(step == 7)
    def _():
        for at in range(8):
            in_copy(at).wait()
        out_copy.wait()
        for chip in range(4):
            down_copy(chip).wait()

        def add(at, unused):
            one, two = at // 4, lax.rem(at, 4)
            keep_in[one, two] = (keep_in[one, two].astype(F32) + got_in[one, two].astype(F32)).astype(BF16)
            keep_rest[one, two] = (keep_rest[one, two].astype(F32) + got_rest[one, two].astype(F32)).astype(BF16)
            return unused

        lax.fori_loop(0, 16, add, 0)


def call_early(act, cot, normed, gate_up, attended, branch, after):
    sequences, local_tokens, model = cot.shape
    tokens = sequences * local_tokens
    every = whole(sequences, local_tokens, model)
    shapes = [(4, 4, IN_ROWS, 128), (4, 4, REST_ROWS, 128)]
    dma = pltpu.SemaphoreType.DMA
    return pl.pallas_call(
        early_kernel,
        grid=(8,),
        in_specs=[
            pl.BlockSpec((sequences, local_tokens, 256), lambda s: (0, 0, s)),
            every,
            every,
            pl.BlockSpec((sequences, local_tokens, 512), lambda s: (0, 0, s)),
            every,
            every,
            ANYWHERE,
        ],
        out_specs=[whole(*shape) for shape in shapes],
        scratch_shapes=[
            pltpu.VMEM(shapes[0], BF16),
            pltpu.VMEM(shapes[0], BF16),
            pltpu.VMEM(shapes[1], BF16),
            pltpu.VMEM(shapes[1], BF16),
            pltpu.VMEM((model, tokens), BF16),
            pltpu.VMEM((model, tokens), BF16),
            pltpu.VMEM((model, 512), BF16),
            dma((8,)), dma((8,)), dma((4,)), dma((4,)), dma, dma,
        ],
        out_shape=[jax.ShapeDtypeStruct(shape, BF16) for shape in shapes],
        compiler_params=pltpu.CompilerParams(vmem_limit_bytes=VMEM_LIMIT, collective_id=1, has_side_effects=True),
        cost_estimate=pl.CostEstimate(flops=11 * 10**9, bytes_accessed=3 * 10**7, transcendentals=0),
        name="early_gradients",
    )(act, cot, normed, gate_up, attended, branch, after)


class ChipSums:
    def __init__(self, source, buffers, sems, chip, core):
        self.source, self.first, self.relay, self.second = (source,) + tuple(buffers)
        self.send, self.recv = sems
        self.chip, self.core = chip, core
        self.beside = chip + 1 - 2 * lax.rem(chip, 2)
        self.above = lax.rem(chip + 2, 4)

    def copy(self, other, source, target, number):
        return pltpu.make_async_remote_copy(
            src_ref=source, dst_ref=target, send_sem=self.send.at[number], recv_sem=self.recv.at[number],
            device_id={"seq": 2 * other + self.core}, device_id_type=pl.DeviceIdType.MESH,
        )

    def ways(self):
        return ((0, self.beside, self.above), (1, self.above, self.beside))

    def one(self):
        made = []
        for way, near, other in self.ways():
            columns = pl.ds(2 * way, 2)
            made.append(self.copy(near, self.source.at[near, columns], self.first.at[way, 0], 2 * way))
            made.append(self.copy(near, self.source.at[3 - self.chip, columns], self.first.at[way, 1], 2 * way + 1))
        return made

    def two(self):
        return [self.copy(other, self.relay.at[way], self.second.at[way], 4 + way) for way, near, other in self.ways()]

    def start(self):
        for copy in self.one():
            copy.start()

    def middle(self):
        for copy in self.one():
            copy.wait()
        for way, near, other in self.ways():
            for at in range(2):
                total = self.source[other, 2 * way + at].astype(F32) + self.first[way, 1, at].astype(F32)
                self.relay[way, at] = total.astype(BF16)
        for copy in self.two():
            copy.start()

    def finish(self, target):
        for copy in self.two():
            copy.wait()
        for way in range(2):
            for at in range(2):
                total = self.source[self.chip, 2 * way + at].astype(F32) + self.first[way, 0, at].astype(F32)
                target[2 * way + at] = (total + self.second[way, at].astype(F32)).astype(BF16)


def chip_scratch(rows):
    return [pltpu.VMEM((2, 2, 2, rows, 128), BF16), pltpu.VMEM((2, 2, rows, 128), BF16), pltpu.VMEM((2, 2, rows, 128), BF16)]


class WeightSums:
    def __init__(self, normed_ref, across_ref, planes_ref, block_of, refs):
        self.normed, self.across, self.planes, self.block_of = normed_ref, across_ref, planes_ref, block_of
        (
            self.in_sum, self.in_got, self.rest_got, self.rest_sum, self.rest_chips, self.normed_t, self.result,
            self.keep, self.other, self.got, self.late_sum, self.late_got,
        ) = refs[:12]
        (
            self.send_in, self.recv_in, self.send_rest, self.recv_rest, self.send_chip, self.recv_chip,
            self.send_a, self.recv_a, self.send_c, self.recv_c,
        ) = refs[18:28]
        self.me, self.plane = lax.axis_index("seq"), lax.axis_index("dp")
        self.core, self.chip = lax.rem(self.me, 2), self.me // 2
        self.in_chips = ChipSums(across_ref, refs[12:15], refs[28:30], self.chip, self.core)
        self.late_chips = ChipSums(self.keep, refs[15:18], refs[30:32], self.chip, self.core)

    def to_plane(self, offset, source, target, send, recv):
        return pltpu.make_async_remote_copy(
            src_ref=source, dst_ref=target, send_sem=send.at[offset - 1], recv_sem=recv.at[offset - 1],
            device_id={"dp": lax.rem(self.plane + offset, 4)}, device_id_type=pl.DeviceIdType.MESH,
        )

    def rest_plane(self, offset):
        peer = lax.rem(self.plane + offset, 4)
        return self.to_plane(offset, self.planes.at[peer], self.rest_got.at[offset - 1], self.send_rest, self.recv_rest)

    def in_plane(self, offset):
        peer = lax.rem(self.plane + offset, 4)
        return self.to_plane(offset, self.in_sum.at[peer], self.in_got.at[offset - 1], self.send_in, self.recv_in)

    def late_plane(self, offset):
        peer = lax.rem(self.plane + offset, 4)
        return self.to_plane(offset, self.late_sum.at[peer], self.late_got.at[offset - 1], self.send_c, self.recv_c)

    def rest_chip(self, offset):
        other = lax.rem(self.chip + offset, 4)
        return pltpu.make_async_remote_copy(
            src_ref=self.rest_sum.at[other], dst_ref=self.rest_chips.at[offset - 1],
            send_sem=self.send_chip.at[offset - 1], recv_sem=self.recv_chip.at[offset - 1],
            device_id={"seq": 2 * other + self.core}, device_id_type=pl.DeviceIdType.MESH,
        )

    def late_core(self, column):
        return to_sibling(self.core, self.other.at[:, column], self.got.at[:, column], self.send_a.at[column], self.recv_a.at[column])

    def begin(self):
        self.in_chips.start()
        for offset in (1, 2, 3):
            self.rest_plane(offset).start()

    def late(self):
        sequences, count, model = self.normed.shape
        self.normed_t[...] = self.normed[...].reshape(sequences * count, model).T
        low = lax.broadcasted_iota(jnp.int32, (model, 128), 1) < 64
        for pair in range(PAIRS):
            rows = jnp.concatenate([self.block_of(one * PAIRS + pair) for one in range(sequences)], axis=0)
            sums = dot(self.normed_t[...], rows, NN)
            query, key, value = sums[:, 0:128], pltpu.roll(sums[:, 128:256], 64, 1), sums[:, 256:384]
            self.result[3 * pair] = jnp.where(low, query, key).astype(BF16)
            self.result[3 * pair + 1] = jnp.where(low, value, query).astype(BF16)
            self.result[3 * pair + 2] = jnp.where(low, key, value).astype(BF16)
        for tile in range(3 * PAIRS):
            within = tile % 9
            spots = [(2 * (tile // 9), within)] if within <= 4 else []
            spots += [(2 * (tile // 9) + 1, within - 4)] if within >= 4 else []
            for column, slot in spots:
                rows_at = slice(96 * slot, 96 * slot + 96)
                spread_rows(self.core, self.result.at[tile], slice(0, 128), self.keep, self.other, lambda chip: (chip, column, rows_at))
        for column in range(4):
            self.late_core(column).start()

    def late_one(self):
        for column in range(4):
            self.late_core(column).wait()
            for at in range(4):
                self.keep[at, column] = (self.keep[at, column].astype(F32) + self.got[at, column].astype(F32)).astype(BF16)
        self.late_chips.start()

    def in_two(self):
        self.in_chips.middle()

    def late_two(self):
        self.late_chips.middle()

    def rest_two(self):
        for offset in (1, 2, 3):
            self.rest_plane(offset).wait()
        for chip in range(4):
            total = self.planes[self.plane, chip].astype(F32)
            for slot in range(3):
                total = total + self.rest_got[slot, chip].astype(F32)
            self.rest_sum[chip] = total.astype(BF16)
        for offset in (1, 2, 3):
            self.rest_chip(offset).start()

    def in_three(self):
        self.in_chips.finish(self.in_sum)
        for offset in (1, 2, 3):
            self.in_plane(offset).start()

    def late_three(self):
        self.late_chips.finish(self.late_sum)
        for offset in (1, 2, 3):
            self.late_plane(offset).start()

    def joined(self, block, columns):
        odd = lax.rem(self.plane, 2) == 1
        count = block.shape[1]
        return jnp.where(odd, pltpu.roll(block, count - 64, 1), block)[:, :columns]

    def finish_rest(self, down_out):
        total = self.rest_sum[self.chip].astype(F32)
        for offset in (1, 2, 3):
            self.rest_chip(offset).wait()
            total = total + self.rest_chips[offset - 1].astype(F32)
        down_out[0:128, :] = total[0:192].T
        down_out[128:256, :] = total[192:384].T

    def finish_in(self, in_out, weight_out):
        total = self.in_sum[self.plane].astype(F32)
        for offset in (1, 2, 3):
            self.in_plane(offset).wait()
            total = total + self.in_got[offset - 1].astype(F32)
        for tile in range(8):
            in_out[:, 128 * tile : 128 * tile + 128] = total[96 * tile : 96 * tile + 96]
        weight_out[...] = self.joined(jnp.concatenate([total[768:864], total[864:960]], axis=1), 192)

    def finish_late(self, qkv_out):
        total = self.late_sum[self.plane].astype(F32)
        for offset in (1, 2, 3):
            self.late_plane(offset).wait()
            total = total + self.late_got[offset - 1].astype(F32)
        qkv_out[...] = self.joined(jnp.concatenate([total[96 * k : 96 * k + 96] for k in range(5)], axis=1), 576)


def weight_scratch(model, tokens):
    dma = pltpu.SemaphoreType.DMA
    late = (4, 4, LATE_ROWS, 128)
    return (
        [
            pltpu.VMEM((4, IN_ROWS, 128), BF16),
            pltpu.VMEM((3, IN_ROWS, 128), BF16),
            pltpu.VMEM((3, 4, REST_ROWS, 128), BF16),
            pltpu.VMEM((4, REST_ROWS, 128), BF16),
            pltpu.VMEM((3, REST_ROWS, 128), BF16),
            pltpu.VMEM((model, tokens), BF16),
            pltpu.VMEM((3 * PAIRS, model, 128), BF16),
            pltpu.VMEM(late, BF16),
            pltpu.VMEM(late, BF16),
            pltpu.VMEM(late, BF16),
            pltpu.VMEM((4, LATE_ROWS, 128), BF16),
            pltpu.VMEM((3, LATE_ROWS, 128), BF16),
        ]
        + chip_scratch(IN_ROWS)
        + chip_scratch(LATE_ROWS)
        + [dma((3,)), dma((3,)), dma((3,)), dma((3,)), dma((3,)), dma((3,)), dma((4,)), dma((4,)), dma((3,)), dma((3,))]
        + [dma((6,)), dma((6,)), dma((6,)), dma((6,))]
    )


SMALL_ROWS = 288


class SmallSums:
    def __init__(self, block, buffers, sems):
        self.block = block
        self.held, self.got_seq, self.planes, self.got_dp, self.whole = buffers
        self.sems = sems
        self.me, self.plane = lax.axis_index("seq"), lax.axis_index("dp")
        self.across, self.along = self.held.shape[0], self.held.shape[1]
        self.paired = self.across == 8
        self.core, self.chip = lax.rem(self.me, 2), self.me // 2
        self.mine = self.across // 2 * self.core + self.chip

    def places(self):
        half = self.held.shape[2] // 2
        units = SMALL_ROWS // half
        tiles = self.block.shape[1] // 128
        for at in range(2 * self.along * self.across):
            spot = (at // (2 * self.along), at // 2 % self.along, slice((at % 2) * half, (at % 2) * half + half))
            tile, unit = at // units, at % units
            if tile < tiles:
                yield spot, (slice(unit * half, unit * half + half), slice(128 * tile, 128 * tile + 128))
            else:
                yield spot, None

    def pack(self):
        for spot, source in self.places():
            if source is None:
                self.held[spot] = jnp.zeros((self.held.shape[2] // 2, 128), BF16)
            else:
                self.held[spot] = self.block[source].astype(BF16)

    def copies(self, axis, source, target, number):
        here, count = {"seq": (self.me, self.across), "chip": (self.chip, self.across // 2), "dp": (self.plane, self.along)}[axis]
        send, recv = self.sems[2 * number], self.sems[2 * number + 1]
        made = []
        for step in range(1, count):
            peer = lax.rem(here + step, count)
            device = {"seq": 2 * peer + self.core} if axis == "chip" else {axis: peer}
            made.append(
                pltpu.make_async_remote_copy(
                    src_ref=source(peer), dst_ref=target(step - 1), send_sem=send.at[step - 1], recv_sem=recv.at[step - 1],
                    device_id=device, device_id_type=pl.DeviceIdType.MESH,
                )
            )
        for copy in made:
            copy.start()
        return made

    def sibling(self, source, target, number):
        made = [to_sibling(self.core, source, target, self.sems[2 * number].at[6], self.sems[2 * number + 1].at[6])]
        made[0].start()
        return made

    def one_start(self):
        if self.paired:
            half = pl.ds(4 * (1 - self.core), 4)
            self.waiting = self.sibling(self.held.at[half], self.got_seq.at[pl.ds(3, 4)], 0)
            return
        self.waiting = self.copies("seq", lambda peer: self.held.at[peer], lambda slot: self.got_seq.at[slot], 0)

    def one_middle(self):
        if self.paired:
            for copy in self.waiting:
                copy.wait()
            for chip in range(4):
                at = 4 * self.core + chip
                self.held[at] = (self.held[at].astype(F32) + self.got_seq[3 + chip].astype(F32)).astype(BF16)
            self.waiting = self.copies("chip", lambda peer: self.held.at[4 * self.core + peer], lambda slot: self.got_seq.at[slot], 0)

    def one_finish(self):
        for copy in self.waiting:
            copy.wait()
        total = self.held[self.mine if self.paired else self.me].astype(F32)
        for slot in range(3 if self.paired else self.across - 1):
            total = total + self.got_seq[slot].astype(F32)
        self.planes[...] = total.astype(BF16)
        self.waiting = self.copies("dp", lambda peer: self.planes.at[peer], lambda slot: self.got_dp.at[slot], 1)

    def two_finish(self):
        for copy in self.waiting:
            copy.wait()
        mine = self.planes[self.plane].astype(F32)
        for slot in range(self.along - 1):
            mine = mine + self.got_dp[slot].astype(F32)
        own = self.mine if self.paired else self.me
        self.whole[own, self.plane] = mine.astype(BF16)
        self.waiting = self.copies("dp", lambda peer: self.whole.at[own, self.plane], lambda slot: self.whole.at[own, self.plane], 2)

    def three_finish(self):
        for copy in self.waiting:
            copy.wait()
        own = self.mine if self.paired else self.me
        self.waiting = self.copies("chip" if self.paired else "seq", lambda peer: self.whole.at[own], lambda slot: self.whole.at[own], 3)

    def three_more(self):
        if self.paired:
            for copy in self.waiting:
                copy.wait()
            half = pl.ds(4 * self.core, 4)
            self.waiting = self.sibling(self.whole.at[half], self.whole.at[half], 3)

    def four_finish(self):
        for copy in self.waiting:
            copy.wait()
        for spot, target in self.places():
            if target is not None:
                self.block[target] = self.whole[spot].astype(F32)


def small_scratch(across, along):
    chunk = max(16, 2048 // (across * along))
    dma = lambda count: pltpu.SemaphoreType.DMA((count,))
    return [
        pltpu.VMEM((across, along, chunk, 128), BF16),
        pltpu.VMEM((across - 1, along, chunk, 128), BF16),
        pltpu.VMEM((along, chunk, 128), BF16),
        pltpu.VMEM((along - 1, chunk, 128), BF16),
        pltpu.VMEM((across, along, chunk, 128), BF16),
        dma(across - 1), dma(across - 1), dma(along - 1), dma(along - 1),
        dma(along - 1), dma(along - 1), dma(across - 1), dma(across - 1),
    ]


def body(
    byte_ids,
    lengths,
    byte_table,
    conv_kernel,
    score_vector,
    norm_gain_one,
    qkv_weight,
    bias_table,
    out_weight,
    norm_gain_two,
    in_weight,
    down_weight,
    cotangent,
):
    devices = lax.axis_size("seq")
    me = lax.axis_index("seq")
    sequences, local_bytes = byte_ids.shape
    local_tokens = local_bytes // 2
    total_bytes = local_bytes * devices
    vocab, model = byte_table.shape
    total = sequences * PAIRS
    per_device = -(-total // devices)
    place = jnp.reshape(me, (1,)).astype(jnp.int32)
    vectors = jnp.concatenate([conv_kernel, norm_gain_one[None, :], norm_gain_two[None, :], score_vector[None, :]], axis=0)
    rows = jnp.dot(near_one_hot(), bias_table, precision="highest").T.reshape(PAIRS, 2, NEAR)

    def exchange(items):
        return lax.all_to_all(items, "seq", split_axis=0, concat_axis=0, tiled=True)

    hidden, normed, conv, mix, share, ids_rows, received = call_front(lengths, byte_ids, byte_table, qkv_weight, vectors, devices, per_device)
    out, aug, cot = attention_forward(received, rows, lengths, place, cotangent)
    layer, act, gate_up, normed_two, attended, branch, grad_residual, grad_items, grad_gain_two, grad_rest = call_mid(
        out, hidden, cot, out_weight, in_weight, down_weight, vectors
    )
    along_count = lax.axis_size("dp")
    custom = devices == 8 and along_count == 4

    def scatter(grad):
        rows_own = lax.psum_scatter(grad, "seq", scatter_dimension=0, tiled=True)
        return lax.psum_scatter(rows_own, "dp", scatter_dimension=1, tiled=True).astype(F32)

    if not custom:
        summed_down = scatter(jnp.einsum("bti,btd->id", act, cot, preferred_element_type=F32).astype(BF16))
        summed_in = scatter(jnp.einsum("btd,bti->di", normed_two, gate_up, preferred_element_type=F32).astype(BF16))
        summed_out = scatter(jnp.einsum("btd,bte->de", attended, branch, preferred_element_type=F32).astype(BF16))
    half = per_device // 2
    grads_two, grads_one, at_two = (grad_items, exchange(grad_rest), 0) if devices == 8 else (grad_items, grad_items, half)
    dqkv_two, bias_two, layer_out = attention_backward(
        received, out, aug, grads_two, rows, lengths, place, layer, grad_gain_two, half, per_device - half, at_two
    )
    items_two = exchange(dqkv_two)
    dqkv_one, bias_one, unused = attention_backward(received, out, aug, grads_one, rows, lengths, place, None, bias_two, 0, half, 0)
    items_one = exchange(dqkv_one)
    bias_rows = jnp.concatenate([bias_one, bias_two], axis=0)
    if custom:
        in_chips, rest_planes = call_early(act, cot, normed_two, gate_up, attended, branch, items_two)
    extra = (normed, in_chips, rest_planes) if custom else ()
    results = call_back(
        custom, items_one, items_two, hidden, grad_residual, conv, mix, share, ids_rows, qkv_weight, byte_table, vectors, bias_rows, grad_gain_two, along_count, extra
    )
    if custom:
        summed_qkv, summed_in, summed_down, summed_out, *smalls = call_finish(results[0], results[1:])
    else:
        smalls = call_finish(results[0], ())
        grad_qkv = jnp.einsum("btd,bte->de", normed, results[1], preferred_element_type=F32).astype(BF16)
        grad_qkv = jnp.swapaxes(grad_qkv.reshape(model, PAIRS, 3, 2, 64), 2, 3).reshape(model, PAIRS * 384)
        summed_qkv = scatter(grad_qkv)
    grad_table, grad_taps, grad_gain_one, grad_score, grad_gain_two, grad_bias = smalls
    return (
        layer_out,
        grad_table,
        grad_taps,
        grad_score,
        grad_gain_one,
        summed_qkv,
        grad_bias,
        summed_out,
        grad_gain_two,
        summed_in,
        summed_down,
    )


def solution(mesh):
    return jax.shard_map(
        body,
        mesh=mesh,
        in_specs=(
            P("dp", "seq"),
            P("dp"),
            P(),
            P(),
            P(),
            P(),
            P(),
            P(),
            P(),
            P(),
            P(),
            P(),
            P("dp", "seq", None),
        ),
        out_specs=(
            P("dp", "seq", None),
            P(),
            P(),
            P(),
            P(),
            P("seq", "dp"),
            P(),
            P("seq", "dp"),
            P(),
            P("seq", "dp"),
            P("seq", "dp"),
        ),
        check_vma=False,
    )
```

```python
import functools
import jax
import jax.numpy as jnp
from jax import lax
from jax.experimental import pallas as pl
from jax.experimental.pallas import tpu as pltpu
from jax.sharding import PartitionSpec as P

thresholds = (12, 16, 23, 32, 46, 64, 91)
KB = 256
NEAR = 1024
F32 = jnp.float32
BF16 = jnp.bfloat16
NT = (((1,), (1,)), ((), ()))
NN = (((1,), (0,)), ((), ()))


def rel_bucket(relative):
    distance = jnp.abs(relative)
    larger = 8 + sum(((distance >= boundary).astype(jnp.int32) for boundary in thresholds))
    bucket = jnp.where(distance < 8, distance, larger)
    return bucket + 16 * (relative > 0).astype(jnp.int32)


def near_one_hot():
    place = jnp.arange(NEAR, dtype=jnp.int32)
    relative = jnp.where(place < NEAR - 128, KB - place, KB + NEAR - place)
    return (rel_bucket(relative)[:, None] == jnp.arange(32, dtype=jnp.int32)[None, :]).astype(F32)


def dot(a, b, dims):
    return lax.dot_general(a, b, dims, preferred_element_type=F32)


STRIP = 5 * KB


def strip_at(block, part):
    return pl.ds(pl.multiple_of((jnp.clip(part - block, -2, 2) + 2) * KB, KB), KB)


def fill_bias(strip, head, row):
    spread = jnp.broadcast_to(row, (128, NEAR))
    rolled = pltpu.roll(spread, 0, 1, stride=1, stride_axis=0)
    far_right = jnp.broadcast_to(row[:, NEAR - 1 :], (KB, 128))
    far_left = jnp.broadcast_to(row[:, 768:769], (KB, 128))
    for start in range(0, KB, 128):
        strip[head, :, start : start + 128] = far_right
        strip[head, :, KB + 768 + start : KB + 896 + start] = far_left
    strip[head, 0:128, KB : KB + 768] = rolled[:, :768]
    strip[head, 128:256, KB : KB + 128] = far_right[:128]
    strip[head, 128:256, KB + 128 : KB + 768] = rolled[:, :640]


def lanes_of(head, shape):
    lane = lax.broadcasted_iota(jnp.int32, shape, 1)
    own = (lane < 64) if head == 0 else (lane >= 64)
    return own, lane - (64 if head == 0 else 0)


def fill_keys(ka, head, keys, valid):
    own, spare = lanes_of(head, keys.shape)
    row = lax.broadcasted_iota(jnp.int32, keys.shape, 0)
    masked = jnp.where(row < valid, 0.0, -1e9)
    extra = jnp.where(spare == 0, masked, jnp.where((spare >= 1) & (spare <= 3), 1.0, 0.0))
    ka[head] = jnp.where(own, keys, extra.astype(BF16))


def item_length(lengths_ref, item):
    length = jnp.int32(0)
    for number, rank in enumerate(ranks_of(lengths_ref)):
        length = jnp.where(rank == item // 6, lengths_ref[number], length)
    return (length + 1) // 2


def move_rows(item, lengths_ref, source, buffer, target, sems, sorting):
    def inward(number):
        return pltpu.make_async_copy(source.at[number if sorting else ranks[number]], buffer.at[number], sems.at[0, number])

    def outward(number):
        return pltpu.make_async_copy(buffer.at[number], target.at[ranks[number] if sorting else number], sems.at[1, number])

    count = source.shape[0]
    ranks = ranks_of(lengths_ref)

    @pl.when(item == 0)
    def _():
        for number in range(count):
            inward(number).start()

    @pl.when(item == jnp.minimum(1, pl.num_programs(0) - 1))
    def _():
        for number in range(count):
            inward(number).wait()
            outward(number).start()

    def finish():
        @pl.when(item == pl.num_programs(0) - 1)
        def _():
            for number in range(count):
                outward(number).wait()

    return finish


def fwd_kernel(
    blocks, lengths_ref, place_ref, qkv_ref, row_ref, cot_ref, out_ref, aug_ref, sorted_ref,
    qa, ka, vt, strip, peak, acc, probs, moving, sems,
):
    item = pl.program_id(0)
    finish = move_rows(item, lengths_ref, cot_ref, moving, sorted_ref, sems, True)
    valid = item_length(lengths_ref, place_ref[0] + qkv_ref.shape[0] * item)
    tokens = blocks * KB
    joined = qkv_ref[:, 0].reshape(tokens, 384)
    queries = joined[:, 0:128]
    keys = joined[:, 128:256]
    turned = joined[:, 256:384].T
    filler = jnp.where(lax.broadcasted_iota(jnp.int32, (16, tokens), 0) == 0, 1.0, 0.0).astype(BF16)
    for head in range(2):
        own, spare = lanes_of(head, queries.shape)
        qa[head] = jnp.where(own, queries, jnp.where(spare == 0, 1.0, 0.0).astype(BF16))
        fill_keys(ka, head, keys, valid)
        vt[head, 0:64] = turned[64 * head : 64 * head + 64]
        vt[head, 64:80] = filler
        fill_bias(strip, head, row_ref[0, head : head + 1, :])
    peak[...] = jnp.full_like(peak, -1e30)
    acc[...] = jnp.zeros_like(acc)

    def step(block, unused):
        first = pl.multiple_of(block * KB, KB)
        alphas = [[], []]
        for part in range(blocks):
            for head in range(2):
                here = slice(part * KB, part * KB + KB)
                logits = dot(ka[head, pl.ds(first, KB), :], qa[head, here, :], NT)
                logits = logits + strip[head, :, strip_at(block, part)]
                before = peak[head, :, here]
                after = jnp.maximum(before, jnp.max(logits, axis=0, keepdims=True))
                probs[head, :, here] = jnp.exp(logits - after).astype(BF16)
                peak[head, :, here] = after
                alphas[head].append(jnp.exp(before - after))
        for head in range(2):
            acc[head] = acc[head] * jnp.concatenate(alphas[head], axis=1) + dot(vt[head, :, pl.ds(first, KB)], probs[head], NN)
        return unused

    lax.fori_loop(0, (valid + KB - 1) // KB, step, 0)
    outs = []
    rows = []
    place = lax.broadcasted_iota(jnp.int32, (64, tokens), 0)
    for head in range(2):
        total = acc[head, 64:65, :]
        outs.append(acc[head, 0:64, :] / total)
        minus = -(peak[head] + jnp.log(total))
        high = minus.astype(BF16).astype(F32)
        rest = minus - high
        middle = rest.astype(BF16).astype(F32)
        low = rest - middle
        rows.append(jnp.where(place == 0, 1.0, jnp.where(place == 1, high, jnp.where(place == 2, middle, jnp.where(place == 3, low, 0.0)))))
    out_ref[:, 0] = jnp.concatenate(outs, axis=0).T.astype(BF16).reshape(out_ref.shape[0], out_ref.shape[2], 128)
    aug_ref[0] = jnp.concatenate([rows[1], rows[0]], axis=0).T.astype(BF16)
    finish()


def bwd_kernel(
    blocks, base_slot, moves, lengths_ref, place_ref, qkv_ref, out_ref, aug_ref, grad_ref, row_ref, layer_ref, after,
    dqkv_ref, bias_ref, moved_ref, qa, ka, va, ga, kt, strip, tally, probs, slopes, dq, *moving,
):
    item = pl.program_id(0)
    finish = move_rows(item, lengths_ref, layer_ref, moving[0], moved_ref, moving[1], False) if moves else lambda: None
    valid = item_length(lengths_ref, place_ref[0] + qkv_ref.shape[0] * (item + base_slot))
    tokens = blocks * KB
    local = qkv_ref.shape[2]
    joined = qkv_ref[:, 0].reshape(tokens, 384)
    queries = joined[:, 0:128]
    keys = joined[:, 128:256]
    values = joined[:, 256:384]
    grads = grad_ref[:, 0].reshape(tokens, 128)
    outs = out_ref[:, 0].reshape(tokens, 128)
    kt[...] = keys.T
    product = grads.astype(F32) * outs.astype(F32)
    high = product.astype(BF16)
    low = (product - high.astype(F32)).astype(BF16)
    row_at = lax.broadcasted_iota(jnp.int32, (128, 128), 0)
    lane_at = lax.broadcasted_iota(jnp.int32, (128, 128), 1)
    pick = jnp.where((row_at < 64) == (lane_at >= 64), -1.0, 0.0).astype(BF16)
    shifts = dot(high, pick, NN) + dot(low, pick, NN)
    shift_high = shifts.astype(BF16)
    shift_low = (shifts - shift_high.astype(F32)).astype(BF16)
    for head in range(2):
        own, spare = lanes_of(head, queries.shape)
        qa[head] = jnp.where(own, queries, aug_ref[0])
        fill_keys(ka, head, keys, valid)
        va[head] = jnp.where(own, values, jnp.where((spare == 0) | (spare == 1), 1.0, 0.0).astype(BF16))
        ga[head] = jnp.where(own, grads, jnp.where(spare == 0, shift_high, jnp.where(spare == 1, shift_low, jnp.zeros_like(shift_low))))
        fill_bias(strip, head, row_ref[0, head : head + 1, :])
    tally[...] = jnp.zeros_like(tally)
    dq[...] = jnp.zeros_like(dq)
    dqkv_ref[...] = jnp.zeros_like(dqkv_ref)

    def step(block, unused):
        first = pl.multiple_of(block * KB, KB)
        key_parts = []
        value_parts = []
        for part in range(blocks):
            for head in range(2):
                here = slice(part * KB, part * KB + KB)
                there = strip_at(block, part)
                logits = dot(ka[head, pl.ds(first, KB), :], qa[head, here, :], NT)
                weights = jnp.exp(logits + strip[head, :, there])
                change = dot(va[head, pl.ds(first, KB), :], ga[head, here, :], NT)
                slope = weights * change
                tally[head, :, there] += slope
                probs[head, :, here] = weights.astype(BF16)
                slopes[head, :, here] = slope.astype(BF16)
        for head in range(2):
            value_parts.append(dot(probs[head], ga[head], NN))
            key_parts.append(dot(slopes[head], qa[head], NN))
            dq[pl.ds(64 * head, 64), :] += dot(kt[pl.ds(64 * head, 64), pl.ds(first, KB)], slopes[head], NN)
        own, unused_spare = lanes_of(0, (KB, 128))
        count = KB // local
        where = pl.ds(block * count, count)
        dqkv_ref[where, 0, :, 128:256] = jnp.where(own, key_parts[0], key_parts[1]).astype(BF16).reshape(count, local, 128)
        dqkv_ref[where, 0, :, 256:384] = jnp.where(own, value_parts[0], value_parts[1]).astype(BF16).reshape(count, local, 128)
        return unused

    lax.fori_loop(0, (valid + KB - 1) // KB, step, 0)
    dqkv_ref[:, 0, :, 0:128] = dq[...].T.astype(BF16).reshape(dqkv_ref.shape[0], local, 128)
    lane = lax.broadcasted_iota(jnp.int32, (1, NEAR), 1)
    flip = jnp.where(row_at + lane_at == 127, 1.0, 0.0).astype(BF16)
    for head in range(2):
        far_right = tally[head, :, 0:128] + tally[head, :, 128:256]
        far_right = far_right[:128] + far_right[128:] + tally[head, 128:256, KB : KB + 128]
        far_left = tally[head, :, KB + 768 : KB + 896] + tally[head, :, KB + 896 : STRIP]
        near = tally[head, 0:128, KB : KB + 768]
        near_low = tally[head, 128:256, KB + 128 : KB + 768]
        near = near + jnp.concatenate([near_low, jnp.zeros((128, 128), F32)], axis=1)
        near = jnp.concatenate([near, jnp.zeros((128, NEAR - 768), F32)], axis=1)
        near_high = near.astype(BF16)
        flipped = dot(flip, near_high, NN) + dot(flip, (near - near_high.astype(F32)).astype(BF16), NN)
        rolled = pltpu.roll(flipped, NEAR - 127, 1, stride=1, stride_axis=0)
        row = jnp.sum(rolled, axis=0, keepdims=True)
        row = row + jnp.where(lane == NEAR - 1, jnp.sum(far_right), 0.0) + jnp.where(lane == 768, jnp.sum(far_left), 0.0)
        bias_ref[0, head : head + 1, :] = row
    finish()


def attention_forward(qkv, rows, lengths, place, cot):
    sources, items, local, unused = qkv.shape
    blocks = sources * local // KB
    tokens = sources * local
    spec = pltpu.PrefetchScalarGridSpec(
        num_scalar_prefetch=2,
        grid=(items,),
        in_specs=[
            pl.BlockSpec((sources, 1, local, 384), lambda i, l, p: (0, i, 0, 0)),
            pl.BlockSpec((1, 2, NEAR), lambda i, l, p: (lax.rem(p[0] + sources * i, 6), 0, 0)),
            pl.BlockSpec(memory_space=pl.ANY),
        ],
        out_specs=[
            pl.BlockSpec((sources, 1, local, 128), lambda i, l, p: (0, i, 0, 0)),
            pl.BlockSpec((1, tokens, 128), lambda i, l, p: (i, 0, 0)),
            pl.BlockSpec(memory_space=pl.ANY),
        ],
        scratch_shapes=[
            pltpu.VMEM((2, tokens, 128), BF16),
            pltpu.VMEM((2, tokens, 128), BF16),
            pltpu.VMEM((2, 80, tokens), BF16),
            pltpu.VMEM((2, KB, STRIP), F32),
            pltpu.VMEM((2, 1, tokens), F32),
            pltpu.VMEM((2, 80, tokens), F32),
            pltpu.VMEM((2, KB, tokens), BF16),
            pltpu.VMEM(cot.shape, cot.dtype),
            pltpu.SemaphoreType.DMA((2,) + cot.shape[:1]),
        ],
    )
    return pl.pallas_call(
        functools.partial(fwd_kernel, blocks),
        grid_spec=spec,
        out_shape=[
            jax.ShapeDtypeStruct((sources, items, local, 128), BF16),
            jax.ShapeDtypeStruct((items, tokens, 128), BF16),
            jax.ShapeDtypeStruct(cot.shape, cot.dtype),
        ],
        compiler_params=pltpu.CompilerParams(vmem_limit_bytes=60 * 2**20),
        cost_estimate=pl.CostEstimate(flops=items * tokens * tokens * 512, bytes_accessed=items * tokens * 2048, transcendentals=items * tokens * tokens * 2),
        name="attention_forward",
    )(lengths, place, qkv, rows, cot)


def attention_backward(qkv, outs, aug, grads, rows, lengths, place, layer, after, first, items, grads_at):
    sources, unused, local, unused = qkv.shape
    moves = layer is not None
    layer = after if layer is None else layer
    moved = layer if moves else jnp.zeros((8, 128), F32)
    blocks = sources * local // KB
    tokens = sources * local
    big = lambda lanes: pl.BlockSpec((sources, 1, local, lanes), lambda i, l, p: (0, i + first, 0, 0))
    spec = pltpu.PrefetchScalarGridSpec(
        num_scalar_prefetch=2,
        grid=(items,),
        in_specs=[
            big(384),
            big(128),
            pl.BlockSpec((1, tokens, 128), lambda i, l, p: (i + first, 0, 0)),
            pl.BlockSpec((sources, 1, local, 128), lambda i, l, p: (0, i + grads_at, 0, 0)),
            pl.BlockSpec((1, 2, NEAR), lambda i, l, p: (lax.rem(p[0] + sources * (i + first), 6), 0, 0)),
            pl.BlockSpec(memory_space=pl.ANY),
            pl.BlockSpec(memory_space=pl.ANY),
        ],
        out_specs=[
            pl.BlockSpec((sources, 1, local, 384), lambda i, l, p: (0, i, 0, 0)),
            pl.BlockSpec((1, 2, NEAR), lambda i, l, p: (i, 0, 0)),
            pl.BlockSpec(memory_space=pl.ANY),
        ],
        scratch_shapes=[
            pltpu.VMEM((2, tokens, 128), BF16),
            pltpu.VMEM((2, tokens, 128), BF16),
            pltpu.VMEM((2, tokens, 128), BF16),
            pltpu.VMEM((2, tokens, 128), BF16),
            pltpu.VMEM((128, tokens), BF16),
            pltpu.VMEM((2, KB, STRIP), F32),
            pltpu.VMEM((2, KB, STRIP), F32),
            pltpu.VMEM((2, KB, tokens), BF16),
            pltpu.VMEM((2, KB, tokens), BF16),
            pltpu.VMEM((128, tokens), F32),
        ]
        + ([pltpu.VMEM(layer.shape, layer.dtype), pltpu.SemaphoreType.DMA((2,) + layer.shape[:1])] if moves else []),
    )
    return pl.pallas_call(
        functools.partial(bwd_kernel, blocks, first, moves),
        grid_spec=spec,
        out_shape=[
            jax.ShapeDtypeStruct((sources, items, local, 384), BF16),
            jax.ShapeDtypeStruct((items, 2, NEAR), F32),
            jax.ShapeDtypeStruct(moved.shape, moved.dtype),
        ],
        compiler_params=pltpu.CompilerParams(vmem_limit_bytes=60 * 2**20),
        cost_estimate=pl.CostEstimate(flops=items * tokens * tokens * 1280, bytes_accessed=items * tokens * 4096, transcendentals=items * tokens * tokens * 2),
        name="attention_backward",
    )(lengths, place, qkv, outs, aug, grads, rows, layer, after)


VPAD = 384
PAIRS = 6
TN = (((0,), (0,)), ((), ()))
SQRT_2_OVER_PI = 0.7978845608028654


def block_masks(masks, first_byte, total_bytes):
    shape = masks.shape[2:]
    conv_at = first_byte - 2 + lax.broadcasted_iota(jnp.int32, shape, 1)
    token = lax.broadcasted_iota(jnp.int32, shape, 0)
    for side in range(2):
        place = first_byte + 2 * token + side
        for size in range(1, 5):
            start = (place // size) * size
            inside = (conv_at >= start) & (conv_at < start + size) & (conv_at < total_bytes)
            masks[side, size - 1] = jnp.where(inside, 1.0 / size, 0.0)


def split_two(values):
    high = values.astype(BF16)
    return high, (values - high.astype(F32)).astype(BF16)


def permute_weight(weight, out):
    rows = weight.shape[0]
    low = lax.broadcasted_iota(jnp.int32, (rows, 128), 1) < 64
    for pair in range(PAIRS):
        at = pair * 384
        one, two, three = (weight[:, at + 128 * k : at + 128 * k + 128] for k in range(3))
        out[:, at : at + 128] = jnp.where(low, one, two)
        out[:, at + 128 : at + 256] = pltpu.roll(jnp.where(low, three, one).astype(F32), 64, 1).astype(BF16)
        out[:, at + 256 : at + 384] = jnp.where(low, two, three)


def greet(axis, here, count):
    barrier = pltpu.get_barrier_semaphore()

    def signal(step, unused):
        pl.semaphore_signal(barrier, inc=1, device_id={axis: lax.rem(here + step, count)}, device_id_type=pl.DeviceIdType.MESH)
        return unused

    lax.fori_loop(1, count, signal, 0)


def item_copy(devices, me, source, target, other, slot, sems):
    send, recv, unused = sems

    def outward():
        offset = lax.rem(other - me + devices, devices)
        return pltpu.make_async_remote_copy(
            src_ref=source, dst_ref=target, send_sem=send.at[offset, slot], recv_sem=recv.at[offset, slot],
            device_id={"seq": other}, device_id_type=pl.DeviceIdType.MESH,
        )

    def inward():
        offset = lax.rem(me - other + devices, devices)
        return pltpu.make_async_remote_copy(
            src_ref=source, dst_ref=target, send_sem=send.at[offset, slot], recv_sem=recv.at[offset, slot],
            device_id={"seq": other}, device_id_type=pl.DeviceIdType.MESH,
        )

    return outward, inward


def start_item(devices, me, source, target, other, slot, sems):
    @pl.when(other == me)
    def _():
        pltpu.make_async_copy(source, target, sems[2].at[slot]).start()

    @pl.when(other != me)
    def _():
        item_copy(devices, me, source, target, other, slot, sems)[0]().start()


def finish_sends(devices, me, total, source_of, target_of, sems):
    def wait(item, unused):
        other, slot = lax.rem(item, devices), item // devices

        @pl.when(other != me)
        def _():
            item_copy(devices, me, source_of(other, slot), target_of(other, slot), other, slot, sems)[0]().wait_send()

        return unused

    lax.fori_loop(0, total, wait, 0)


def finish_receives(devices, me, total, source_of, target_of, sems):
    per_device = -(-total // devices)

    def wait(at, unused):
        other, slot = at // per_device, lax.rem(at, per_device)

        @pl.when((slot * devices + me < total) & (other != me))
        def _():
            item_copy(devices, me, source_of(other, slot), target_of(other, slot), other, slot, sems)[1]().wait_recv()

        @pl.when((slot * devices + me < total) & (other == me))
        def _():
            pltpu.make_async_copy(source_of(other, slot), target_of(other, slot), sems[2].at[slot]).wait()

        return unused

    lax.fori_loop(0, devices * per_device, wait, 0)


def ranks_of(lengths_ref):
    count = lengths_ref.shape[0]
    ranks = []
    for one in range(count):
        rank = jnp.int32(0)
        for two in range(count):
            if two != one:
                ahead = lengths_ref[two] > lengths_ref[one] if two > one else lengths_ref[two] >= lengths_ref[one]
                rank = rank + ahead.astype(jnp.int32)
        ranks.append(rank)
    return ranks


def spread_ids(lengths_ref, ids_ref, from_left, from_right, extended, sems, me, devices):
    sequences, local_bytes = ids_ref.shape
    left_copy = pltpu.make_async_remote_copy(
        src_ref=ids_ref.at[:, 0:128], dst_ref=from_right, send_sem=sems.at[0], recv_sem=sems.at[1],
        device_id={"seq": jnp.maximum(me - 1, 0)}, device_id_type=pl.DeviceIdType.MESH,
    )
    right_copy = pltpu.make_async_remote_copy(
        src_ref=ids_ref.at[:, local_bytes - 128 : local_bytes], dst_ref=from_left, send_sem=sems.at[2], recv_sem=sems.at[3],
        device_id={"seq": jnp.minimum(me + 1, devices - 1)}, device_id_type=pl.DeviceIdType.MESH,
    )

    @pl.when(me > 0)
    def _():
        left_copy.start()

    @pl.when(me < devices - 1)
    def _():
        right_copy.start()

    @pl.when(me > 0)
    def _():
        left_copy.wait_send()
        right_copy.wait_recv()

    @pl.when(me < devices - 1)
    def _():
        right_copy.wait_send()
        left_copy.wait_recv()

    joined = jnp.concatenate([from_left[...], ids_ref[...], from_right[...]], axis=1).astype(F32)
    width = joined.shape[1]
    moved = pltpu.roll(joined, width - 124, 1)
    row = lax.broadcasted_iota(jnp.int32, (sequences, width), 0)
    lane = lax.broadcasted_iota(jnp.int32, (sequences, width), 1)
    position = me * local_bytes - 4 + lane
    length = jnp.zeros((sequences, width), jnp.int32)
    for one in range(sequences):
        length = jnp.where(row == one, lengths_ref[one], length)
    outside = (position < 0) | (position >= local_bytes * devices) | (lane >= local_bytes + 8)
    picked = jnp.where(outside, -1.0, jnp.where(position < length, moved, 0.0))
    ordered = jnp.zeros((sequences, width), F32)
    for one, rank in enumerate(ranks_of(lengths_ref)):
        ordered = jnp.where(row == rank, picked[one : one + 1, :], ordered)
    extended[...] = ordered


def front_kernel(
    sizes, lengths_ref, ids_ref, table_ref, weight_ref, vectors_ref,
    hidden_ref, normed_ref, conv_ref, mix_ref, share_ref, rows_ref, items_ref,
    masks, wide, permuted, stage, taps, from_left, from_right, extended, side_sems, *sems,
):
    local_tokens, window, devices, total = sizes
    step = pl.program_id(0)
    me = lax.axis_index("seq")

    @pl.when(step == 0)
    def _():
        from_left[...] = jnp.zeros_like(from_left)
        from_right[...] = jnp.zeros_like(from_right)
        greet("seq", me, devices)
        block_masks(masks, me * 2 * local_tokens, devices * 2 * local_tokens)
        permute_weight(weight_ref, permuted)
        table = table_ref[...].astype(F32)
        taps[...] = jnp.zeros_like(taps)
        for tap in range(5):
            taps[tap, 0 : table.shape[0], :] = (vectors_ref[tap : tap + 1, :] * table).astype(BF16)
        pl.semaphore_wait(pltpu.get_barrier_semaphore(), devices - 1)
        spread_ids(lengths_ref, ids_ref, from_left, from_right, extended, side_sems, me, devices)

    together = 1
    width_ids = extended.shape[1]
    row = jnp.broadcast_to(extended[pl.ds(step, 1), :], (8, width_ids))
    rows = pltpu.roll(pltpu.roll(row, width_ids - 4, 1), 0, 1, stride=1, stride_axis=0)
    rows_ref[0] = rows
    ids = rows.T[0:window]
    score = vectors_ref[7:8, :]
    gain = vectors_ref[5:6, :]
    model = score.shape[1]
    score_high, score_low = split_two(score)
    row16 = lax.broadcasted_iota(jnp.int32, (16, model), 0)
    score_rows = jnp.where(row16 == 0, score_high.astype(F32), jnp.where(row16 == 1, score_low.astype(F32), 0.0)).astype(BF16)
    lane = lax.broadcasted_iota(jnp.int32, (together * window, VPAD), 1).astype(F32)
    width = masks.shape[3]
    conv_all = jnp.zeros((together * window, model), F32)
    for tap in range(5):
        hot = jnp.where(ids[:, 4 - tap : 5 - tap] == lane, 1.0, 0.0).astype(BF16)
        conv_all = conv_all + dot(hot, taps[tap], NN)
    for one in range(together):
        high, low = split_two(conv_all[one * window : (one + 1) * window])
        conv_ref[one, 0:window] = high
        wide[one, 0, 0:window] = high
        wide[one, 1, 0:window] = low
        if width > window:
            wide[one, :, window:width] = jnp.zeros((2, width - window, model), BF16)
            conv_ref[one, window:width] = jnp.zeros((width - window, model), BF16)
        high = wide[one, 0]
        low = wide[one, 1]
        along = jnp.sum(dot(score_rows, high, NT), axis=0, keepdims=True) + dot(score_rows, low, NT)[0:1]
        mixed = jnp.zeros((local_tokens, width), F32)
        kept = jnp.zeros((local_tokens, 128), F32)
        lane128 = lax.broadcasted_iota(jnp.int32, (local_tokens, 128), 1)
        for side in range(2):
            scores = [jnp.sum(masks[side, k] * along, axis=1, keepdims=True) for k in range(4)]
            top = jnp.maximum(jnp.maximum(scores[0], scores[1]), jnp.maximum(scores[2], scores[3]))
            powers = [jnp.exp(value - top) for value in scores]
            under = 1.0 / (powers[0] + powers[1] + powers[2] + powers[3])
            for k in range(4):
                share = powers[k] * under
                mixed = mixed + share * masks[side, k]
                kept = jnp.where(lane128 == 4 * side + k, share, kept)
        share_ref[one] = kept
        mix_high, mix_low = split_two(mixed * 0.5)
        mix_ref[one] = mix_high
        hidden = dot(mix_high, high, NN) + dot(mix_high, low, NN) + dot(mix_low, high, NN)
        hidden_ref[one] = hidden
        scale = lax.rsqrt(jnp.mean(hidden * hidden, axis=1, keepdims=True) + 1e-06)
        normed_ref[one] = (hidden * scale * gain).astype(BF16)
    normed = normed_ref[...].reshape(together * local_tokens, model)
    for pair in range(PAIRS):
        piece = dot(normed, permuted[:, pair * 384 : pair * 384 + 384], NN).astype(BF16)
        for one in range(together):
            item = (step * together + one) * PAIRS + pair
            other, slot = lax.rem(item, devices), item // devices
            stage[other, slot] = piece[one * local_tokens : (one + 1) * local_tokens]

    if devices == 8:

        def send(at, unused):
            item = step * PAIRS + at
            other, slot = lax.rem(item, 8), item // 8

            @pl.when(other != me)
            def _():
                to_device(other, stage.at[other, slot], items_ref.at[me, slot], sems[0].at[0], sems[1].at[0]).start()

            return unused

        lax.fori_loop(0, PAIRS, send, 0)

        @pl.when(step == pl.num_programs(0) - 1)
        def _():
            finish_back(me, stage, items_ref, sems)

        return
    send_items(devices, me, step * together * PAIRS, together * PAIRS, stage, items_ref, sems)

    @pl.when(step == pl.num_programs(0) - 1)
    def _():
        finish_sends(devices, me, total, lambda other, slot: stage.at[other, slot], lambda other, slot: items_ref.at[me, slot], sems)
        finish_receives(devices, me, total, lambda other, slot: stage.at[other, slot], lambda other, slot: items_ref.at[other, slot], sems)


def to_device(other, source, target, send, recv):
    return pltpu.make_async_remote_copy(
        src_ref=source, dst_ref=target, send_sem=send, recv_sem=recv, device_id={"seq": other}, device_id_type=pl.DeviceIdType.MESH
    )


SLOT_GROUPS = ((0, 2), (2, 1), (3, 2), (5, 1))


def send_slots(me, number, source, arrived, sems):
    first, count = SLOT_GROUPS[number]
    slots = pl.ds(first, count)

    def send(offset, unused):
        other = lax.rem(me + offset, 8)
        to_device(other, source.at[other, slots], arrived.at[me, slots], sems[0].at[number], sems[1].at[number]).start()
        return unused

    lax.fori_loop(1, 8, send, 0)
    pltpu.make_async_copy(source.at[me, slots], arrived.at[me, slots], sems[2].at[number]).start()


def wait_slots(me, number, source, arrived, sems, sends):
    first, count = SLOT_GROUPS[number]
    slots = pl.ds(first, count)
    seven = pl.ds(0, 7)
    copies = to_device(lax.rem(me + 1, 8), source.at[seven, slots], arrived.at[seven, slots], sems[0].at[number], sems[1].at[number])
    if sends:
        copies.wait_send()
    else:
        copies.wait_recv()
        pltpu.make_async_copy(source.at[me, slots], arrived.at[me, slots], sems[2].at[number]).wait()


def send_back(me, step, stage, target, sems):
    base, base_to = 3, 0
    for parity in range(2):

        def send(offset, unused):
            other = lax.rem(me + offset, 8)

            @pl.when(other < 4)
            def _():
                first, count = (0, 2) if parity == 0 else (2, 1)
                to_device(other, stage.at[other, pl.ds(base + first, count)], target.at[me, pl.ds(base_to + first, count)], sems[0].at[0], sems[1].at[0]).start()

            @pl.when(other >= 4)
            def _():
                first, count = (0, 1) if parity == 0 else (1, 2)
                to_device(other, stage.at[other, pl.ds(base + first, count)], target.at[me, pl.ds(base_to + first, count)], sems[0].at[0], sems[1].at[0]).start()

            return unused

        @pl.when(lax.rem(step, 2) == parity)
        def _():
            lax.fori_loop(1, 8, send, 0)


def finish_half(me, stage, target, sems):
    slots = pl.ds(3, 3)
    local = pltpu.make_async_copy(stage.at[me, slots], target.at[me], sems[2].at[0])
    local.start()
    seven = pl.ds(0, 7)
    copies = to_device(lax.rem(me + 1, 8), stage.at[seven, slots], target.at[seven], sems[0].at[0], sems[1].at[0])
    copies.wait_send()
    copies.wait_recv()
    local.wait()


def finish_back(me, stage, target, sems):
    local = pltpu.make_async_copy(stage.at[me], target.at[me], sems[2].at[0])
    local.start()
    seven = pl.ds(0, 7)
    copies = to_device(lax.rem(me + 1, 8), stage.at[seven], target.at[seven], sems[0].at[0], sems[1].at[0])
    copies.wait_send()
    copies.wait_recv()
    local.wait()


def send_group(devices, me, total, group, number, source, arrived, sems):
    for slot in range(-(-total // devices)):
        item = slot * devices + me

        @pl.when((item < total) & (item // group == number))
        def _():
            def send(offset, unused):
                other = lax.rem(me + offset, devices)
                start_item(devices, me, source.at[other, slot], arrived.at[me, slot], other, slot, sems)
                return unused

            lax.fori_loop(0, devices, send, 0)


def send_items(devices, me, first, count, stage, target, sems):
    def send(at, unused):
        item = first + at
        other, slot = lax.rem(item, devices), item // devices
        start_item(devices, me, stage.at[other, slot], target.at[me, slot], other, slot, sems)
        return unused

    lax.fori_loop(0, count, send, 0)


def take_items(devices, me, first, count, source, arrived, sems):
    def take(at, unused):
        item = first + at
        take_item(devices, me, lax.rem(item, devices), item // devices, source, arrived, sems)
        return unused

    lax.fori_loop(0, count, take, 0)


def finish_groups(devices, me, total, source, arrived, sems):
    per_device = -(-total // devices)

    def wait(at, unused):
        slot, offset = at // devices, lax.rem(at, devices)
        other = lax.rem(me + offset, devices)

        @pl.when((slot * devices + me < total) & (offset != 0))
        def _():
            item_copy(devices, me, source.at[other, slot], arrived.at[me, slot], other, slot, sems)[0]().wait_send()

        return unused

    lax.fori_loop(0, devices * per_device, wait, 0)


def take_item(devices, me, other, slot, source, arrived, sems):
    @pl.when(other == me)
    def _():
        pltpu.make_async_copy(source.at[me, slot], arrived.at[me, slot], sems[2].at[slot]).wait()

    @pl.when(other != me)
    def _():
        item_copy(devices, me, source.at[other, slot], arrived.at[other, slot], other, slot, sems)[1]().wait_recv()


def mid_kernel(
    sizes, att_ref, hidden_ref, cot_ref, out_weight_ref, in_weight_ref, down_ref, vectors_ref,
    layer_ref, act_ref, gate_up_ref, normed_ref, attended_ref, branch_ref, residual_ref, items_ref, gain_out, rest_ref,
    arrived, stage, keep_gain, grad_act, *sems,
):
    local_tokens, devices, total = sizes
    in_sems, out_sems = sems[:3], sems[3:]
    step = pl.program_id(0)
    me = lax.axis_index("seq")

    @pl.when(step == 0)
    def _():
        greet("seq", me, devices)
        keep_gain[...] = jnp.zeros_like(keep_gain)
        pl.semaphore_wait(pltpu.get_barrier_semaphore(), devices - 1)

    together = hidden_ref.shape[0]
    group = together * PAIRS
    turn = lax.rem(step + 2, 4) if devices == 8 else step
    rows = together * local_tokens
    model = vectors_ref.shape[1]

    here_rows = pl.ds(pl.multiple_of(turn * rows, 128), rows)

    @pl.when(step == 0)
    def _():
        if devices == 8:
            for number in (2, 3, 0, 1):
                send_slots(me, number, att_ref, arrived, in_sems)
        else:
            send_group(devices, me, total, group, 0, att_ref, arrived, in_sems)
        every = cot_ref[...].reshape(grad_act.shape[0], model)
        for first in range(0, down_ref.shape[0], 512):
            grad_act[:, first : first + 512] = dot(every, down_ref[first : first + 512, :], NT)

    if devices == 8:
        for number in range(4):

            @pl.when(turn == number)
            def _():
                wait_slots(me, number, att_ref, arrived, in_sems, False)

    else:
        take_items(devices, me, step * group, group, att_ref, arrived, in_sems)

        @pl.when(step + 1 < pl.num_programs(0))
        def _():
            send_group(devices, me, total, group, step + 1, att_ref, arrived, in_sems)

    gathered = []
    for one in range(together):
        pieces = []
        for pair in range(PAIRS):
            item = (turn * together + one) * PAIRS + pair
            other, slot = lax.rem(item, devices), item // devices
            pieces.append(arrived[other, slot])
        gathered.append(jnp.concatenate(pieces, axis=1))
    attended = jnp.concatenate(gathered, axis=0)
    attended_ref[...] = attended.reshape(attended_ref.shape)
    residual = hidden_ref[...].reshape(rows, model) + dot(attended, out_weight_ref[...], NN)
    gain = vectors_ref[6:7, :]
    scale = lax.rsqrt(jnp.mean(residual * residual, axis=1, keepdims=True) + 1e-06)
    normed = (residual * scale * gain).astype(BF16)
    normed_ref[...] = normed.reshape(normed_ref.shape)
    cot = cot_ref[pl.ds(turn * together, together)].reshape(rows, model)
    hidden_units = down_ref.shape[0]
    chunk = 512
    layer = residual
    back = jnp.zeros_like(residual)
    for first in range(0, hidden_units, chunk):
        here = slice(first, first + chunk)
        there = slice(hidden_units + first, hidden_units + first + chunk)
        gate = dot(normed, in_weight_ref[:, here], NN)
        up = dot(normed, in_weight_ref[:, there], NN)
        grad = grad_act[here_rows, here]
        square = gate * gate
        inner = gate * (SQRT_2_OVER_PI + (SQRT_2_OVER_PI * 0.044715) * square)
        curve = jnp.tanh(inner)
        half_plus = 0.5 + 0.5 * curve
        smooth = gate * half_plus
        slope = half_plus + (0.5 * gate) * (1.0 - curve * curve) * (SQRT_2_OVER_PI + (3 * SQRT_2_OVER_PI * 0.044715) * square)
        act = (smooth * up).astype(BF16)
        grad_gate = (grad * up * slope).astype(BF16)
        grad_up = (grad * smooth).astype(BF16)
        act_ref[:, :, here] = act.reshape(together, local_tokens, chunk)
        gate_up_ref[:, :, here] = grad_gate.reshape(together, local_tokens, chunk)
        gate_up_ref[:, :, there] = grad_up.reshape(together, local_tokens, chunk)
        layer = layer + dot(act, down_ref[here, :], NN)
        back = back + dot(grad_gate, in_weight_ref[:, here], NT) + dot(grad_up, in_weight_ref[:, there], NT)
    layer_ref[...] = layer.reshape(layer_ref.shape)
    weighted = gain * back
    inner_mean = jnp.mean(residual * weighted, axis=1, keepdims=True)
    grad_residual = cot.astype(F32) + scale * weighted - residual * (scale * scale * scale * inner_mean)
    residual_ref[...] = grad_residual.reshape(residual_ref.shape)
    branch = grad_residual.astype(BF16)
    branch_ref[...] = branch.reshape(branch_ref.shape)
    grad_attended = dot(branch, out_weight_ref[...], NT).astype(BF16)
    for one in range(together):
        for pair in range(PAIRS):
            item = (turn * together + one) * PAIRS + pair
            other, slot = lax.rem(item, devices), item // devices
            stage[other, slot] = grad_attended[one * local_tokens : (one + 1) * local_tokens, pair * 128 : pair * 128 + 128]
    keep_gain[...] += jnp.sum((back * residual * scale).reshape(rows // 8, 8, model), axis=0)
    gain_out[...] = jnp.sum(keep_gain[...], axis=0, keepdims=True)
    if devices == 8:
        @pl.when(step < 2)
        def _():
            send_back(me, turn, stage, items_ref, out_sems)

        @pl.when(step == 3)
        def _():
            for number in range(4):
                wait_slots(me, number, att_ref, arrived, in_sems, True)
            finish_half(me, stage, items_ref, out_sems)
            rest_ref[...] = stage[:, 0:3]

        return
    send_items(devices, me, step * group, group, stage, items_ref, out_sems)

    @pl.when(step == pl.num_programs(0) - 1)
    def _():
        finish_groups(devices, me, total, att_ref, arrived, in_sems)
        finish_sends(devices, me, total, lambda other, slot: stage.at[other, slot], lambda other, slot: items_ref.at[me, slot], out_sems)
        finish_receives(devices, me, total, lambda other, slot: stage.at[other, slot], lambda other, slot: items_ref.at[other, slot], out_sems)


def back_kernel(
    sizes, custom, one_ref, two_ref, hidden_ref, residual_ref, conv_ref, mix_ref, share_ref, ids_ref, weight_ref,
    table_ref, vectors_ref, bias_ref, bias_hot_ref, gain_two_ref, *refs,
):
    local_tokens, window, devices = sizes
    step = pl.program_id(0)
    last = step == pl.num_programs(0) - 1
    me = lax.axis_index("seq")
    plane = lax.axis_index("dp")
    model = vectors_ref.shape[1]
    if custom:
        normed_ref, across_ref, planes_ref = refs[:3]
        block, qkv_out, in_out, down_out, weight_out = refs[3:8]
        refs = refs[8:]
    else:
        block, flat_out, refs = refs[0], refs[1], refs[2:]
    masks, permuted, tap_sums, keep_gain, keep_score = refs[:5]
    refs = refs[5:]
    small = SmallSums(block, refs[:5], refs[5:13])
    refs = refs[13:]

    @pl.when(step == 0)
    def _():
        greet("seq", me, devices)
        greet("dp", plane, small.along)
        keep_gain[...] = jnp.zeros_like(keep_gain)
        keep_score[...] = jnp.zeros_like(keep_score)
        tap_sums[...] = jnp.zeros_like(tap_sums)
        pl.semaphore_wait(pltpu.get_barrier_semaphore(), devices + small.along - 2)

    half = one_ref.shape[1]

    def block_of(item):
        other, slot = lax.rem(item, devices), item // devices
        if isinstance(item, int):
            return (one_ref if slot < half else two_ref)[other, slot % half]
        return jnp.where(slot < half, one_ref[other, jnp.minimum(slot, half - 1)], two_ref[other, jnp.maximum(slot - half, 0)])

    if custom:
        reduce = WeightSums(normed_ref, across_ref, planes_ref, block_of, refs)

        @pl.when(step == 0)
        def _():
            reduce.begin()
            reduce.late()

        @pl.when(step == 2)
        def _():
            reduce.late_one()

        @pl.when(step == 3)
        def _():
            reduce.in_three()
            reduce.rest_two()

    @pl.when(step == 0)
    def _():
        block_masks(masks, me * 2 * local_tokens, devices * 2 * local_tokens)
        permute_weight(weight_ref, permuted)

    together = hidden_ref.shape[0]
    rows = together * local_tokens
    projected = jnp.concatenate(
        [
            jnp.concatenate([block_of((step * together + one) * PAIRS + pair) for pair in range(PAIRS)], axis=1)
            for one in range(together)
        ],
        axis=0,
    )
    if not custom:
        flat_out[...] = projected.reshape(flat_out.shape)
    width = masks.shape[3]
    grad_normed = dot(projected, permuted[...], NT)
    hidden = hidden_ref[...].reshape(rows, model)
    gain = vectors_ref[5:6, :]
    score = vectors_ref[7:8, :]
    scale = lax.rsqrt(jnp.mean(hidden * hidden, axis=1, keepdims=True) + 1e-06)
    weighted = gain * grad_normed
    inner_mean = jnp.mean(hidden * weighted, axis=1, keepdims=True)
    grad_hidden = residual_ref[...].reshape(rows, model) + scale * weighted - hidden * (scale * scale * scale * inner_mean)
    keep_gain[...] += jnp.sum((grad_normed * hidden * scale).reshape(rows // 8, 8, model), axis=0)
    high_all, low_all = split_two(grad_hidden)
    vector = jnp.broadcast_to(score.astype(BF16), (local_tokens, model))
    row16 = lax.broadcasted_iota(jnp.int32, (16, width), 0)
    slopes = []
    for one in range(together):
        if custom and one == 1:

            @pl.when(step == 1)
            def _():
                reduce.in_two()

            @pl.when(last)
            def _():
                reduce.late_two()

        own = slice(one * local_tokens, (one + 1) * local_tokens)
        high, low = high_all[own], low_all[own]
        conv = conv_ref[one]
        cross = 0.5 * (dot(high, conv, NT) + dot(low, conv, NT))
        kept = share_ref[one]
        total = jnp.zeros((local_tokens, width), F32)
        for side in range(2):
            shares = [kept[:, 4 * side + k : 4 * side + k + 1] for k in range(4)]
            grads = [jnp.sum(masks[side, k] * cross, axis=1, keepdims=True) for k in range(4)]
            mean = sum(share * grad for share, grad in zip(shares, grads))
            for k in range(4):
                total = total + (shares[k] * (grads[k] - mean)) * masks[side, k]
        column = jnp.sum(total, axis=0, keepdims=True)
        column_high, column_low = split_two(column)
        column_rows = jnp.where(row16 == 0, column_high.astype(F32), jnp.where(row16 == 1, column_low.astype(F32), 0.0)).astype(BF16)
        keep_score[...] += dot(column_rows, conv, NN)
        left = jnp.concatenate([mix_ref[one], total.astype(BF16)], axis=0)
        right = jnp.concatenate([high, vector], axis=0)
        slopes.append(dot(left, right, TN)[0:window].astype(BF16))
    slope = jnp.concatenate(slopes, axis=0)
    row = lax.broadcasted_iota(jnp.int32, (SMALL_ROWS, window), 0).astype(F32)
    for tap in range(5):
        hot = jnp.concatenate(
            [jnp.where(ids_ref[one, 4 - tap : 5 - tap, 0:window] == row, 1.0, 0.0).astype(BF16) for one in range(together)], axis=1
        )
        tap_sums[tap] += dot(hot, slope, NN)

    @pl.when(last)
    def _():
        if custom:
            reduce.late_three()
        table_grad = jnp.zeros((SMALL_ROWS, model), F32)
        table = table_ref[...].astype(F32)
        place = lax.broadcasted_iota(jnp.int32, (SMALL_ROWS, model), 0)
        extra = []
        for tap in range(5):
            sums = tap_sums[tap]
            table_grad = table_grad + vectors_ref[tap : tap + 1, :] * sums
            extra.append(jnp.sum(sums[0 : table.shape[0]] * table, axis=0, keepdims=True))
        extra.append(jnp.sum(keep_gain[...], axis=0, keepdims=True))
        extra.append(jnp.sum(keep_score[...], axis=0, keepdims=True))
        extra.append(gain_two_ref[...])
        for index, value in enumerate(extra):
            table_grad = jnp.where(place == 259 + index, value, table_grad)
        block[...] = table_grad
        heads = jnp.zeros((16, 128), F32)
        head_row = lax.broadcasted_iota(jnp.int32, (16, 128), 0)
        for slot in range(bias_ref.shape[0]):
            first, second = split_two(bias_ref[slot])
            sums = dot(first, bias_hot_ref[...], NN) + dot(second, bias_hot_ref[...], NN)
            pair = lax.rem(slot * devices + me, PAIRS)
            heads = heads + jnp.where(head_row == 2 * pair, sums[0:1], 0.0) + jnp.where(head_row == 2 * pair + 1, sums[1:2], 0.0)
        block[272:288, 0:128] = heads
        small.pack()
        small.one_start()
        small.one_middle()
        if custom:
            reduce.finish_rest(down_out)
        small.one_finish()
        small.two_finish()
        small.three_finish()
        small.three_more()
        if custom:
            reduce.finish_in(in_out, weight_out)
            reduce.finish_late(qkv_out)
        small.four_finish()


def finish_kernel(block, *refs):
    refs = list(refs)
    count = (len(refs) - 6) // 2
    for source, target in zip(refs[:count], refs[count : 2 * count]):
        target[...] = source[...]
    table_out, taps_out, one_out, score_out, two_out, bias_out = refs[2 * count :]
    table_out[...] = block[0:259, :]
    taps_out[...] = block[259:264, :]
    one_out[...] = block[264, :]
    score_out[...] = block[265, :]
    two_out[...] = block[266, :]
    bias_out[...] = block[272:284, 0:32]


def call_finish(block, sums):
    model = block.shape[1]
    shape = lambda *dims: jax.ShapeDtypeStruct(dims, F32)
    return pl.pallas_call(
        finish_kernel,
        out_shape=[shape(*x.shape) for x in sums] + [shape(259, model), shape(5, model), shape(model), shape(model), shape(model), shape(12, 32)],
        compiler_params=pltpu.CompilerParams(vmem_limit_bytes=VMEM_LIMIT),
        name="finish",
    )(block, *sums)


VMEM_LIMIT = 60 * 2**20
TOGETHER = 2


def item_sems(devices, per_device):
    dma = pltpu.SemaphoreType.DMA
    if devices == 8:
        return [dma((4,)), dma((4,)), dma((4,))]
    return [dma((devices, per_device)), dma((devices, per_device)), dma((per_device,))]


def whole(*shape):
    return pl.BlockSpec(shape, lambda s, *_: (0,) * len(shape), pipeline_mode=pl.Buffered(1))


def part(*shape):
    return pl.BlockSpec(shape, lambda s, *_: (s,) + (0,) * (len(shape) - 1))


ANYWHERE = pl.BlockSpec(memory_space=pl.ANY)


def remote_params(number):
    return pltpu.CompilerParams(vmem_limit_bytes=VMEM_LIMIT, collective_id=number, has_side_effects=True)


def call_front(lengths, ids, table, weight, vectors, devices, per_device):
    sequences, local_bytes = ids.shape
    local_tokens = local_bytes // 2
    window = local_bytes + 16
    width = -(-window // 128) * 128
    model = weight.shape[0]
    return pl.pallas_call(
        functools.partial(front_kernel, (local_tokens, window, devices, sequences * PAIRS)),
        grid=(sequences,),
        in_specs=[pl.BlockSpec(memory_space=pltpu.SMEM), whole(*ids.shape), whole(*table.shape), whole(*weight.shape), whole(*vectors.shape)],
        out_specs=[
            part(1, local_tokens, model),
            part(1, local_tokens, model),
            part(1, width, model),
            part(1, local_tokens, width),
            part(1, local_tokens, 128),
            part(1, 8, local_bytes + 256),
            ANYWHERE,
        ],
        scratch_shapes=[
            pltpu.VMEM((2, 4, local_tokens, width), F32),
            pltpu.VMEM((1, 2, width, model), BF16),
            pltpu.VMEM(weight.shape, BF16),
            pltpu.VMEM((devices, per_device, local_tokens, 384), BF16),
            pltpu.VMEM((5, VPAD, model), BF16),
            pltpu.VMEM((sequences, 128), jnp.int32),
            pltpu.VMEM((sequences, 128), jnp.int32),
            pltpu.VMEM((sequences, local_bytes + 256), F32),
            pltpu.SemaphoreType.DMA((4,)),
        ]
        + item_sems(devices, per_device),
        out_shape=[
            jax.ShapeDtypeStruct((sequences, local_tokens, model), F32),
            jax.ShapeDtypeStruct((sequences, local_tokens, model), BF16),
            jax.ShapeDtypeStruct((sequences, width, model), BF16),
            jax.ShapeDtypeStruct((sequences, local_tokens, width), BF16),
            jax.ShapeDtypeStruct((sequences, local_tokens, 128), F32),
            jax.ShapeDtypeStruct((sequences, 8, local_bytes + 256), F32),
            jax.ShapeDtypeStruct((devices, per_device, local_tokens, 384), BF16),
        ],
        compiler_params=remote_params(3),
        cost_estimate=pl.CostEstimate(flops=5 * 10**10, bytes_accessed=2 * 10**7, transcendentals=10**5),
        name="front",
    )(lengths, ids, table, weight, vectors)


def call_mid(att, hidden, cot, out_weight, in_weight, down_weight, vectors):
    devices, per_device, local_tokens, unused = att.shape
    sequences, unused, model = hidden.shape
    hidden_units = down_weight.shape[0]
    fast = devices == 8
    rows = lambda lanes: pl.BlockSpec((TOGETHER, local_tokens, lanes), lambda s: (lax.rem(s + 2, 4) if fast else s, 0, 0))
    shape = (devices, per_device // 2 if fast else per_device, local_tokens, 128)
    rest = shape if fast else (1, 1, 8, 128)
    full = lambda lanes, kind: jax.ShapeDtypeStruct((sequences, local_tokens, lanes), kind)
    return pl.pallas_call(
        functools.partial(mid_kernel, (local_tokens, devices, sequences * PAIRS)),
        grid=(sequences // TOGETHER,),
        in_specs=[
            ANYWHERE,
            rows(model),
            whole(*cot.shape),
            whole(*out_weight.shape),
            whole(*in_weight.shape),
            whole(*down_weight.shape),
            whole(*vectors.shape),
        ],
        out_specs=[
            rows(model),
            rows(hidden_units),
            rows(2 * hidden_units),
            rows(model),
            rows(model),
            rows(model),
            rows(model),
            ANYWHERE,
            whole(1, model),
            whole(*rest),
        ],
        scratch_shapes=[pltpu.VMEM(att.shape, BF16), pltpu.VMEM(att.shape, BF16), pltpu.VMEM((8, model), F32), pltpu.VMEM((sequences * local_tokens, hidden_units), F32)]
        + item_sems(devices, per_device)
        + item_sems(devices, per_device),
        out_shape=[
            full(model, F32),
            full(hidden_units, BF16),
            full(2 * hidden_units, BF16),
            full(model, BF16),
            full(model, BF16),
            full(model, BF16),
            full(model, F32),
            jax.ShapeDtypeStruct(shape, BF16),
            jax.ShapeDtypeStruct((1, model), F32),
            jax.ShapeDtypeStruct(rest, BF16),
        ],
        compiler_params=remote_params(4),
        cost_estimate=pl.CostEstimate(flops=5 * 10**10, bytes_accessed=4 * 10**7, transcendentals=10**6),
        name="middle",
    )(att, hidden, cot, out_weight, in_weight, down_weight, vectors)


def call_back(custom, one, two, hidden, residual, conv, mix, share, ids, weight, table, vectors, bias_rows, gain_two, along, extra):
    devices, unused, local_tokens, unused = one.shape
    sequences, unused, model = hidden.shape
    width = conv.shape[1]
    window = 2 * local_tokens + 16
    bias_hot = jnp.pad(near_one_hot(), ((0, 0), (0, 96))).astype(BF16)
    out_specs = [whole(SMALL_ROWS, model)]
    out_shape = [jax.ShapeDtypeStruct((SMALL_ROWS, model), F32)]
    scratch = []
    specs = []
    if custom:
        specs = [whole(*x.shape) for x in extra]
        sums = [(96, 576), (96, 1024), (192, 256), (96, 192)]
        out_specs = out_specs + [whole(*shape) for shape in sums]
        out_shape = out_shape + [jax.ShapeDtypeStruct(shape, F32) for shape in sums]
        scratch = weight_scratch(model, sequences * local_tokens)
    else:
        out_specs = out_specs + [part(TOGETHER, local_tokens, PAIRS * 384)]
        out_shape = out_shape + [jax.ShapeDtypeStruct((sequences, local_tokens, PAIRS * 384), BF16)]
    return pl.pallas_call(
        functools.partial(back_kernel, (local_tokens, window, devices), custom),
        grid=(sequences // TOGETHER,),
        in_specs=[
            whole(*one.shape),
            whole(*two.shape),
            part(TOGETHER, local_tokens, model),
            part(TOGETHER, local_tokens, model),
            part(TOGETHER, width, model),
            part(TOGETHER, local_tokens, width),
            part(TOGETHER, local_tokens, 128),
            part(TOGETHER, 8, ids.shape[2]),
            whole(*weight.shape),
            whole(*table.shape),
            whole(*vectors.shape),
            whole(*bias_rows.shape),
            whole(*bias_hot.shape),
            whole(1, model),
        ]
        + specs,
        out_specs=out_specs,
        scratch_shapes=[
            pltpu.VMEM((2, 4, local_tokens, width), F32),
            pltpu.VMEM(weight.shape, BF16),
            pltpu.VMEM((5, SMALL_ROWS, model), F32),
            pltpu.VMEM((8, model), F32),
            pltpu.VMEM((16, model), F32),
        ]
        + small_scratch(devices, along)
        + scratch,
        out_shape=out_shape,
        compiler_params=remote_params(5),
        cost_estimate=pl.CostEstimate(flops=10**11, bytes_accessed=2 * 10**7, transcendentals=10**5),
        name="back",
    )(one, two, hidden, residual, conv, mix, share, ids, weight, table, vectors, bias_rows, bias_hot, gain_two, *extra)


IN_ROWS = 8 * 96 + 2 * 96
REST_ROWS = 2 * 192
LATE_ROWS = 5 * 96


def meet_sibling(core):
    barrier = pltpu.get_barrier_semaphore()
    sibling = lax.axis_index("seq") + 1 - 2 * core
    pl.semaphore_signal(barrier, inc=1, device_id={"seq": sibling}, device_id_type=pl.DeviceIdType.MESH)
    pl.semaphore_wait(barrier, 1)


def to_sibling(core, source, target, send_sem, recv_sem):
    sibling = lax.axis_index("seq") + 1 - 2 * core
    return pltpu.make_async_remote_copy(
        src_ref=source, dst_ref=target, send_sem=send_sem, recv_sem=recv_sem,
        device_id={"seq": sibling}, device_id_type=pl.DeviceIdType.MESH,
    )


def spread_rows(core, source, lanes, keep_ref, send_ref, index_of):
    for chip in range(4):
        for other, ref in ((0, keep_ref), (1, send_ref)):
            device = 2 * chip + lax.rem(core + other, 2)
            rows = pl.ds(pl.multiple_of(device * 96, 32), 96)
            ref[index_of(chip)] = source[rows, lanes]


def early_kernel(
    act_ref, cot_ref, normed_ref, gate_up_ref, attended_ref, branch_ref, after, keep_in, keep_rest,
    other_in, got_in, other_rest, got_rest, cot_t, normed_t, result, send_in, recv_in, send_down, recv_down, send_out, recv_out,
):
    step = pl.program_id(0)
    core = lax.rem(lax.axis_index("seq"), 2)
    model = cot_t.shape[0]
    tokens = cot_t.shape[1]
    out_rows = pl.ds(768, 192)
    out_copy = to_sibling(core, other_in.at[:, :, out_rows], got_in.at[:, :, out_rows], send_out, recv_out)

    def in_copy(at):
        rows = pl.ds(pl.multiple_of(384 * lax.rem(at, 2), 384), 384)
        return to_sibling(core, other_in.at[:, at // 2, rows], got_in.at[:, at // 2, rows], send_in.at[at], recv_in.at[at])

    def down_copy(chip):
        return to_sibling(core, other_rest.at[:, chip], got_rest.at[:, chip], send_down.at[chip], recv_down.at[chip])

    @pl.when(step == 0)
    def _():
        meet_sibling(core)
        cot_t[...] = cot_ref[...].reshape(tokens, model).T
        normed_t[...] = attended_ref[...].reshape(tokens, model).T
        for first in range(0, model, 256):
            result[:, 0:256] = dot(normed_t[...], branch_ref[:, :, first : first + 256].reshape(tokens, 256), NN).astype(BF16)
            for half in range(2):
                tile = first // 128 + half
                for column, slot in {0: ((0, 0),), 1: ((0, 1), (1, 0)), 2: ((1, 1),), 3: ((2, 0),), 4: ((2, 1), (3, 0)), 5: ((3, 1),)}[tile]:
                    rows = slice(768 + 96 * slot, 864 + 96 * slot)
                    spread_rows(core, result, slice(128 * half, 128 * half + 128), keep_in, other_in, lambda chip: (chip, column, rows))
        normed_t[...] = normed_ref[...].reshape(tokens, model).T

    result[...] = dot(normed_t[...], gate_up_ref[...].reshape(tokens, 512), NN).astype(BF16)
    column_at = step // 2
    for quarter in range(4):
        rows = pl.ds(pl.multiple_of((4 * lax.rem(step, 2) + quarter) * 96, 32), 96)
        spread_rows(core, result, slice(128 * quarter, 128 * quarter + 128), keep_in, other_in, lambda chip: (chip, column_at, rows))
    down = dot(cot_t[...], act_ref[...].reshape(tokens, 256), NN).astype(BF16)

    def put_down(ref):
        for column in range(4):
            for half in range(2):
                ref[column, step // 2, 192 * half : 192 * half + 192] = down[192 * column : 192 * column + 192, 128 * half : 128 * half + 128]

    @pl.when(lax.rem(step, 2) == core)
    def _():
        put_down(keep_rest)

    @pl.when(lax.rem(step, 2) != core)
    def _():
        put_down(other_rest)
        down_copy(step // 2).start()

    in_copy(step).start()

    @pl.when(step == 0)
    def _():
        out_copy.start()

    @pl.when(step == 7)
    def _():
        for at in range(8):
            in_copy(at).wait()
        out_copy.wait()
        for chip in range(4):
            down_copy(chip).wait()

        def add(at, unused):
            one, two = at // 4, lax.rem(at, 4)
            keep_in[one, two] = (keep_in[one, two].astype(F32) + got_in[one, two].astype(F32)).astype(BF16)
            keep_rest[one, two] = (keep_rest[one, two].astype(F32) + got_rest[one, two].astype(F32)).astype(BF16)
            return unused

        lax.fori_loop(0, 16, add, 0)


def call_early(act, cot, normed, gate_up, attended, branch, after):
    sequences, local_tokens, model = cot.shape
    tokens = sequences * local_tokens
    every = whole(sequences, local_tokens, model)
    shapes = [(4, 4, IN_ROWS, 128), (4, 4, REST_ROWS, 128)]
    dma = pltpu.SemaphoreType.DMA
    return pl.pallas_call(
        early_kernel,
        grid=(8,),
        in_specs=[
            pl.BlockSpec((sequences, local_tokens, 256), lambda s: (0, 0, s)),
            every,
            every,
            pl.BlockSpec((sequences, local_tokens, 512), lambda s: (0, 0, s)),
            every,
            every,
            ANYWHERE,
        ],
        out_specs=[whole(*shape) for shape in shapes],
        scratch_shapes=[
            pltpu.VMEM(shapes[0], BF16),
            pltpu.VMEM(shapes[0], BF16),
            pltpu.VMEM(shapes[1], BF16),
            pltpu.VMEM(shapes[1], BF16),
            pltpu.VMEM((model, tokens), BF16),
            pltpu.VMEM((model, tokens), BF16),
            pltpu.VMEM((model, 512), BF16),
            dma((8,)), dma((8,)), dma((4,)), dma((4,)), dma, dma,
        ],
        out_shape=[jax.ShapeDtypeStruct(shape, BF16) for shape in shapes],
        compiler_params=pltpu.CompilerParams(vmem_limit_bytes=VMEM_LIMIT, collective_id=1, has_side_effects=True),
        cost_estimate=pl.CostEstimate(flops=11 * 10**9, bytes_accessed=3 * 10**7, transcendentals=0),
        name="early_gradients",
    )(act, cot, normed, gate_up, attended, branch, after)


class ChipSums:
    def __init__(self, source, buffers, sems, chip, core):
        self.source, self.first, self.relay, self.second = (source,) + tuple(buffers)
        self.send, self.recv = sems
        self.chip, self.core = chip, core
        self.beside = chip + 1 - 2 * lax.rem(chip, 2)
        self.above = lax.rem(chip + 2, 4)

    def copy(self, other, source, target, number):
        return pltpu.make_async_remote_copy(
            src_ref=source, dst_ref=target, send_sem=self.send.at[number], recv_sem=self.recv.at[number],
            device_id={"seq": 2 * other + self.core}, device_id_type=pl.DeviceIdType.MESH,
        )

    def ways(self):
        return ((0, self.beside, self.above), (1, self.above, self.beside))

    def one(self):
        made = []
        for way, near, other in self.ways():
            columns = pl.ds(2 * way, 2)
            made.append(self.copy(near, self.source.at[near, columns], self.first.at[way, 0], 2 * way))
            made.append(self.copy(near, self.source.at[3 - self.chip, columns], self.first.at[way, 1], 2 * way + 1))
        return made

    def two(self):
        return [self.copy(other, self.relay.at[way], self.second.at[way], 4 + way) for way, near, other in self.ways()]

    def start(self):
        for copy in self.one():
            copy.start()

    def middle(self):
        for copy in self.one():
            copy.wait()
        for way, near, other in self.ways():
            for at in range(2):
                total = self.source[other, 2 * way + at].astype(F32) + self.first[way, 1, at].astype(F32)
                self.relay[way, at] = total.astype(BF16)
        for copy in self.two():
            copy.start()

    def finish(self, target):
        for copy in self.two():
            copy.wait()
        for way in range(2):
            for at in range(2):
                total = self.source[self.chip, 2 * way + at].astype(F32) + self.first[way, 0, at].astype(F32)
                target[2 * way + at] = (total + self.second[way, at].astype(F32)).astype(BF16)


def chip_scratch(rows):
    return [pltpu.VMEM((2, 2, 2, rows, 128), BF16), pltpu.VMEM((2, 2, rows, 128), BF16), pltpu.VMEM((2, 2, rows, 128), BF16)]


class WeightSums:
    def __init__(self, normed_ref, across_ref, planes_ref, block_of, refs):
        self.normed, self.across, self.planes, self.block_of = normed_ref, across_ref, planes_ref, block_of
        (
            self.in_sum, self.in_got, self.rest_got, self.rest_sum, self.rest_chips, self.normed_t, self.result,
            self.keep, self.other, self.got, self.late_sum, self.late_got,
        ) = refs[:12]
        (
            self.send_in, self.recv_in, self.send_rest, self.recv_rest, self.send_chip, self.recv_chip,
            self.send_a, self.recv_a, self.send_c, self.recv_c,
        ) = refs[18:28]
        self.me, self.plane = lax.axis_index("seq"), lax.axis_index("dp")
        self.core, self.chip = lax.rem(self.me, 2), self.me // 2
        self.in_chips = ChipSums(across_ref, refs[12:15], refs[28:30], self.chip, self.core)
        self.late_chips = ChipSums(self.keep, refs[15:18], refs[30:32], self.chip, self.core)

    def to_plane(self, offset, source, target, send, recv):
        return pltpu.make_async_remote_copy(
            src_ref=source, dst_ref=target, send_sem=send.at[offset - 1], recv_sem=recv.at[offset - 1],
            device_id={"dp": lax.rem(self.plane + offset, 4)}, device_id_type=pl.DeviceIdType.MESH,
        )

    def rest_plane(self, offset):
        peer = lax.rem(self.plane + offset, 4)
        return self.to_plane(offset, self.planes.at[peer], self.rest_got.at[offset - 1], self.send_rest, self.recv_rest)

    def in_plane(self, offset):
        peer = lax.rem(self.plane + offset, 4)
        return self.to_plane(offset, self.in_sum.at[peer], self.in_got.at[offset - 1], self.send_in, self.recv_in)

    def late_plane(self, offset):
        peer = lax.rem(self.plane + offset, 4)
        return self.to_plane(offset, self.late_sum.at[peer], self.late_got.at[offset - 1], self.send_c, self.recv_c)

    def rest_chip(self, offset):
        other = lax.rem(self.chip + offset, 4)
        return pltpu.make_async_remote_copy(
            src_ref=self.rest_sum.at[other], dst_ref=self.rest_chips.at[offset - 1],
            send_sem=self.send_chip.at[offset - 1], recv_sem=self.recv_chip.at[offset - 1],
            device_id={"seq": 2 * other + self.core}, device_id_type=pl.DeviceIdType.MESH,
        )

    def late_core(self, column):
        return to_sibling(self.core, self.other.at[:, column], self.got.at[:, column], self.send_a.at[column], self.recv_a.at[column])

    def begin(self):
        self.in_chips.start()
        for offset in (1, 2, 3):
            self.rest_plane(offset).start()

    def late(self):
        sequences, count, model = self.normed.shape
        self.normed_t[...] = self.normed[...].reshape(sequences * count, model).T
        low = lax.broadcasted_iota(jnp.int32, (model, 128), 1) < 64
        for pair in range(PAIRS):
            rows = jnp.concatenate([self.block_of(one * PAIRS + pair) for one in range(sequences)], axis=0)
            sums = dot(self.normed_t[...], rows, NN)
            query, key, value = sums[:, 0:128], pltpu.roll(sums[:, 128:256], 64, 1), sums[:, 256:384]
            self.result[3 * pair] = jnp.where(low, query, key).astype(BF16)
            self.result[3 * pair + 1] = jnp.where(low, value, query).astype(BF16)
            self.result[3 * pair + 2] = jnp.where(low, key, value).astype(BF16)
        for tile in range(3 * PAIRS):
            within = tile % 9
            spots = [(2 * (tile // 9), within)] if within <= 4 else []
            spots += [(2 * (tile // 9) + 1, within - 4)] if within >= 4 else []
            for column, slot in spots:
                rows_at = slice(96 * slot, 96 * slot + 96)
                spread_rows(self.core, self.result.at[tile], slice(0, 128), self.keep, self.other, lambda chip: (chip, column, rows_at))
        for column in range(4):
            self.late_core(column).start()

    def late_one(self):
        for column in range(4):
            self.late_core(column).wait()
            for at in range(4):
                self.keep[at, column] = (self.keep[at, column].astype(F32) + self.got[at, column].astype(F32)).astype(BF16)
        self.late_chips.start()

    def in_two(self):
        self.in_chips.middle()

    def late_two(self):
        self.late_chips.middle()

    def rest_two(self):
        for offset in (1, 2, 3):
            self.rest_plane(offset).wait()
        for chip in range(4):
            total = self.planes[self.plane, chip].astype(F32)
            for slot in range(3):
                total = total + self.rest_got[slot, chip].astype(F32)
            self.rest_sum[chip] = total.astype(BF16)
        for offset in (1, 2, 3):
            self.rest_chip(offset).start()

    def in_three(self):
        self.in_chips.finish(self.in_sum)
        for offset in (1, 2, 3):
            self.in_plane(offset).start()

    def late_three(self):
        self.late_chips.finish(self.late_sum)
        for offset in (1, 2, 3):
            self.late_plane(offset).start()

    def joined(self, block, columns):
        odd = lax.rem(self.plane, 2) == 1
        count = block.shape[1]
        return jnp.where(odd, pltpu.roll(block, count - 64, 1), block)[:, :columns]

    def finish_rest(self, down_out):
        total = self.rest_sum[self.chip].astype(F32)
        for offset in (1, 2, 3):
            self.rest_chip(offset).wait()
            total = total + self.rest_chips[offset - 1].astype(F32)
        down_out[:, 0:128] = total[0:192]
        down_out[:, 128:256] = total[192:384]

    def finish_in(self, in_out, weight_out):
        total = self.in_sum[self.plane].astype(F32)
        for offset in (1, 2, 3):
            self.in_plane(offset).wait()
            total = total + self.in_got[offset - 1].astype(F32)
        for tile in range(8):
            in_out[:, 128 * tile : 128 * tile + 128] = total[96 * tile : 96 * tile + 96]
        weight_out[...] = self.joined(jnp.concatenate([total[768:864], total[864:960]], axis=1), 192)

    def finish_late(self, qkv_out):
        total = self.late_sum[self.plane].astype(F32)
        for offset in (1, 2, 3):
            self.late_plane(offset).wait()
            total = total + self.late_got[offset - 1].astype(F32)
        qkv_out[...] = self.joined(jnp.concatenate([total[96 * k : 96 * k + 96] for k in range(5)], axis=1), 576)


def weight_scratch(model, tokens):
    dma = pltpu.SemaphoreType.DMA
    late = (4, 4, LATE_ROWS, 128)
    return (
        [
            pltpu.VMEM((4, IN_ROWS, 128), BF16),
            pltpu.VMEM((3, IN_ROWS, 128), BF16),
            pltpu.VMEM((3, 4, REST_ROWS, 128), BF16),
            pltpu.VMEM((4, REST_ROWS, 128), BF16),
            pltpu.VMEM((3, REST_ROWS, 128), BF16),
            pltpu.VMEM((model, tokens), BF16),
            pltpu.VMEM((3 * PAIRS, model, 128), BF16),
            pltpu.VMEM(late, BF16),
            pltpu.VMEM(late, BF16),
            pltpu.VMEM(late, BF16),
            pltpu.VMEM((4, LATE_ROWS, 128), BF16),
            pltpu.VMEM((3, LATE_ROWS, 128), BF16),
        ]
        + chip_scratch(IN_ROWS)
        + chip_scratch(LATE_ROWS)
        + [dma((3,)), dma((3,)), dma((3,)), dma((3,)), dma((3,)), dma((3,)), dma((4,)), dma((4,)), dma((3,)), dma((3,))]
        + [dma((6,)), dma((6,)), dma((6,)), dma((6,))]
    )


SMALL_ROWS = 288


class SmallSums:
    def __init__(self, block, buffers, sems):
        self.block = block
        self.held, self.got_seq, self.planes, self.got_dp, self.whole = buffers
        self.sems = sems
        self.me, self.plane = lax.axis_index("seq"), lax.axis_index("dp")
        self.across, self.along = self.held.shape[0], self.held.shape[1]
        self.paired = self.across == 8
        self.core, self.chip = lax.rem(self.me, 2), self.me // 2
        self.mine = self.across // 2 * self.core + self.chip

    def places(self):
        half = self.held.shape[2] // 2
        units = SMALL_ROWS // half
        tiles = self.block.shape[1] // 128
        for at in range(2 * self.along * self.across):
            spot = (at // (2 * self.along), at // 2 % self.along, slice((at % 2) * half, (at % 2) * half + half))
            tile, unit = at // units, at % units
            if tile < tiles:
                yield spot, (slice(unit * half, unit * half + half), slice(128 * tile, 128 * tile + 128))
            else:
                yield spot, None

    def pack(self):
        for spot, source in self.places():
            if source is None:
                self.held[spot] = jnp.zeros((self.held.shape[2] // 2, 128), BF16)
            else:
                self.held[spot] = self.block[source].astype(BF16)

    def copies(self, axis, source, target, number):
        here, count = {"seq": (self.me, self.across), "chip": (self.chip, self.across // 2), "dp": (self.plane, self.along)}[axis]
        send, recv = self.sems[2 * number], self.sems[2 * number + 1]
        made = []
        for step in range(1, count):
            peer = lax.rem(here + step, count)
            device = {"seq": 2 * peer + self.core} if axis == "chip" else {axis: peer}
            made.append(
                pltpu.make_async_remote_copy(
                    src_ref=source(peer), dst_ref=target(step - 1), send_sem=send.at[step - 1], recv_sem=recv.at[step - 1],
                    device_id=device, device_id_type=pl.DeviceIdType.MESH,
                )
            )
        for copy in made:
            copy.start()
        return made

    def sibling(self, source, target, number):
        made = [to_sibling(self.core, source, target, self.sems[2 * number].at[6], self.sems[2 * number + 1].at[6])]
        made[0].start()
        return made

    def one_start(self):
        if self.paired:
            half = pl.ds(4 * (1 - self.core), 4)
            self.waiting = self.sibling(self.held.at[half], self.got_seq.at[pl.ds(3, 4)], 0)
            return
        self.waiting = self.copies("seq", lambda peer: self.held.at[peer], lambda slot: self.got_seq.at[slot], 0)

    def one_middle(self):
        if self.paired:
            for copy in self.waiting:
                copy.wait()
            for chip in range(4):
                at = 4 * self.core + chip
                self.held[at] = (self.held[at].astype(F32) + self.got_seq[3 + chip].astype(F32)).astype(BF16)
            self.waiting = self.copies("chip", lambda peer: self.held.at[4 * self.core + peer], lambda slot: self.got_seq.at[slot], 0)

    def one_finish(self):
        for copy in self.waiting:
            copy.wait()
        total = self.held[self.mine if self.paired else self.me].astype(F32)
        for slot in range(3 if self.paired else self.across - 1):
            total = total + self.got_seq[slot].astype(F32)
        self.planes[...] = total.astype(BF16)
        self.waiting = self.copies("dp", lambda peer: self.planes.at[peer], lambda slot: self.got_dp.at[slot], 1)

    def two_finish(self):
        for copy in self.waiting:
            copy.wait()
        mine = self.planes[self.plane].astype(F32)
        for slot in range(self.along - 1):
            mine = mine + self.got_dp[slot].astype(F32)
        own = self.mine if self.paired else self.me
        self.whole[own, self.plane] = mine.astype(BF16)
        self.waiting = self.copies("dp", lambda peer: self.whole.at[own, self.plane], lambda slot: self.whole.at[own, self.plane], 2)

    def three_finish(self):
        for copy in self.waiting:
            copy.wait()
        own = self.mine if self.paired else self.me
        self.waiting = self.copies("chip" if self.paired else "seq", lambda peer: self.whole.at[own], lambda slot: self.whole.at[own], 3)

    def three_more(self):
        if self.paired:
            for copy in self.waiting:
                copy.wait()
            half = pl.ds(4 * self.core, 4)
            self.waiting = self.sibling(self.whole.at[half], self.whole.at[half], 3)

    def four_finish(self):
        for copy in self.waiting:
            copy.wait()
        for spot, target in self.places():
            if target is not None:
                self.block[target] = self.whole[spot].astype(F32)


def small_scratch(across, along):
    chunk = max(16, 2048 // (across * along))
    dma = lambda count: pltpu.SemaphoreType.DMA((count,))
    return [
        pltpu.VMEM((across, along, chunk, 128), BF16),
        pltpu.VMEM((across - 1, along, chunk, 128), BF16),
        pltpu.VMEM((along, chunk, 128), BF16),
        pltpu.VMEM((along - 1, chunk, 128), BF16),
        pltpu.VMEM((across, along, chunk, 128), BF16),
        dma(across - 1), dma(across - 1), dma(along - 1), dma(along - 1),
        dma(along - 1), dma(along - 1), dma(across - 1), dma(across - 1),
    ]


def body(
    byte_ids,
    lengths,
    byte_table,
    conv_kernel,
    score_vector,
    norm_gain_one,
    qkv_weight,
    bias_table,
    out_weight,
    norm_gain_two,
    in_weight,
    down_weight,
    cotangent,
):
    devices = lax.axis_size("seq")
    me = lax.axis_index("seq")
    sequences, local_bytes = byte_ids.shape
    local_tokens = local_bytes // 2
    total_bytes = local_bytes * devices
    vocab, model = byte_table.shape
    total = sequences * PAIRS
    per_device = -(-total // devices)
    place = jnp.reshape(me, (1,)).astype(jnp.int32)
    vectors = jnp.concatenate([conv_kernel, norm_gain_one[None, :], norm_gain_two[None, :], score_vector[None, :]], axis=0)
    rows = jnp.dot(near_one_hot(), bias_table, precision="highest").T.reshape(PAIRS, 2, NEAR)

    def exchange(items):
        return lax.all_to_all(items, "seq", split_axis=0, concat_axis=0, tiled=True)

    hidden, normed, conv, mix, share, ids_rows, received = call_front(lengths, byte_ids, byte_table, qkv_weight, vectors, devices, per_device)
    out, aug, cot = attention_forward(received, rows, lengths, place, cotangent)
    layer, act, gate_up, normed_two, attended, branch, grad_residual, grad_items, grad_gain_two, grad_rest = call_mid(
        out, hidden, cot, out_weight, in_weight, down_weight, vectors
    )
    along_count = lax.axis_size("dp")
    custom = devices == 8 and along_count == 4

    def scatter(grad):
        rows_own = lax.psum_scatter(grad, "seq", scatter_dimension=0, tiled=True)
        return lax.psum_scatter(rows_own, "dp", scatter_dimension=1, tiled=True).astype(F32)

    if not custom:
        summed_down = scatter(jnp.einsum("bti,btd->id", act, cot, preferred_element_type=F32).astype(BF16))
        summed_in = scatter(jnp.einsum("btd,bti->di", normed_two, gate_up, preferred_element_type=F32).astype(BF16))
        summed_out = scatter(jnp.einsum("btd,bte->de", attended, branch, preferred_element_type=F32).astype(BF16))
    half = per_device // 2
    grads_two, grads_one, at_two = (grad_items, exchange(grad_rest), 0) if devices == 8 else (grad_items, grad_items, half)
    dqkv_two, bias_two, layer_out = attention_backward(
        received, out, aug, grads_two, rows, lengths, place, layer, grad_gain_two, half, per_device - half, at_two
    )
    items_two = exchange(dqkv_two)
    dqkv_one, bias_one, unused = attention_backward(received, out, aug, grads_one, rows, lengths, place, None, bias_two, 0, half, 0)
    items_one = exchange(dqkv_one)
    bias_rows = jnp.concatenate([bias_one, bias_two], axis=0)
    if custom:
        in_chips, rest_planes = call_early(act, cot, normed_two, gate_up, attended, branch, items_two)
    extra = (normed, in_chips, rest_planes) if custom else ()
    results = call_back(
        custom, items_one, items_two, hidden, grad_residual, conv, mix, share, ids_rows, qkv_weight, byte_table, vectors, bias_rows, grad_gain_two, along_count, extra
    )
    if custom:
        summed_qkv, summed_in, summed_down, summed_out, *smalls = call_finish(results[0], results[1:])
        summed_down = summed_down.T
    else:
        smalls = call_finish(results[0], ())
        grad_qkv = jnp.einsum("btd,bte->de", normed, results[1], preferred_element_type=F32).astype(BF16)
        grad_qkv = jnp.swapaxes(grad_qkv.reshape(model, PAIRS, 3, 2, 64), 2, 3).reshape(model, PAIRS * 384)
        summed_qkv = scatter(grad_qkv)
    grad_table, grad_taps, grad_gain_one, grad_score, grad_gain_two, grad_bias = smalls
    return (
        layer_out,
        grad_table,
        grad_taps,
        grad_score,
        grad_gain_one,
        summed_qkv,
        grad_bias.T,
        summed_out,
        grad_gain_two,
        summed_in,
        summed_down,
    )


def solution(mesh):
    return jax.shard_map(
        body,
        mesh=mesh,
        in_specs=(
            P("dp", "seq"),
            P("dp"),
            P(),
            P(),
            P(),
            P(),
            P(),
            P(),
            P(),
            P(),
            P(),
            P(),
            P("dp", "seq", None),
        ),
        out_specs=(
            P("dp", "seq", None),
            P(),
            P(),
            P(),
            P(),
            P("seq", "dp"),
            P(),
            P("seq", "dp"),
            P(),
            P("seq", "dp"),
            P("seq", "dp"),
        ),
        check_vma=False,
    )
```

```python
import functools
import jax
import jax.numpy as jnp
from jax import lax
from jax.experimental import pallas as pl
from jax.experimental.pallas import tpu as pltpu
from jax.sharding import PartitionSpec as P

thresholds = (12, 16, 23, 32, 46, 64, 91)
KB = 256
NEAR = 1024
F32 = jnp.float32
BF16 = jnp.bfloat16
NT = (((1,), (1,)), ((), ()))
NN = (((1,), (0,)), ((), ()))


def rel_bucket(relative):
    distance = jnp.abs(relative)
    larger = 8 + sum(((distance >= boundary).astype(jnp.int32) for boundary in thresholds))
    bucket = jnp.where(distance < 8, distance, larger)
    return bucket + 16 * (relative > 0).astype(jnp.int32)


def near_one_hot():
    place = jnp.arange(NEAR, dtype=jnp.int32)
    relative = jnp.where(place < NEAR - 128, KB - place, KB + NEAR - place)
    return (rel_bucket(relative)[:, None] == jnp.arange(32, dtype=jnp.int32)[None, :]).astype(F32)


def dot(a, b, dims):
    return lax.dot_general(a, b, dims, preferred_element_type=F32)


STRIP = 5 * KB


def strip_at(block, part):
    return pl.ds(pl.multiple_of((jnp.clip(part - block, -2, 2) + 2) * KB, KB), KB)


def fill_bias(strip, head, row):
    spread = jnp.broadcast_to(row, (128, NEAR))
    rolled = pltpu.roll(spread, 0, 1, stride=1, stride_axis=0)
    far_right = jnp.broadcast_to(row[:, NEAR - 1 :], (KB, 128))
    far_left = jnp.broadcast_to(row[:, 768:769], (KB, 128))
    for start in range(0, KB, 128):
        strip[head, :, start : start + 128] = far_right
        strip[head, :, KB + 768 + start : KB + 896 + start] = far_left
    strip[head, 0:128, KB : KB + 768] = rolled[:, :768]
    strip[head, 128:256, KB : KB + 128] = far_right[:128]
    strip[head, 128:256, KB + 128 : KB + 768] = rolled[:, :640]


def lanes_of(head, shape):
    lane = lax.broadcasted_iota(jnp.int32, shape, 1)
    own = (lane < 64) if head == 0 else (lane >= 64)
    return own, lane - (64 if head == 0 else 0)


def fill_keys(ka, head, keys, valid):
    own, spare = lanes_of(head, keys.shape)
    row = lax.broadcasted_iota(jnp.int32, keys.shape, 0)
    masked = jnp.where(row < valid, 0.0, -1e9)
    extra = jnp.where(spare == 0, masked, jnp.where((spare >= 1) & (spare <= 3), 1.0, 0.0))
    ka[head] = jnp.where(own, keys, extra.astype(BF16))


def item_length(lengths_ref, item):
    length = jnp.int32(0)
    for number, rank in enumerate(ranks_of(lengths_ref)):
        length = jnp.where(rank == item // 6, lengths_ref[number], length)
    return (length + 1) // 2


def move_rows(item, lengths_ref, source, buffer, target, sems, sorting):
    def inward(number):
        return pltpu.make_async_copy(source.at[number if sorting else ranks[number]], buffer.at[number], sems.at[0, number])

    def outward(number):
        return pltpu.make_async_copy(buffer.at[number], target.at[ranks[number] if sorting else number], sems.at[1, number])

    count = source.shape[0]
    ranks = ranks_of(lengths_ref)

    @pl.when(item == 0)
    def _():
        for number in range(count):
            inward(number).start()

    @pl.when(item == jnp.minimum(1, pl.num_programs(0) - 1))
    def _():
        for number in range(count):
            inward(number).wait()
            outward(number).start()

    def finish():
        @pl.when(item == pl.num_programs(0) - 1)
        def _():
            for number in range(count):
                outward(number).wait()

    return finish


def fwd_kernel(
    blocks, lengths_ref, place_ref, qkv_ref, row_ref, cot_ref, out_ref, aug_ref, sorted_ref,
    qa, ka, vt, strip, peak, acc, probs, moving, sems,
):
    item = pl.program_id(0)
    finish = move_rows(item, lengths_ref, cot_ref, moving, sorted_ref, sems, True)
    valid = item_length(lengths_ref, place_ref[0] + qkv_ref.shape[0] * item)
    tokens = blocks * KB
    joined = qkv_ref[:, 0].reshape(tokens, 384)
    queries = joined[:, 0:128]
    keys = joined[:, 128:256]
    turned = joined[:, 256:384].T
    filler = jnp.where(lax.broadcasted_iota(jnp.int32, (16, tokens), 0) == 0, 1.0, 0.0).astype(BF16)
    for head in range(2):
        own, spare = lanes_of(head, queries.shape)
        qa[head] = jnp.where(own, queries, jnp.where(spare == 0, 1.0, 0.0).astype(BF16))
        fill_keys(ka, head, keys, valid)
        vt[head, 0:64] = turned[64 * head : 64 * head + 64]
        vt[head, 64:80] = filler
        fill_bias(strip, head, row_ref[0, head : head + 1, :])
    peak[...] = jnp.full_like(peak, -1e30)
    acc[...] = jnp.zeros_like(acc)

    def step(block, unused):
        first = pl.multiple_of(block * KB, KB)
        alphas = [[], []]
        for part in range(blocks):
            for head in range(2):
                here = slice(part * KB, part * KB + KB)
                logits = dot(ka[head, pl.ds(first, KB), :], qa[head, here, :], NT)
                logits = logits + strip[head, :, strip_at(block, part)]
                before = peak[head, :, here]
                after = jnp.maximum(before, jnp.max(logits, axis=0, keepdims=True))
                probs[head, :, here] = jnp.exp(logits - after).astype(BF16)
                peak[head, :, here] = after
                alphas[head].append(jnp.exp(before - after))
        for head in range(2):
            acc[head] = acc[head] * jnp.concatenate(alphas[head], axis=1) + dot(vt[head, :, pl.ds(first, KB)], probs[head], NN)
        return unused

    lax.fori_loop(0, (valid + KB - 1) // KB, step, 0)
    outs = []
    rows = []
    place = lax.broadcasted_iota(jnp.int32, (64, tokens), 0)
    for head in range(2):
        total = acc[head, 64:65, :]
        outs.append(acc[head, 0:64, :] / total)
        minus = -(peak[head] + jnp.log(total))
        high = minus.astype(BF16).astype(F32)
        rest = minus - high
        middle = rest.astype(BF16).astype(F32)
        low = rest - middle
        rows.append(jnp.where(place == 0, 1.0, jnp.where(place == 1, high, jnp.where(place == 2, middle, jnp.where(place == 3, low, 0.0)))))
    out_ref[:, 0] = jnp.concatenate(outs, axis=0).T.astype(BF16).reshape(out_ref.shape[0], out_ref.shape[2], 128)
    aug_ref[0] = jnp.concatenate([rows[1], rows[0]], axis=0).T.astype(BF16)
    finish()


def bwd_kernel(
    blocks, base_slot, moves, lengths_ref, place_ref, qkv_ref, out_ref, aug_ref, grad_ref, row_ref, layer_ref, after,
    dqkv_ref, bias_ref, moved_ref, qa, ka, va, ga, kt, strip, tally, probs, slopes, dq, *moving,
):
    item = pl.program_id(0)
    finish = move_rows(item, lengths_ref, layer_ref, moving[0], moved_ref, moving[1], False) if moves else lambda: None
    valid = item_length(lengths_ref, place_ref[0] + qkv_ref.shape[0] * (item + base_slot))
    tokens = blocks * KB
    local = qkv_ref.shape[2]
    joined = qkv_ref[:, 0].reshape(tokens, 384)
    queries = joined[:, 0:128]
    keys = joined[:, 128:256]
    values = joined[:, 256:384]
    grads = grad_ref[:, 0].reshape(tokens, 128)
    outs = out_ref[:, 0].reshape(tokens, 128)
    kt[...] = keys.T
    product = grads.astype(F32) * outs.astype(F32)
    high = product.astype(BF16)
    low = (product - high.astype(F32)).astype(BF16)
    row_at = lax.broadcasted_iota(jnp.int32, (128, 128), 0)
    lane_at = lax.broadcasted_iota(jnp.int32, (128, 128), 1)
    pick = jnp.where((row_at < 64) == (lane_at >= 64), -1.0, 0.0).astype(BF16)
    shifts = dot(high, pick, NN) + dot(low, pick, NN)
    shift_high = shifts.astype(BF16)
    shift_low = (shifts - shift_high.astype(F32)).astype(BF16)
    for head in range(2):
        own, spare = lanes_of(head, queries.shape)
        qa[head] = jnp.where(own, queries, aug_ref[0])
        fill_keys(ka, head, keys, valid)
        va[head] = jnp.where(own, values, jnp.where((spare == 0) | (spare == 1), 1.0, 0.0).astype(BF16))
        ga[head] = jnp.where(own, grads, jnp.where(spare == 0, shift_high, jnp.where(spare == 1, shift_low, jnp.zeros_like(shift_low))))
        fill_bias(strip, head, row_ref[0, head : head + 1, :])
    tally[...] = jnp.zeros_like(tally)
    dq[...] = jnp.zeros_like(dq)
    dqkv_ref[...] = jnp.zeros_like(dqkv_ref)

    def step(block, unused):
        first = pl.multiple_of(block * KB, KB)
        key_parts = []
        value_parts = []
        for part in range(blocks):
            for head in range(2):
                here = slice(part * KB, part * KB + KB)
                there = strip_at(block, part)
                logits = dot(ka[head, pl.ds(first, KB), :], qa[head, here, :], NT)
                weights = jnp.exp(logits + strip[head, :, there])
                change = dot(va[head, pl.ds(first, KB), :], ga[head, here, :], NT)
                slope = weights * change
                tally[head, :, there] += slope
                probs[head, :, here] = weights.astype(BF16)
                slopes[head, :, here] = slope.astype(BF16)
        for head in range(2):
            value_parts.append(dot(probs[head], ga[head], NN))
            key_parts.append(dot(slopes[head], qa[head], NN))
            dq[pl.ds(64 * head, 64), :] += dot(kt[pl.ds(64 * head, 64), pl.ds(first, KB)], slopes[head], NN)
        own, unused_spare = lanes_of(0, (KB, 128))
        count = KB // local
        where = pl.ds(block * count, count)
        dqkv_ref[where, 0, :, 128:256] = jnp.where(own, key_parts[0], key_parts[1]).astype(BF16).reshape(count, local, 128)
        dqkv_ref[where, 0, :, 256:384] = jnp.where(own, value_parts[0], value_parts[1]).astype(BF16).reshape(count, local, 128)
        return unused

    lax.fori_loop(0, (valid + KB - 1) // KB, step, 0)
    dqkv_ref[:, 0, :, 0:128] = dq[...].T.astype(BF16).reshape(dqkv_ref.shape[0], local, 128)
    lane = lax.broadcasted_iota(jnp.int32, (1, NEAR), 1)
    flip = jnp.where(row_at + lane_at == 127, 1.0, 0.0).astype(BF16)
    for head in range(2):
        far_right = tally[head, :, 0:128] + tally[head, :, 128:256]
        far_right = far_right[:128] + far_right[128:] + tally[head, 128:256, KB : KB + 128]
        far_left = tally[head, :, KB + 768 : KB + 896] + tally[head, :, KB + 896 : STRIP]
        near = tally[head, 0:128, KB : KB + 768]
        near_low = tally[head, 128:256, KB + 128 : KB + 768]
        near = near + jnp.concatenate([near_low, jnp.zeros((128, 128), F32)], axis=1)
        near = jnp.concatenate([near, jnp.zeros((128, NEAR - 768), F32)], axis=1)
        near_high = near.astype(BF16)
        flipped = dot(flip, near_high, NN) + dot(flip, (near - near_high.astype(F32)).astype(BF16), NN)
        rolled = pltpu.roll(flipped, NEAR - 127, 1, stride=1, stride_axis=0)
        row = jnp.sum(rolled, axis=0, keepdims=True)
        row = row + jnp.where(lane == NEAR - 1, jnp.sum(far_right), 0.0) + jnp.where(lane == 768, jnp.sum(far_left), 0.0)
        bias_ref[0, head : head + 1, :] = row
    finish()


def attention_forward(qkv, rows, lengths, place, cot):
    sources, items, local, unused = qkv.shape
    blocks = sources * local // KB
    tokens = sources * local
    spec = pltpu.PrefetchScalarGridSpec(
        num_scalar_prefetch=2,
        grid=(items,),
        in_specs=[
            pl.BlockSpec((sources, 1, local, 384), lambda i, l, p: (0, i, 0, 0)),
            pl.BlockSpec((1, 2, NEAR), lambda i, l, p: (lax.rem(p[0] + sources * i, 6), 0, 0)),
            pl.BlockSpec(memory_space=pl.ANY),
        ],
        out_specs=[
            pl.BlockSpec((sources, 1, local, 128), lambda i, l, p: (0, i, 0, 0)),
            pl.BlockSpec((1, tokens, 128), lambda i, l, p: (i, 0, 0)),
            pl.BlockSpec(memory_space=pl.ANY),
        ],
        scratch_shapes=[
            pltpu.VMEM((2, tokens, 128), BF16),
            pltpu.VMEM((2, tokens, 128), BF16),
            pltpu.VMEM((2, 80, tokens), BF16),
            pltpu.VMEM((2, KB, STRIP), F32),
            pltpu.VMEM((2, 1, tokens), F32),
            pltpu.VMEM((2, 80, tokens), F32),
            pltpu.VMEM((2, KB, tokens), BF16),
            pltpu.VMEM(cot.shape, cot.dtype),
            pltpu.SemaphoreType.DMA((2,) + cot.shape[:1]),
        ],
    )
    return pl.pallas_call(
        functools.partial(fwd_kernel, blocks),
        grid_spec=spec,
        out_shape=[
            jax.ShapeDtypeStruct((sources, items, local, 128), BF16),
            jax.ShapeDtypeStruct((items, tokens, 128), BF16),
            jax.ShapeDtypeStruct(cot.shape, cot.dtype),
        ],
        compiler_params=pltpu.CompilerParams(vmem_limit_bytes=60 * 2**20),
        cost_estimate=pl.CostEstimate(flops=items * tokens * tokens * 512, bytes_accessed=items * tokens * 2048, transcendentals=items * tokens * tokens * 2),
        name="attention_forward",
    )(lengths, place, qkv, rows, cot)


def attention_backward(qkv, outs, aug, grads, rows, lengths, place, layer, after, first, items, grads_at):
    sources, unused, local, unused = qkv.shape
    moves = layer is not None
    layer = after if layer is None else layer
    moved = layer if moves else jnp.zeros((8, 128), F32)
    blocks = sources * local // KB
    tokens = sources * local
    big = lambda lanes: pl.BlockSpec((sources, 1, local, lanes), lambda i, l, p: (0, i + first, 0, 0))
    spec = pltpu.PrefetchScalarGridSpec(
        num_scalar_prefetch=2,
        grid=(items,),
        in_specs=[
            big(384),
            big(128),
            pl.BlockSpec((1, tokens, 128), lambda i, l, p: (i + first, 0, 0)),
            pl.BlockSpec((sources, 1, local, 128), lambda i, l, p: (0, i + grads_at, 0, 0)),
            pl.BlockSpec((1, 2, NEAR), lambda i, l, p: (lax.rem(p[0] + sources * (i + first), 6), 0, 0)),
            pl.BlockSpec(memory_space=pl.ANY),
            pl.BlockSpec(memory_space=pl.ANY),
        ],
        out_specs=[
            pl.BlockSpec((sources, 1, local, 384), lambda i, l, p: (0, i, 0, 0)),
            pl.BlockSpec((1, 2, NEAR), lambda i, l, p: (i, 0, 0)),
            pl.BlockSpec(memory_space=pl.ANY),
        ],
        scratch_shapes=[
            pltpu.VMEM((2, tokens, 128), BF16),
            pltpu.VMEM((2, tokens, 128), BF16),
            pltpu.VMEM((2, tokens, 128), BF16),
            pltpu.VMEM((2, tokens, 128), BF16),
            pltpu.VMEM((128, tokens), BF16),
            pltpu.VMEM((2, KB, STRIP), F32),
            pltpu.VMEM((2, KB, STRIP), F32),
            pltpu.VMEM((2, KB, tokens), BF16),
            pltpu.VMEM((2, KB, tokens), BF16),
            pltpu.VMEM((128, tokens), F32),
        ]
        + ([pltpu.VMEM(layer.shape, layer.dtype), pltpu.SemaphoreType.DMA((2,) + layer.shape[:1])] if moves else []),
    )
    return pl.pallas_call(
        functools.partial(bwd_kernel, blocks, first, moves),
        grid_spec=spec,
        out_shape=[
            jax.ShapeDtypeStruct((sources, items, local, 384), BF16),
            jax.ShapeDtypeStruct((items, 2, NEAR), F32),
            jax.ShapeDtypeStruct(moved.shape, moved.dtype),
        ],
        compiler_params=pltpu.CompilerParams(vmem_limit_bytes=60 * 2**20),
        cost_estimate=pl.CostEstimate(flops=items * tokens * tokens * 1280, bytes_accessed=items * tokens * 4096, transcendentals=items * tokens * tokens * 2),
        name="attention_backward",
    )(lengths, place, qkv, outs, aug, grads, rows, layer, after)


VPAD = 384
PAIRS = 6
TN = (((0,), (0,)), ((), ()))
SQRT_2_OVER_PI = 0.7978845608028654


def block_masks(masks, first_byte, total_bytes):
    shape = masks.shape[2:]
    conv_at = first_byte - 2 + lax.broadcasted_iota(jnp.int32, shape, 1)
    token = lax.broadcasted_iota(jnp.int32, shape, 0)
    for side in range(2):
        place = first_byte + 2 * token + side
        for size in range(1, 5):
            start = (place // size) * size
            inside = (conv_at >= start) & (conv_at < start + size) & (conv_at < total_bytes)
            masks[side, size - 1] = jnp.where(inside, 1.0 / size, 0.0)


def split_two(values):
    high = values.astype(BF16)
    return high, (values - high.astype(F32)).astype(BF16)


def permute_weight(weight, out):
    rows = weight.shape[0]
    low = lax.broadcasted_iota(jnp.int32, (rows, 128), 1) < 64
    for pair in range(PAIRS):
        at = pair * 384
        one, two, three = (weight[:, at + 128 * k : at + 128 * k + 128] for k in range(3))
        out[:, at : at + 128] = jnp.where(low, one, two)
        out[:, at + 128 : at + 256] = pltpu.roll(jnp.where(low, three, one).astype(F32), 64, 1).astype(BF16)
        out[:, at + 256 : at + 384] = jnp.where(low, two, three)


def greet(axis, here, count):
    barrier = pltpu.get_barrier_semaphore()

    def signal(step, unused):
        pl.semaphore_signal(barrier, inc=1, device_id={axis: lax.rem(here + step, count)}, device_id_type=pl.DeviceIdType.MESH)
        return unused

    lax.fori_loop(1, count, signal, 0)


def item_copy(devices, me, source, target, other, slot, sems):
    send, recv, unused = sems

    def outward():
        offset = lax.rem(other - me + devices, devices)
        return pltpu.make_async_remote_copy(
            src_ref=source, dst_ref=target, send_sem=send.at[offset, slot], recv_sem=recv.at[offset, slot],
            device_id={"seq": other}, device_id_type=pl.DeviceIdType.MESH,
        )

    def inward():
        offset = lax.rem(me - other + devices, devices)
        return pltpu.make_async_remote_copy(
            src_ref=source, dst_ref=target, send_sem=send.at[offset, slot], recv_sem=recv.at[offset, slot],
            device_id={"seq": other}, device_id_type=pl.DeviceIdType.MESH,
        )

    return outward, inward


def start_item(devices, me, source, target, other, slot, sems):
    @pl.when(other == me)
    def _():
        pltpu.make_async_copy(source, target, sems[2].at[slot]).start()

    @pl.when(other != me)
    def _():
        item_copy(devices, me, source, target, other, slot, sems)[0]().start()


def finish_sends(devices, me, total, source_of, target_of, sems):
    def wait(item, unused):
        other, slot = lax.rem(item, devices), item // devices

        @pl.when(other != me)
        def _():
            item_copy(devices, me, source_of(other, slot), target_of(other, slot), other, slot, sems)[0]().wait_send()

        return unused

    lax.fori_loop(0, total, wait, 0)


def finish_receives(devices, me, total, source_of, target_of, sems):
    per_device = -(-total // devices)

    def wait(at, unused):
        other, slot = at // per_device, lax.rem(at, per_device)

        @pl.when((slot * devices + me < total) & (other != me))
        def _():
            item_copy(devices, me, source_of(other, slot), target_of(other, slot), other, slot, sems)[1]().wait_recv()

        @pl.when((slot * devices + me < total) & (other == me))
        def _():
            pltpu.make_async_copy(source_of(other, slot), target_of(other, slot), sems[2].at[slot]).wait()

        return unused

    lax.fori_loop(0, devices * per_device, wait, 0)


def ranks_of(lengths_ref):
    count = lengths_ref.shape[0]
    ranks = []
    for one in range(count):
        rank = jnp.int32(0)
        for two in range(count):
            if two != one:
                ahead = lengths_ref[two] > lengths_ref[one] if two > one else lengths_ref[two] >= lengths_ref[one]
                rank = rank + ahead.astype(jnp.int32)
        ranks.append(rank)
    return ranks


def spread_ids(lengths_ref, ids_ref, from_left, from_right, extended, sems, me, devices):
    sequences, local_bytes = ids_ref.shape
    left_copy = pltpu.make_async_remote_copy(
        src_ref=ids_ref.at[:, 0:128], dst_ref=from_right, send_sem=sems.at[0], recv_sem=sems.at[1],
        device_id={"seq": jnp.maximum(me - 1, 0)}, device_id_type=pl.DeviceIdType.MESH,
    )
    right_copy = pltpu.make_async_remote_copy(
        src_ref=ids_ref.at[:, local_bytes - 128 : local_bytes], dst_ref=from_left, send_sem=sems.at[2], recv_sem=sems.at[3],
        device_id={"seq": jnp.minimum(me + 1, devices - 1)}, device_id_type=pl.DeviceIdType.MESH,
    )

    @pl.when(me > 0)
    def _():
        left_copy.start()

    @pl.when(me < devices - 1)
    def _():
        right_copy.start()

    @pl.when(me > 0)
    def _():
        left_copy.wait_send()
        right_copy.wait_recv()

    @pl.when(me < devices - 1)
    def _():
        right_copy.wait_send()
        left_copy.wait_recv()

    joined = jnp.concatenate([from_left[...], ids_ref[...], from_right[...]], axis=1).astype(F32)
    width = joined.shape[1]
    moved = pltpu.roll(joined, width - 124, 1)
    row = lax.broadcasted_iota(jnp.int32, (sequences, width), 0)
    lane = lax.broadcasted_iota(jnp.int32, (sequences, width), 1)
    position = me * local_bytes - 4 + lane
    length = jnp.zeros((sequences, width), jnp.int32)
    for one in range(sequences):
        length = jnp.where(row == one, lengths_ref[one], length)
    outside = (position < 0) | (position >= local_bytes * devices) | (lane >= local_bytes + 8)
    picked = jnp.where(outside, -1.0, jnp.where(position < length, moved, 0.0))
    ordered = jnp.zeros((sequences, width), F32)
    for one, rank in enumerate(ranks_of(lengths_ref)):
        ordered = jnp.where(row == rank, picked[one : one + 1, :], ordered)
    extended[...] = ordered


def front_kernel(
    sizes, lengths_ref, ids_ref, table_ref, weight_source, vectors_ref,
    hidden_ref, normed_ref, conv_ref, mix_ref, share_ref, rows_ref, items_ref,
    masks, wide, permuted, stage, taps, from_left, from_right, extended, side_sems, weight_ref, weight_sem, *sems,
):
    local_tokens, window, devices, total = sizes
    step = pl.program_id(0)
    me = lax.axis_index("seq")

    @pl.when(step == 0)
    def _():
        pltpu.make_async_copy(weight_source, weight_ref, weight_sem).start()
        from_left[...] = jnp.zeros_like(from_left)
        from_right[...] = jnp.zeros_like(from_right)
        greet("seq", me, devices)
        block_masks(masks, me * 2 * local_tokens, devices * 2 * local_tokens)
        table = table_ref[...].astype(F32)
        taps[...] = jnp.zeros_like(taps)
        for tap in range(5):
            taps[tap, 0 : table.shape[0], :] = (vectors_ref[tap : tap + 1, :] * table).astype(BF16)
        pltpu.make_async_copy(weight_source, weight_ref, weight_sem).wait()
        permute_weight(weight_ref, permuted)
        pl.semaphore_wait(pltpu.get_barrier_semaphore(), devices - 1)
        spread_ids(lengths_ref, ids_ref, from_left, from_right, extended, side_sems, me, devices)

    together = 1
    width_ids = extended.shape[1]
    row = jnp.broadcast_to(extended[pl.ds(step, 1), :], (8, width_ids))
    rows = pltpu.roll(pltpu.roll(row, width_ids - 4, 1), 0, 1, stride=1, stride_axis=0)
    rows_ref[0] = rows
    ids = rows.T[0:window]
    score = vectors_ref[7:8, :]
    gain = vectors_ref[5:6, :]
    model = score.shape[1]
    score_high, score_low = split_two(score)
    row16 = lax.broadcasted_iota(jnp.int32, (16, model), 0)
    score_rows = jnp.where(row16 == 0, score_high.astype(F32), jnp.where(row16 == 1, score_low.astype(F32), 0.0)).astype(BF16)
    lane = lax.broadcasted_iota(jnp.int32, (together * window, VPAD), 1).astype(F32)
    width = masks.shape[3]
    conv_all = jnp.zeros((together * window, model), F32)
    for tap in range(5):
        hot = jnp.where(ids[:, 4 - tap : 5 - tap] == lane, 1.0, 0.0).astype(BF16)
        conv_all = conv_all + dot(hot, taps[tap], NN)
    for one in range(together):
        high, low = split_two(conv_all[one * window : (one + 1) * window])
        conv_ref[one, 0:window] = high
        wide[one, 0, 0:window] = high
        wide[one, 1, 0:window] = low
        if width > window:
            wide[one, :, window:width] = jnp.zeros((2, width - window, model), BF16)
            conv_ref[one, window:width] = jnp.zeros((width - window, model), BF16)
        high = wide[one, 0]
        low = wide[one, 1]
        along = jnp.sum(dot(score_rows, high, NT), axis=0, keepdims=True) + dot(score_rows, low, NT)[0:1]
        mixed = jnp.zeros((local_tokens, width), F32)
        kept = jnp.zeros((local_tokens, 128), F32)
        lane128 = lax.broadcasted_iota(jnp.int32, (local_tokens, 128), 1)
        for side in range(2):
            scores = [jnp.sum(masks[side, k] * along, axis=1, keepdims=True) for k in range(4)]
            top = jnp.maximum(jnp.maximum(scores[0], scores[1]), jnp.maximum(scores[2], scores[3]))
            powers = [jnp.exp(value - top) for value in scores]
            under = 1.0 / (powers[0] + powers[1] + powers[2] + powers[3])
            for k in range(4):
                share = powers[k] * under
                mixed = mixed + share * masks[side, k]
                kept = jnp.where(lane128 == 4 * side + k, share, kept)
        share_ref[one] = kept
        mix_high, mix_low = split_two(mixed * 0.5)
        mix_ref[one] = mix_high
        hidden = dot(mix_high, high, NN) + dot(mix_high, low, NN) + dot(mix_low, high, NN)
        hidden_ref[one] = hidden
        scale = lax.rsqrt(jnp.mean(hidden * hidden, axis=1, keepdims=True) + 1e-06)
        normed_ref[one] = (hidden * scale * gain).astype(BF16)
    normed = normed_ref[...].reshape(together * local_tokens, model)
    for pair in range(PAIRS):
        piece = dot(normed, permuted[:, pair * 384 : pair * 384 + 384], NN).astype(BF16)
        for one in range(together):
            item = (step * together + one) * PAIRS + pair
            other, slot = lax.rem(item, devices), item // devices
            stage[other, slot] = piece[one * local_tokens : (one + 1) * local_tokens]

    if devices == 8:

        def send(at, unused):
            item = step * PAIRS + at
            other, slot = lax.rem(item, 8), item // 8

            @pl.when(other != me)
            def _():
                to_device(other, stage.at[other, slot], items_ref.at[me, slot], sems[0].at[0], sems[1].at[0]).start()

            return unused

        lax.fori_loop(0, PAIRS, send, 0)

        @pl.when(step == pl.num_programs(0) - 1)
        def _():
            finish_back(me, stage, items_ref, sems)

        return
    send_items(devices, me, step * together * PAIRS, together * PAIRS, stage, items_ref, sems)

    @pl.when(step == pl.num_programs(0) - 1)
    def _():
        finish_sends(devices, me, total, lambda other, slot: stage.at[other, slot], lambda other, slot: items_ref.at[me, slot], sems)
        finish_receives(devices, me, total, lambda other, slot: stage.at[other, slot], lambda other, slot: items_ref.at[other, slot], sems)


def to_device(other, source, target, send, recv):
    return pltpu.make_async_remote_copy(
        src_ref=source, dst_ref=target, send_sem=send, recv_sem=recv, device_id={"seq": other}, device_id_type=pl.DeviceIdType.MESH
    )


SLOT_GROUPS = ((0, 2), (2, 1), (3, 2), (5, 1))


def send_slots(me, number, source, arrived, sems):
    first, count = SLOT_GROUPS[number]
    slots = pl.ds(first, count)

    def send(offset, unused):
        other = lax.rem(me + offset, 8)
        to_device(other, source.at[other, slots], arrived.at[me, slots], sems[0].at[number], sems[1].at[number]).start()
        return unused

    lax.fori_loop(1, 8, send, 0)
    pltpu.make_async_copy(source.at[me, slots], arrived.at[me, slots], sems[2].at[number]).start()


def wait_slots(me, number, source, arrived, sems, sends):
    first, count = SLOT_GROUPS[number]
    slots = pl.ds(first, count)
    seven = pl.ds(0, 7)
    copies = to_device(lax.rem(me + 1, 8), source.at[seven, slots], arrived.at[seven, slots], sems[0].at[number], sems[1].at[number])
    if sends:
        copies.wait_send()
    else:
        copies.wait_recv()
        pltpu.make_async_copy(source.at[me, slots], arrived.at[me, slots], sems[2].at[number]).wait()


def send_back(me, step, stage, target, sems):
    base, base_to = 3, 0
    for parity in range(2):

        def send(offset, unused):
            other = lax.rem(me + offset, 8)

            @pl.when(other < 4)
            def _():
                first, count = (0, 2) if parity == 0 else (2, 1)
                to_device(other, stage.at[other, pl.ds(base + first, count)], target.at[me, pl.ds(base_to + first, count)], sems[0].at[0], sems[1].at[0]).start()

            @pl.when(other >= 4)
            def _():
                first, count = (0, 1) if parity == 0 else (1, 2)
                to_device(other, stage.at[other, pl.ds(base + first, count)], target.at[me, pl.ds(base_to + first, count)], sems[0].at[0], sems[1].at[0]).start()

            return unused

        @pl.when(lax.rem(step, 2) == parity)
        def _():
            lax.fori_loop(1, 8, send, 0)


def finish_half(me, stage, target, sems):
    slots = pl.ds(3, 3)
    local = pltpu.make_async_copy(stage.at[me, slots], target.at[me], sems[2].at[0])
    local.start()
    seven = pl.ds(0, 7)
    copies = to_device(lax.rem(me + 1, 8), stage.at[seven, slots], target.at[seven], sems[0].at[0], sems[1].at[0])
    copies.wait_send()
    copies.wait_recv()
    local.wait()


def finish_back(me, stage, target, sems):
    local = pltpu.make_async_copy(stage.at[me], target.at[me], sems[2].at[0])
    local.start()
    seven = pl.ds(0, 7)
    copies = to_device(lax.rem(me + 1, 8), stage.at[seven], target.at[seven], sems[0].at[0], sems[1].at[0])
    copies.wait_send()
    copies.wait_recv()
    local.wait()


def send_group(devices, me, total, group, number, source, arrived, sems):
    for slot in range(-(-total // devices)):
        item = slot * devices + me

        @pl.when((item < total) & (item // group == number))
        def _():
            def send(offset, unused):
                other = lax.rem(me + offset, devices)
                start_item(devices, me, source.at[other, slot], arrived.at[me, slot], other, slot, sems)
                return unused

            lax.fori_loop(0, devices, send, 0)


def send_items(devices, me, first, count, stage, target, sems):
    def send(at, unused):
        item = first + at
        other, slot = lax.rem(item, devices), item // devices
        start_item(devices, me, stage.at[other, slot], target.at[me, slot], other, slot, sems)
        return unused

    lax.fori_loop(0, count, send, 0)


def take_items(devices, me, first, count, source, arrived, sems):
    def take(at, unused):
        item = first + at
        take_item(devices, me, lax.rem(item, devices), item // devices, source, arrived, sems)
        return unused

    lax.fori_loop(0, count, take, 0)


def finish_groups(devices, me, total, source, arrived, sems):
    per_device = -(-total // devices)

    def wait(at, unused):
        slot, offset = at // devices, lax.rem(at, devices)
        other = lax.rem(me + offset, devices)

        @pl.when((slot * devices + me < total) & (offset != 0))
        def _():
            item_copy(devices, me, source.at[other, slot], arrived.at[me, slot], other, slot, sems)[0]().wait_send()

        return unused

    lax.fori_loop(0, devices * per_device, wait, 0)


def take_item(devices, me, other, slot, source, arrived, sems):
    @pl.when(other == me)
    def _():
        pltpu.make_async_copy(source.at[me, slot], arrived.at[me, slot], sems[2].at[slot]).wait()

    @pl.when(other != me)
    def _():
        item_copy(devices, me, source.at[other, slot], arrived.at[other, slot], other, slot, sems)[1]().wait_recv()


def mid_kernel(
    sizes, att_ref, hidden_ref, cot_ref, out_weight_ref, in_source, down_ref, vectors_ref,
    layer_ref, act_ref, gate_up_ref, normed_ref, attended_ref, branch_ref, residual_ref, items_ref, gain_out, rest_ref,
    arrived, stage, keep_gain, grad_act, in_weight_ref, in_sem, *sems,
):
    local_tokens, devices, total = sizes
    in_sems, out_sems = sems[:3], sems[3:]
    step = pl.program_id(0)
    me = lax.axis_index("seq")

    @pl.when(step == 0)
    def _():
        greet("seq", me, devices)
        pltpu.make_async_copy(in_source, in_weight_ref, in_sem).start()
        keep_gain[...] = jnp.zeros_like(keep_gain)
        pl.semaphore_wait(pltpu.get_barrier_semaphore(), devices - 1)

    together = hidden_ref.shape[0]
    group = together * PAIRS
    turn = lax.rem(step + 2, 4) if devices == 8 else step
    rows = together * local_tokens
    model = vectors_ref.shape[1]

    here_rows = pl.ds(pl.multiple_of(turn * rows, 128), rows)

    @pl.when(step == 0)
    def _():
        if devices == 8:
            for number in (2, 3, 0, 1):
                send_slots(me, number, att_ref, arrived, in_sems)
        else:
            send_group(devices, me, total, group, 0, att_ref, arrived, in_sems)
        every = cot_ref[...].reshape(grad_act.shape[0], model)
        for first in range(0, down_ref.shape[0], 512):
            grad_act[:, first : first + 512] = dot(every, down_ref[first : first + 512, :], NT)
        pltpu.make_async_copy(in_source, in_weight_ref, in_sem).wait()

    if devices == 8:
        for number in range(4):

            @pl.when(turn == number)
            def _():
                wait_slots(me, number, att_ref, arrived, in_sems, False)

    else:
        take_items(devices, me, step * group, group, att_ref, arrived, in_sems)

        @pl.when(step + 1 < pl.num_programs(0))
        def _():
            send_group(devices, me, total, group, step + 1, att_ref, arrived, in_sems)

    gathered = []
    for one in range(together):
        pieces = []
        for pair in range(PAIRS):
            item = (turn * together + one) * PAIRS + pair
            other, slot = lax.rem(item, devices), item // devices
            pieces.append(arrived[other, slot])
        gathered.append(jnp.concatenate(pieces, axis=1))
    attended = jnp.concatenate(gathered, axis=0)
    attended_ref[...] = attended.reshape(attended_ref.shape)
    residual = hidden_ref[...].reshape(rows, model) + dot(attended, out_weight_ref[...], NN)
    gain = vectors_ref[6:7, :]
    scale = lax.rsqrt(jnp.mean(residual * residual, axis=1, keepdims=True) + 1e-06)
    normed = (residual * scale * gain).astype(BF16)
    normed_ref[...] = normed.reshape(normed_ref.shape)
    cot = cot_ref[pl.ds(turn * together, together)].reshape(rows, model)
    hidden_units = down_ref.shape[0]
    chunk = 512
    layer = residual
    back = jnp.zeros_like(residual)
    for first in range(0, hidden_units, chunk):
        here = slice(first, first + chunk)
        there = slice(hidden_units + first, hidden_units + first + chunk)
        gate = dot(normed, in_weight_ref[:, here], NN)
        up = dot(normed, in_weight_ref[:, there], NN)
        grad = grad_act[here_rows, here]
        square = gate * gate
        inner = gate * (SQRT_2_OVER_PI + (SQRT_2_OVER_PI * 0.044715) * square)
        curve = jnp.tanh(inner)
        half_plus = 0.5 + 0.5 * curve
        smooth = gate * half_plus
        slope = half_plus + (0.5 * gate) * (1.0 - curve * curve) * (SQRT_2_OVER_PI + (3 * SQRT_2_OVER_PI * 0.044715) * square)
        act = (smooth * up).astype(BF16)
        grad_gate = (grad * up * slope).astype(BF16)
        grad_up = (grad * smooth).astype(BF16)
        act_ref[:, :, here] = act.reshape(together, local_tokens, chunk)
        gate_up_ref[:, :, here] = grad_gate.reshape(together, local_tokens, chunk)
        gate_up_ref[:, :, there] = grad_up.reshape(together, local_tokens, chunk)
        layer = layer + dot(act, down_ref[here, :], NN)
        back = back + dot(grad_gate, in_weight_ref[:, here], NT) + dot(grad_up, in_weight_ref[:, there], NT)
    layer_ref[...] = layer.reshape(layer_ref.shape)
    weighted = gain * back
    inner_mean = jnp.mean(residual * weighted, axis=1, keepdims=True)
    grad_residual = cot.astype(F32) + scale * weighted - residual * (scale * scale * scale * inner_mean)
    residual_ref[...] = grad_residual.reshape(residual_ref.shape)
    branch = grad_residual.astype(BF16)
    branch_ref[...] = branch.reshape(branch_ref.shape)
    grad_attended = dot(branch, out_weight_ref[...], NT).astype(BF16)
    for one in range(together):
        for pair in range(PAIRS):
            item = (turn * together + one) * PAIRS + pair
            other, slot = lax.rem(item, devices), item // devices
            stage[other, slot] = grad_attended[one * local_tokens : (one + 1) * local_tokens, pair * 128 : pair * 128 + 128]
    keep_gain[...] += jnp.sum((back * residual * scale).reshape(rows // 8, 8, model), axis=0)
    gain_out[...] = jnp.sum(keep_gain[...], axis=0, keepdims=True)
    if devices == 8:
        @pl.when(step < 2)
        def _():
            send_back(me, turn, stage, items_ref, out_sems)

        @pl.when(step == 3)
        def _():
            for number in range(4):
                wait_slots(me, number, att_ref, arrived, in_sems, True)
            finish_half(me, stage, items_ref, out_sems)
            rest_ref[...] = stage[:, 0:3]

        return
    send_items(devices, me, step * group, group, stage, items_ref, out_sems)

    @pl.when(step == pl.num_programs(0) - 1)
    def _():
        finish_groups(devices, me, total, att_ref, arrived, in_sems)
        finish_sends(devices, me, total, lambda other, slot: stage.at[other, slot], lambda other, slot: items_ref.at[me, slot], out_sems)
        finish_receives(devices, me, total, lambda other, slot: stage.at[other, slot], lambda other, slot: items_ref.at[other, slot], out_sems)


def back_kernel(
    sizes, custom, one_ref, two_ref, hidden_ref, residual_ref, conv_ref, mix_ref, share_ref, ids_ref, weight_source,
    table_ref, vectors_ref, bias_ref, bias_hot_ref, gain_two_ref, *refs,
):
    local_tokens, window, devices = sizes
    step = pl.program_id(0)
    last = step == pl.num_programs(0) - 1
    me = lax.axis_index("seq")
    plane = lax.axis_index("dp")
    model = vectors_ref.shape[1]
    if custom:
        normed_ref, across_ref, planes_ref = refs[:3]
        block, qkv_out, in_out, down_out, weight_out = refs[3:8]
        refs = refs[8:]
    else:
        block, flat_out, refs = refs[0], refs[1], refs[2:]
    masks, permuted, tap_sums, keep_gain, keep_score, weight_ref, weight_sem = refs[:7]
    refs = refs[7:]
    small = SmallSums(block, refs[:4], refs[4:10])
    refs = refs[10:]

    @pl.when(step == 0)
    def _():
        pltpu.make_async_copy(weight_source, weight_ref, weight_sem).start()
        greet("seq", me, devices)
        greet("dp", plane, small.along)
        keep_gain[...] = jnp.zeros_like(keep_gain)
        keep_score[...] = jnp.zeros_like(keep_score)
        tap_sums[...] = jnp.zeros_like(tap_sums)
        pl.semaphore_wait(pltpu.get_barrier_semaphore(), devices + small.along - 2)

    half = one_ref.shape[1]

    def block_of(item):
        other, slot = lax.rem(item, devices), item // devices
        if isinstance(item, int):
            return (one_ref if slot < half else two_ref)[other, slot % half]
        return jnp.where(slot < half, one_ref[other, jnp.minimum(slot, half - 1)], two_ref[other, jnp.maximum(slot - half, 0)])

    if custom:
        reduce = WeightSums(normed_ref, across_ref, planes_ref, block_of, refs)

        @pl.when(step == 0)
        def _():
            reduce.begin()
            reduce.late()

        @pl.when(step == 2)
        def _():
            reduce.late_one()

        @pl.when(step == 3)
        def _():
            reduce.in_three()
            reduce.rest_two()

    @pl.when(step == 0)
    def _():
        block_masks(masks, me * 2 * local_tokens, devices * 2 * local_tokens)
        pltpu.make_async_copy(weight_source, weight_ref, weight_sem).wait()
        permute_weight(weight_ref, permuted)

    together = hidden_ref.shape[0]
    rows = together * local_tokens
    projected = jnp.concatenate(
        [
            jnp.concatenate([block_of((step * together + one) * PAIRS + pair) for pair in range(PAIRS)], axis=1)
            for one in range(together)
        ],
        axis=0,
    )
    if not custom:
        flat_out[...] = projected.reshape(flat_out.shape)
    width = masks.shape[3]
    grad_normed = dot(projected, permuted[...], NT)
    hidden = hidden_ref[...].reshape(rows, model)
    gain = vectors_ref[5:6, :]
    score = vectors_ref[7:8, :]
    scale = lax.rsqrt(jnp.mean(hidden * hidden, axis=1, keepdims=True) + 1e-06)
    weighted = gain * grad_normed
    inner_mean = jnp.mean(hidden * weighted, axis=1, keepdims=True)
    grad_hidden = residual_ref[...].reshape(rows, model) + scale * weighted - hidden * (scale * scale * scale * inner_mean)
    keep_gain[...] += jnp.sum((grad_normed * hidden * scale).reshape(rows // 8, 8, model), axis=0)
    high_all, low_all = split_two(grad_hidden)
    vector = jnp.broadcast_to(score.astype(BF16), (local_tokens, model))
    row16 = lax.broadcasted_iota(jnp.int32, (16, width), 0)
    slopes = []
    for one in range(together):
        if custom and one == 1:

            @pl.when(step == 1)
            def _():
                reduce.in_two()

            @pl.when(last)
            def _():
                reduce.late_two()

        own = slice(one * local_tokens, (one + 1) * local_tokens)
        high, low = high_all[own], low_all[own]
        conv = conv_ref[one]
        cross = 0.5 * (dot(high, conv, NT) + dot(low, conv, NT))
        kept = share_ref[one]
        total = jnp.zeros((local_tokens, width), F32)
        for side in range(2):
            shares = [kept[:, 4 * side + k : 4 * side + k + 1] for k in range(4)]
            grads = [jnp.sum(masks[side, k] * cross, axis=1, keepdims=True) for k in range(4)]
            mean = sum(share * grad for share, grad in zip(shares, grads))
            for k in range(4):
                total = total + (shares[k] * (grads[k] - mean)) * masks[side, k]
        column = jnp.sum(total, axis=0, keepdims=True)
        column_high, column_low = split_two(column)
        column_rows = jnp.where(row16 == 0, column_high.astype(F32), jnp.where(row16 == 1, column_low.astype(F32), 0.0)).astype(BF16)
        keep_score[...] += dot(column_rows, conv, NN)
        left = jnp.concatenate([mix_ref[one], total.astype(BF16)], axis=0)
        right = jnp.concatenate([high, vector], axis=0)
        slopes.append(dot(left, right, TN)[0:window].astype(BF16))
    slope = jnp.concatenate(slopes, axis=0)
    row = lax.broadcasted_iota(jnp.int32, (SMALL_ROWS, window), 0).astype(F32)
    for tap in range(5):
        hot = jnp.concatenate(
            [jnp.where(ids_ref[one, 4 - tap : 5 - tap, 0:window] == row, 1.0, 0.0).astype(BF16) for one in range(together)], axis=1
        )
        tap_sums[tap] += dot(hot, slope, NN)

    @pl.when(last)
    def _():
        table_grad = jnp.zeros((SMALL_ROWS, model), F32)
        table = table_ref[...].astype(F32)
        place = lax.broadcasted_iota(jnp.int32, (SMALL_ROWS, model), 0)
        extra = []
        for tap in range(5):
            sums = tap_sums[tap]
            table_grad = table_grad + vectors_ref[tap : tap + 1, :] * sums
            extra.append(jnp.sum(sums[0 : table.shape[0]] * table, axis=0, keepdims=True))
        extra.append(jnp.sum(keep_gain[...], axis=0, keepdims=True))
        extra.append(jnp.sum(keep_score[...], axis=0, keepdims=True))
        extra.append(gain_two_ref[...])
        for index, value in enumerate(extra):
            table_grad = jnp.where(place == 259 + index, value, table_grad)
        block[...] = table_grad
        heads = jnp.zeros((16, 128), F32)
        head_row = lax.broadcasted_iota(jnp.int32, (16, 128), 0)
        for slot in range(bias_ref.shape[0]):
            first, second = split_two(bias_ref[slot])
            sums = dot(first, bias_hot_ref[...], NN) + dot(second, bias_hot_ref[...], NN)
            pair = lax.rem(slot * devices + me, PAIRS)
            heads = heads + jnp.where(head_row == 2 * pair, sums[0:1], 0.0) + jnp.where(head_row == 2 * pair + 1, sums[1:2], 0.0)
        block[272:288, 0:128] = heads
        small.pack()
        small.one_start()
        small.one_middle()
        small.one_finish()
        if custom:
            reduce.late_three()
            reduce.finish_rest(down_out)
        small.two_finish()
        small.three_finish()
        if custom:
            reduce.finish_in(in_out, weight_out)
            reduce.finish_late(qkv_out)
        small.four_finish()


def finish_kernel(block, *refs):
    refs = list(refs)
    count = (len(refs) - 6) // 2
    for source, target in zip(refs[:count], refs[count : 2 * count]):
        target[...] = source[...]
    table_out, taps_out, one_out, score_out, two_out, bias_out = refs[2 * count :]
    table_out[...] = block[0:259, :]
    taps_out[...] = block[259:264, :]
    one_out[...] = block[264, :]
    score_out[...] = block[265, :]
    two_out[...] = block[266, :]
    bias_out[...] = block[272:284, 0:32]


def call_finish(block, sums):
    model = block.shape[1]
    shape = lambda *dims: jax.ShapeDtypeStruct(dims, F32)
    return pl.pallas_call(
        finish_kernel,
        out_shape=[shape(*x.shape) for x in sums] + [shape(259, model), shape(5, model), shape(model), shape(model), shape(model), shape(12, 32)],
        compiler_params=pltpu.CompilerParams(vmem_limit_bytes=VMEM_LIMIT),
        name="finish",
    )(block, *sums)


VMEM_LIMIT = 60 * 2**20
TOGETHER = 2


def item_sems(devices, per_device):
    dma = pltpu.SemaphoreType.DMA
    if devices == 8:
        return [dma((4,)), dma((4,)), dma((4,))]
    return [dma((devices, per_device)), dma((devices, per_device)), dma((per_device,))]


def whole(*shape):
    return pl.BlockSpec(shape, lambda s, *_: (0,) * len(shape), pipeline_mode=pl.Buffered(1))


def part(*shape):
    return pl.BlockSpec(shape, lambda s, *_: (s,) + (0,) * (len(shape) - 1))


ANYWHERE = pl.BlockSpec(memory_space=pl.ANY)


def remote_params(number):
    return pltpu.CompilerParams(vmem_limit_bytes=VMEM_LIMIT, collective_id=number, has_side_effects=True)


def call_front(lengths, ids, table, weight, vectors, devices, per_device):
    sequences, local_bytes = ids.shape
    local_tokens = local_bytes // 2
    window = local_bytes + 16
    width = -(-window // 128) * 128
    model = weight.shape[0]
    return pl.pallas_call(
        functools.partial(front_kernel, (local_tokens, window, devices, sequences * PAIRS)),
        grid=(sequences,),
        in_specs=[pl.BlockSpec(memory_space=pltpu.SMEM), whole(*ids.shape), whole(*table.shape), ANYWHERE, whole(*vectors.shape)],
        out_specs=[
            part(1, local_tokens, model),
            part(1, local_tokens, model),
            part(1, width, model),
            part(1, local_tokens, width),
            part(1, local_tokens, 128),
            part(1, 8, local_bytes + 256),
            ANYWHERE,
        ],
        scratch_shapes=[
            pltpu.VMEM((2, 4, local_tokens, width), F32),
            pltpu.VMEM((1, 2, width, model), BF16),
            pltpu.VMEM(weight.shape, BF16),
            pltpu.VMEM((devices, per_device, local_tokens, 384), BF16),
            pltpu.VMEM((5, VPAD, model), BF16),
            pltpu.VMEM((sequences, 128), jnp.int32),
            pltpu.VMEM((sequences, 128), jnp.int32),
            pltpu.VMEM((sequences, local_bytes + 256), F32),
            pltpu.SemaphoreType.DMA((4,)),
            pltpu.VMEM(weight.shape, BF16),
            pltpu.SemaphoreType.DMA,
        ]
        + item_sems(devices, per_device),
        out_shape=[
            jax.ShapeDtypeStruct((sequences, local_tokens, model), F32),
            jax.ShapeDtypeStruct((sequences, local_tokens, model), BF16),
            jax.ShapeDtypeStruct((sequences, width, model), BF16),
            jax.ShapeDtypeStruct((sequences, local_tokens, width), BF16),
            jax.ShapeDtypeStruct((sequences, local_tokens, 128), F32),
            jax.ShapeDtypeStruct((sequences, 8, local_bytes + 256), F32),
            jax.ShapeDtypeStruct((devices, per_device, local_tokens, 384), BF16),
        ],
        compiler_params=remote_params(3),
        cost_estimate=pl.CostEstimate(flops=5 * 10**10, bytes_accessed=2 * 10**7, transcendentals=10**5),
        name="front",
    )(lengths, ids, table, weight, vectors)


def call_mid(att, hidden, cot, out_weight, in_weight, down_weight, vectors):
    devices, per_device, local_tokens, unused = att.shape
    sequences, unused, model = hidden.shape
    hidden_units = down_weight.shape[0]
    fast = devices == 8
    rows = lambda lanes: pl.BlockSpec((TOGETHER, local_tokens, lanes), lambda s: (lax.rem(s + 2, 4) if fast else s, 0, 0))
    shape = (devices, per_device // 2 if fast else per_device, local_tokens, 128)
    rest = shape if fast else (1, 1, 8, 128)
    full = lambda lanes, kind: jax.ShapeDtypeStruct((sequences, local_tokens, lanes), kind)
    return pl.pallas_call(
        functools.partial(mid_kernel, (local_tokens, devices, sequences * PAIRS)),
        grid=(sequences // TOGETHER,),
        in_specs=[
            ANYWHERE,
            rows(model),
            whole(*cot.shape),
            whole(*out_weight.shape),
            ANYWHERE,
            whole(*down_weight.shape),
            whole(*vectors.shape),
        ],
        out_specs=[
            rows(model),
            rows(hidden_units),
            rows(2 * hidden_units),
            rows(model),
            rows(model),
            rows(model),
            rows(model),
            ANYWHERE,
            whole(1, model),
            whole(*rest),
        ],
        scratch_shapes=[pltpu.VMEM(att.shape, BF16), pltpu.VMEM(att.shape, BF16), pltpu.VMEM((8, model), F32), pltpu.VMEM((sequences * local_tokens, hidden_units), F32),
            pltpu.VMEM(in_weight.shape, BF16),
            pltpu.SemaphoreType.DMA,
        ]
        + item_sems(devices, per_device)
        + item_sems(devices, per_device),
        out_shape=[
            full(model, F32),
            full(hidden_units, BF16),
            full(2 * hidden_units, BF16),
            full(model, BF16),
            full(model, BF16),
            full(model, BF16),
            full(model, F32),
            jax.ShapeDtypeStruct(shape, BF16),
            jax.ShapeDtypeStruct((1, model), F32),
            jax.ShapeDtypeStruct(rest, BF16),
        ],
        compiler_params=remote_params(4),
        cost_estimate=pl.CostEstimate(flops=5 * 10**10, bytes_accessed=4 * 10**7, transcendentals=10**6),
        name="middle",
    )(att, hidden, cot, out_weight, in_weight, down_weight, vectors)


def call_back(custom, one, two, hidden, residual, conv, mix, share, ids, weight, table, vectors, bias_rows, gain_two, along, extra):
    devices, unused, local_tokens, unused = one.shape
    sequences, unused, model = hidden.shape
    width = conv.shape[1]
    window = 2 * local_tokens + 16
    bias_hot = jnp.pad(near_one_hot(), ((0, 0), (0, 96))).astype(BF16)
    out_specs = [whole(SMALL_ROWS, model)]
    out_shape = [jax.ShapeDtypeStruct((SMALL_ROWS, model), F32)]
    scratch = []
    specs = []
    if custom:
        specs = [whole(*x.shape) for x in extra]
        sums = [(96, 576), (96, 1024), (192, 256), (96, 192)]
        out_specs = out_specs + [whole(*shape) for shape in sums]
        out_shape = out_shape + [jax.ShapeDtypeStruct(shape, F32) for shape in sums]
        scratch = weight_scratch(model, sequences * local_tokens)
    else:
        out_specs = out_specs + [part(TOGETHER, local_tokens, PAIRS * 384)]
        out_shape = out_shape + [jax.ShapeDtypeStruct((sequences, local_tokens, PAIRS * 384), BF16)]
    return pl.pallas_call(
        functools.partial(back_kernel, (local_tokens, window, devices), custom),
        grid=(sequences // TOGETHER,),
        in_specs=[
            whole(*one.shape),
            whole(*two.shape),
            part(TOGETHER, local_tokens, model),
            part(TOGETHER, local_tokens, model),
            part(TOGETHER, width, model),
            part(TOGETHER, local_tokens, width),
            part(TOGETHER, local_tokens, 128),
            part(TOGETHER, 8, ids.shape[2]),
            ANYWHERE,
            whole(*table.shape),
            whole(*vectors.shape),
            whole(*bias_rows.shape),
            whole(*bias_hot.shape),
            whole(1, model),
        ]
        + specs,
        out_specs=out_specs,
        scratch_shapes=[
            pltpu.VMEM((2, 4, local_tokens, width), F32),
            pltpu.VMEM(weight.shape, BF16),
            pltpu.VMEM((5, SMALL_ROWS, model), F32),
            pltpu.VMEM((8, model), F32),
            pltpu.VMEM((16, model), F32),
            pltpu.VMEM(weight.shape, BF16),
            pltpu.SemaphoreType.DMA,
        ]
        + small_scratch(devices, along)
        + scratch,
        out_shape=out_shape,
        compiler_params=remote_params(5),
        cost_estimate=pl.CostEstimate(flops=10**11, bytes_accessed=2 * 10**7, transcendentals=10**5),
        name="back",
    )(one, two, hidden, residual, conv, mix, share, ids, weight, table, vectors, bias_rows, bias_hot, gain_two, *extra)


IN_ROWS = 8 * 96 + 2 * 96
REST_ROWS = 2 * 192
LATE_ROWS = 5 * 96


def meet_sibling(core):
    barrier = pltpu.get_barrier_semaphore()
    sibling = lax.axis_index("seq") + 1 - 2 * core
    pl.semaphore_signal(barrier, inc=1, device_id={"seq": sibling}, device_id_type=pl.DeviceIdType.MESH)
    pl.semaphore_wait(barrier, 1)


def to_sibling(core, source, target, send_sem, recv_sem):
    sibling = lax.axis_index("seq") + 1 - 2 * core
    return pltpu.make_async_remote_copy(
        src_ref=source, dst_ref=target, send_sem=send_sem, recv_sem=recv_sem,
        device_id={"seq": sibling}, device_id_type=pl.DeviceIdType.MESH,
    )


def spread_rows(core, source, lanes, keep_ref, send_ref, index_of):
    for chip in range(4):
        for other, ref in ((0, keep_ref), (1, send_ref)):
            device = 2 * chip + lax.rem(core + other, 2)
            rows = pl.ds(pl.multiple_of(device * 96, 32), 96)
            ref[index_of(chip)] = source[rows, lanes]


def early_kernel(
    act_ref, cot_ref, normed_ref, gate_up_ref, attended_ref, branch_ref, after, keep_in, keep_rest,
    other_in, got_in, other_rest, got_rest, cot_t, normed_t, result, send_in, recv_in, send_down, recv_down, send_out, recv_out,
):
    step = pl.program_id(0)
    core = lax.rem(lax.axis_index("seq"), 2)
    model = cot_t.shape[0]
    tokens = cot_t.shape[1]
    out_rows = pl.ds(768, 192)
    out_copy = to_sibling(core, other_in.at[:, :, out_rows], got_in.at[:, :, out_rows], send_out, recv_out)

    def in_copy(at):
        rows = pl.ds(pl.multiple_of(384 * lax.rem(at, 2), 384), 384)
        return to_sibling(core, other_in.at[:, at // 2, rows], got_in.at[:, at // 2, rows], send_in.at[at], recv_in.at[at])

    def down_copy(chip):
        return to_sibling(core, other_rest.at[:, chip], got_rest.at[:, chip], send_down.at[chip], recv_down.at[chip])

    @pl.when(step == 0)
    def _():
        meet_sibling(core)
        cot_t[...] = cot_ref[...].reshape(tokens, model).T
        normed_t[...] = attended_ref[...].reshape(tokens, model).T
        for first in range(0, model, 256):
            result[:, 0:256] = dot(normed_t[...], branch_ref[:, :, first : first + 256].reshape(tokens, 256), NN).astype(BF16)
            for half in range(2):
                tile = first // 128 + half
                for column, slot in {0: ((0, 0),), 1: ((0, 1), (1, 0)), 2: ((1, 1),), 3: ((2, 0),), 4: ((2, 1), (3, 0)), 5: ((3, 1),)}[tile]:
                    rows = slice(768 + 96 * slot, 864 + 96 * slot)
                    spread_rows(core, result, slice(128 * half, 128 * half + 128), keep_in, other_in, lambda chip: (chip, column, rows))
        normed_t[...] = normed_ref[...].reshape(tokens, model).T

    result[...] = dot(normed_t[...], gate_up_ref[...].reshape(tokens, 512), NN).astype(BF16)
    column_at = step // 2
    for quarter in range(4):
        rows = pl.ds(pl.multiple_of((4 * lax.rem(step, 2) + quarter) * 96, 32), 96)
        spread_rows(core, result, slice(128 * quarter, 128 * quarter + 128), keep_in, other_in, lambda chip: (chip, column_at, rows))
    down = dot(cot_t[...], act_ref[...].reshape(tokens, 256), NN).astype(BF16)

    def put_down(ref):
        for column in range(4):
            for half in range(2):
                ref[column, step // 2, 192 * half : 192 * half + 192] = down[192 * column : 192 * column + 192, 128 * half : 128 * half + 128]

    @pl.when(lax.rem(step, 2) == core)
    def _():
        put_down(keep_rest)

    @pl.when(lax.rem(step, 2) != core)
    def _():
        put_down(other_rest)
        down_copy(step // 2).start()

    in_copy(step).start()

    @pl.when(step == 0)
    def _():
        out_copy.start()

    @pl.when(step == 7)
    def _():
        for at in range(8):
            in_copy(at).wait()
        out_copy.wait()
        for chip in range(4):
            down_copy(chip).wait()

        def add(at, unused):
            one, two = at // 4, lax.rem(at, 4)
            keep_in[one, two] = (keep_in[one, two].astype(F32) + got_in[one, two].astype(F32)).astype(BF16)
            keep_rest[one, two] = (keep_rest[one, two].astype(F32) + got_rest[one, two].astype(F32)).astype(BF16)
            return unused

        lax.fori_loop(0, 16, add, 0)


def call_early(act, cot, normed, gate_up, attended, branch, after):
    sequences, local_tokens, model = cot.shape
    tokens = sequences * local_tokens
    every = whole(sequences, local_tokens, model)
    shapes = [(4, 4, IN_ROWS, 128), (4, 4, REST_ROWS, 128)]
    dma = pltpu.SemaphoreType.DMA
    return pl.pallas_call(
        early_kernel,
        grid=(8,),
        in_specs=[
            pl.BlockSpec((sequences, local_tokens, 256), lambda s: (0, 0, s)),
            every,
            every,
            pl.BlockSpec((sequences, local_tokens, 512), lambda s: (0, 0, s)),
            every,
            every,
            ANYWHERE,
        ],
        out_specs=[whole(*shape) for shape in shapes],
        scratch_shapes=[
            pltpu.VMEM(shapes[0], BF16),
            pltpu.VMEM(shapes[0], BF16),
            pltpu.VMEM(shapes[1], BF16),
            pltpu.VMEM(shapes[1], BF16),
            pltpu.VMEM((model, tokens), BF16),
            pltpu.VMEM((model, tokens), BF16),
            pltpu.VMEM((model, 512), BF16),
            dma((8,)), dma((8,)), dma((4,)), dma((4,)), dma, dma,
        ],
        out_shape=[jax.ShapeDtypeStruct(shape, BF16) for shape in shapes],
        compiler_params=pltpu.CompilerParams(vmem_limit_bytes=VMEM_LIMIT, collective_id=1, has_side_effects=True),
        cost_estimate=pl.CostEstimate(flops=11 * 10**9, bytes_accessed=3 * 10**7, transcendentals=0),
        name="early_gradients",
    )(act, cot, normed, gate_up, attended, branch, after)


class ChipSums:
    def __init__(self, source, buffers, sems, chip, core):
        self.source, self.first, self.relay, self.second = (source,) + tuple(buffers)
        self.send, self.recv = sems
        self.chip, self.core = chip, core
        self.beside = chip + 1 - 2 * lax.rem(chip, 2)
        self.above = lax.rem(chip + 2, 4)

    def copy(self, other, source, target, number):
        return pltpu.make_async_remote_copy(
            src_ref=source, dst_ref=target, send_sem=self.send.at[number], recv_sem=self.recv.at[number],
            device_id={"seq": 2 * other + self.core}, device_id_type=pl.DeviceIdType.MESH,
        )

    def ways(self):
        return ((0, self.beside, self.above), (1, self.above, self.beside))

    def one(self):
        made = []
        for way, near, other in self.ways():
            columns = pl.ds(2 * way, 2)
            made.append(self.copy(near, self.source.at[near, columns], self.first.at[way, 0], 2 * way))
            made.append(self.copy(near, self.source.at[3 - self.chip, columns], self.first.at[way, 1], 2 * way + 1))
        return made

    def two(self):
        return [self.copy(other, self.relay.at[way], self.second.at[way], 4 + way) for way, near, other in self.ways()]

    def start(self):
        for copy in self.one():
            copy.start()

    def middle(self):
        for copy in self.one():
            copy.wait()
        for way, near, other in self.ways():
            for at in range(2):
                total = self.source[other, 2 * way + at].astype(F32) + self.first[way, 1, at].astype(F32)
                self.relay[way, at] = total.astype(BF16)
        for copy in self.two():
            copy.start()

    def finish(self, target):
        for copy in self.two():
            copy.wait()
        for way in range(2):
            for at in range(2):
                total = self.source[self.chip, 2 * way + at].astype(F32) + self.first[way, 0, at].astype(F32)
                target[2 * way + at] = (total + self.second[way, at].astype(F32)).astype(BF16)


def chip_scratch(rows):
    return [pltpu.VMEM((2, 2, 2, rows, 128), BF16), pltpu.VMEM((2, 2, rows, 128), BF16), pltpu.VMEM((2, 2, rows, 128), BF16)]


class WeightSums:
    def __init__(self, normed_ref, across_ref, planes_ref, block_of, refs):
        self.normed, self.across, self.planes, self.block_of = normed_ref, across_ref, planes_ref, block_of
        (
            self.in_sum, self.in_got, self.rest_got, self.rest_sum, self.rest_chips, self.normed_t, self.result,
            self.keep, self.other, self.got, self.late_sum, self.late_got,
        ) = refs[:12]
        (
            self.send_in, self.recv_in, self.send_rest, self.recv_rest, self.send_chip, self.recv_chip,
            self.send_a, self.recv_a, self.send_c, self.recv_c,
        ) = refs[18:28]
        self.me, self.plane = lax.axis_index("seq"), lax.axis_index("dp")
        self.core, self.chip = lax.rem(self.me, 2), self.me // 2
        self.in_chips = ChipSums(across_ref, refs[12:15], refs[28:30], self.chip, self.core)
        self.late_chips = ChipSums(self.keep, refs[15:18], refs[30:32], self.chip, self.core)

    def to_plane(self, offset, source, target, send, recv):
        return pltpu.make_async_remote_copy(
            src_ref=source, dst_ref=target, send_sem=send.at[offset - 1], recv_sem=recv.at[offset - 1],
            device_id={"dp": lax.rem(self.plane + offset, 4)}, device_id_type=pl.DeviceIdType.MESH,
        )

    def rest_plane(self, offset):
        peer = lax.rem(self.plane + offset, 4)
        return self.to_plane(offset, self.planes.at[peer], self.rest_got.at[offset - 1], self.send_rest, self.recv_rest)

    def in_plane(self, offset):
        peer = lax.rem(self.plane + offset, 4)
        return self.to_plane(offset, self.in_sum.at[peer], self.in_got.at[offset - 1], self.send_in, self.recv_in)

    def late_plane(self, offset):
        peer = lax.rem(self.plane + offset, 4)
        return self.to_plane(offset, self.late_sum.at[peer], self.late_got.at[offset - 1], self.send_c, self.recv_c)

    def rest_chip(self, offset):
        other = lax.rem(self.chip + offset, 4)
        return pltpu.make_async_remote_copy(
            src_ref=self.rest_sum.at[other], dst_ref=self.rest_chips.at[offset - 1],
            send_sem=self.send_chip.at[offset - 1], recv_sem=self.recv_chip.at[offset - 1],
            device_id={"seq": 2 * other + self.core}, device_id_type=pl.DeviceIdType.MESH,
        )

    def late_core(self, column):
        return to_sibling(self.core, self.other.at[:, column], self.got.at[:, column], self.send_a.at[column], self.recv_a.at[column])

    def begin(self):
        self.in_chips.start()
        for offset in (1, 2, 3):
            self.rest_plane(offset).start()

    def late(self):
        sequences, count, model = self.normed.shape
        self.normed_t[...] = self.normed[...].reshape(sequences * count, model).T
        low = lax.broadcasted_iota(jnp.int32, (model, 128), 1) < 64
        for pair in range(PAIRS):
            rows = jnp.concatenate([self.block_of(one * PAIRS + pair) for one in range(sequences)], axis=0)
            sums = dot(self.normed_t[...], rows, NN)
            query, key, value = sums[:, 0:128], pltpu.roll(sums[:, 128:256], 64, 1), sums[:, 256:384]
            self.result[3 * pair] = jnp.where(low, query, key).astype(BF16)
            self.result[3 * pair + 1] = jnp.where(low, value, query).astype(BF16)
            self.result[3 * pair + 2] = jnp.where(low, key, value).astype(BF16)
        for tile in range(3 * PAIRS):
            within = tile % 9
            spots = [(2 * (tile // 9), within)] if within <= 4 else []
            spots += [(2 * (tile // 9) + 1, within - 4)] if within >= 4 else []
            for column, slot in spots:
                rows_at = slice(96 * slot, 96 * slot + 96)
                spread_rows(self.core, self.result.at[tile], slice(0, 128), self.keep, self.other, lambda chip: (chip, column, rows_at))
        for column in range(4):
            self.late_core(column).start()

    def late_one(self):
        for column in range(4):
            self.late_core(column).wait()
            for at in range(4):
                self.keep[at, column] = (self.keep[at, column].astype(F32) + self.got[at, column].astype(F32)).astype(BF16)
        self.late_chips.start()

    def in_two(self):
        self.in_chips.middle()

    def late_two(self):
        self.late_chips.middle()

    def rest_two(self):
        for offset in (1, 2, 3):
            self.rest_plane(offset).wait()
        for chip in range(4):
            total = self.planes[self.plane, chip].astype(F32)
            for slot in range(3):
                total = total + self.rest_got[slot, chip].astype(F32)
            self.rest_sum[chip] = total.astype(BF16)
        for offset in (1, 2, 3):
            self.rest_chip(offset).start()

    def in_three(self):
        self.in_chips.finish(self.in_sum)
        for offset in (1, 2, 3):
            self.in_plane(offset).start()

    def late_three(self):
        self.late_chips.finish(self.late_sum)
        for offset in (1, 2, 3):
            self.late_plane(offset).start()

    def joined(self, block, columns):
        odd = lax.rem(self.plane, 2) == 1
        count = block.shape[1]
        return jnp.where(odd, pltpu.roll(block, count - 64, 1), block)[:, :columns]

    def finish_rest(self, down_out):
        total = self.rest_sum[self.chip].astype(F32)
        for offset in (1, 2, 3):
            self.rest_chip(offset).wait()
            total = total + self.rest_chips[offset - 1].astype(F32)
        down_out[:, 0:128] = total[0:192]
        down_out[:, 128:256] = total[192:384]

    def finish_in(self, in_out, weight_out):
        total = self.in_sum[self.plane].astype(F32)
        for offset in (1, 2, 3):
            self.in_plane(offset).wait()
            total = total + self.in_got[offset - 1].astype(F32)
        for tile in range(8):
            in_out[:, 128 * tile : 128 * tile + 128] = total[96 * tile : 96 * tile + 96]
        weight_out[...] = self.joined(jnp.concatenate([total[768:864], total[864:960]], axis=1), 192)

    def finish_late(self, qkv_out):
        total = self.late_sum[self.plane].astype(F32)
        for offset in (1, 2, 3):
            self.late_plane(offset).wait()
            total = total + self.late_got[offset - 1].astype(F32)
        qkv_out[...] = self.joined(jnp.concatenate([total[96 * k : 96 * k + 96] for k in range(5)], axis=1), 576)


def weight_scratch(model, tokens):
    dma = pltpu.SemaphoreType.DMA
    late = (4, 4, LATE_ROWS, 128)
    return (
        [
            pltpu.VMEM((4, IN_ROWS, 128), BF16),
            pltpu.VMEM((3, IN_ROWS, 128), BF16),
            pltpu.VMEM((3, 4, REST_ROWS, 128), BF16),
            pltpu.VMEM((4, REST_ROWS, 128), BF16),
            pltpu.VMEM((3, REST_ROWS, 128), BF16),
            pltpu.VMEM((model, tokens), BF16),
            pltpu.VMEM((3 * PAIRS, model, 128), BF16),
            pltpu.VMEM(late, BF16),
            pltpu.VMEM(late, BF16),
            pltpu.VMEM(late, BF16),
            pltpu.VMEM((4, LATE_ROWS, 128), BF16),
            pltpu.VMEM((3, LATE_ROWS, 128), BF16),
        ]
        + chip_scratch(IN_ROWS)
        + chip_scratch(LATE_ROWS)
        + [dma((3,)), dma((3,)), dma((3,)), dma((3,)), dma((3,)), dma((3,)), dma((4,)), dma((4,)), dma((3,)), dma((3,))]
        + [dma((6,)), dma((6,)), dma((6,)), dma((6,))]
    )


SMALL_ROWS = 288


class SmallSums:
    def __init__(self, block, buffers, sems):
        self.block = block
        self.held, self.got_seq, self.planes, self.whole = buffers
        self.sems = sems
        self.me, self.plane = lax.axis_index("seq"), lax.axis_index("dp")
        self.across, self.along = self.held.shape[0], self.held.shape[1]
        self.paired = self.across == 8
        self.core, self.chip = lax.rem(self.me, 2), self.me // 2
        self.mine = self.across // 2 * self.core + self.chip

    def places(self):
        half = self.held.shape[2] // 2
        units = SMALL_ROWS // half
        tiles = self.block.shape[1] // 128
        for at in range(2 * self.along * self.across):
            spot = (at // (2 * self.along), at // 2 % self.along, slice((at % 2) * half, (at % 2) * half + half))
            tile, unit = at // units, at % units
            if tile < tiles:
                yield spot, (slice(unit * half, unit * half + half), slice(128 * tile, 128 * tile + 128))
            else:
                yield spot, None

    def pack(self):
        for spot, source in self.places():
            if source is None:
                self.held[spot] = jnp.zeros((self.held.shape[2] // 2, 128), BF16)
            else:
                self.held[spot] = self.block[source].astype(BF16)

    def copies(self, axis, source, target, number):
        here, count = {"seq": (self.me, self.across), "chip": (self.chip, self.across // 2), "dp": (self.plane, self.along)}[axis]
        send, recv = self.sems[2 * number], self.sems[2 * number + 1]
        made = []
        for step in range(1, count):
            peer = lax.rem(here + step, count)
            device = {"seq": 2 * peer + self.core} if axis == "chip" else {axis: peer}
            made.append(
                pltpu.make_async_remote_copy(
                    src_ref=source(peer), dst_ref=target(step - 1), send_sem=send.at[step - 1], recv_sem=recv.at[step - 1],
                    device_id=device, device_id_type=pl.DeviceIdType.MESH,
                )
            )
        for copy in made:
            copy.start()
        return made

    def sibling(self, source, target, number):
        made = [to_sibling(self.core, source, target, self.sems[2 * number].at[6], self.sems[2 * number + 1].at[6])]
        made[0].start()
        return made

    def one_start(self):
        if self.paired:
            half = pl.ds(4 * (1 - self.core), 4)
            self.waiting = self.sibling(self.held.at[half], self.got_seq.at[pl.ds(3, 4)], 0)
            return
        self.waiting = self.copies("seq", lambda peer: self.held.at[peer], lambda slot: self.got_seq.at[slot], 0)

    def one_middle(self):
        if self.paired:
            for copy in self.waiting:
                copy.wait()
            for chip in range(4):
                at = 4 * self.core + chip
                self.held[at] = (self.held[at].astype(F32) + self.got_seq[3 + chip].astype(F32)).astype(BF16)
            self.waiting = self.copies("chip", lambda peer: self.held.at[4 * self.core + peer], lambda slot: self.got_seq.at[slot], 0)

    def one_finish(self):
        for copy in self.waiting:
            copy.wait()
        total = self.held[self.mine if self.paired else self.me].astype(F32)
        for slot in range(3 if self.paired else self.across - 1):
            total = total + self.got_seq[slot].astype(F32)
        self.planes[self.plane] = total.astype(BF16)
        self.waiting = self.copies("dp", lambda peer: self.planes.at[self.plane], lambda slot: self.planes.at[self.plane], 1)

    def two_finish(self):
        for copy in self.waiting:
            copy.wait()
        total = self.planes[0].astype(F32)
        for plane in range(1, self.along):
            total = total + self.planes[plane].astype(F32)
        own = self.mine if self.paired else self.me
        self.whole[own] = total.astype(BF16)
        self.waiting = self.copies("chip" if self.paired else "seq", lambda peer: self.whole.at[own], lambda slot: self.whole.at[own], 2)

    def three_finish(self):
        if self.paired:
            for copy in self.waiting:
                copy.wait()
            half = pl.ds(4 * self.core, 4)
            self.waiting = self.sibling(self.whole.at[half], self.whole.at[half], 2)

    def four_finish(self):
        for copy in self.waiting:
            copy.wait()
        for spot, target in self.places():
            if target is not None:
                self.block[target] = self.whole[spot].astype(F32)


def small_scratch(across, along):
    chunk = max(16, 2048 // (across * along))
    dma = lambda count: pltpu.SemaphoreType.DMA((count,))
    return [
        pltpu.VMEM((across, along, chunk, 128), BF16),
        pltpu.VMEM((across - 1, along, chunk, 128), BF16),
        pltpu.VMEM((along, along, chunk, 128), BF16),
        pltpu.VMEM((across, along, chunk, 128), BF16),
        dma(across - 1), dma(across - 1), dma(along - 1), dma(along - 1), dma(across - 1), dma(across - 1),
    ]


def body(
    byte_ids,
    lengths,
    byte_table,
    conv_kernel,
    score_vector,
    norm_gain_one,
    qkv_weight,
    bias_table,
    out_weight,
    norm_gain_two,
    in_weight,
    down_weight,
    cotangent,
):
    devices = lax.axis_size("seq")
    me = lax.axis_index("seq")
    sequences, local_bytes = byte_ids.shape
    local_tokens = local_bytes // 2
    total_bytes = local_bytes * devices
    vocab, model = byte_table.shape
    total = sequences * PAIRS
    per_device = -(-total // devices)
    place = jnp.reshape(me, (1,)).astype(jnp.int32)
    vectors = jnp.concatenate([conv_kernel, norm_gain_one[None, :], norm_gain_two[None, :], score_vector[None, :]], axis=0)
    rows = jnp.dot(near_one_hot(), bias_table, precision="highest").T.reshape(PAIRS, 2, NEAR)

    def exchange(items):
        return lax.all_to_all(items, "seq", split_axis=0, concat_axis=0, tiled=True)

    hidden, normed, conv, mix, share, ids_rows, received = call_front(lengths, byte_ids, byte_table, qkv_weight, vectors, devices, per_device)
    out, aug, cot = attention_forward(received, rows, lengths, place, cotangent)
    layer, act, gate_up, normed_two, attended, branch, grad_residual, grad_items, grad_gain_two, grad_rest = call_mid(
        out, hidden, cot, out_weight, in_weight, down_weight, vectors
    )
    along_count = lax.axis_size("dp")
    custom = devices == 8 and along_count == 4

    def scatter(grad):
        rows_own = lax.psum_scatter(grad, "seq", scatter_dimension=0, tiled=True)
        return lax.psum_scatter(rows_own, "dp", scatter_dimension=1, tiled=True).astype(F32)

    if not custom:
        summed_down = scatter(jnp.einsum("bti,btd->id", act, cot, preferred_element_type=F32).astype(BF16))
        summed_in = scatter(jnp.einsum("btd,bti->di", normed_two, gate_up, preferred_element_type=F32).astype(BF16))
        summed_out = scatter(jnp.einsum("btd,bte->de", attended, branch, preferred_element_type=F32).astype(BF16))
    half = per_device // 2
    grads_two, grads_one, at_two = (grad_items, exchange(grad_rest), 0) if devices == 8 else (grad_items, grad_items, half)
    dqkv_two, bias_two, layer_out = attention_backward(
        received, out, aug, grads_two, rows, lengths, place, layer, grad_gain_two, half, per_device - half, at_two
    )
    items_two = exchange(dqkv_two)
    dqkv_one, bias_one, unused = attention_backward(received, out, aug, grads_one, rows, lengths, place, None, bias_two, 0, half, 0)
    items_one = exchange(dqkv_one)
    bias_rows = jnp.concatenate([bias_one, bias_two], axis=0)
    if custom:
        in_chips, rest_planes = call_early(act, cot, normed_two, gate_up, attended, branch, items_two)
    extra = (normed, in_chips, rest_planes) if custom else ()
    results = call_back(
        custom, items_one, items_two, hidden, grad_residual, conv, mix, share, ids_rows, qkv_weight, byte_table, vectors, bias_rows, grad_gain_two, along_count, extra
    )
    if custom:
        summed_qkv, summed_in, summed_down, summed_out, *smalls = call_finish(results[0], results[1:])
        summed_down = summed_down.T
    else:
        smalls = call_finish(results[0], ())
        grad_qkv = jnp.einsum("btd,bte->de", normed, results[1], preferred_element_type=F32).astype(BF16)
        grad_qkv = jnp.swapaxes(grad_qkv.reshape(model, PAIRS, 3, 2, 64), 2, 3).reshape(model, PAIRS * 384)
        summed_qkv = scatter(grad_qkv)
    grad_table, grad_taps, grad_gain_one, grad_score, grad_gain_two, grad_bias = smalls
    return (
        layer_out,
        grad_table,
        grad_taps,
        grad_score,
        grad_gain_one,
        summed_qkv,
        grad_bias.T,
        summed_out,
        grad_gain_two,
        summed_in,
        summed_down,
    )


def solution(mesh):
    return jax.shard_map(
        body,
        mesh=mesh,
        in_specs=(
            P("dp", "seq"),
            P("dp"),
            P(),
            P(),
            P(),
            P(),
            P(),
            P(),
            P(),
            P(),
            P(),
            P(),
            P("dp", "seq", None),
        ),
        out_specs=(
            P("dp", "seq", None),
            P(),
            P(),
            P(),
            P(),
            P("seq", "dp"),
            P(),
            P("seq", "dp"),
            P(),
            P("seq", "dp"),
            P("seq", "dp"),
        ),
        check_vma=False,
    )
```

```python
import functools
import jax
import jax.numpy as jnp
from jax import lax
from jax.experimental import pallas as pl
from jax.experimental.pallas import tpu as pltpu
from jax.sharding import PartitionSpec as P

thresholds = (12, 16, 23, 32, 46, 64, 91)
KB = 256
NEAR = 1024
F32 = jnp.float32
BF16 = jnp.bfloat16
NT = (((1,), (1,)), ((), ()))
NN = (((1,), (0,)), ((), ()))


def rel_bucket(relative):
    distance = jnp.abs(relative)
    larger = 8 + sum(((distance >= boundary).astype(jnp.int32) for boundary in thresholds))
    bucket = jnp.where(distance < 8, distance, larger)
    return bucket + 16 * (relative > 0).astype(jnp.int32)


def near_one_hot():
    place = jnp.arange(NEAR, dtype=jnp.int32)
    relative = jnp.where(place < NEAR - 128, KB - place, KB + NEAR - place)
    return (rel_bucket(relative)[:, None] == jnp.arange(32, dtype=jnp.int32)[None, :]).astype(F32)


def dot(a, b, dims):
    return lax.dot_general(a, b, dims, preferred_element_type=F32)


STRIP = 5 * KB


def strip_at(block, part):
    return pl.ds(pl.multiple_of((jnp.clip(part - block, -2, 2) + 2) * KB, KB), KB)


def fill_bias(strip, head, row):
    spread = jnp.broadcast_to(row, (128, NEAR))
    rolled = pltpu.roll(spread, 0, 1, stride=1, stride_axis=0)
    far_right = jnp.broadcast_to(row[:, NEAR - 1 :], (KB, 128))
    far_left = jnp.broadcast_to(row[:, 768:769], (KB, 128))
    for start in range(0, KB, 128):
        strip[head, :, start : start + 128] = far_right
        strip[head, :, KB + 768 + start : KB + 896 + start] = far_left
    strip[head, 0:128, KB : KB + 768] = rolled[:, :768]
    strip[head, 128:256, KB : KB + 128] = far_right[:128]
    strip[head, 128:256, KB + 128 : KB + 768] = rolled[:, :640]


def lanes_of(head, shape):
    lane = lax.broadcasted_iota(jnp.int32, shape, 1)
    own = (lane < 64) if head == 0 else (lane >= 64)
    return own, lane - (64 if head == 0 else 0)


def fill_keys(ka, head, keys, valid):
    own, spare = lanes_of(head, keys.shape)
    row = lax.broadcasted_iota(jnp.int32, keys.shape, 0)
    masked = jnp.where(row < valid, 0.0, -1e9)
    extra = jnp.where(spare == 0, masked, jnp.where((spare >= 1) & (spare <= 3), 1.0, 0.0))
    ka[head] = jnp.where(own, keys, extra.astype(BF16))


def item_length(lengths_ref, item):
    length = jnp.int32(0)
    for number, rank in enumerate(ranks_of(lengths_ref)):
        length = jnp.where(rank == item // 6, lengths_ref[number], length)
    return (length + 1) // 2


def move_rows(item, lengths_ref, source, buffer, target, sems, sorting):
    def inward(number):
        return pltpu.make_async_copy(source.at[number if sorting else ranks[number]], buffer.at[number], sems.at[0, number])

    def outward(number):
        return pltpu.make_async_copy(buffer.at[number], target.at[ranks[number] if sorting else number], sems.at[1, number])

    count = source.shape[0]
    ranks = ranks_of(lengths_ref)

    @pl.when(item == 0)
    def _():
        for number in range(count):
            inward(number).start()

    @pl.when(item == jnp.minimum(1, pl.num_programs(0) - 1))
    def _():
        for number in range(count):
            inward(number).wait()
            outward(number).start()

    def finish():
        @pl.when(item == pl.num_programs(0) - 1)
        def _():
            for number in range(count):
                outward(number).wait()

    return finish


def fwd_kernel(
    blocks, lengths_ref, place_ref, qkv_ref, row_ref, cot_ref, out_ref, aug_ref, sorted_ref,
    qa, ka, vt, strip, peak, acc, probs, moving, sems,
):
    item = pl.program_id(0)
    finish = move_rows(item, lengths_ref, cot_ref, moving, sorted_ref, sems, True)
    valid = item_length(lengths_ref, place_ref[0] + qkv_ref.shape[0] * item)
    tokens = blocks * KB
    joined = qkv_ref[:, 0].reshape(tokens, 384)
    queries = joined[:, 0:128]
    keys = joined[:, 128:256]
    turned = joined[:, 256:384].T
    filler = jnp.where(lax.broadcasted_iota(jnp.int32, (16, tokens), 0) == 0, 1.0, 0.0).astype(BF16)
    for head in range(2):
        own, spare = lanes_of(head, queries.shape)
        qa[head] = jnp.where(own, queries, jnp.where(spare == 0, 1.0, 0.0).astype(BF16))
        fill_keys(ka, head, keys, valid)
        vt[head, 0:64] = turned[64 * head : 64 * head + 64]
        vt[head, 64:80] = filler
        fill_bias(strip, head, row_ref[0, head : head + 1, :])
    peak[...] = jnp.full_like(peak, -1e30)
    acc[...] = jnp.zeros_like(acc)

    def step(block, unused):
        first = pl.multiple_of(block * KB, KB)
        alphas = [[], []]
        for part in range(blocks):
            for head in range(2):
                here = slice(part * KB, part * KB + KB)
                logits = dot(ka[head, pl.ds(first, KB), :], qa[head, here, :], NT)
                logits = logits + strip[head, :, strip_at(block, part)]
                before = peak[head, :, here]
                after = jnp.maximum(before, jnp.max(logits, axis=0, keepdims=True))
                probs[head, :, here] = jnp.exp(logits - after).astype(BF16)
                peak[head, :, here] = after
                alphas[head].append(jnp.exp(before - after))
        for head in range(2):
            acc[head] = acc[head] * jnp.concatenate(alphas[head], axis=1) + dot(vt[head, :, pl.ds(first, KB)], probs[head], NN)
        return unused

    lax.fori_loop(0, (valid + KB - 1) // KB, step, 0)
    outs = []
    rows = []
    place = lax.broadcasted_iota(jnp.int32, (64, tokens), 0)
    for head in range(2):
        total = acc[head, 64:65, :]
        outs.append(acc[head, 0:64, :] / total)
        minus = -(peak[head] + jnp.log(total))
        high = minus.astype(BF16).astype(F32)
        rest = minus - high
        middle = rest.astype(BF16).astype(F32)
        low = rest - middle
        rows.append(jnp.where(place == 0, 1.0, jnp.where(place == 1, high, jnp.where(place == 2, middle, jnp.where(place == 3, low, 0.0)))))
    out_ref[:, 0] = jnp.concatenate(outs, axis=0).T.astype(BF16).reshape(out_ref.shape[0], out_ref.shape[2], 128)
    aug_ref[0] = jnp.concatenate([rows[1], rows[0]], axis=0).T.astype(BF16)
    finish()


def bwd_kernel(
    blocks, base_slot, moves, lengths_ref, place_ref, qkv_ref, out_ref, aug_ref, grad_ref, row_ref, layer_ref, after,
    dqkv_ref, bias_ref, moved_ref, qa, ka, va, ga, kt, strip, tally, probs, slopes, dq, *moving,
):
    item = pl.program_id(0)
    finish = move_rows(item, lengths_ref, layer_ref, moving[0], moved_ref, moving[1], False) if moves else lambda: None
    valid = item_length(lengths_ref, place_ref[0] + qkv_ref.shape[0] * (item + base_slot))
    tokens = blocks * KB
    local = qkv_ref.shape[2]
    joined = qkv_ref[:, 0].reshape(tokens, 384)
    queries = joined[:, 0:128]
    keys = joined[:, 128:256]
    values = joined[:, 256:384]
    grads = grad_ref[:, 0].reshape(tokens, 128)
    outs = out_ref[:, 0].reshape(tokens, 128)
    kt[...] = keys.T
    product = grads.astype(F32) * outs.astype(F32)
    high = product.astype(BF16)
    low = (product - high.astype(F32)).astype(BF16)
    row_at = lax.broadcasted_iota(jnp.int32, (128, 128), 0)
    lane_at = lax.broadcasted_iota(jnp.int32, (128, 128), 1)
    pick = jnp.where((row_at < 64) == (lane_at >= 64), -1.0, 0.0).astype(BF16)
    shifts = dot(high, pick, NN) + dot(low, pick, NN)
    shift_high = shifts.astype(BF16)
    shift_low = (shifts - shift_high.astype(F32)).astype(BF16)
    for head in range(2):
        own, spare = lanes_of(head, queries.shape)
        qa[head] = jnp.where(own, queries, aug_ref[0])
        fill_keys(ka, head, keys, valid)
        va[head] = jnp.where(own, values, jnp.where((spare == 0) | (spare == 1), 1.0, 0.0).astype(BF16))
        ga[head] = jnp.where(own, grads, jnp.where(spare == 0, shift_high, jnp.where(spare == 1, shift_low, jnp.zeros_like(shift_low))))
        fill_bias(strip, head, row_ref[0, head : head + 1, :])
    tally[...] = jnp.zeros_like(tally)
    dq[...] = jnp.zeros_like(dq)
    dqkv_ref[...] = jnp.zeros_like(dqkv_ref)

    def step(block, unused):
        first = pl.multiple_of(block * KB, KB)
        key_parts = []
        value_parts = []
        for part in range(blocks):
            for head in range(2):
                here = slice(part * KB, part * KB + KB)
                there = strip_at(block, part)
                logits = dot(ka[head, pl.ds(first, KB), :], qa[head, here, :], NT)
                weights = jnp.exp(logits + strip[head, :, there])
                change = dot(va[head, pl.ds(first, KB), :], ga[head, here, :], NT)
                slope = weights * change
                tally[head, :, there] += slope
                probs[head, :, here] = weights.astype(BF16)
                slopes[head, :, here] = slope.astype(BF16)
        for head in range(2):
            value_parts.append(dot(probs[head], ga[head], NN))
            key_parts.append(dot(slopes[head], qa[head], NN))
            dq[pl.ds(64 * head, 64), :] += dot(kt[pl.ds(64 * head, 64), pl.ds(first, KB)], slopes[head], NN)
        own, unused_spare = lanes_of(0, (KB, 128))
        count = KB // local
        where = pl.ds(block * count, count)
        dqkv_ref[where, 0, :, 128:256] = jnp.where(own, key_parts[0], key_parts[1]).astype(BF16).reshape(count, local, 128)
        dqkv_ref[where, 0, :, 256:384] = jnp.where(own, value_parts[0], value_parts[1]).astype(BF16).reshape(count, local, 128)
        return unused

    lax.fori_loop(0, (valid + KB - 1) // KB, step, 0)
    dqkv_ref[:, 0, :, 0:128] = dq[...].T.astype(BF16).reshape(dqkv_ref.shape[0], local, 128)
    lane = lax.broadcasted_iota(jnp.int32, (1, NEAR), 1)
    flip = jnp.where(row_at + lane_at == 127, 1.0, 0.0).astype(BF16)
    for head in range(2):
        far_right = tally[head, :, 0:128] + tally[head, :, 128:256]
        far_right = far_right[:128] + far_right[128:] + tally[head, 128:256, KB : KB + 128]
        far_left = tally[head, :, KB + 768 : KB + 896] + tally[head, :, KB + 896 : STRIP]
        near = tally[head, 0:128, KB : KB + 768]
        near_low = tally[head, 128:256, KB + 128 : KB + 768]
        near = near + jnp.concatenate([near_low, jnp.zeros((128, 128), F32)], axis=1)
        near = jnp.concatenate([near, jnp.zeros((128, NEAR - 768), F32)], axis=1)
        near_high = near.astype(BF16)
        flipped = dot(flip, near_high, NN) + dot(flip, (near - near_high.astype(F32)).astype(BF16), NN)
        rolled = pltpu.roll(flipped, NEAR - 127, 1, stride=1, stride_axis=0)
        row = jnp.sum(rolled, axis=0, keepdims=True)
        row = row + jnp.where(lane == NEAR - 1, jnp.sum(far_right), 0.0) + jnp.where(lane == 768, jnp.sum(far_left), 0.0)
        bias_ref[0, head : head + 1, :] = row
    finish()


def attention_forward(qkv, rows, lengths, place, cot):
    sources, items, local, unused = qkv.shape
    blocks = sources * local // KB
    tokens = sources * local
    spec = pltpu.PrefetchScalarGridSpec(
        num_scalar_prefetch=2,
        grid=(items,),
        in_specs=[
            pl.BlockSpec((sources, 1, local, 384), lambda i, l, p: (0, i, 0, 0)),
            pl.BlockSpec((1, 2, NEAR), lambda i, l, p: (lax.rem(p[0] + sources * i, 6), 0, 0)),
            pl.BlockSpec(memory_space=pl.ANY),
        ],
        out_specs=[
            pl.BlockSpec((sources, 1, local, 128), lambda i, l, p: (0, i, 0, 0)),
            pl.BlockSpec((1, tokens, 128), lambda i, l, p: (i, 0, 0)),
            pl.BlockSpec(memory_space=pl.ANY),
        ],
        scratch_shapes=[
            pltpu.VMEM((2, tokens, 128), BF16),
            pltpu.VMEM((2, tokens, 128), BF16),
            pltpu.VMEM((2, 80, tokens), BF16),
            pltpu.VMEM((2, KB, STRIP), F32),
            pltpu.VMEM((2, 1, tokens), F32),
            pltpu.VMEM((2, 80, tokens), F32),
            pltpu.VMEM((2, KB, tokens), BF16),
            pltpu.VMEM(cot.shape, cot.dtype),
            pltpu.SemaphoreType.DMA((2,) + cot.shape[:1]),
        ],
    )
    return pl.pallas_call(
        functools.partial(fwd_kernel, blocks),
        grid_spec=spec,
        out_shape=[
            jax.ShapeDtypeStruct((sources, items, local, 128), BF16),
            jax.ShapeDtypeStruct((items, tokens, 128), BF16),
            jax.ShapeDtypeStruct(cot.shape, cot.dtype),
        ],
        compiler_params=pltpu.CompilerParams(vmem_limit_bytes=60 * 2**20),
        cost_estimate=pl.CostEstimate(flops=items * tokens * tokens * 512, bytes_accessed=items * tokens * 2048, transcendentals=items * tokens * tokens * 2),
        name="attention_forward",
    )(lengths, place, qkv, rows, cot)


def attention_backward(qkv, outs, aug, grads, rows, lengths, place, layer, after, first, items, grads_at):
    sources, unused, local, unused = qkv.shape
    moves = layer is not None
    layer = after if layer is None else layer
    moved = layer if moves else jnp.zeros((8, 128), F32)
    blocks = sources * local // KB
    tokens = sources * local
    big = lambda lanes: pl.BlockSpec((sources, 1, local, lanes), lambda i, l, p: (0, i + first, 0, 0))
    spec = pltpu.PrefetchScalarGridSpec(
        num_scalar_prefetch=2,
        grid=(items,),
        in_specs=[
            big(384),
            big(128),
            pl.BlockSpec((1, tokens, 128), lambda i, l, p: (i + first, 0, 0)),
            pl.BlockSpec((sources, 1, local, 128), lambda i, l, p: (0, i + grads_at, 0, 0)),
            pl.BlockSpec((1, 2, NEAR), lambda i, l, p: (lax.rem(p[0] + sources * (i + first), 6), 0, 0)),
            pl.BlockSpec(memory_space=pl.ANY),
            pl.BlockSpec(memory_space=pl.ANY),
        ],
        out_specs=[
            pl.BlockSpec((sources, 1, local, 384), lambda i, l, p: (0, i, 0, 0)),
            pl.BlockSpec((1, 2, NEAR), lambda i, l, p: (i, 0, 0)),
            pl.BlockSpec(memory_space=pl.ANY),
        ],
        scratch_shapes=[
            pltpu.VMEM((2, tokens, 128), BF16),
            pltpu.VMEM((2, tokens, 128), BF16),
            pltpu.VMEM((2, tokens, 128), BF16),
            pltpu.VMEM((2, tokens, 128), BF16),
            pltpu.VMEM((128, tokens), BF16),
            pltpu.VMEM((2, KB, STRIP), F32),
            pltpu.VMEM((2, KB, STRIP), F32),
            pltpu.VMEM((2, KB, tokens), BF16),
            pltpu.VMEM((2, KB, tokens), BF16),
            pltpu.VMEM((128, tokens), F32),
        ]
        + ([pltpu.VMEM(layer.shape, layer.dtype), pltpu.SemaphoreType.DMA((2,) + layer.shape[:1])] if moves else []),
    )
    return pl.pallas_call(
        functools.partial(bwd_kernel, blocks, first, moves),
        grid_spec=spec,
        out_shape=[
            jax.ShapeDtypeStruct((sources, items, local, 384), BF16),
            jax.ShapeDtypeStruct((items, 2, NEAR), F32),
            jax.ShapeDtypeStruct(moved.shape, moved.dtype),
        ],
        compiler_params=pltpu.CompilerParams(vmem_limit_bytes=60 * 2**20),
        cost_estimate=pl.CostEstimate(flops=items * tokens * tokens * 1280, bytes_accessed=items * tokens * 4096, transcendentals=items * tokens * tokens * 2),
        name="attention_backward",
    )(lengths, place, qkv, outs, aug, grads, rows, layer, after)


VPAD = 384
PAIRS = 6
TN = (((0,), (0,)), ((), ()))
SQRT_2_OVER_PI = 0.7978845608028654


def block_masks(masks, first_byte, total_bytes):
    shape = masks.shape[2:]
    conv_at = first_byte - 2 + lax.broadcasted_iota(jnp.int32, shape, 1)
    token = lax.broadcasted_iota(jnp.int32, shape, 0)
    for side in range(2):
        place = first_byte + 2 * token + side
        for size in range(1, 5):
            start = (place // size) * size
            inside = (conv_at >= start) & (conv_at < start + size) & (conv_at < total_bytes)
            masks[side, size - 1] = jnp.where(inside, 1.0 / size, 0.0)


def split_two(values):
    high = values.astype(BF16)
    return high, (values - high.astype(F32)).astype(BF16)


def permute_weight(weight, out):
    rows = weight.shape[0]
    low = lax.broadcasted_iota(jnp.int32, (rows, 128), 1) < 64
    for pair in range(PAIRS):
        at = pair * 384
        one, two, three = (weight[:, at + 128 * k : at + 128 * k + 128] for k in range(3))
        out[:, at : at + 128] = jnp.where(low, one, two)
        out[:, at + 128 : at + 256] = pltpu.roll(jnp.where(low, three, one).astype(F32), 64, 1).astype(BF16)
        out[:, at + 256 : at + 384] = jnp.where(low, two, three)


def greet(axis, here, count):
    barrier = pltpu.get_barrier_semaphore()

    def signal(step, unused):
        pl.semaphore_signal(barrier, inc=1, device_id={axis: lax.rem(here + step, count)}, device_id_type=pl.DeviceIdType.MESH)
        return unused

    lax.fori_loop(1, count, signal, 0)


def item_copy(devices, me, source, target, other, slot, sems):
    send, recv, unused = sems

    def outward():
        offset = lax.rem(other - me + devices, devices)
        return pltpu.make_async_remote_copy(
            src_ref=source, dst_ref=target, send_sem=send.at[offset, slot], recv_sem=recv.at[offset, slot],
            device_id={"seq": other}, device_id_type=pl.DeviceIdType.MESH,
        )

    def inward():
        offset = lax.rem(me - other + devices, devices)
        return pltpu.make_async_remote_copy(
            src_ref=source, dst_ref=target, send_sem=send.at[offset, slot], recv_sem=recv.at[offset, slot],
            device_id={"seq": other}, device_id_type=pl.DeviceIdType.MESH,
        )

    return outward, inward


def start_item(devices, me, source, target, other, slot, sems):
    @pl.when(other == me)
    def _():
        pltpu.make_async_copy(source, target, sems[2].at[slot]).start()

    @pl.when(other != me)
    def _():
        item_copy(devices, me, source, target, other, slot, sems)[0]().start()


def finish_sends(devices, me, total, source_of, target_of, sems):
    def wait(item, unused):
        other, slot = lax.rem(item, devices), item // devices

        @pl.when(other != me)
        def _():
            item_copy(devices, me, source_of(other, slot), target_of(other, slot), other, slot, sems)[0]().wait_send()

        return unused

    lax.fori_loop(0, total, wait, 0)


def finish_receives(devices, me, total, source_of, target_of, sems):
    per_device = -(-total // devices)

    def wait(at, unused):
        other, slot = at // per_device, lax.rem(at, per_device)

        @pl.when((slot * devices + me < total) & (other != me))
        def _():
            item_copy(devices, me, source_of(other, slot), target_of(other, slot), other, slot, sems)[1]().wait_recv()

        @pl.when((slot * devices + me < total) & (other == me))
        def _():
            pltpu.make_async_copy(source_of(other, slot), target_of(other, slot), sems[2].at[slot]).wait()

        return unused

    lax.fori_loop(0, devices * per_device, wait, 0)


def ranks_of(lengths_ref):
    count = lengths_ref.shape[0]
    ranks = []
    for one in range(count):
        rank = jnp.int32(0)
        for two in range(count):
            if two != one:
                ahead = lengths_ref[two] > lengths_ref[one] if two > one else lengths_ref[two] >= lengths_ref[one]
                rank = rank + ahead.astype(jnp.int32)
        ranks.append(rank)
    return ranks


def spread_ids(lengths_ref, ids_ref, from_left, from_right, extended, sems, me, devices):
    sequences, local_bytes = ids_ref.shape
    left_copy = pltpu.make_async_remote_copy(
        src_ref=ids_ref.at[:, 0:128], dst_ref=from_right, send_sem=sems.at[0], recv_sem=sems.at[1],
        device_id={"seq": jnp.maximum(me - 1, 0)}, device_id_type=pl.DeviceIdType.MESH,
    )
    right_copy = pltpu.make_async_remote_copy(
        src_ref=ids_ref.at[:, local_bytes - 128 : local_bytes], dst_ref=from_left, send_sem=sems.at[2], recv_sem=sems.at[3],
        device_id={"seq": jnp.minimum(me + 1, devices - 1)}, device_id_type=pl.DeviceIdType.MESH,
    )

    @pl.when(me > 0)
    def _():
        left_copy.start()

    @pl.when(me < devices - 1)
    def _():
        right_copy.start()

    @pl.when(me > 0)
    def _():
        left_copy.wait_send()
        right_copy.wait_recv()

    @pl.when(me < devices - 1)
    def _():
        right_copy.wait_send()
        left_copy.wait_recv()

    joined = jnp.concatenate([from_left[...], ids_ref[...], from_right[...]], axis=1).astype(F32)
    width = joined.shape[1]
    moved = pltpu.roll(joined, width - 124, 1)
    row = lax.broadcasted_iota(jnp.int32, (sequences, width), 0)
    lane = lax.broadcasted_iota(jnp.int32, (sequences, width), 1)
    position = me * local_bytes - 4 + lane
    length = jnp.zeros((sequences, width), jnp.int32)
    for one in range(sequences):
        length = jnp.where(row == one, lengths_ref[one], length)
    outside = (position < 0) | (position >= local_bytes * devices) | (lane >= local_bytes + 8)
    picked = jnp.where(outside, -1.0, jnp.where(position < length, moved, 0.0))
    ordered = jnp.zeros((sequences, width), F32)
    for one, rank in enumerate(ranks_of(lengths_ref)):
        ordered = jnp.where(row == rank, picked[one : one + 1, :], ordered)
    extended[...] = ordered


def front_kernel(
    sizes, lengths_ref, ids_ref, table_ref, weight_source, vectors_ref,
    hidden_ref, normed_ref, conv_ref, mix_ref, share_ref, rows_ref, items_ref,
    masks, wide, permuted, stage, taps, from_left, from_right, extended, side_sems, weight_ref, weight_sem, *sems,
):
    local_tokens, window, devices, total = sizes
    step = pl.program_id(0)
    me = lax.axis_index("seq")

    @pl.when(step == 0)
    def _():
        pltpu.make_async_copy(weight_source, weight_ref, weight_sem).start()
        from_left[...] = jnp.zeros_like(from_left)
        from_right[...] = jnp.zeros_like(from_right)
        greet("seq", me, devices)
        block_masks(masks, me * 2 * local_tokens, devices * 2 * local_tokens)
        table = table_ref[...].astype(F32)
        taps[...] = jnp.zeros_like(taps)
        for tap in range(5):
            taps[tap, 0 : table.shape[0], :] = (vectors_ref[tap : tap + 1, :] * table).astype(BF16)
        pltpu.make_async_copy(weight_source, weight_ref, weight_sem).wait()
        permute_weight(weight_ref, permuted)
        pl.semaphore_wait(pltpu.get_barrier_semaphore(), devices - 1)
        spread_ids(lengths_ref, ids_ref, from_left, from_right, extended, side_sems, me, devices)

    together = 1
    width_ids = extended.shape[1]
    row = jnp.broadcast_to(extended[pl.ds(step, 1), :], (8, width_ids))
    rows = pltpu.roll(pltpu.roll(row, width_ids - 4, 1), 0, 1, stride=1, stride_axis=0)
    rows_ref[0] = rows
    ids = rows.T[0:window]
    score = vectors_ref[7:8, :]
    gain = vectors_ref[5:6, :]
    model = score.shape[1]
    score_high, score_low = split_two(score)
    row16 = lax.broadcasted_iota(jnp.int32, (16, model), 0)
    score_rows = jnp.where(row16 == 0, score_high.astype(F32), jnp.where(row16 == 1, score_low.astype(F32), 0.0)).astype(BF16)
    lane = lax.broadcasted_iota(jnp.int32, (together * window, VPAD), 1).astype(F32)
    width = masks.shape[3]
    conv_all = jnp.zeros((together * window, model), F32)
    for tap in range(5):
        hot = jnp.where(ids[:, 4 - tap : 5 - tap] == lane, 1.0, 0.0).astype(BF16)
        conv_all = conv_all + dot(hot, taps[tap], NN)
    for one in range(together):
        high, low = split_two(conv_all[one * window : (one + 1) * window])
        conv_ref[one, 0:window] = high
        wide[one, 0, 0:window] = high
        wide[one, 1, 0:window] = low
        if width > window:
            wide[one, :, window:width] = jnp.zeros((2, width - window, model), BF16)
            conv_ref[one, window:width] = jnp.zeros((width - window, model), BF16)
        high = wide[one, 0]
        low = wide[one, 1]
        along = jnp.sum(dot(score_rows, high, NT), axis=0, keepdims=True) + dot(score_rows, low, NT)[0:1]
        mixed = jnp.zeros((local_tokens, width), F32)
        kept = jnp.zeros((local_tokens, 128), F32)
        lane128 = lax.broadcasted_iota(jnp.int32, (local_tokens, 128), 1)
        for side in range(2):
            scores = [jnp.sum(masks[side, k] * along, axis=1, keepdims=True) for k in range(4)]
            top = jnp.maximum(jnp.maximum(scores[0], scores[1]), jnp.maximum(scores[2], scores[3]))
            powers = [jnp.exp(value - top) for value in scores]
            under = 1.0 / (powers[0] + powers[1] + powers[2] + powers[3])
            for k in range(4):
                share = powers[k] * under
                mixed = mixed + share * masks[side, k]
                kept = jnp.where(lane128 == 4 * side + k, share, kept)
        share_ref[one] = kept
        mix_high, mix_low = split_two(mixed * 0.5)
        mix_ref[one] = mix_high
        hidden = dot(mix_high, high, NN) + dot(mix_high, low, NN) + dot(mix_low, high, NN)
        hidden_ref[one] = hidden
        scale = lax.rsqrt(jnp.mean(hidden * hidden, axis=1, keepdims=True) + 1e-06)
        normed_ref[one] = (hidden * scale * gain).astype(BF16)
    normed = normed_ref[...].reshape(together * local_tokens, model)
    for pair in range(PAIRS):
        piece = dot(normed, permuted[:, pair * 384 : pair * 384 + 384], NN).astype(BF16)
        for one in range(together):
            item = (step * together + one) * PAIRS + pair
            other, slot = lax.rem(item, devices), item // devices
            stage[other, slot] = piece[one * local_tokens : (one + 1) * local_tokens]

    if devices == 8:

        def send(at, unused):
            item = step * PAIRS + lax.rem(at + me, PAIRS)
            other, slot = lax.rem(item, 8), item // 8

            @pl.when(other != me)
            def _():
                to_device(other, stage.at[other, slot], items_ref.at[me, slot], sems[0].at[0], sems[1].at[0]).start()

            return unused

        lax.fori_loop(0, PAIRS, send, 0)

        @pl.when(step == pl.num_programs(0) - 1)
        def _():
            finish_back(me, stage, items_ref, sems)

        return
    send_items(devices, me, step * together * PAIRS, together * PAIRS, stage, items_ref, sems)

    @pl.when(step == pl.num_programs(0) - 1)
    def _():
        finish_sends(devices, me, total, lambda other, slot: stage.at[other, slot], lambda other, slot: items_ref.at[me, slot], sems)
        finish_receives(devices, me, total, lambda other, slot: stage.at[other, slot], lambda other, slot: items_ref.at[other, slot], sems)


def to_device(other, source, target, send, recv):
    return pltpu.make_async_remote_copy(
        src_ref=source, dst_ref=target, send_sem=send, recv_sem=recv, device_id={"seq": other}, device_id_type=pl.DeviceIdType.MESH
    )


SLOT_GROUPS = ((0, 2), (2, 1), (3, 2), (5, 1))


def send_slots(me, number, source, arrived, sems):
    first, count = SLOT_GROUPS[number]
    slots = pl.ds(first, count)

    def send(offset, unused):
        other = lax.rem(me + offset, 8)
        to_device(other, source.at[other, slots], arrived.at[me, slots], sems[0].at[number], sems[1].at[number]).start()
        return unused

    lax.fori_loop(1, 8, send, 0)
    pltpu.make_async_copy(source.at[me, slots], arrived.at[me, slots], sems[2].at[number]).start()


def wait_slots(me, number, source, arrived, sems, sends):
    first, count = SLOT_GROUPS[number]
    slots = pl.ds(first, count)
    seven = pl.ds(0, 7)
    copies = to_device(lax.rem(me + 1, 8), source.at[seven, slots], arrived.at[seven, slots], sems[0].at[number], sems[1].at[number])
    if sends:
        copies.wait_send()
    else:
        copies.wait_recv()
        pltpu.make_async_copy(source.at[me, slots], arrived.at[me, slots], sems[2].at[number]).wait()


def send_back(me, step, stage, target, sems):
    base, base_to = 3, 0
    for parity in range(2):

        def send(offset, unused):
            other = lax.rem(me + offset, 8)

            @pl.when(other < 4)
            def _():
                first, count = (0, 2) if parity == 0 else (2, 1)
                to_device(other, stage.at[other, pl.ds(base + first, count)], target.at[me, pl.ds(base_to + first, count)], sems[0].at[0], sems[1].at[0]).start()

            @pl.when(other >= 4)
            def _():
                first, count = (0, 1) if parity == 0 else (1, 2)
                to_device(other, stage.at[other, pl.ds(base + first, count)], target.at[me, pl.ds(base_to + first, count)], sems[0].at[0], sems[1].at[0]).start()

            return unused

        @pl.when(lax.rem(step, 2) == parity)
        def _():
            lax.fori_loop(1, 8, send, 0)


def finish_half(me, stage, target, sems):
    slots = pl.ds(3, 3)
    local = pltpu.make_async_copy(stage.at[me, slots], target.at[me], sems[2].at[0])
    local.start()
    seven = pl.ds(0, 7)
    copies = to_device(lax.rem(me + 1, 8), stage.at[seven, slots], target.at[seven], sems[0].at[0], sems[1].at[0])
    copies.wait_send()
    copies.wait_recv()
    local.wait()


def finish_back(me, stage, target, sems):
    local = pltpu.make_async_copy(stage.at[me], target.at[me], sems[2].at[0])
    local.start()
    seven = pl.ds(0, 7)
    copies = to_device(lax.rem(me + 1, 8), stage.at[seven], target.at[seven], sems[0].at[0], sems[1].at[0])
    copies.wait_send()
    copies.wait_recv()
    local.wait()


def send_group(devices, me, total, group, number, source, arrived, sems):
    for slot in range(-(-total // devices)):
        item = slot * devices + me

        @pl.when((item < total) & (item // group == number))
        def _():
            def send(offset, unused):
                other = lax.rem(me + offset, devices)
                start_item(devices, me, source.at[other, slot], arrived.at[me, slot], other, slot, sems)
                return unused

            lax.fori_loop(0, devices, send, 0)


def send_items(devices, me, first, count, stage, target, sems):
    def send(at, unused):
        item = first + at
        other, slot = lax.rem(item, devices), item // devices
        start_item(devices, me, stage.at[other, slot], target.at[me, slot], other, slot, sems)
        return unused

    lax.fori_loop(0, count, send, 0)


def take_items(devices, me, first, count, source, arrived, sems):
    def take(at, unused):
        item = first + at
        take_item(devices, me, lax.rem(item, devices), item // devices, source, arrived, sems)
        return unused

    lax.fori_loop(0, count, take, 0)


def finish_groups(devices, me, total, source, arrived, sems):
    per_device = -(-total // devices)

    def wait(at, unused):
        slot, offset = at // devices, lax.rem(at, devices)
        other = lax.rem(me + offset, devices)

        @pl.when((slot * devices + me < total) & (offset != 0))
        def _():
            item_copy(devices, me, source.at[other, slot], arrived.at[me, slot], other, slot, sems)[0]().wait_send()

        return unused

    lax.fori_loop(0, devices * per_device, wait, 0)


def take_item(devices, me, other, slot, source, arrived, sems):
    @pl.when(other == me)
    def _():
        pltpu.make_async_copy(source.at[me, slot], arrived.at[me, slot], sems[2].at[slot]).wait()

    @pl.when(other != me)
    def _():
        item_copy(devices, me, source.at[other, slot], arrived.at[other, slot], other, slot, sems)[1]().wait_recv()


def mid_kernel(
    sizes, att_ref, hidden_ref, cot_ref, out_weight_ref, in_source, down_ref, vectors_ref,
    layer_ref, act_ref, gate_up_ref, normed_ref, attended_ref, branch_ref, residual_ref, items_ref, gain_out, rest_ref,
    arrived, stage, keep_gain, grad_act, in_weight_ref, in_sem, *sems,
):
    local_tokens, devices, total = sizes
    in_sems, out_sems = sems[:3], sems[3:]
    step = pl.program_id(0)
    me = lax.axis_index("seq")

    @pl.when(step == 0)
    def _():
        greet("seq", me, devices)
        pltpu.make_async_copy(in_source, in_weight_ref, in_sem).start()
        keep_gain[...] = jnp.zeros_like(keep_gain)
        pl.semaphore_wait(pltpu.get_barrier_semaphore(), devices - 1)

    together = hidden_ref.shape[0]
    group = together * PAIRS
    turn = lax.rem(step + 2, 4) if devices == 8 else step
    rows = together * local_tokens
    model = vectors_ref.shape[1]

    here_rows = pl.ds(pl.multiple_of(turn * rows, 128), rows)

    @pl.when(step == 0)
    def _():
        if devices == 8:
            for number in (2, 3, 0, 1):
                send_slots(me, number, att_ref, arrived, in_sems)
        else:
            send_group(devices, me, total, group, 0, att_ref, arrived, in_sems)
        every = cot_ref[...].reshape(grad_act.shape[0], model)
        for first in range(0, down_ref.shape[0], 512):
            grad_act[:, first : first + 512] = dot(every, down_ref[first : first + 512, :], NT)
        pltpu.make_async_copy(in_source, in_weight_ref, in_sem).wait()

    if devices == 8:
        for number in range(4):

            @pl.when(turn == number)
            def _():
                wait_slots(me, number, att_ref, arrived, in_sems, False)

    else:
        take_items(devices, me, step * group, group, att_ref, arrived, in_sems)

        @pl.when(step + 1 < pl.num_programs(0))
        def _():
            send_group(devices, me, total, group, step + 1, att_ref, arrived, in_sems)

    gathered = []
    for one in range(together):
        pieces = []
        for pair in range(PAIRS):
            item = (turn * together + one) * PAIRS + pair
            other, slot = lax.rem(item, devices), item // devices
            pieces.append(arrived[other, slot])
        gathered.append(jnp.concatenate(pieces, axis=1))
    attended = jnp.concatenate(gathered, axis=0)
    attended_ref[...] = attended.reshape(attended_ref.shape)
    residual = hidden_ref[...].reshape(rows, model) + dot(attended, out_weight_ref[...], NN)
    gain = vectors_ref[6:7, :]
    scale = lax.rsqrt(jnp.mean(residual * residual, axis=1, keepdims=True) + 1e-06)
    normed = (residual * scale * gain).astype(BF16)
    normed_ref[...] = normed.reshape(normed_ref.shape)
    cot = cot_ref[pl.ds(turn * together, together)].reshape(rows, model)
    hidden_units = down_ref.shape[0]
    chunk = 512
    layer = residual
    back = jnp.zeros_like(residual)
    for first in range(0, hidden_units, chunk):
        here = slice(first, first + chunk)
        there = slice(hidden_units + first, hidden_units + first + chunk)
        gate = dot(normed, in_weight_ref[:, here], NN)
        up = dot(normed, in_weight_ref[:, there], NN)
        grad = grad_act[here_rows, here]
        square = gate * gate
        inner = gate * (SQRT_2_OVER_PI + (SQRT_2_OVER_PI * 0.044715) * square)
        curve = jnp.tanh(inner)
        half_plus = 0.5 + 0.5 * curve
        smooth = gate * half_plus
        slope = half_plus + (0.5 * gate) * (1.0 - curve * curve) * (SQRT_2_OVER_PI + (3 * SQRT_2_OVER_PI * 0.044715) * square)
        act = (smooth * up).astype(BF16)
        grad_gate = (grad * up * slope).astype(BF16)
        grad_up = (grad * smooth).astype(BF16)
        act_ref[:, :, here] = act.reshape(together, local_tokens, chunk)
        gate_up_ref[:, :, here] = grad_gate.reshape(together, local_tokens, chunk)
        gate_up_ref[:, :, there] = grad_up.reshape(together, local_tokens, chunk)
        layer = layer + dot(act, down_ref[here, :], NN)
        back = back + dot(grad_gate, in_weight_ref[:, here], NT) + dot(grad_up, in_weight_ref[:, there], NT)
    layer_ref[...] = layer.reshape(layer_ref.shape)
    weighted = gain * back
    inner_mean = jnp.mean(residual * weighted, axis=1, keepdims=True)
    grad_residual = cot.astype(F32) + scale * weighted - residual * (scale * scale * scale * inner_mean)
    residual_ref[...] = grad_residual.reshape(residual_ref.shape)
    branch = grad_residual.astype(BF16)
    branch_ref[...] = branch.reshape(branch_ref.shape)
    grad_attended = dot(branch, out_weight_ref[...], NT).astype(BF16)
    for one in range(together):
        for pair in range(PAIRS):
            item = (turn * together + one) * PAIRS + pair
            other, slot = lax.rem(item, devices), item // devices
            stage[other, slot] = grad_attended[one * local_tokens : (one + 1) * local_tokens, pair * 128 : pair * 128 + 128]
    keep_gain[...] += jnp.sum((back * residual * scale).reshape(rows // 8, 8, model), axis=0)
    gain_out[...] = jnp.sum(keep_gain[...], axis=0, keepdims=True)
    if devices == 8:
        @pl.when(step < 2)
        def _():
            send_back(me, turn, stage, items_ref, out_sems)

        @pl.when(step == 3)
        def _():
            for number in range(4):
                wait_slots(me, number, att_ref, arrived, in_sems, True)
            finish_half(me, stage, items_ref, out_sems)
            rest_ref[...] = stage[:, 0:3]

        return
    send_items(devices, me, step * group, group, stage, items_ref, out_sems)

    @pl.when(step == pl.num_programs(0) - 1)
    def _():
        finish_groups(devices, me, total, att_ref, arrived, in_sems)
        finish_sends(devices, me, total, lambda other, slot: stage.at[other, slot], lambda other, slot: items_ref.at[me, slot], out_sems)
        finish_receives(devices, me, total, lambda other, slot: stage.at[other, slot], lambda other, slot: items_ref.at[other, slot], out_sems)


def back_kernel(
    sizes, custom, one_ref, two_ref, hidden_ref, residual_ref, conv_ref, mix_ref, share_ref, ids_ref, weight_source,
    table_ref, vectors_ref, bias_ref, bias_hot_ref, gain_two_ref, *refs,
):
    local_tokens, window, devices = sizes
    step = pl.program_id(0)
    last = step == pl.num_programs(0) - 1
    me = lax.axis_index("seq")
    plane = lax.axis_index("dp")
    model = vectors_ref.shape[1]
    if custom:
        normed_ref, across_ref, planes_ref = refs[:3]
        block, qkv_out, in_out, down_out, weight_out = refs[3:8]
        refs = refs[8:]
    else:
        block, flat_out, refs = refs[0], refs[1], refs[2:]
    masks, permuted, tap_sums, keep_gain, keep_score, weight_ref, weight_sem = refs[:7]
    refs = refs[7:]
    small = SmallSums(block, refs[:4], refs[4:10])
    refs = refs[10:]

    @pl.when(step == 0)
    def _():
        pltpu.make_async_copy(weight_source, weight_ref, weight_sem).start()
        greet("seq", me, devices)
        greet("dp", plane, small.along)
        keep_gain[...] = jnp.zeros_like(keep_gain)
        keep_score[...] = jnp.zeros_like(keep_score)
        tap_sums[...] = jnp.zeros_like(tap_sums)
        pl.semaphore_wait(pltpu.get_barrier_semaphore(), devices + small.along - 2)

    half = one_ref.shape[1]

    def block_of(item):
        other, slot = lax.rem(item, devices), item // devices
        if isinstance(item, int):
            return (one_ref if slot < half else two_ref)[other, slot % half]
        return jnp.where(slot < half, one_ref[other, jnp.minimum(slot, half - 1)], two_ref[other, jnp.maximum(slot - half, 0)])

    if custom:
        reduce = WeightSums(normed_ref, across_ref, planes_ref, block_of, refs)

        @pl.when(step == 0)
        def _():
            reduce.begin()
            reduce.late()

        @pl.when(step == 2)
        def _():
            reduce.late_one()

        @pl.when(step == 3)
        def _():
            reduce.in_three()
            reduce.rest_two()

    @pl.when(step == 0)
    def _():
        block_masks(masks, me * 2 * local_tokens, devices * 2 * local_tokens)
        pltpu.make_async_copy(weight_source, weight_ref, weight_sem).wait()
        permute_weight(weight_ref, permuted)

    together = hidden_ref.shape[0]
    rows = together * local_tokens
    projected = jnp.concatenate(
        [
            jnp.concatenate([block_of((step * together + one) * PAIRS + pair) for pair in range(PAIRS)], axis=1)
            for one in range(together)
        ],
        axis=0,
    )
    if not custom:
        flat_out[...] = projected.reshape(flat_out.shape)
    width = masks.shape[3]
    grad_normed = dot(projected, permuted[...], NT)
    hidden = hidden_ref[...].reshape(rows, model)
    gain = vectors_ref[5:6, :]
    score = vectors_ref[7:8, :]
    scale = lax.rsqrt(jnp.mean(hidden * hidden, axis=1, keepdims=True) + 1e-06)
    weighted = gain * grad_normed
    inner_mean = jnp.mean(hidden * weighted, axis=1, keepdims=True)
    grad_hidden = residual_ref[...].reshape(rows, model) + scale * weighted - hidden * (scale * scale * scale * inner_mean)
    keep_gain[...] += jnp.sum((grad_normed * hidden * scale).reshape(rows // 8, 8, model), axis=0)
    high_all, low_all = split_two(grad_hidden)
    vector = jnp.broadcast_to(score.astype(BF16), (local_tokens, model))
    row16 = lax.broadcasted_iota(jnp.int32, (16, width), 0)
    slopes = []
    for one in range(together):
        if custom and one == 1:

            @pl.when(step == 1)
            def _():
                reduce.in_two()

            @pl.when(last)
            def _():
                reduce.late_two()

        own = slice(one * local_tokens, (one + 1) * local_tokens)
        high, low = high_all[own], low_all[own]
        conv = conv_ref[one]
        cross = 0.5 * (dot(high, conv, NT) + dot(low, conv, NT))
        kept = share_ref[one]
        total = jnp.zeros((local_tokens, width), F32)
        for side in range(2):
            shares = [kept[:, 4 * side + k : 4 * side + k + 1] for k in range(4)]
            grads = [jnp.sum(masks[side, k] * cross, axis=1, keepdims=True) for k in range(4)]
            mean = sum(share * grad for share, grad in zip(shares, grads))
            for k in range(4):
                total = total + (shares[k] * (grads[k] - mean)) * masks[side, k]
        column = jnp.sum(total, axis=0, keepdims=True)
        column_high, column_low = split_two(column)
        column_rows = jnp.where(row16 == 0, column_high.astype(F32), jnp.where(row16 == 1, column_low.astype(F32), 0.0)).astype(BF16)
        keep_score[...] += dot(column_rows, conv, NN)
        left = jnp.concatenate([mix_ref[one], total.astype(BF16)], axis=0)
        right = jnp.concatenate([high, vector], axis=0)
        slopes.append(dot(left, right, TN)[0:window].astype(BF16))
    slope = jnp.concatenate(slopes, axis=0)
    row = lax.broadcasted_iota(jnp.int32, (SMALL_ROWS, window), 0).astype(F32)
    for tap in range(5):
        hot = jnp.concatenate(
            [jnp.where(ids_ref[one, 4 - tap : 5 - tap, 0:window] == row, 1.0, 0.0).astype(BF16) for one in range(together)], axis=1
        )
        tap_sums[tap] += dot(hot, slope, NN)

    @pl.when(last)
    def _():
        table_grad = jnp.zeros((SMALL_ROWS, model), F32)
        table = table_ref[...].astype(F32)
        place = lax.broadcasted_iota(jnp.int32, (SMALL_ROWS, model), 0)
        extra = []
        for tap in range(5):
            sums = tap_sums[tap]
            table_grad = table_grad + vectors_ref[tap : tap + 1, :] * sums
            extra.append(jnp.sum(sums[0 : table.shape[0]] * table, axis=0, keepdims=True))
        extra.append(jnp.sum(keep_gain[...], axis=0, keepdims=True))
        extra.append(jnp.sum(keep_score[...], axis=0, keepdims=True))
        extra.append(gain_two_ref[...])
        for index, value in enumerate(extra):
            table_grad = jnp.where(place == 259 + index, value, table_grad)
        block[...] = table_grad
        heads = jnp.zeros((16, 128), F32)
        head_row = lax.broadcasted_iota(jnp.int32, (16, 128), 0)
        for slot in range(bias_ref.shape[0]):
            first, second = split_two(bias_ref[slot])
            sums = dot(first, bias_hot_ref[...], NN) + dot(second, bias_hot_ref[...], NN)
            pair = lax.rem(slot * devices + me, PAIRS)
            heads = heads + jnp.where(head_row == 2 * pair, sums[0:1], 0.0) + jnp.where(head_row == 2 * pair + 1, sums[1:2], 0.0)
        block[272:288, 0:128] = heads
        small.pack()
        small.one_start()
        small.one_middle()
        small.one_finish()
        if custom:
            reduce.late_three()
            reduce.finish_rest(down_out)
        small.two_finish()
        small.three_finish()
        if custom:
            reduce.finish_in(in_out, weight_out)
            reduce.finish_late(qkv_out)
        small.four_finish()


def finish_kernel(block, *refs):
    refs = list(refs)
    count = (len(refs) - 6) // 2
    for source, target in zip(refs[:count], refs[count : 2 * count]):
        target[...] = source[...]
    table_out, taps_out, one_out, score_out, two_out, bias_out = refs[2 * count :]
    table_out[...] = block[0:259, :]
    taps_out[...] = block[259:264, :]
    one_out[...] = block[264, :]
    score_out[...] = block[265, :]
    two_out[...] = block[266, :]
    bias_out[...] = block[272:284, 0:32]


def call_finish(block, sums):
    model = block.shape[1]
    shape = lambda *dims: jax.ShapeDtypeStruct(dims, F32)
    return pl.pallas_call(
        finish_kernel,
        out_shape=[shape(*x.shape) for x in sums] + [shape(259, model), shape(5, model), shape(model), shape(model), shape(model), shape(12, 32)],
        compiler_params=pltpu.CompilerParams(vmem_limit_bytes=VMEM_LIMIT),
        name="finish",
    )(block, *sums)


VMEM_LIMIT = 60 * 2**20
TOGETHER = 2


def item_sems(devices, per_device):
    dma = pltpu.SemaphoreType.DMA
    if devices == 8:
        return [dma((4,)), dma((4,)), dma((4,))]
    return [dma((devices, per_device)), dma((devices, per_device)), dma((per_device,))]


def whole(*shape):
    return pl.BlockSpec(shape, lambda s, *_: (0,) * len(shape), pipeline_mode=pl.Buffered(1))


def part(*shape):
    return pl.BlockSpec(shape, lambda s, *_: (s,) + (0,) * (len(shape) - 1))


ANYWHERE = pl.BlockSpec(memory_space=pl.ANY)


def remote_params(number):
    return pltpu.CompilerParams(vmem_limit_bytes=VMEM_LIMIT, collective_id=number, has_side_effects=True)


def call_front(lengths, ids, table, weight, vectors, devices, per_device):
    sequences, local_bytes = ids.shape
    local_tokens = local_bytes // 2
    window = local_bytes + 16
    width = -(-window // 128) * 128
    model = weight.shape[0]
    return pl.pallas_call(
        functools.partial(front_kernel, (local_tokens, window, devices, sequences * PAIRS)),
        grid=(sequences,),
        in_specs=[pl.BlockSpec(memory_space=pltpu.SMEM), whole(*ids.shape), whole(*table.shape), ANYWHERE, whole(*vectors.shape)],
        out_specs=[
            part(1, local_tokens, model),
            part(1, local_tokens, model),
            part(1, width, model),
            part(1, local_tokens, width),
            part(1, local_tokens, 128),
            part(1, 8, local_bytes + 256),
            ANYWHERE,
        ],
        scratch_shapes=[
            pltpu.VMEM((2, 4, local_tokens, width), F32),
            pltpu.VMEM((1, 2, width, model), BF16),
            pltpu.VMEM(weight.shape, BF16),
            pltpu.VMEM((devices, per_device, local_tokens, 384), BF16),
            pltpu.VMEM((5, VPAD, model), BF16),
            pltpu.VMEM((sequences, 128), jnp.int32),
            pltpu.VMEM((sequences, 128), jnp.int32),
            pltpu.VMEM((sequences, local_bytes + 256), F32),
            pltpu.SemaphoreType.DMA((4,)),
            pltpu.VMEM(weight.shape, BF16),
            pltpu.SemaphoreType.DMA,
        ]
        + item_sems(devices, per_device),
        out_shape=[
            jax.ShapeDtypeStruct((sequences, local_tokens, model), F32),
            jax.ShapeDtypeStruct((sequences, local_tokens, model), BF16),
            jax.ShapeDtypeStruct((sequences, width, model), BF16),
            jax.ShapeDtypeStruct((sequences, local_tokens, width), BF16),
            jax.ShapeDtypeStruct((sequences, local_tokens, 128), F32),
            jax.ShapeDtypeStruct((sequences, 8, local_bytes + 256), F32),
            jax.ShapeDtypeStruct((devices, per_device, local_tokens, 384), BF16),
        ],
        compiler_params=remote_params(3),
        cost_estimate=pl.CostEstimate(flops=5 * 10**10, bytes_accessed=2 * 10**7, transcendentals=10**5),
        name="front",
    )(lengths, ids, table, weight, vectors)


def call_mid(att, hidden, cot, out_weight, in_weight, down_weight, vectors):
    devices, per_device, local_tokens, unused = att.shape
    sequences, unused, model = hidden.shape
    hidden_units = down_weight.shape[0]
    fast = devices == 8
    rows = lambda lanes: pl.BlockSpec((TOGETHER, local_tokens, lanes), lambda s: (lax.rem(s + 2, 4) if fast else s, 0, 0))
    shape = (devices, per_device // 2 if fast else per_device, local_tokens, 128)
    rest = shape if fast else (1, 1, 8, 128)
    full = lambda lanes, kind: jax.ShapeDtypeStruct((sequences, local_tokens, lanes), kind)
    return pl.pallas_call(
        functools.partial(mid_kernel, (local_tokens, devices, sequences * PAIRS)),
        grid=(sequences // TOGETHER,),
        in_specs=[
            ANYWHERE,
            rows(model),
            whole(*cot.shape),
            whole(*out_weight.shape),
            ANYWHERE,
            whole(*down_weight.shape),
            whole(*vectors.shape),
        ],
        out_specs=[
            rows(model),
            rows(hidden_units),
            rows(2 * hidden_units),
            rows(model),
            rows(model),
            rows(model),
            rows(model),
            ANYWHERE,
            whole(1, model),
            whole(*rest),
        ],
        scratch_shapes=[pltpu.VMEM(att.shape, BF16), pltpu.VMEM(att.shape, BF16), pltpu.VMEM((8, model), F32), pltpu.VMEM((sequences * local_tokens, hidden_units), F32),
            pltpu.VMEM(in_weight.shape, BF16),
            pltpu.SemaphoreType.DMA,
        ]
        + item_sems(devices, per_device)
        + item_sems(devices, per_device),
        out_shape=[
            full(model, F32),
            full(hidden_units, BF16),
            full(2 * hidden_units, BF16),
            full(model, BF16),
            full(model, BF16),
            full(model, BF16),
            full(model, F32),
            jax.ShapeDtypeStruct(shape, BF16),
            jax.ShapeDtypeStruct((1, model), F32),
            jax.ShapeDtypeStruct(rest, BF16),
        ],
        compiler_params=remote_params(4),
        cost_estimate=pl.CostEstimate(flops=5 * 10**10, bytes_accessed=4 * 10**7, transcendentals=10**6),
        name="middle",
    )(att, hidden, cot, out_weight, in_weight, down_weight, vectors)


def call_back(custom, one, two, hidden, residual, conv, mix, share, ids, weight, table, vectors, bias_rows, gain_two, along, extra):
    devices, unused, local_tokens, unused = one.shape
    sequences, unused, model = hidden.shape
    width = conv.shape[1]
    window = 2 * local_tokens + 16
    bias_hot = jnp.pad(near_one_hot(), ((0, 0), (0, 96))).astype(BF16)
    out_specs = [whole(SMALL_ROWS, model)]
    out_shape = [jax.ShapeDtypeStruct((SMALL_ROWS, model), F32)]
    scratch = []
    specs = []
    if custom:
        specs = [whole(*x.shape) for x in extra]
        sums = [(96, 576), (96, 1024), (192, 256), (96, 192)]
        out_specs = out_specs + [whole(*shape) for shape in sums]
        out_shape = out_shape + [jax.ShapeDtypeStruct(shape, F32) for shape in sums]
        scratch = weight_scratch(model, sequences * local_tokens)
    else:
        out_specs = out_specs + [part(TOGETHER, local_tokens, PAIRS * 384)]
        out_shape = out_shape + [jax.ShapeDtypeStruct((sequences, local_tokens, PAIRS * 384), BF16)]
    return pl.pallas_call(
        functools.partial(back_kernel, (local_tokens, window, devices), custom),
        grid=(sequences // TOGETHER,),
        in_specs=[
            whole(*one.shape),
            whole(*two.shape),
            part(TOGETHER, local_tokens, model),
            part(TOGETHER, local_tokens, model),
            part(TOGETHER, width, model),
            part(TOGETHER, local_tokens, width),
            part(TOGETHER, local_tokens, 128),
            part(TOGETHER, 8, ids.shape[2]),
            ANYWHERE,
            whole(*table.shape),
            whole(*vectors.shape),
            whole(*bias_rows.shape),
            whole(*bias_hot.shape),
            whole(1, model),
        ]
        + specs,
        out_specs=out_specs,
        scratch_shapes=[
            pltpu.VMEM((2, 4, local_tokens, width), F32),
            pltpu.VMEM(weight.shape, BF16),
            pltpu.VMEM((5, SMALL_ROWS, model), F32),
            pltpu.VMEM((8, model), F32),
            pltpu.VMEM((16, model), F32),
            pltpu.VMEM(weight.shape, BF16),
            pltpu.SemaphoreType.DMA,
        ]
        + small_scratch(devices, along)
        + scratch,
        out_shape=out_shape,
        compiler_params=remote_params(5),
        cost_estimate=pl.CostEstimate(flops=10**11, bytes_accessed=2 * 10**7, transcendentals=10**5),
        name="back",
    )(one, two, hidden, residual, conv, mix, share, ids, weight, table, vectors, bias_rows, bias_hot, gain_two, *extra)


IN_ROWS = 8 * 96 + 2 * 96
REST_ROWS = 2 * 192
LATE_ROWS = 5 * 96


def meet_sibling(core):
    barrier = pltpu.get_barrier_semaphore()
    sibling = lax.axis_index("seq") + 1 - 2 * core
    pl.semaphore_signal(barrier, inc=1, device_id={"seq": sibling}, device_id_type=pl.DeviceIdType.MESH)
    pl.semaphore_wait(barrier, 1)


def to_sibling(core, source, target, send_sem, recv_sem):
    sibling = lax.axis_index("seq") + 1 - 2 * core
    return pltpu.make_async_remote_copy(
        src_ref=source, dst_ref=target, send_sem=send_sem, recv_sem=recv_sem,
        device_id={"seq": sibling}, device_id_type=pl.DeviceIdType.MESH,
    )


def spread_rows(core, source, lanes, keep_ref, send_ref, index_of):
    for chip in range(4):
        for other, ref in ((0, keep_ref), (1, send_ref)):
            device = 2 * chip + lax.rem(core + other, 2)
            rows = pl.ds(pl.multiple_of(device * 96, 32), 96)
            ref[index_of(chip)] = source[rows, lanes]


def early_kernel(
    act_ref, cot_ref, normed_ref, gate_up_ref, attended_ref, branch_ref, after, keep_in, keep_rest,
    other_in, got_in, other_rest, got_rest, cot_t, normed_t, result, send_in, recv_in, send_down, recv_down, send_out, recv_out,
):
    step = pl.program_id(0)
    core = lax.rem(lax.axis_index("seq"), 2)
    model = cot_t.shape[0]
    tokens = cot_t.shape[1]
    out_rows = pl.ds(768, 192)
    out_copy = to_sibling(core, other_in.at[:, :, out_rows], got_in.at[:, :, out_rows], send_out, recv_out)

    def in_copy(at):
        rows = pl.ds(pl.multiple_of(384 * lax.rem(at, 2), 384), 384)
        return to_sibling(core, other_in.at[:, at // 2, rows], got_in.at[:, at // 2, rows], send_in.at[at], recv_in.at[at])

    def down_copy(chip):
        return to_sibling(core, other_rest.at[:, chip], got_rest.at[:, chip], send_down.at[chip], recv_down.at[chip])

    @pl.when(step == 0)
    def _():
        meet_sibling(core)
        cot_t[...] = cot_ref[...].reshape(tokens, model).T
        normed_t[...] = attended_ref[...].reshape(tokens, model).T
        for first in range(0, model, 256):
            result[:, 0:256] = dot(normed_t[...], branch_ref[:, :, first : first + 256].reshape(tokens, 256), NN).astype(BF16)
            for half in range(2):
                tile = first // 128 + half
                for column, slot in {0: ((0, 0),), 1: ((0, 1), (1, 0)), 2: ((1, 1),), 3: ((2, 0),), 4: ((2, 1), (3, 0)), 5: ((3, 1),)}[tile]:
                    rows = slice(768 + 96 * slot, 864 + 96 * slot)
                    spread_rows(core, result, slice(128 * half, 128 * half + 128), keep_in, other_in, lambda chip: (chip, column, rows))
        normed_t[...] = normed_ref[...].reshape(tokens, model).T

    result[...] = dot(normed_t[...], gate_up_ref[...].reshape(tokens, 512), NN).astype(BF16)
    column_at = step // 2
    for quarter in range(4):
        rows = pl.ds(pl.multiple_of((4 * lax.rem(step, 2) + quarter) * 96, 32), 96)
        spread_rows(core, result, slice(128 * quarter, 128 * quarter + 128), keep_in, other_in, lambda chip: (chip, column_at, rows))
    down = dot(cot_t[...], act_ref[...].reshape(tokens, 256), NN).astype(BF16)

    def put_down(ref):
        for column in range(4):
            for half in range(2):
                ref[column, step // 2, 192 * half : 192 * half + 192] = down[192 * column : 192 * column + 192, 128 * half : 128 * half + 128]

    @pl.when(lax.rem(step, 2) == core)
    def _():
        put_down(keep_rest)

    @pl.when(lax.rem(step, 2) != core)
    def _():
        put_down(other_rest)
        down_copy(step // 2).start()

    in_copy(step).start()

    @pl.when(step == 0)
    def _():
        out_copy.start()

    @pl.when(step == 7)
    def _():
        for at in range(8):
            in_copy(at).wait()
        out_copy.wait()
        for chip in range(4):
            down_copy(chip).wait()

        def add(at, unused):
            one, two = at // 4, lax.rem(at, 4)
            keep_in[one, two] = (keep_in[one, two].astype(F32) + got_in[one, two].astype(F32)).astype(BF16)
            keep_rest[one, two] = (keep_rest[one, two].astype(F32) + got_rest[one, two].astype(F32)).astype(BF16)
            return unused

        lax.fori_loop(0, 16, add, 0)


def call_early(act, cot, normed, gate_up, attended, branch, after):
    sequences, local_tokens, model = cot.shape
    tokens = sequences * local_tokens
    every = whole(sequences, local_tokens, model)
    shapes = [(4, 4, IN_ROWS, 128), (4, 4, REST_ROWS, 128)]
    dma = pltpu.SemaphoreType.DMA
    return pl.pallas_call(
        early_kernel,
        grid=(8,),
        in_specs=[
            pl.BlockSpec((sequences, local_tokens, 256), lambda s: (0, 0, s)),
            every,
            every,
            pl.BlockSpec((sequences, local_tokens, 512), lambda s: (0, 0, s)),
            every,
            every,
            ANYWHERE,
        ],
        out_specs=[whole(*shape) for shape in shapes],
        scratch_shapes=[
            pltpu.VMEM(shapes[0], BF16),
            pltpu.VMEM(shapes[0], BF16),
            pltpu.VMEM(shapes[1], BF16),
            pltpu.VMEM(shapes[1], BF16),
            pltpu.VMEM((model, tokens), BF16),
            pltpu.VMEM((model, tokens), BF16),
            pltpu.VMEM((model, 512), BF16),
            dma((8,)), dma((8,)), dma((4,)), dma((4,)), dma, dma,
        ],
        out_shape=[jax.ShapeDtypeStruct(shape, BF16) for shape in shapes],
        compiler_params=pltpu.CompilerParams(vmem_limit_bytes=VMEM_LIMIT, collective_id=1, has_side_effects=True),
        cost_estimate=pl.CostEstimate(flops=11 * 10**9, bytes_accessed=3 * 10**7, transcendentals=0),
        name="early_gradients",
    )(act, cot, normed, gate_up, attended, branch, after)


class ChipSums:
    def __init__(self, source, buffers, sems, chip, core):
        self.source, self.first, self.relay, self.second = (source,) + tuple(buffers)
        self.send, self.recv = sems
        self.chip, self.core = chip, core
        self.beside = chip + 1 - 2 * lax.rem(chip, 2)
        self.above = lax.rem(chip + 2, 4)

    def copy(self, other, source, target, number):
        return pltpu.make_async_remote_copy(
            src_ref=source, dst_ref=target, send_sem=self.send.at[number], recv_sem=self.recv.at[number],
            device_id={"seq": 2 * other + self.core}, device_id_type=pl.DeviceIdType.MESH,
        )

    def ways(self):
        return ((0, self.beside, self.above), (1, self.above, self.beside))

    def one(self):
        made = []
        for way, near, other in self.ways():
            columns = pl.ds(2 * way, 2)
            made.append(self.copy(near, self.source.at[near, columns], self.first.at[way, 0], 2 * way))
            made.append(self.copy(near, self.source.at[3 - self.chip, columns], self.first.at[way, 1], 2 * way + 1))
        return made

    def two(self):
        return [self.copy(other, self.relay.at[way], self.second.at[way], 4 + way) for way, near, other in self.ways()]

    def start(self):
        for copy in self.one():
            copy.start()

    def middle(self):
        for copy in self.one():
            copy.wait()
        for way, near, other in self.ways():
            for at in range(2):
                total = self.source[other, 2 * way + at].astype(F32) + self.first[way, 1, at].astype(F32)
                self.relay[way, at] = total.astype(BF16)
        for copy in self.two():
            copy.start()

    def finish(self, target):
        for copy in self.two():
            copy.wait()
        for way in range(2):
            for at in range(2):
                total = self.source[self.chip, 2 * way + at].astype(F32) + self.first[way, 0, at].astype(F32)
                target[2 * way + at] = (total + self.second[way, at].astype(F32)).astype(BF16)


def chip_scratch(rows):
    return [pltpu.VMEM((2, 2, 2, rows, 128), BF16), pltpu.VMEM((2, 2, rows, 128), BF16), pltpu.VMEM((2, 2, rows, 128), BF16)]


class WeightSums:
    def __init__(self, normed_ref, across_ref, planes_ref, block_of, refs):
        self.normed, self.across, self.planes, self.block_of = normed_ref, across_ref, planes_ref, block_of
        (
            self.in_sum, self.in_got, self.rest_got, self.rest_sum, self.rest_chips, self.normed_t, self.result,
            self.keep, self.other, self.got, self.late_sum, self.late_got,
        ) = refs[:12]
        (
            self.send_in, self.recv_in, self.send_rest, self.recv_rest, self.send_chip, self.recv_chip,
            self.send_a, self.recv_a, self.send_c, self.recv_c,
        ) = refs[18:28]
        self.me, self.plane = lax.axis_index("seq"), lax.axis_index("dp")
        self.core, self.chip = lax.rem(self.me, 2), self.me // 2
        self.in_chips = ChipSums(across_ref, refs[12:15], refs[28:30], self.chip, self.core)
        self.late_chips = ChipSums(self.keep, refs[15:18], refs[30:32], self.chip, self.core)

    def to_plane(self, offset, source, target, send, recv):
        return pltpu.make_async_remote_copy(
            src_ref=source, dst_ref=target, send_sem=send.at[offset - 1], recv_sem=recv.at[offset - 1],
            device_id={"dp": lax.rem(self.plane + offset, 4)}, device_id_type=pl.DeviceIdType.MESH,
        )

    def rest_plane(self, offset):
        peer = lax.rem(self.plane + offset, 4)
        return self.to_plane(offset, self.planes.at[peer], self.rest_got.at[offset - 1], self.send_rest, self.recv_rest)

    def in_plane(self, offset):
        peer = lax.rem(self.plane + offset, 4)
        return self.to_plane(offset, self.in_sum.at[peer], self.in_got.at[offset - 1], self.send_in, self.recv_in)

    def late_plane(self, offset):
        peer = lax.rem(self.plane + offset, 4)
        return self.to_plane(offset, self.late_sum.at[peer], self.late_got.at[offset - 1], self.send_c, self.recv_c)

    def rest_chip(self, offset):
        other = lax.rem(self.chip + offset, 4)
        return pltpu.make_async_remote_copy(
            src_ref=self.rest_sum.at[other], dst_ref=self.rest_chips.at[offset - 1],
            send_sem=self.send_chip.at[offset - 1], recv_sem=self.recv_chip.at[offset - 1],
            device_id={"seq": 2 * other + self.core}, device_id_type=pl.DeviceIdType.MESH,
        )

    def late_core(self, column):
        return to_sibling(self.core, self.other.at[:, column], self.got.at[:, column], self.send_a.at[column], self.recv_a.at[column])

    def begin(self):
        self.in_chips.start()
        for offset in (1, 2, 3):
            self.rest_plane(offset).start()

    def late(self):
        sequences, count, model = self.normed.shape
        self.normed_t[...] = self.normed[...].reshape(sequences * count, model).T
        low = lax.broadcasted_iota(jnp.int32, (model, 128), 1) < 64
        for pair in range(PAIRS):
            rows = jnp.concatenate([self.block_of(one * PAIRS + pair) for one in range(sequences)], axis=0)
            sums = dot(self.normed_t[...], rows, NN)
            query, key, value = sums[:, 0:128], pltpu.roll(sums[:, 128:256], 64, 1), sums[:, 256:384]
            self.result[3 * pair] = jnp.where(low, query, key).astype(BF16)
            self.result[3 * pair + 1] = jnp.where(low, value, query).astype(BF16)
            self.result[3 * pair + 2] = jnp.where(low, key, value).astype(BF16)
        for tile in range(3 * PAIRS):
            within = tile % 9
            spots = [(2 * (tile // 9), within)] if within <= 4 else []
            spots += [(2 * (tile // 9) + 1, within - 4)] if within >= 4 else []
            for column, slot in spots:
                rows_at = slice(96 * slot, 96 * slot + 96)
                spread_rows(self.core, self.result.at[tile], slice(0, 128), self.keep, self.other, lambda chip: (chip, column, rows_at))
        for column in range(4):
            self.late_core(column).start()

    def late_one(self):
        for column in range(4):
            self.late_core(column).wait()
            for at in range(4):
                self.keep[at, column] = (self.keep[at, column].astype(F32) + self.got[at, column].astype(F32)).astype(BF16)
        self.late_chips.start()

    def in_two(self):
        self.in_chips.middle()

    def late_two(self):
        self.late_chips.middle()

    def rest_two(self):
        for offset in (1, 2, 3):
            self.rest_plane(offset).wait()
        for chip in range(4):
            total = self.planes[self.plane, chip].astype(F32)
            for slot in range(3):
                total = total + self.rest_got[slot, chip].astype(F32)
            self.rest_sum[chip] = total.astype(BF16)
        for offset in (1, 2, 3):
            self.rest_chip(offset).start()

    def in_three(self):
        self.in_chips.finish(self.in_sum)
        for offset in (1, 2, 3):
            self.in_plane(offset).start()

    def late_three(self):
        self.late_chips.finish(self.late_sum)
        for offset in (1, 2, 3):
            self.late_plane(offset).start()

    def joined(self, block, columns):
        odd = lax.rem(self.plane, 2) == 1
        count = block.shape[1]
        return jnp.where(odd, pltpu.roll(block, count - 64, 1), block)[:, :columns]

    def finish_rest(self, down_out):
        total = self.rest_sum[self.chip].astype(F32)
        for offset in (1, 2, 3):
            self.rest_chip(offset).wait()
            total = total + self.rest_chips[offset - 1].astype(F32)
        down_out[:, 0:128] = total[0:192]
        down_out[:, 128:256] = total[192:384]

    def finish_in(self, in_out, weight_out):
        total = self.in_sum[self.plane].astype(F32)
        for offset in (1, 2, 3):
            self.in_plane(offset).wait()
            total = total + self.in_got[offset - 1].astype(F32)
        for tile in range(8):
            in_out[:, 128 * tile : 128 * tile + 128] = total[96 * tile : 96 * tile + 96]
        weight_out[...] = self.joined(jnp.concatenate([total[768:864], total[864:960]], axis=1), 192)

    def finish_late(self, qkv_out):
        total = self.late_sum[self.plane].astype(F32)
        for offset in (1, 2, 3):
            self.late_plane(offset).wait()
            total = total + self.late_got[offset - 1].astype(F32)
        qkv_out[...] = self.joined(jnp.concatenate([total[96 * k : 96 * k + 96] for k in range(5)], axis=1), 576)


def weight_scratch(model, tokens):
    dma = pltpu.SemaphoreType.DMA
    late = (4, 4, LATE_ROWS, 128)
    return (
        [
            pltpu.VMEM((4, IN_ROWS, 128), BF16),
            pltpu.VMEM((3, IN_ROWS, 128), BF16),
            pltpu.VMEM((3, 4, REST_ROWS, 128), BF16),
            pltpu.VMEM((4, REST_ROWS, 128), BF16),
            pltpu.VMEM((3, REST_ROWS, 128), BF16),
            pltpu.VMEM((model, tokens), BF16),
            pltpu.VMEM((3 * PAIRS, model, 128), BF16),
            pltpu.VMEM(late, BF16),
            pltpu.VMEM(late, BF16),
            pltpu.VMEM(late, BF16),
            pltpu.VMEM((4, LATE_ROWS, 128), BF16),
            pltpu.VMEM((3, LATE_ROWS, 128), BF16),
        ]
        + chip_scratch(IN_ROWS)
        + chip_scratch(LATE_ROWS)
        + [dma((3,)), dma((3,)), dma((3,)), dma((3,)), dma((3,)), dma((3,)), dma((4,)), dma((4,)), dma((3,)), dma((3,))]
        + [dma((6,)), dma((6,)), dma((6,)), dma((6,))]
    )


SMALL_ROWS = 288


class SmallSums:
    def __init__(self, block, buffers, sems):
        self.block = block
        self.held, self.got_seq, self.planes, self.whole = buffers
        self.sems = sems
        self.me, self.plane = lax.axis_index("seq"), lax.axis_index("dp")
        self.across, self.along = self.held.shape[0], self.held.shape[1]
        self.paired = self.across == 8
        self.core, self.chip = lax.rem(self.me, 2), self.me // 2
        self.mine = self.across // 2 * self.core + self.chip

    def places(self):
        half = self.held.shape[2] // 2
        units = SMALL_ROWS // half
        tiles = self.block.shape[1] // 128
        for at in range(2 * self.along * self.across):
            spot = (at // (2 * self.along), at // 2 % self.along, slice((at % 2) * half, (at % 2) * half + half))
            tile, unit = at // units, at % units
            if tile < tiles:
                yield spot, (slice(unit * half, unit * half + half), slice(128 * tile, 128 * tile + 128))
            else:
                yield spot, None

    def pack(self):
        for spot, source in self.places():
            if source is None:
                self.held[spot] = jnp.zeros((self.held.shape[2] // 2, 128), BF16)
            else:
                self.held[spot] = self.block[source].astype(BF16)

    def copies(self, axis, source, target, number):
        here, count = {"seq": (self.me, self.across), "chip": (self.chip, self.across // 2), "dp": (self.plane, self.along)}[axis]
        send, recv = self.sems[2 * number], self.sems[2 * number + 1]
        made = []
        for step in range(1, count):
            peer = lax.rem(here + step, count)
            device = {"seq": 2 * peer + self.core} if axis == "chip" else {axis: peer}
            made.append(
                pltpu.make_async_remote_copy(
                    src_ref=source(peer), dst_ref=target(step - 1), send_sem=send.at[step - 1], recv_sem=recv.at[step - 1],
                    device_id=device, device_id_type=pl.DeviceIdType.MESH,
                )
            )
        for copy in made:
            copy.start()
        return made

    def sibling(self, source, target, number):
        made = [to_sibling(self.core, source, target, self.sems[2 * number].at[6], self.sems[2 * number + 1].at[6])]
        made[0].start()
        return made

    def one_start(self):
        if self.paired:
            half = pl.ds(4 * (1 - self.core), 4)
            self.waiting = self.sibling(self.held.at[half], self.got_seq.at[pl.ds(3, 4)], 0)
            return
        self.waiting = self.copies("seq", lambda peer: self.held.at[peer], lambda slot: self.got_seq.at[slot], 0)

    def one_middle(self):
        if self.paired:
            for copy in self.waiting:
                copy.wait()
            for chip in range(4):
                at = 4 * self.core + chip
                self.held[at] = (self.held[at].astype(F32) + self.got_seq[3 + chip].astype(F32)).astype(BF16)
            self.waiting = self.copies("chip", lambda peer: self.held.at[4 * self.core + peer], lambda slot: self.got_seq.at[slot], 0)

    def one_finish(self):
        for copy in self.waiting:
            copy.wait()
        total = self.held[self.mine if self.paired else self.me].astype(F32)
        for slot in range(3 if self.paired else self.across - 1):
            total = total + self.got_seq[slot].astype(F32)
        self.planes[self.plane] = total.astype(BF16)
        self.waiting = self.copies("dp", lambda peer: self.planes.at[self.plane], lambda slot: self.planes.at[self.plane], 1)

    def two_finish(self):
        for copy in self.waiting:
            copy.wait()
        total = self.planes[0].astype(F32)
        for plane in range(1, self.along):
            total = total + self.planes[plane].astype(F32)
        own = self.mine if self.paired else self.me
        self.whole[own] = total.astype(BF16)
        self.waiting = self.copies("chip" if self.paired else "seq", lambda peer: self.whole.at[own], lambda slot: self.whole.at[own], 2)

    def three_finish(self):
        if self.paired:
            for copy in self.waiting:
                copy.wait()
            half = pl.ds(4 * self.core, 4)
            self.waiting = self.sibling(self.whole.at[half], self.whole.at[half], 2)

    def four_finish(self):
        for copy in self.waiting:
            copy.wait()
        for spot, target in self.places():
            if target is not None:
                self.block[target] = self.whole[spot].astype(F32)


def small_scratch(across, along):
    chunk = max(16, 2048 // (across * along))
    dma = lambda count: pltpu.SemaphoreType.DMA((count,))
    return [
        pltpu.VMEM((across, along, chunk, 128), BF16),
        pltpu.VMEM((across - 1, along, chunk, 128), BF16),
        pltpu.VMEM((along, along, chunk, 128), BF16),
        pltpu.VMEM((across, along, chunk, 128), BF16),
        dma(across - 1), dma(across - 1), dma(along - 1), dma(along - 1), dma(across - 1), dma(across - 1),
    ]


def body(
    byte_ids,
    lengths,
    byte_table,
    conv_kernel,
    score_vector,
    norm_gain_one,
    qkv_weight,
    bias_table,
    out_weight,
    norm_gain_two,
    in_weight,
    down_weight,
    cotangent,
):
    devices = lax.axis_size("seq")
    me = lax.axis_index("seq")
    sequences, local_bytes = byte_ids.shape
    local_tokens = local_bytes // 2
    total_bytes = local_bytes * devices
    vocab, model = byte_table.shape
    total = sequences * PAIRS
    per_device = -(-total // devices)
    place = jnp.reshape(me, (1,)).astype(jnp.int32)
    vectors = jnp.concatenate([conv_kernel, norm_gain_one[None, :], norm_gain_two[None, :], score_vector[None, :]], axis=0)
    rows = jnp.dot(near_one_hot(), bias_table, precision="highest").T.reshape(PAIRS, 2, NEAR)

    def exchange(items):
        return lax.all_to_all(items, "seq", split_axis=0, concat_axis=0, tiled=True)

    hidden, normed, conv, mix, share, ids_rows, received = call_front(lengths, byte_ids, byte_table, qkv_weight, vectors, devices, per_device)
    out, aug, cot = attention_forward(received, rows, lengths, place, cotangent)
    layer, act, gate_up, normed_two, attended, branch, grad_residual, grad_items, grad_gain_two, grad_rest = call_mid(
        out, hidden, cot, out_weight, in_weight, down_weight, vectors
    )
    along_count = lax.axis_size("dp")
    custom = devices == 8 and along_count == 4

    def scatter(grad):
        rows_own = lax.psum_scatter(grad, "seq", scatter_dimension=0, tiled=True)
        return lax.psum_scatter(rows_own, "dp", scatter_dimension=1, tiled=True).astype(F32)

    if not custom:
        summed_down = scatter(jnp.einsum("bti,btd->id", act, cot, preferred_element_type=F32).astype(BF16))
        summed_in = scatter(jnp.einsum("btd,bti->di", normed_two, gate_up, preferred_element_type=F32).astype(BF16))
        summed_out = scatter(jnp.einsum("btd,bte->de", attended, branch, preferred_element_type=F32).astype(BF16))
    half = per_device // 2
    grads_two, grads_one, at_two = (grad_items, exchange(grad_rest), 0) if devices == 8 else (grad_items, grad_items, half)
    dqkv_two, bias_two, layer_out = attention_backward(
        received, out, aug, grads_two, rows, lengths, place, layer, grad_gain_two, half, per_device - half, at_two
    )
    items_two = exchange(dqkv_two)
    dqkv_one, bias_one, unused = attention_backward(received, out, aug, grads_one, rows, lengths, place, None, bias_two, 0, half, 0)
    items_one = exchange(dqkv_one)
    bias_rows = jnp.concatenate([bias_one, bias_two], axis=0)
    if custom:
        in_chips, rest_planes = call_early(act, cot, normed_two, gate_up, attended, branch, items_two)
    extra = (normed, in_chips, rest_planes) if custom else ()
    results = call_back(
        custom, items_one, items_two, hidden, grad_residual, conv, mix, share, ids_rows, qkv_weight, byte_table, vectors, bias_rows, grad_gain_two, along_count, extra
    )
    if custom:
        summed_qkv, summed_in, summed_down, summed_out, *smalls = call_finish(results[0], results[1:])
        summed_down = summed_down.T
    else:
        smalls = call_finish(results[0], ())
        grad_qkv = jnp.einsum("btd,bte->de", normed, results[1], preferred_element_type=F32).astype(BF16)
        grad_qkv = jnp.swapaxes(grad_qkv.reshape(model, PAIRS, 3, 2, 64), 2, 3).reshape(model, PAIRS * 384)
        summed_qkv = scatter(grad_qkv)
    grad_table, grad_taps, grad_gain_one, grad_score, grad_gain_two, grad_bias = smalls
    return (
        layer_out,
        grad_table,
        grad_taps,
        grad_score,
        grad_gain_one,
        summed_qkv,
        grad_bias.T,
        summed_out,
        grad_gain_two,
        summed_in,
        summed_down,
    )


def solution(mesh):
    return jax.shard_map(
        body,
        mesh=mesh,
        in_specs=(
            P("dp", "seq"),
            P("dp"),
            P(),
            P(),
            P(),
            P(),
            P(),
            P(),
            P(),
            P(),
            P(),
            P(),
            P("dp", "seq", None),
        ),
        out_specs=(
            P("dp", "seq", None),
            P(),
            P(),
            P(),
            P(),
            P("seq", "dp"),
            P(),
            P("seq", "dp"),
            P(),
            P("seq", "dp"),
            P("seq", "dp"),
        ),
        check_vma=False,
    )
```
